32 devices in a mesh: dp: 8 (over z, x), mp: 4 (over y, core).
Axes of the slice: x: 2, y: 2, z: 4, core: 2. Of those that a mesh axis runs over, the one named last changes fastest.
Arguments:
- block_input: bfloat16 [1024, 1152], P('dp'), may hold values from -6 to 6
- cotangent: bfloat16 [1024, 1152], P('dp'), may hold values from -6 to 6
- segments: int32 [8, 128], P('dp'), may hold values from 0 to 7, never falling along the last dimension, each value on 1 to 64 neighbouring positions
- mixer_gain: float32 [1152], replicated, may hold values from 0.5 to 1.5
- feed_gain: float32 [1152], replicated, may hold values from 0.5 to 1.5
- query_matrix: bfloat16 [1152, 1024], P(None, 'mp'), may hold values from -0.1875 to 0.1875
- key_value_weight: bfloat16 [1152, 512], replicated, may hold values from -0.1875 to 0.1875
- output_matrix: bfloat16 [1024, 1152], P('mp'), may hold values from -0.75 to 0.75
- gate_up_weight: bfloat16 [1152, 2, 6912], P(None, None, 'mp'), may hold values from -0.1875 to 0.1875
- down_matrix: bfloat16 [6912, 1152], P('mp'), may hold values from -0.078125 to 0.078125
- query_adapter_inner: bfloat16 [2, 1152, 256], replicated, may hold values from -0.1875 to 0.1875
- query_adapter_outer: bfloat16 [2, 256, 1024], P(None, None, 'mp'), may hold values from -0.375 to 0.375
- key_value_inner: bfloat16 [2, 1152, 2, 256], replicated, may hold values from -0.1875 to 0.1875
- key_value_outer: bfloat16 [2, 2, 256, 256], replicated, may hold values from -0.375 to 0.375
- output_adapter_inner: bfloat16 [2, 1024, 256], P(None, 'mp'), may hold values from -0.75 to 0.75
- output_adapter_outer: bfloat16 [2, 256, 1152], replicated, may hold values from -0.375 to 0.375
- widen_inner_adapter: bfloat16 [2, 1152, 2, 256], replicated, may hold values from -0.1875 to 0.1875
- widen_outer_adapter: bfloat16 [2, 2, 256, 6912], P(None, None, None, 'mp'), may hold values from -0.375 to 0.375
- down_adapter_inner: bfloat16 [2, 6912, 256], P(None, 'mp'), may hold values from -0.078125 to 0.078125
- down_adapter_outer: bfloat16 [2, 256, 1152], replicated, may hold values from -0.375 to 0.375
Outputs:
- block_output: bfloat16 [1024, 1152], P('dp')
- input_grad: float32 [1024, 1152], P('dp')
- mixer_gain_grad: float32 [1152], P('dp')
- feed_gain_grad: float32 [1152], P('dp')
- query_weight_grad: float32 [1152, 1024], P('dp', 'mp')
- pair_weight_grad: float32 [1152, 512], P(('dp', 'mp'))
- output_weight_grad: float32 [1024, 1152], P('mp', 'dp')
- expand_weight_grad: float32 [1152, 2, 6912], P('dp', None, 'mp')
- shrink_weight_grad: float32 [6912, 1152], P('mp', 'dp')
- query_inner_grad: float32 [2, 1152, 256], P(None, ('dp', 'mp'))
- query_outer_grad: float32 [2, 256, 1024], P(None, 'dp', 'mp')
- pair_inner_grad: float32 [2, 1152, 2, 256], P(None, ('dp', 'mp'))
- pair_outer_grad: float32 [2, 2, 256, 256], P(None, None, ('dp', 'mp'))
- output_inner_grad: float32 [2, 1024, 256], P(None, 'mp', 'dp')
- output_outer_grad: float32 [2, 256, 1152], P(None, None, 'dp')
- expand_inner_grad: float32 [2, 1152, 2, 256], P(None, ('dp', 'mp'))
- expand_outer_grad: float32 [2, 2, 256, 6912], P(None, None, 'dp', 'mp')
- shrink_inner_grad: float32 [2, 6912, 256], P(None, 'mp', 'dp')
- shrink_outer_grad: float32 [2, 256, 1152], P(None, None, 'dp')
The draws below stay inside these ranges and needn't reach their ends.
Inputs may be any that keep to these rules, and one draw needn't show every extreme that they name: `segments`: in each row ids never fall; each of the 8 documents has 1 to 64 tokens, one exactly 64.
All inputs are finite; a program needn't handle non-finite values.
Results may differ from the reference program's by a relative error of at most 0.04.
Values sent between devices are 32-bit elements; how exact they have to be, the bound alone decides.
A program may use at most 256 MiB of HBM per device.

```python
import math
import jax
import jax.numpy as jnp
import numpy as np
from jax import lax

D = 1152
HEADS = 4
HEAD_WIDTH = 256
FF = 6912
R = 256
REPEATS = 2
DOCS = 8
TOK_DEV = 128
ROWS = 8
TOKENS = 1024


def shard_levels(rng, extent, split, least, high):
    factor_of, own = 1.0, jax.random.fold_in(rng, 6)
    for axis_at, shards_of in split:
        heights = jnp.exp(jax.random.uniform(jax.random.fold_in(own, axis_at), (shards_of,), jnp.float32, least / len(split), high / len(split)))
        factor_of = factor_of * jnp.repeat(heights, extent[axis_at] // shards_of).reshape([-1 if axis == axis_at else 1 for axis in range(len(extent))])
    return factor_of


def profile(number_of, total, limit, slope):
    portions = [(1 << 20) // math.isqrt(standing ** slope) + 1 for standing in range(2, number_of + 1)]
    spare, counts = total - limit - (number_of - 1), [1] * (number_of - 1)
    while spare > 0:
        candidates = [i for i in range(number_of - 1) if counts[i] < limit]
        whole, budget = sum([portions[i] for i in candidates]), spare
        for i in candidates:
            extra = min(limit - counts[i], max(1, budget * portions[i] // whole), spare)
            counts[i] = counts[i] + extra
            spare = spare - extra
    return np.array([limit] + counts)


def uneven(stream_key, count, total, limit, slope):
    if count == 2:
        one = jax.random.randint(stream_key, (), max(1, total - limit), min(limit, total - 1) + 1)
        return jnp.stack([one, total - one])
    lengths = jnp.asarray(profile(count, total, limit, slope), jnp.int32)
    pairs = (count - 1) // 2
    source_of, taker = lengths[1:1 + 2 * pairs:2], lengths[2:2 + 2 * pairs:2]
    margin = jnp.minimum(source_of - 1, limit - taker)
    passed = jax.random.randint(jax.random.fold_in(stream_key, 1), (pairs,), 0, 1 << 20) % (margin + 1)
    lengths = lengths.at[1:1 + 2 * pairs:2].set(source_of - passed).at[2:2 + 2 * pairs:2].set(taker + passed)
    return lengths[jax.random.permutation(jax.random.fold_in(stream_key, 2), count)]


def gaussian(key, extent, spread, limit, shards=(), held_as=jnp.bfloat16):
    level = shard_levels(key, extent, shards, -0.22, 0.18) if shards else 1.0
    drawn = jax.random.normal(key, extent, jnp.float32) * spread * level
    return jnp.minimum(jnp.maximum(drawn, -limit), limit).astype(held_as)


def setup_inputs(seed: int = 0) -> dict:
    key_of = jax.random.split(jax.random.key(seed), 21)
    return {
        "block_input": gaussian(key_of[0], (TOKENS, D), 1.0, 6.0, ((0, 8),)),
        "cotangent": gaussian(key_of[1], (TOKENS, D), 1.0, 6.0, ((0, 8),)),
        "segments": jax.vmap(lambda own: jnp.searchsorted(jnp.cumsum(uneven(own, DOCS, TOK_DEV, TOK_DEV // 2, 2)), jnp.arange(TOK_DEV), side="right"))(jax.random.split(key_of[2], ROWS)).reshape((ROWS, TOK_DEV)).astype(jnp.int32),
        "mixer_gain": jnp.clip(1.0 + 0.1 * jax.random.normal(key_of[3], (D,), jnp.float32), 0.5, 1.5),
        "feed_gain": jnp.clip(1.0 + 0.1 * jax.random.normal(key_of[4], (D,), jnp.float32), 0.5, 1.5),
        "query_matrix": gaussian(key_of[5], (D, HEADS * HEAD_WIDTH), D ** -0.5, 0.1875, ((1, 4),)),
        "key_value_weight": gaussian(key_of[6], (D, 2 * HEAD_WIDTH), D ** -0.5, 0.1875),
        "output_matrix": gaussian(key_of[7], (HEADS * HEAD_WIDTH, D), (HEADS * HEAD_WIDTH // 16) ** -0.5, 0.75, ((0, 4),)),
        "gate_up_weight": gaussian(key_of[8], (D, 2, FF), D ** -0.5, 0.1875, ((2, 4),)),
        "down_matrix": gaussian(key_of[9], (FF, D), FF ** -0.5, 0.078125, ((0, 4),)),
        "query_adapter_inner": gaussian(key_of[10], (REPEATS, D, R), D ** -0.5, 0.1875),
        "query_adapter_outer": gaussian(key_of[11], (REPEATS, R, HEADS * HEAD_WIDTH), R ** -0.5, 0.375, ((2, 4),)),
        "key_value_inner": gaussian(key_of[12], (REPEATS, D, 2, R), D ** -0.5, 0.1875),
        "key_value_outer": gaussian(key_of[13], (REPEATS, 2, R, HEAD_WIDTH), R ** -0.5, 0.375),
        "output_adapter_inner": gaussian(key_of[14], (REPEATS, HEADS * HEAD_WIDTH, R), (HEADS * HEAD_WIDTH // 16) ** -0.5, 0.75, ((1, 4),)),
        "output_adapter_outer": gaussian(key_of[15], (REPEATS, R, D), R ** -0.5, 0.375),
        "widen_inner_adapter": gaussian(key_of[16], (REPEATS, D, 2, R), D ** -0.5, 0.1875),
        "widen_outer_adapter": gaussian(key_of[17], (REPEATS, 2, R, FF), R ** -0.5, 0.375, ((3, 4),)),
        "down_adapter_inner": gaussian(key_of[18], (REPEATS, FF, R), FF ** -0.5, 0.078125, ((1, 4),)),
        "down_adapter_outer": gaussian(key_of[19], (REPEATS, R, D), R ** -0.5, 0.375),
    }


EPSILON = 1e-06
MASKED = -1e+30

@jax.custom_vjp
def low(v):
    return lax.optimization_barrier(v.astype(jnp.bfloat16)).astype(jnp.float32)

@jax.custom_vjp
def low_back(v):
    return v

def low_keep(v):
    return (low(v), None)

def low_pass(kept, grad):
    return (grad,)

def back_keep(v):
    return (v, None)

def back_low(kept, grad):
    return (low(grad),)
low.defvjp(low_keep, low_pass)
low_back.defvjp(back_keep, back_low)

def precise_einsum(form, left, right):
    return jnp.einsum(form, left, right, precision=lax.Precision.HIGHEST)

def normalize(hidden_state, gain):
    return hidden_state * lax.rsqrt(lax.optimization_barrier(jnp.mean(hidden_state * hidden_state, axis=-1, keepdims=True)) + EPSILON) * gain

def rotate(values, cosine_table, sine_table):
    half_width = values.shape[-1] // 2
    first = values[..., :half_width]
    second = values[..., half_width:]
    return jnp.concatenate([first * cosine_table - second * sine_table, second * cosine_table + first * sine_table], axis=-1)

def prepare(segments):
    length_value = segments.shape[1]
    earlier = lax.optimization_barrier(jnp.sum((segments[:, None, :] < segments[:, :, None]).astype(jnp.int32), axis=-1))
    position = (jnp.arange(length_value, dtype=jnp.int32)[None, :] - earlier).astype(jnp.float32)
    steps_half = jnp.arange(HEAD_WIDTH // 2, dtype=jnp.float32)
    frequency = 10000.0 ** (-2.0 * steps_half / HEAD_WIDTH)
    angles = position[:, :, None] * frequency[None, None, :]
    same_segment = segments[:, :, None] == segments[:, None, :]
    ordinal = jnp.arange(length_value, dtype=jnp.int32)
    allowed_mask = same_segment & (ordinal[:, None] >= ordinal[None, :])[None]
    return (jnp.cos(angles), jnp.sin(angles), allowed_mask)

def single_block_step(hidden_state, shared_weights, low_rank_adapter, cosine_table, sine_table, allowed_mask):
    mixer_gain, feed_gain, query_matrix, key_value_weight, output_matrix, gate_up_weight, down_matrix = shared_weights
    query_adapter_inner, query_adapter_outer, key_value_inner, key_value_outer, output_adapter_inner, output_adapter_outer, widen_inner_adapter, widen_outer_adapter, down_adapter_inner, down_adapter_outer = low_rank_adapter
    row_total, length_value, width = hidden_state.shape
    score_scale = 1.0 / math.sqrt(HEAD_WIDTH)
    normalized_state = low(normalize(hidden_state, mixer_gain))
    query_rank_value = low_back(low(precise_einsum('img,gq->imq', normalized_state, query_adapter_inner)))
    query_projected = low_back(precise_einsum('kbz,zp->kbp', normalized_state, query_matrix) + precise_einsum('ubi,iv->ubv', query_rank_value, query_adapter_outer))
    key_value_rank_value = low_back(low(precise_einsum('iqu,uet->iqet', normalized_state, key_value_inner)))
    key_value_linear = low_back(precise_einsum('kbz,zp->kbp', normalized_state, key_value_weight) + precise_einsum('wzox,oxk->wzok', key_value_rank_value, key_value_outer).reshape(row_total, length_value, 2 * HEAD_WIDTH))
    queries = low(rotate(query_projected.reshape(row_total, length_value, HEADS, HEAD_WIDTH), cosine_table[:, :, None], sine_table[:, :, None]))
    keys = low(rotate(key_value_linear[..., :HEAD_WIDTH], cosine_table, sine_table))
    values = low(key_value_linear[..., HEAD_WIDTH:])
    scores = low_back(precise_einsum('sihd,sjd->shij', queries, keys) * score_scale)
    masked = jnp.where(allowed_mask[:, None], scores, MASKED)
    probs = low(jax.nn.softmax(masked, axis=-1))
    attention_mixed = low(low_back(precise_einsum('shij,sjd->sihd', probs, values))).reshape(row_total, length_value, HEADS * HEAD_WIDTH)
    output_rank_value = low_back(precise_einsum('slq,qr->slr', attention_mixed, output_adapter_inner))
    attention_step = low_back(precise_einsum('mhj,jt->mht', attention_mixed, output_matrix) + precise_einsum('cat,tx->cax', output_rank_value, output_adapter_outer))
    middle = hidden_state + attention_step
    feed_result = low(normalize(middle, feed_gain))
    widen_rank_value = low_back(low(precise_einsum('iqu,uet->iqet', feed_result, widen_inner_adapter)))
    widened_hidden = low_back(precise_einsum('eyk,ktr->eytr', feed_result, gate_up_weight) + precise_einsum('hmtn,tnx->hmtx', widen_rank_value, widen_outer_adapter))
    gated_hidden = low(jax.nn.gelu(widened_hidden[:, :, 0], approximate=True) * widened_hidden[:, :, 1])
    down_rank_value = low_back(precise_einsum('slf,fr->slr', gated_hidden, down_adapter_inner))
    feed_forward_step = low_back(precise_einsum('bng,gh->bnh', gated_hidden, down_matrix) + precise_einsum('cat,tx->cax', down_rank_value, down_adapter_outer))
    return middle + feed_forward_step

def all_loops(hidden_state, parameter_set, cosine_table, sine_table, allowed_mask):
    shared_weights = parameter_set[:7]
    for repeat_index in range(REPEATS):
        low_rank_adapter = tuple((entry_value[repeat_index] for entry_value in parameter_set[7:]))
        hidden_state = single_block_step(hidden_state, shared_weights, low_rank_adapter, cosine_table, sine_table, allowed_mask)
    return hidden_state

def reference(block_input, cotangent, segments, mixer_gain, feed_gain, query_matrix, key_value_weight, output_matrix, gate_up_weight, down_matrix, query_adapter_inner, query_adapter_outer, key_value_inner, key_value_outer, output_adapter_inner, output_adapter_outer, widen_inner_adapter, widen_outer_adapter, down_adapter_inner, down_adapter_outer):
    row_total, length_value = segments.shape
    cosine_table, sine_table, allowed_mask = prepare(segments)
    parameter_set = tuple((entry_value.astype(jnp.float32) for entry_value in (mixer_gain, feed_gain, query_matrix, key_value_weight, output_matrix, gate_up_weight, down_matrix, query_adapter_inner, query_adapter_outer, key_value_inner, key_value_outer, output_adapter_inner, output_adapter_outer, widen_inner_adapter, widen_outer_adapter, down_adapter_inner, down_adapter_outer)))
    inputs = block_input.astype(jnp.float32).reshape(row_total, 1, length_value, D)
    upstream_gradient = cotangent.astype(jnp.float32).reshape(row_total, 1, length_value, D)
    cosine_table = cosine_table.reshape(row_total, 1, length_value, HEAD_WIDTH // 2)
    sine_table = sine_table.reshape(row_total, 1, length_value, HEAD_WIDTH // 2)
    allowed_mask = allowed_mask.reshape(row_total, 1, length_value, length_value)

    def per_row(totals, row):
        row_input, row_upstream, row_cosine, row_sine, row_allowed = row

        def forward(hidden_state, *weights):
            return all_loops(hidden_state, weights, row_cosine, row_sine, row_allowed)
        result, pullback = jax.vjp(forward, row_input, *parameter_set)
        pulled = pullback(row_upstream)
        totals = tuple((first + second for first, second in zip(totals, pulled[1:])))
        return (totals, (result, pulled[0]))
    initial = tuple((jnp.zeros_like(entry_value) for entry_value in parameter_set))
    grads, (outputs, input_grads) = lax.scan(per_row, initial, (inputs, upstream_gradient, cosine_table, sine_table, allowed_mask))
    block_output = outputs.reshape(row_total * length_value, D).astype(jnp.bfloat16)
    input_grad = input_grads.reshape(row_total * length_value, D)
    return (block_output, input_grad, grads[0], grads[1], grads[2], grads[3], grads[4], grads[5], grads[6], grads[7], grads[8], grads[9], grads[10], grads[11], grads[12], grads[13], grads[14], grads[15], grads[16])
```

```python
import functools
import math
from types import SimpleNamespace

import jax
import jax.numpy as jnp
from jax import lax
from jax.experimental import pallas as pl
from jax.experimental.pallas import tpu as pltpu
from jax.sharding import PartitionSpec as P

EPSILON = 1e-06
MASKED = -1e30
MESH = pl.DeviceIdType.MESH


def product(left, right):
    return jnp.dot(left, right, preferred_element_type=jnp.float32)


def product_t(left, right):
    return lax.dot_general(
        left, right, (((1,), (1,)), ((), ())), preferred_element_type=jnp.float32
    )


def product_tn(left, right):
    return lax.dot_general(
        left, right, (((0,), (0,)), ((), ())), preferred_element_type=jnp.float32
    )


def exact_product(left, right):
    return jnp.dot(left, right, precision=lax.Precision.HIGHEST, preferred_element_type=jnp.float32)


def exact_tn(left, right):
    return lax.dot_general(
        left,
        right,
        (((0,), (0,)), ((), ())),
        precision=lax.Precision.HIGHEST,
        preferred_element_type=jnp.float32,
    )


def normalize(hidden_state, gain):
    factor = lax.rsqrt(jnp.mean(hidden_state * hidden_state, axis=-1, keepdims=True) + EPSILON)
    return (hidden_state * factor * gain, factor)


def normalize_back(hidden_state, factor, gain, upstream_gradient):
    unit = hidden_state * factor
    scaled = upstream_gradient * gain
    downstream = factor * (scaled - unit * jnp.mean(scaled * unit, axis=-1, keepdims=True))
    return (downstream, jnp.sum(upstream_gradient * unit, axis=0))


def rotate(values, cosine_table, sine_table):
    half_width = values.shape[-1] // 2
    first = values[..., :half_width]
    second = values[..., half_width:]
    return jnp.concatenate(
        [first * cosine_table - second * sine_table, second * cosine_table + first * sine_table],
        axis=-1,
    )


def rotary_tables(segment_row, head_size):
    length_value = segment_row.shape[0]
    earlier = jnp.sum((segment_row[None, :] < segment_row[:, None]).astype(jnp.int32), axis=1)
    position = (jnp.arange(length_value, dtype=jnp.int32) - earlier).astype(jnp.float32)
    steps_half = jnp.arange(head_size // 2, dtype=jnp.float32)
    frequency = 10000.0 ** (-2.0 * steps_half / head_size)
    angles = position[:, None] * frequency[None, :]
    same_segment = segment_row[:, None] == segment_row[None, :]
    ordinal = jnp.arange(length_value, dtype=jnp.int32)
    allowed_mask = same_segment & (ordinal[:, None] >= ordinal[None, :])
    return (jnp.cos(angles), jnp.sin(angles), allowed_mask)


def gelu_tanh(values):
    return jax.nn.gelu(values, approximate=True)


def attention_probs(queries, keys, allowed_mask, score_scale):
    scores = (
        jnp.einsum("ihd,jd->hij", queries, keys, preferred_element_type=jnp.float32) * score_scale
    )
    return jnp.where(allowed_mask[None], scores, MASKED)


def mp_total(size):
    def kernel(part, out, near, mine, far, core_send, core_recv, y_send, y_recv, back_send, back_recv):
        dp, mp = lax.axis_index("dp"), lax.axis_index("mp")
        side = lax.rem(mp, 2)
        core = (dp, mp + 1 - 2 * side)
        other = (dp, lax.rem(mp + 2, 4))
        half = part.shape[0] // 2
        pieces = near.shape[0]
        width = part.shape[1] // pieces
        own = pl.ds(pl.multiple_of(side * half, half), half)
        theirs = pl.ds(pl.multiple_of((1 - side) * half, half), half)

        def columns(i):
            return pl.ds(i * width, width)

        barrier = pltpu.get_barrier_semaphore()
        for device in (core, other):
            pl.semaphore_signal(barrier, inc=1, device_id=device, device_id_type=MESH)
        pl.semaphore_wait(barrier, 2)
        first = [
            pltpu.make_async_remote_copy(
                part.at[theirs, columns(i)], near.at[i], core_send.at[i], core_recv.at[i],
                device_id=core, device_id_type=MESH,
            )
            for i in range(pieces)
        ]
        second = [
            pltpu.make_async_remote_copy(
                mine.at[i], far.at[i], y_send.at[i], y_recv.at[i],
                device_id=other, device_id_type=MESH,
            )
            for i in range(pieces)
        ]
        third = [
            pltpu.make_async_remote_copy(
                out.at[own, columns(i)], out.at[own, columns(i)], back_send.at[i], back_recv.at[i],
                device_id=core, device_id_type=MESH,
            )
            for i in range(pieces)
        ]
        for copy in first:
            copy.start()
        for i in range(pieces):
            first[i].wait_recv()
            mine[i] = part[own, columns(i)] + near[i]
            second[i].start()
        for i in range(pieces):
            second[i].wait_recv()
            out[own, columns(i)] = mine[i] + far[i]
            third[i].start()
        for copy in third:
            copy.wait_recv()
        for copy in first + second + third:
            copy.wait_send()

    def total(identity, *parts):
        if size != 4:
            return lax.psum(parts, "mp")
        joined = jnp.concatenate(parts, axis=1)
        tokens_here, columns_here = joined.shape
        pieces = 1
        for count in (5, 4, 3, 2):
            if columns_here % (128 * count) == 0:
                pieces = count
                break
        half = (pieces, tokens_here // 2, columns_here // pieces)
        summed = pl.pallas_call(
            kernel,
            out_shape=jax.ShapeDtypeStruct(joined.shape, jnp.float32),
            in_specs=[pl.BlockSpec(memory_space=pltpu.VMEM)],
            out_specs=pl.BlockSpec(memory_space=pltpu.VMEM),
            scratch_shapes=[pltpu.VMEM(half, jnp.float32)] * 3
            + [pltpu.SemaphoreType.DMA((pieces,))] * 6,
            compiler_params=pltpu.CompilerParams(
                collective_id=identity, has_side_effects=True, vmem_limit_bytes=16 << 20
            ),
        )(joined)
        edges, start = [], 0
        for part in parts:
            edges.append(summed[:, start : start + part.shape[1]])
            start += part.shape[1]
        return tuple(edges)

    return total


def forward_loop(hidden_state, shared, adapters, tables, total, identity):
    (mixer_gain, feed_gain, query_matrix, pair_matrix, output_matrix, widen_matrix, down_matrix) = shared
    (q_in, q_out, kv_in, kv_out, o_in, o_out, w_in, w_out, d_in, d_out) = adapters
    cosine, sine, allowed = tables
    tokens_here, width = hidden_state.shape
    head = pair_matrix.shape[1] // 2
    heads = query_matrix.shape[1] // head
    rank = q_in.shape[1]
    hidden = down_matrix.shape[0]
    kept = SimpleNamespace(h=hidden_state)
    normed, kept.mixer_factor = normalize(hidden_state, mixer_gain)
    normed = normed.astype(jnp.bfloat16)
    query_rank = product(normed, q_in).astype(jnp.bfloat16)
    query_linear = product(normed, query_matrix) + product(query_rank, q_out)
    pair_rank = product(normed, kv_in.reshape(width, 2 * rank)).astype(jnp.bfloat16)
    pair_linear = product(normed, pair_matrix) + jnp.concatenate(
        [product(pair_rank[:, :rank], kv_out[0]), product(pair_rank[:, rank:], kv_out[1])], axis=1
    )
    queries = rotate(
        query_linear.reshape(tokens_here, heads, head), cosine[:, None], sine[:, None]
    ).astype(jnp.bfloat16)
    keys = rotate(pair_linear[:, :head], cosine, sine).astype(jnp.bfloat16)
    values = pair_linear[:, head:].astype(jnp.bfloat16)
    masked = attention_probs(queries, keys, allowed, 1.0 / math.sqrt(head))
    expo = jnp.exp(masked - jnp.max(masked, axis=-1, keepdims=True))
    probs = expo / jnp.sum(expo, axis=-1, keepdims=True)
    mixed = jnp.einsum(
        "hij,jd->ihd", probs.astype(jnp.bfloat16), values, preferred_element_type=jnp.float32
    )
    mixed = mixed.reshape(tokens_here, heads * head).astype(jnp.bfloat16)
    summed, output_rank = total(identity, product(mixed, output_matrix), product(mixed, o_in))
    middle = hidden_state + summed + exact_product(output_rank, o_out.astype(jnp.float32))
    fed, kept.feed_factor = normalize(middle, feed_gain)
    fed = fed.astype(jnp.bfloat16)
    widen_rank = product(fed, w_in.reshape(width, 2 * rank)).astype(jnp.bfloat16)
    gate = product(fed, widen_matrix[:, 0]) + product(widen_rank[:, :rank], w_out[0])
    up = product(fed, widen_matrix[:, 1]) + product(widen_rank[:, rank:], w_out[1])
    activated = (gelu_tanh(gate) * up).astype(jnp.bfloat16)
    shrunk, shrink_rank = total(identity + 1, product(activated, down_matrix), product(activated, d_in))
    result = middle + shrunk + exact_product(shrink_rank, d_out.astype(jnp.float32))
    vars(kept).update(
        normed=normed, query_rank=query_rank, pair_rank=pair_rank, queries=queries, keys=keys,
        values=values, probs=probs, mixed=mixed, output_rank=output_rank, middle=middle, fed=fed,
        widen_rank=widen_rank, gate=gate, up=up, activated=activated, shrink_rank=shrink_rank,
    )
    return result, kept


def reverse_loop(upstream, kept, shared, adapters, tables, total, identity):
    (mixer_gain, feed_gain, query_matrix, pair_matrix, output_matrix, widen_matrix, down_matrix) = shared
    (q_in, q_out, kv_in, kv_out, o_in, o_out, w_in, w_out, d_in, d_out) = adapters
    cosine, sine, allowed = tables
    tokens_here, width = upstream.shape
    head = pair_matrix.shape[1] // 2
    heads = query_matrix.shape[1] // head
    rank = q_in.shape[1]
    scale = 1.0 / math.sqrt(head)
    grad_feed = upstream.astype(jnp.bfloat16)
    grad_shrink_rank = product_t(grad_feed, d_out).astype(jnp.bfloat16)
    grad_activated = product_t(grad_feed, down_matrix) + product_t(grad_shrink_rank, d_in)
    gelu_value, gelu_pullback = jax.vjp(gelu_tanh, kept.gate)
    grad_gate = gelu_pullback(grad_activated * kept.up)[0].astype(jnp.bfloat16)
    grad_up = (grad_activated * gelu_value).astype(jnp.bfloat16)
    grad_fed, grad_widen_rank = total(
        identity,
        product_t(grad_gate, widen_matrix[:, 0]) + product_t(grad_up, widen_matrix[:, 1]),
        jnp.concatenate([product_t(grad_gate, w_out[0]), product_t(grad_up, w_out[1])], axis=1),
    )
    grad_widen_rank = grad_widen_rank.astype(jnp.bfloat16)
    grad_fed = grad_fed + product_t(grad_widen_rank, w_in.reshape(width, 2 * rank))
    grad_norm, feed_gain_grad = normalize_back(kept.middle, kept.feed_factor, feed_gain, grad_fed)
    grad_middle = upstream + grad_norm
    grad_attend = grad_middle.astype(jnp.bfloat16)
    grad_output_rank = product_t(grad_attend, o_out).astype(jnp.bfloat16)
    grad_mixed = product_t(grad_attend, output_matrix) + product_t(grad_output_rank, o_in)
    grad_mixed = grad_mixed.astype(jnp.bfloat16).reshape(tokens_here, heads, head)
    queries, keys, values, probs = kept.queries, kept.keys, kept.values, kept.probs
    grad_probs = jnp.einsum("ihd,jd->hij", grad_mixed, values, preferred_element_type=jnp.float32)
    delta = jnp.sum(grad_probs * probs, axis=-1, keepdims=True)
    grad_scores = (probs * (grad_probs - delta)).astype(jnp.bfloat16)
    grad_queries = scale * jnp.einsum(
        "hij,jd->ihd", grad_scores, keys, preferred_element_type=jnp.float32
    )
    grad_keys = scale * jnp.einsum(
        "hij,ihd->jd", grad_scores, queries, preferred_element_type=jnp.float32
    )
    grad_values = jnp.einsum(
        "hij,ihd->jd", probs.astype(jnp.bfloat16), grad_mixed, preferred_element_type=jnp.float32
    )
    grad_query = rotate(grad_queries, cosine[:, None], -sine[:, None])
    grad_query = grad_query.reshape(tokens_here, heads * head).astype(jnp.bfloat16)
    grad_normed, grad_query_rank, grad_pair = total(
        identity + 1,
        product_t(grad_query, query_matrix),
        product_t(grad_query, q_out),
        jnp.concatenate([rotate(grad_keys, cosine, -sine), grad_values], axis=1),
    )
    grad_query_rank = grad_query_rank.astype(jnp.bfloat16)
    grad_pair = grad_pair.astype(jnp.bfloat16)
    grad_pair_rank = jnp.concatenate(
        [product_t(grad_pair[:, :head], kv_out[0]), product_t(grad_pair[:, head:], kv_out[1])], axis=1
    ).astype(jnp.bfloat16)
    grad_normed = (
        grad_normed
        + product_t(grad_query_rank, q_in)
        + product_t(grad_pair, pair_matrix)
        + product_t(grad_pair_rank, kv_in.reshape(width, 2 * rank))
    )
    grad_norm, mixer_gain_grad = normalize_back(
        kept.h, kept.mixer_factor, mixer_gain, grad_normed
    )
    vars(kept).update(
        grad_feed=grad_feed, grad_shrink_rank=grad_shrink_rank, grad_gate=grad_gate, grad_up=grad_up,
        grad_widen_rank=grad_widen_rank, grad_attend=grad_attend, grad_output_rank=grad_output_rank,
        grad_query=grad_query, grad_query_rank=grad_query_rank, grad_pair=grad_pair,
        grad_pair_rank=grad_pair_rank, feed_gain_grad=feed_gain_grad, mixer_gain_grad=mixer_gain_grad,
    )
    return grad_middle + grad_norm


def scattered_gradients(kept, dp_size, mp_size):
    def scatter(value, axis):
        return lax.psum_scatter(value, "dp", scatter_dimension=axis, tiled=True)

    def shared_of(factors):
        return sum(product_tn(*factors(k)) for k in kept)

    def each(function):
        return jnp.stack([function(k) for k in kept], axis=0)

    def quarter(value, axis):
        block = scatter(value, axis)
        size = block.shape[axis] // mp_size
        return lax.dynamic_slice_in_dim(block, lax.axis_index("mp") * size, size, axis)

    width = kept[0].normed.shape[1]
    rank = kept[0].query_rank.shape[1]
    head = kept[0].grad_pair.shape[1] // 2

    def pair_outer(k):
        left, right = k.pair_rank, k.grad_pair
        return jnp.stack(
            [product_tn(left[:, :rank], right[:, :head]), product_tn(left[:, rank:], right[:, head:])]
        )

    def expand_outer(k):
        left = k.widen_rank
        return jnp.stack(
            [product_tn(left[:, :rank], k.grad_gate), product_tn(left[:, rank:], k.grad_up)]
        )

    return (
        scatter(sum(k.mixer_gain_grad for k in kept), 0),
        scatter(sum(k.feed_gain_grad for k in kept), 0),
        scatter(shared_of(lambda k: (k.normed, k.grad_query)), 0),
        quarter(shared_of(lambda k: (k.normed, k.grad_pair)), 0),
        scatter(shared_of(lambda k: (k.mixed, k.grad_attend)), 1),
        scatter(jnp.stack([shared_of(lambda k: (k.fed, k.grad_gate)), shared_of(lambda k: (k.fed, k.grad_up))], axis=1), 0),
        scatter(shared_of(lambda k: (k.activated, k.grad_feed)), 1),
        quarter(each(lambda k: product_tn(k.normed, k.grad_query_rank)), 1),
        scatter(each(lambda k: product_tn(k.query_rank, k.grad_query)), 1),
        quarter(
            each(lambda k: product_tn(k.normed, k.grad_pair_rank).reshape(width, 2, rank)), 1
        ),
        quarter(each(pair_outer), 2),
        scatter(each(lambda k: product_tn(k.mixed, k.grad_output_rank)), 2),
        scatter(
            each(lambda k: exact_tn(k.output_rank, k.grad_attend.astype(jnp.float32))), 2
        ),
        quarter(
            each(lambda k: product_tn(k.fed, k.grad_widen_rank).reshape(width, 2, rank)), 1
        ),
        scatter(each(expand_outer), 2),
        scatter(each(lambda k: product_tn(k.activated, k.grad_shrink_rank)), 2),
        scatter(each(lambda k: exact_tn(k.shrink_rank, k.grad_feed.astype(jnp.float32))), 2),
    )


WIDE = 896


def split3(value):
    high = value.astype(jnp.bfloat16)
    rest = value - high.astype(jnp.float32)
    middle = rest.astype(jnp.bfloat16)
    low = (rest - middle.astype(jnp.float32)).astype(jnp.bfloat16)
    return high, middle, low


WEIGHTS = (
    "q_in", "query", "q_out", "kv_in", "pair", "kv_out", "output", "o_in", "o_out",
    "w_in", "gate", "up", "w_out", "down", "d_in", "d_out",
)
SUM_STEP = 384


def block_kernel(*refs):
    (h_in, cot, cosine_ref, sine_ref, mask_ref, mixer_gain, feed_gain), refs = refs[:7], refs[7:]
    count = len(WEIGHTS)
    sources, refs = refs[:count], refs[count:]
    (out_ref, grad_ref, xt_ref, rt_ref, b_ref, q_ref, raw_ref), refs = refs[:7], refs[7:]
    weights, refs = refs[:count], refs[count:]
    (
        h_s, mid_s, normed_s, qr_s, kvr_s, q_s, k_s, v_s, probs_s, mixed_s, or_s, fed_s, er_s,
        gate_s, up_s, act_s, sr_s, gg_s, gu_s, g_s, gain_s, select,
        part, total, near, mine, far,
        load_sems, c_s, c_r, y_s, y_r, e_s, e_r,
    ) = refs
    W = SimpleNamespace(**dict(zip(WEIGHTS, weights)))
    dp, mp = lax.axis_index("dp"), lax.axis_index("mp")
    side = lax.rem(mp, 2)
    core = (dp, mp + 1 - 2 * side)
    other = (dp, lax.rem(mp + 2, 4))
    loads = [
        pltpu.make_async_copy(source, target, load_sems.at[i])
        for i, (source, target) in enumerate(zip(sources, weights))
    ]
    load = SimpleNamespace(**dict(zip(WEIGHTS, loads)))
    for copy in loads:
        copy.start()
    barrier = pltpu.get_barrier_semaphore()
    for device in (core, other):
        pl.semaphore_signal(barrier, inc=1, device_id=device, device_id_type=MESH)
    pl.semaphore_wait(barrier, 2)

    tokens, width = h_in.shape
    half = tokens // 2
    head = W.query.shape[1]
    rank = W.q_in.shape[2]
    hidden = W.down.shape[0]
    scale = 1.0 / math.sqrt(head)
    own = pl.ds(pl.multiple_of(side * half, half), half)
    theirs = pl.ds(pl.multiple_of((1 - side) * half, half), half)
    blocks = xt_ref.shape[1] * xt_ref.shape[2]
    block = width // blocks
    quarter = block // 4
    rank_quarter = rank // (4 * blocks)
    chunks = [(0, WIDE), (WIDE, hidden - WIDE)]

    def columns_of(size):
        return [(at, min(SUM_STEP, size - at)) for at in range(0, size, SUM_STEP)]

    def sum_over_mp(size, fill, turn):
        def pieces_of(make):
            return [make(i, pl.ds(at, n)) for i, (at, n) in enumerate(columns_of(size))]

        def remote(source, target, send, recv, device):
            return pltpu.make_async_remote_copy(
                source, target, send, recv, device_id=device, device_id_type=MESH
            )

        first = pieces_of(
            lambda i, c: remote(part.at[theirs, c], near.at[:, c], c_s.at[i], c_r.at[i], core)
        )
        second = pieces_of(
            lambda i, c: remote(
                mine.at[:, c], far.at[turn, :, c], y_s.at[turn, i], y_r.at[turn, i], other
            )
        )
        third = pieces_of(
            lambda i, c: remote(total.at[own, c], total.at[own, c], e_s.at[i], e_r.at[i], core)
        )

        def middle(i):
            at, n = columns_of(size)[i]
            first[i].wait_recv()
            mine[:, at : at + n] = part[own, at : at + n] + near[:, at : at + n]
            second[i].start()

        for i, (at, n) in enumerate(columns_of(size)):
            fill(at, n)
            first[i].start()
            if i:
                middle(i - 1)
        middle(len(first) - 1)
        for i, (at, n) in enumerate(columns_of(size)):
            second[i].wait_recv()
            total[own, at : at + n] = mine[:, at : at + n] + far[turn, :, at : at + n]
            third[i].start()
        for copy in third:
            copy.wait_recv()
        for copy in first + second + third:
            copy.wait_send()

    def dot(left, right):
        return jnp.dot(left, right, preferred_element_type=jnp.float32)

    def low(value):
        return value.astype(jnp.bfloat16)

    def spin(value, sign):
        a, b = value[:, : head // 2], value[:, head // 2 :]
        cosine, sine = cosine_ref[...], sign * sine_ref[...]
        return jnp.concatenate([a * cosine - b * sine, b * cosine + a * sine], axis=1)

    def factor_of(value):
        return lax.rsqrt(jnp.mean(value * value, axis=-1, keepdims=True) + EPSILON)

    def gelu_parts(value):
        c = math.sqrt(2.0 / math.pi)
        square = value * value
        t = jnp.tanh(c * value * (1.0 + 0.044715 * square))
        gelu = 0.5 * value * (1.0 + t)
        slope = 0.5 * (1.0 + t) + 0.5 * value * (1.0 - t * t) * c * (1.0 + 3 * 0.044715 * square)
        return gelu, slope

    h_s[0] = h_in[...].astype(jnp.float32)
    mixer, feed = mixer_gain[...], feed_gain[...]

    def forward(l, carry):
        def need(*copies):
            @pl.when(l == 0)
            def _():
                for copy in copies:
                    copy.wait()

        h = h_s[l]
        normed = low(h * factor_of(h) * mixer)
        normed_s[l] = normed
        need(load.q_in, load.query, load.q_out, load.kv_in, load.pair, load.kv_out)
        query_rank = low(dot(normed, W.q_in[l]))
        qr_s[l] = query_rank
        queries = dot(normed, W.query[...]) + dot(query_rank, W.q_out[l])
        q_s[l] = low(spin(queries, 1.0))
        pair_rank = low(dot(normed, W.kv_in[l]))
        kvr_s[l] = pair_rank
        keys = dot(normed, W.pair[:, :head]) + dot(pair_rank[:, :rank], W.kv_out[l, 0])
        k_s[l] = low(spin(keys, 1.0))
        values = dot(normed, W.pair[:, head:]) + dot(pair_rank[:, rank:], W.kv_out[l, 1])
        v_s[l] = low(values)
        scores = product_t(q_s[l], k_s[l]) * scale
        scores = jnp.where(mask_ref[...] > 0, scores, MASKED)
        expo = jnp.exp(scores - jnp.max(scores, axis=-1, keepdims=True))
        probs = expo / jnp.sum(expo, axis=-1, keepdims=True)
        probs_s[l] = probs
        mixed = low(dot(low(probs), v_s[l]))
        mixed_s[l] = mixed
        need(load.output, load.o_in, load.o_out)

        def fill_attend(at, n):
            cut = min(n, max(0, width - at))
            if cut:
                part[:, at : at + cut] = dot(mixed, W.output[:, at : at + cut])
            if cut < n:
                start = at + cut - width
                part[:, at + cut : at + n] = dot(mixed, W.o_in[l, :, start : start + n - cut])

        sum_over_mp(width + rank, fill_attend, 0)
        output_rank = total[:, width : width + rank]
        or_s[l] = output_rank
        middle = h_s[l] + total[:, :width]
        for piece in split3(output_rank):
            middle = middle + dot(piece, W.o_out[l])
        mid_s[l] = middle
        fed = low(middle * factor_of(middle) * feed)
        fed_s[l] = fed
        need(load.w_in, load.gate, load.up, load.w_out)
        widen_rank = low(dot(fed, W.w_in[l]))
        er_s[l] = widen_rank
        for at, n in chunks:
            gate = dot(fed, W.gate[:, at : at + n]) + dot(
                widen_rank[:, :rank], W.w_out[l, 0, :, at : at + n]
            )
            gate_s[l, :, at : at + n] = gate
            up = dot(fed, W.up[:, at : at + n]) + dot(
                widen_rank[:, rank:], W.w_out[l, 1, :, at : at + n]
            )
            up_s[l, :, at : at + n] = up
            act_s[:, at : at + n] = low(gelu_parts(gate)[0] * up)
        rows = pl.ds(pl.multiple_of(l * tokens, tokens), tokens)
        for i, (at, n) in enumerate(chunks):
            b_ref[4 + i, rows, :n] = act_s[:, at : at + n]
            if n < WIDE:
                b_ref[4 + i, rows, n:] = jnp.zeros((tokens, WIDE - n), jnp.bfloat16)
        need(load.down, load.d_in, load.d_out)

        def fill_feed(at, n):
            cut = min(n, max(0, width - at))
            if cut:
                part[:, at : at + cut] = dot(act_s[...], W.down[:, at : at + cut])
            if cut < n:
                start = at + cut - width
                part[:, at + cut : at + n] = dot(act_s[...], W.d_in[l, :, start : start + n - cut])

        sum_over_mp(width + rank, fill_feed, 1)
        shrink_rank = total[:, width : width + rank]
        sr_s[l] = shrink_rank
        result = mid_s[l] + total[:, :width]
        for piece in split3(shrink_rank):
            result = result + dot(piece, W.d_out[l])
        h_s[l + 1] = result
        return carry

    loops = W.q_in.shape[0]
    lax.fori_loop(0, loops, forward, 0)
    out_ref[...] = low(h_s[loops])

    g_s[...] = cot[...].astype(jnp.float32)
    gain_s[...] = jnp.zeros_like(gain_s)
    padded_quarter = select.shape[0] // blocks
    row = lax.broadcasted_iota(jnp.int32, (padded_quarter, width), 0)
    column = lax.broadcasted_iota(jnp.int32, (padded_quarter, width), 1)
    for b in range(blocks):
        hit = jnp.logical_and(column == row + (b * 4 + mp) * quarter, row < quarter)
        select[b * padded_quarter : (b + 1) * padded_quarter] = low(
            jnp.where(hit, 1.0, 0.0)
        )
    small_row = lax.broadcasted_iota(jnp.int32, (rank_quarter, rank), 0)
    small_column = lax.broadcasted_iota(jnp.int32, (rank_quarter, rank), 1)
    rank_select = low(
        jnp.concatenate(
            [
                jnp.where(small_column == small_row + (b * 4 + mp) * rank_quarter, 1.0, 0.0)
                for b in range(blocks)
            ],
            axis=0,
        )
    )
    raw_rows = raw_layout(quarter, rank_quarter, loops)

    def back(step, carry):
        l = loops - 1 - step
        lanes = pl.ds(pl.multiple_of(l * tokens, tokens), tokens)
        rows = lanes

        def keep_t(i, value):
            turned = low(value.astype(jnp.float32).T)
            for b in range(blocks):
                xt_ref[i, b % 2, b // 2, :, lanes] = turned[b * block : (b + 1) * block]

        def keep_rank(i, value):
            turned = low(value.astype(jnp.float32).T)
            size = rank // blocks
            for b in range(blocks):
                rt_ref[i, b % 2, b // 2, :, lanes] = turned[b * size : (b + 1) * size]

        upstream = g_s[...]
        grad_feed = low(upstream)
        grad_shrink = low(product_t(grad_feed, W.d_out[l]))
        for i, (at, n) in enumerate(chunks):
            grad_act = product_t(grad_feed, W.down[at : at + n]) + product_t(
                grad_shrink, W.d_in[l, at : at + n]
            )
            gelu, slope = gelu_parts(gate_s[l, :, at : at + n])
            grad_gate = low(grad_act * up_s[l, :, at : at + n] * slope)
            grad_up = low(grad_act * gelu)
            gg_s[:, at : at + n] = grad_gate
            gu_s[:, at : at + n] = grad_up
            b_ref[i, rows, :n] = grad_gate
            b_ref[2 + i, rows, :n] = grad_up
            if n < WIDE:
                b_ref[i, rows, n:] = jnp.zeros((tokens, WIDE - n), jnp.bfloat16)
                b_ref[2 + i, rows, n:] = jnp.zeros((tokens, WIDE - n), jnp.bfloat16)

        def fill_fed(at, n):
            cut = min(n, max(0, width - at))
            if cut:
                part[:, at : at + cut] = product_t(
                    gg_s[...], W.gate[at : at + cut]
                ) + product_t(gu_s[...], W.up[at : at + cut])
            while cut < n:
                start = at + cut - width
                j, offset = divmod(start, rank)
                size = min(n - cut, rank - offset)
                value = (gg_s, gu_s)[j][...]
                part[:, at + cut : at + cut + size] = product_t(
                    value, W.w_out[l, j, offset : offset + size]
                )
                cut += size

        sum_over_mp(width + 2 * rank, fill_fed, 0)
        grad_widen = low(total[:, width : width + 2 * rank])
        grad_fed = total[:, :width] + product_t(grad_widen, W.w_in[l])
        middle = mid_s[l]
        factor = factor_of(middle)
        unit = middle * factor
        scaled = grad_fed * feed
        grad_middle = upstream + factor * (
            scaled - unit * jnp.mean(scaled * unit, axis=-1, keepdims=True)
        )
        gain_s[1:2] += jnp.sum(grad_fed * unit, axis=0, keepdims=True)
        g_s[...] = grad_middle
        grad_attend = low(grad_middle)
        grad_output = low(product_t(grad_attend, W.o_out[l]))
        grad_mixed = low(
            product_t(grad_attend, W.output[...]) + product_t(grad_output, W.o_in[l])
        )
        probs = probs_s[l]
        grad_probs = product_t(grad_mixed, v_s[l])
        delta = jnp.sum(grad_probs * probs, axis=-1, keepdims=True)
        grad_scores = low(probs * (grad_probs - delta))
        grad_query = low(spin(dot(grad_scores, k_s[l]) * scale, -1.0))
        q_ref[0, rows, :] = grad_query
        q_ref[1, rows, :] = mixed_s[l]

        def fill_normed(at, n):
            if at == columns_of(width + rank + 2 * head)[0][0]:
                part[:, width + rank : width + rank + head] = spin(
                    product_tn(grad_scores, q_s[l]) * scale, -1.0
                )
                part[:, width + rank + head :] = product_tn(low(probs), grad_mixed)
            cut = min(n, max(0, width - at))
            if cut:
                part[:, at : at + cut] = product_t(grad_query, W.query[at : at + cut])
            end = min(at + n, width + rank)
            if at + cut < end:
                start = at + cut - width
                part[:, at + cut : end] = product_t(
                    grad_query, W.q_out[l, start : end - width]
                )

        sum_over_mp(width + rank + 2 * head, fill_normed, 1)
        grad_rank = low(total[:, width : width + rank])
        grad_pair = low(total[:, width + rank : width + rank + 2 * head])
        grad_pair_rank = low(
            jnp.concatenate(
                [
                    product_t(grad_pair[:, :head], W.kv_out[l, 0]),
                    product_t(grad_pair[:, head:], W.kv_out[l, 1]),
                ],
                axis=1,
            )
        )
        grad_normed = (
            total[:, :width]
            + product_t(grad_rank, W.q_in[l])
            + product_t(grad_pair, W.pair[...])
            + product_t(grad_pair_rank, W.kv_in[l])
        )
        h = h_s[l]
        factor = factor_of(h)
        unit = h * factor
        scaled = grad_normed * mixer
        g_s[...] += factor * (scaled - unit * jnp.mean(scaled * unit, axis=-1, keepdims=True))
        gain_s[0:1] += jnp.sum(grad_normed * unit, axis=0, keepdims=True)

        keep_t(0, fed_s[l])
        keep_t(1, grad_feed)
        keep_t(2, normed_s[l])
        keep_t(3, grad_attend)
        keep_rank(0, er_s[l, :, :rank])
        keep_rank(1, er_s[l, :, rank:])
        keep_rank(2, grad_shrink)
        keep_rank(3, qr_s[l])
        keep_rank(4, grad_output)

        def put(start, size, stride, value, add=False):
            for b in range(blocks):
                piece = value[b * stride : b * stride + size]
                at = pl.ds(start, size)
                if add:
                    raw_ref[b % 2, b // 2, at] += piece
                else:
                    raw_ref[b % 2, b // 2, at] = piece

        tall = raw_rows.tall
        normed_own = low(product_t(select[...], normed_s[l]))
        pair_weight = dot(normed_own, grad_pair)

        @pl.when(step == 0)
        def _():
            for j in range(2):
                put(j * tall, tall, padded_quarter, pair_weight[:, j * head : (j + 1) * head])

        @pl.when(step > 0)
        def _():
            for j in range(2):
                put(j * tall, tall, padded_quarter, pair_weight[:, j * head : (j + 1) * head], True)

        base = 2 * tall + l * raw_rows.loop

        def put_loop(i, value):
            put(pl.multiple_of(base + i * tall, 8), tall, padded_quarter, value)

        put_loop(0, dot(normed_own, grad_rank))
        for j in range(2):
            put_loop(1 + j, dot(normed_own, grad_pair_rank[:, j * rank : (j + 1) * rank]))
        fed_own = low(product_t(select[...], fed_s[l]))
        for j in range(2):
            put_loop(3 + j, dot(fed_own, grad_widen[:, j * rank : (j + 1) * rank]))
        attend_own = low(product_t(select[...], grad_attend))
        put_loop(5, sum(dot(attend_own, piece) for piece in split3(or_s[l])))
        feed_own = low(product_t(select[...], grad_feed))
        put_loop(6, sum(dot(feed_own, piece) for piece in split3(sr_s[l])))
        for j in range(2):
            rank_own = low(product_t(rank_select, kvr_s[l, :, j * rank : (j + 1) * rank]))
            put(
                pl.multiple_of(base + 7 * tall + j * rank_quarter, 8), rank_quarter, rank_quarter,
                dot(rank_own, grad_pair[:, j * head : (j + 1) * head]),
            )
        return carry

    lax.fori_loop(0, loops, back, 0)
    grad_ref[...] = g_s[...]
    for b in range(blocks):
        ends = jnp.zeros((8, head), jnp.float32)
        raw_ref[b % 2, b // 2, raw_rows.gains :] = ends
        raw_ref[b % 2, b // 2, raw_rows.gains : raw_rows.gains + 2, :block] = gain_s[
            :2, b * block : (b + 1) * block
        ]


def raw_layout(quarter, rank_quarter, loops):
    tall = -(-quarter // 8) * 8
    loop = 7 * tall + 2 * rank_quarter
    gains = 2 * tall + loops * loop
    return SimpleNamespace(tall=tall, loop=loop, gains=gains, all=gains + 8)


def block_and_factors(block_input, cotangent, segments, shared, stacked, dp_size):
    (mixer_gain, feed_gain, query, pair, output, widen, down) = shared
    (q_in, q_out, kv_in, kv_out, o_in, o_out, w_in, w_out, d_in, d_out) = stacked
    tokens, width = block_input.shape
    head = query.shape[1]
    loops, _, rank = q_in.shape
    hidden = down.shape[0]
    cosine, sine, allowed = rotary_tables(segments[0], head)
    weights = (
        q_in, query, q_out, kv_in.reshape(loops, width, 2 * rank), pair, kv_out, output, o_in, o_out,
        w_in.reshape(loops, width, 2 * rank), widen[:, 0], widen[:, 1], w_out, down, d_in, d_out,
    )
    layout = raw_layout(width // (4 * dp_size), rank // (4 * dp_size), loops)
    line = dp_size // 2
    f32, bf16 = jnp.float32, jnp.bfloat16
    shape = jax.ShapeDtypeStruct
    out_shape = (
        shape((tokens, width), bf16),
        shape((tokens, width), f32),
        shape((4, 2, line, width // dp_size, loops * tokens), bf16),
        shape((5, 2, line, rank // dp_size, loops * tokens), bf16),
        shape((6, loops * tokens, WIDE), bf16),
        shape((2, loops * tokens, head), bf16),
        shape((2, line, layout.all, head), f32),
    )
    vmem = pl.BlockSpec(memory_space=pltpu.VMEM)
    hbm = pl.BlockSpec(memory_space=pl.ANY)
    widest = width + rank + 2 * head
    pieces = -(-widest // SUM_STEP)
    dma = pltpu.SemaphoreType.DMA

    def kept(columns, dtype, count=loops):
        return pltpu.VMEM((count, tokens, columns), dtype)

    scratch = [pltpu.VMEM(w.shape, bf16) for w in weights] + [
        kept(width, f32, loops + 1), kept(width, f32), kept(width, bf16), kept(rank, bf16),
        kept(2 * rank, bf16), kept(head, bf16), kept(head, bf16), kept(head, bf16), kept(tokens, f32),
        kept(head, bf16), kept(rank, f32), kept(width, bf16), kept(2 * rank, bf16),
        kept(hidden, f32), kept(hidden, f32), pltpu.VMEM((tokens, hidden), bf16), kept(rank, f32),
        pltpu.VMEM((tokens, hidden), bf16), pltpu.VMEM((tokens, hidden), bf16),
        pltpu.VMEM((tokens, width), f32), pltpu.VMEM((8, width), f32),
        pltpu.VMEM((dp_size * 48, width), bf16),
        pltpu.VMEM((tokens, widest), f32), pltpu.VMEM((tokens, widest), f32),
        pltpu.VMEM((tokens // 2, widest), f32), pltpu.VMEM((tokens // 2, widest), f32),
        pltpu.VMEM((2, tokens // 2, widest), f32),
        dma((len(weights),)), dma((pieces,)), dma((pieces,)), dma((2, pieces)), dma((2, pieces)),
        dma((pieces,)), dma((pieces,)),
    ]
    return pl.pallas_call(
        block_kernel,
        out_shape=out_shape,
        in_specs=[vmem] * 7 + [hbm] * len(weights),
        out_specs=(vmem,) * len(out_shape),
        scratch_shapes=scratch,
        compiler_params=pltpu.CompilerParams(
            collective_id=21, has_side_effects=True, vmem_limit_bytes=60 << 20
        ),
    )(
        block_input, cotangent, cosine, sine, allowed.astype(f32), mixer_gain[None], feed_gain[None],
        *weights,
    )


def line_kernel(
    x_all, r_all, b_own, q_own, raw_all,
    main_out, side_out, raw_out,
    x_send, r_send, b_send, q_send, x_far, r_far, b_far, q_far, raw_own, raw_far,
    main_right, main_left, side_right, side_left, raw_right, raw_left,
    x_s, x_r, r_s, r_r, b_s, b_r, q_s, q_r, w_s, w_r, own_sem,
    mr_s, mr_r, ml_s, ml_r, sr_s, sr_r, sl_s, sl_r, rr_s, rr_r, rl_s, rl_r,
    credit_right, credit_left,
):
    dp, mp = lax.axis_index("dp"), lax.axis_index("mp")
    x = lax.rem(dp, 2)
    z = dp // 2
    last = 3
    pair = (dp + 1 - 2 * x, mp)
    up, down = (dp + 2, mp), (dp - 2, mp)

    barrier = pltpu.get_barrier_semaphore()
    pl.semaphore_signal(barrier, inc=1, device_id=pair, device_id_type=MESH)

    @pl.when(z > 0)
    def _():
        pl.semaphore_signal(barrier, inc=1, device_id=down, device_id_type=MESH)

    @pl.when(z < last)
    def _():
        pl.semaphore_signal(barrier, inc=1, device_id=up, device_id_type=MESH)

    pl.semaphore_wait(barrier, 1 + jnp.minimum(z, 1) + jnp.minimum(last - z, 1))

    def across(source, target, send, recv):
        return pltpu.make_async_remote_copy(
            source, target, send, recv, device_id=pair, device_id_type=MESH
        )

    def x_copy(i):
        return across(x_send.at[i], x_far.at[i], x_s.at[i], x_r.at[i])

    def r_copy(i):
        return across(r_send.at[i], r_far.at[i], r_s.at[i], r_r.at[i])

    def b_copy(i):
        return across(b_send.at[i], b_far.at[i], b_s.at[i], b_r.at[i])

    def send_x(i):
        x_send[i] = x_all[i, 1 - x].astype(jnp.float32)
        x_copy(i).start()

    def send_r(i):
        r_send[i] = r_all[i, 1 - x].astype(jnp.float32)
        r_copy(i).start()

    def send_b(i):
        b_send[i] = b_own[i].astype(jnp.float32)
        b_copy(i).start()

    q_copy = across(q_send, q_far, q_s, q_r)
    w_copy = across(raw_all.at[1 - x], raw_far, w_s, w_r)
    own_copy = pltpu.make_async_copy(raw_all.at[x], raw_own, own_sem)

    send_x(0)
    send_r(0)
    send_b(0)
    send_b(1)
    own_copy.start()

    def chain(target, step, slot, steps, value, out, right, left, r_s, r_r, l_s, l_r, credits):
        def move(buffer, send, recv, i, s, device):
            return pltpu.make_async_remote_copy(
                buffer.at[i, s], buffer.at[i, s], send.at[i, s], recv.at[i, s],
                device_id=device, device_id_type=MESH,
            )

        def pass_on(i, buffer, send, recv, onward, source, is_first, credit):
            if credits:

                @pl.when(step >= 1)
                def _():
                    move(buffer, send, recv, i, 1 - slot, onward).wait_send()

                    @pl.when(jnp.logical_and(jnp.logical_not(is_first), step <= steps - 2))
                    def _():
                        pl.semaphore_signal(
                            credit.at[i], inc=1, device_id=source, device_id_type=MESH
                        )

            @pl.when(is_first)
            def _():
                buffer[i, slot] = value

            @pl.when(jnp.logical_not(is_first))
            def _():
                move(buffer, send, recv, i, slot, onward).wait_recv()
                buffer[i, slot] += value

            if credits:

                @pl.when(step >= 2)
                def _():
                    pl.semaphore_wait(credit.at[i], 1)

            move(buffer, send, recv, i, slot, onward).start()

        @pl.when(target > z)
        def _():
            pass_on(target - 1, right, r_s, r_r, up, down, z == 0, credit_right)

        @pl.when(target < z)
        def _():
            pass_on(target, left, l_s, l_r, down, up, z == last, credit_left)

        @pl.when(target == z)
        def _():
            out[...] = value

            @pl.when(z > 0)
            def _():
                move(right, r_s, r_r, z - 1, slot, up).wait_recv()
                out[...] += right[z - 1, slot]
                if credits:

                    @pl.when(step <= steps - 3)
                    def _():
                        pl.semaphore_signal(
                            credit_right.at[z - 1], inc=1, device_id=down, device_id_type=MESH
                        )

            @pl.when(z < last)
            def _():
                move(left, l_s, l_r, z, slot, down).wait_recv()
                out[...] += left[z, slot]
                if credits:

                    @pl.when(step <= steps - 3)
                    def _():
                        pl.semaphore_signal(
                            credit_left.at[z], inc=1, device_id=up, device_id_type=MESH
                        )

    def settle(slot, right, left, r_s, l_s):
        for target in range(4):

            @pl.when(target > z)
            def _():
                i = target - 1
                pltpu.make_async_remote_copy(
                    right.at[i, slot], right.at[i, slot], r_s.at[i, slot], r_s.at[i, slot],
                    device_id=up, device_id_type=MESH,
                ).wait_send()

            @pl.when(target < z)
            def _():
                pltpu.make_async_remote_copy(
                    left.at[target, slot], left.at[target, slot], l_s.at[target, slot], l_s.at[target, slot],
                    device_id=down, device_id_type=MESH,
                ).wait_send()

    def order(turn):
        def near(end):
            return jnp.where(
                end == 0,
                3 - turn,
                jnp.where(turn == 0, 3, jnp.where(turn == 1, 0, 4 - turn)),
            )

        return jnp.where(z < 2, near(z), 3 - near(3 - z))

    def dot(left, right):
        return jnp.dot(
            left.astype(jnp.bfloat16), right.astype(jnp.bfloat16), preferred_element_type=jnp.float32
        )

    steps = b_own.shape[0]

    def left_times(x_index, group, target, own, far):
        half = own.shape[0] // 2
        rank_own, rank_far = r_all[group, x, target], r_far[group, target].astype(jnp.bfloat16)
        return [
            dot(x_all[x_index, x, target], own) + dot(x_far[x_index, target], far),
            dot(rank_own[:, :half], own[:half]) + dot(rank_far[:, :half], far[:half]),
            dot(rank_own[:, half:], own[half:]) + dot(rank_far[:, half:], far[half:]),
        ]

    def turn_body(at, carry):
        step, turn = at // 4, lax.rem(at, 4)
        slot = lax.rem(step, 2)
        group = step // 2
        target = order(turn)

        @pl.when(turn == 0)
        def _():
            b_copy(step).wait_recv()

            @pl.when(slot == 0)
            def _():
                r_copy(group).wait_recv()

            @pl.when(step == 0)
            def _():
                x_copy(0).wait_recv()

            @pl.when(step == 4)
            def _():
                x_copy(1).wait_recv()

            @pl.when(step + 2 < steps)
            def _():
                @pl.when(slot == 0)
                def _():
                    send_r(group + 1)

                @pl.when(step == 2)
                def _():
                    send_x(1)

                send_b(step + 2)

            @pl.when(step == steps - 2)
            def _():
                send_x(2)
                send_x(3)
                send_r(3)
                send_r(4)
                q_send[...] = q_own[...].astype(jnp.float32)
                q_copy.start()

            @pl.when(step == steps - 1)
            def _():
                w_copy.start()

        value = jnp.concatenate(
            left_times(
                group // 2, group, target, b_own[step], b_far[step].astype(jnp.bfloat16)
            ),
            axis=0,
        )
        chain(
            target, step, slot, steps, value, main_out.at[step], main_right, main_left,
            mr_s, mr_r, ml_s, ml_r, True,
        )
        return carry

    lax.fori_loop(0, 4 * steps, turn_body, 0)

    for i in (2, 3):
        x_copy(i).wait_recv()
    for i in (3, 4):
        r_copy(i).wait_recv()
    q_copy.wait_recv()

    def side_body(turn, carry):
        target = order(turn)
        value = jnp.concatenate(
            [
                jnp.concatenate(
                    left_times(
                        2 + i, 3 + i, target, q_own[i], q_far[i].astype(jnp.bfloat16)
                    ),
                    axis=0,
                )
                for i in range(2)
            ],
            axis=1,
        )
        chain(
            target, 0, 0, 1, value, side_out, side_right, side_left,
            sr_s, sr_r, sl_s, sl_r, False,
        )
        return carry

    lax.fori_loop(0, 4, side_body, 0)

    w_copy.wait_recv()
    own_copy.wait()

    def raw_body(turn, carry):
        target = order(turn)
        chain(
            target, 0, 0, 1, raw_own[target] + raw_far[target], raw_out, raw_right, raw_left,
            rr_s, rr_r, rl_s, rl_r, False,
        )
        return carry

    lax.fori_loop(0, 4, raw_body, 0)

    settle((steps - 1) % 2, main_right, main_left, mr_s, ml_s)
    settle(0, side_right, side_left, sr_s, sl_s)
    settle(0, raw_right, raw_left, rr_s, rl_s)
    for i in range(4):
        x_copy(i).wait_send()
    for i in range(5):
        r_copy(i).wait_send()
    for i in range(steps):
        b_copy(i).wait_send()
    q_copy.wait_send()
    w_copy.wait_send()


def line_gradients(factors, loops, dp_size, mp_size, hidden):
    x_all, r_all, b_own, q_own, raw = factors
    block, rank_block, head = x_all.shape[3], r_all.shape[3], q_own.shape[2]
    quarter, rank_quarter = block // mp_size, rank_block // mp_size
    layout = raw_layout(quarter, rank_quarter, loops)
    rows = block + loops * rank_block
    steps = b_own.shape[0]
    vmem = pl.BlockSpec(memory_space=pltpu.VMEM)
    hbm = pl.BlockSpec(memory_space=pl.ANY)
    dma = pltpu.SemaphoreType.DMA
    f32 = jnp.float32
    line = dp_size // 2 - 1
    half_x = pltpu.VMEM((x_all.shape[0], *x_all.shape[2:]), f32)
    half_r = pltpu.VMEM((r_all.shape[0], *r_all.shape[2:]), f32)
    whole_b, whole_q = pltpu.VMEM(b_own.shape, f32), pltpu.VMEM(q_own.shape, f32)
    main, side, rest = pl.pallas_call(
        line_kernel,
        out_shape=(
            jax.ShapeDtypeStruct((steps, rows, WIDE), f32),
            jax.ShapeDtypeStruct((rows, 2 * head), f32),
            jax.ShapeDtypeStruct((layout.all, head), f32),
        ),
        in_specs=[vmem] * 4 + [hbm],
        out_specs=(vmem, vmem, vmem),
        scratch_shapes=[half_x, half_r, whole_b, whole_q] * 2
        + [pltpu.VMEM(raw.shape[1:], f32)] * 2
        + [pltpu.VMEM((line, 2, rows, WIDE), f32)] * 2
        + [pltpu.VMEM((line, 1, rows, 2 * head), f32)] * 2
        + [pltpu.VMEM((line, 1, layout.all, head), f32)] * 2
        + [dma((4,))] * 2 + [dma((5,))] * 2 + [dma((steps,))] * 2 + [dma] * 5
        + [dma((line, 2))] * 4 + [dma((line, 1))] * 8
        + [pltpu.SemaphoreType.REGULAR((line,))] * 2,
        compiler_params=pltpu.CompilerParams(
            collective_id=20, has_side_effects=True, vmem_limit_bytes=60 << 20
        ),
    )(x_all, r_all, b_own, q_own, raw)

    wide = [
        jnp.concatenate([main[2 * i], main[2 * i + 1][:, : hidden - WIDE]], axis=1) for i in range(3)
    ]
    narrow = [side[:, :head], side[:, head:]]

    def shared_rows(value):
        return value[:block]

    def loop_rows(value, i):
        return value[block + i * rank_block : block + (i + 1) * rank_block]

    tall = layout.tall

    def raw_rows(start, size):
        return rest[start : start + size]

    pair_weight = jnp.concatenate([raw_rows(0, quarter), raw_rows(tall, quarter)], axis=1)
    query_inner, pair_inner, expand_inner, pair_outer, outers = [], [], [], [], []
    for i in range(loops):
        base = 2 * tall + i * layout.loop
        own = [raw_rows(base + j * tall, quarter) for j in range(7)]
        query_inner.append(own[0])
        pair_inner.append(jnp.stack(own[1:3], axis=1))
        expand_inner.append(jnp.stack(own[3:5], axis=1))
        outers += own[5:7]
        pair_outer.append(
            jnp.stack([raw_rows(base + 7 * tall + j * rank_quarter, rank_quarter) for j in range(2)])
        )
    outers = lax.all_gather(jnp.stack(outers), "mp")
    outers = jnp.swapaxes(outers, 0, 1).reshape(2 * loops, block, -1).swapaxes(1, 2)
    gains = rest[layout.gains : layout.gains + 2, :block]
    stack = jnp.stack
    return (
        gains[0],
        gains[1],
        shared_rows(narrow[0]),
        pair_weight,
        shared_rows(narrow[1]).T,
        stack([shared_rows(wide[0]), shared_rows(wide[1])], axis=1),
        shared_rows(wide[2]).T,
        stack(query_inner),
        stack([loop_rows(narrow[0], i) for i in range(loops)]),
        stack(pair_inner),
        stack(pair_outer),
        stack([loop_rows(narrow[1], i).T for i in range(loops)]),
        outers[0::2],
        stack(expand_inner),
        stack([stack([loop_rows(wide[j], i) for j in range(2)]) for i in range(loops)]),
        stack([loop_rows(wide[2], i).T for i in range(loops)]),
        outers[1::2],
    )


def per_device(dp_size, mp_size, block_input, cotangent, segments, *parameters):
    shared, stacked = parameters[:7], parameters[7:]
    loops = stacked[0].shape[0]
    if dp_size == 8 and mp_size == 4 and loops == 2:
        output, input_grad, *factors = block_and_factors(
            block_input, cotangent, segments, shared, stacked, dp_size
        )
        gradients = line_gradients(factors, loops, dp_size, mp_size, shared[6].shape[0])
        return (output, input_grad, *gradients)
    tables = rotary_tables(segments[0], shared[3].shape[1] // 2)
    total = mp_total(mp_size)
    state = block_input.astype(jnp.float32)
    kept_all = []
    for i in range(loops):
        state, kept = forward_loop(state, shared, [v[i] for v in stacked], tables, total, 1)
        kept_all.append(kept)
    upstream = cotangent.astype(jnp.float32)
    for i in reversed(range(loops)):
        upstream = reverse_loop(
            upstream, kept_all[i], shared, [v[i] for v in stacked], tables, total, 3
        )
    return (state.astype(jnp.bfloat16), upstream, *scattered_gradients(kept_all, dp_size, mp_size))


def solution(mesh):
    in_specs = (
        P("dp", None),
        P("dp", None),
        P("dp", None),
        P(),
        P(),
        P(None, "mp"),
        P(),
        P("mp", None),
        P(None, None, "mp"),
        P("mp", None),
        P(),
        P(None, None, "mp"),
        P(),
        P(),
        P(None, "mp", None),
        P(),
        P(),
        P(None, None, None, "mp"),
        P(None, "mp", None),
        P(),
    )
    out_specs = (
        P("dp", None),
        P("dp", None),
        P("dp"),
        P("dp"),
        P("dp", "mp"),
        P(("dp", "mp"), None),
        P("mp", "dp"),
        P("dp", None, "mp"),
        P("mp", "dp"),
        P(None, ("dp", "mp"), None),
        P(None, "dp", "mp"),
        P(None, ("dp", "mp"), None, None),
        P(None, None, ("dp", "mp"), None),
        P(None, "mp", "dp"),
        P(None, None, "dp"),
        P(None, ("dp", "mp"), None, None),
        P(None, None, "dp", "mp"),
        P(None, "mp", "dp"),
        P(None, None, "dp"),
    )
    return jax.shard_map(
        functools.partial(per_device, mesh.shape["dp"], mesh.shape["mp"]),
        mesh=mesh, in_specs=in_specs, out_specs=out_specs, check_vma=False
    )
```

```python
import functools
import math
from types import SimpleNamespace

import jax
import jax.numpy as jnp
from jax import lax
from jax.experimental import pallas as pl
from jax.experimental.pallas import tpu as pltpu
from jax.sharding import PartitionSpec as P

EPSILON = 1e-06
MASKED = -1e30
MESH = pl.DeviceIdType.MESH


def product(left, right):
    return jnp.dot(left, right, preferred_element_type=jnp.float32)


def product_t(left, right):
    return lax.dot_general(
        left, right, (((1,), (1,)), ((), ())), preferred_element_type=jnp.float32
    )


def product_tn(left, right):
    return lax.dot_general(
        left, right, (((0,), (0,)), ((), ())), preferred_element_type=jnp.float32
    )


def exact_product(left, right):
    return jnp.dot(left, right, precision=lax.Precision.HIGHEST, preferred_element_type=jnp.float32)


def exact_tn(left, right):
    return lax.dot_general(
        left,
        right,
        (((0,), (0,)), ((), ())),
        precision=lax.Precision.HIGHEST,
        preferred_element_type=jnp.float32,
    )


def normalize(hidden_state, gain):
    factor = lax.rsqrt(jnp.mean(hidden_state * hidden_state, axis=-1, keepdims=True) + EPSILON)
    return (hidden_state * factor * gain, factor)


def normalize_back(hidden_state, factor, gain, upstream_gradient):
    unit = hidden_state * factor
    scaled = upstream_gradient * gain
    downstream = factor * (scaled - unit * jnp.mean(scaled * unit, axis=-1, keepdims=True))
    return (downstream, jnp.sum(upstream_gradient * unit, axis=0))


def rotate(values, cosine_table, sine_table):
    half_width = values.shape[-1] // 2
    first = values[..., :half_width]
    second = values[..., half_width:]
    return jnp.concatenate(
        [first * cosine_table - second * sine_table, second * cosine_table + first * sine_table],
        axis=-1,
    )


def rotary_tables(segment_row, head_size):
    length_value = segment_row.shape[0]
    earlier = jnp.sum((segment_row[None, :] < segment_row[:, None]).astype(jnp.int32), axis=1)
    position = (jnp.arange(length_value, dtype=jnp.int32) - earlier).astype(jnp.float32)
    steps_half = jnp.arange(head_size // 2, dtype=jnp.float32)
    frequency = 10000.0 ** (-2.0 * steps_half / head_size)
    angles = position[:, None] * frequency[None, :]
    same_segment = segment_row[:, None] == segment_row[None, :]
    ordinal = jnp.arange(length_value, dtype=jnp.int32)
    allowed_mask = same_segment & (ordinal[:, None] >= ordinal[None, :])
    return (jnp.cos(angles), jnp.sin(angles), allowed_mask)


def gelu_tanh(values):
    return jax.nn.gelu(values, approximate=True)


def attention_probs(queries, keys, allowed_mask, score_scale):
    scores = (
        jnp.einsum("ihd,jd->hij", queries, keys, preferred_element_type=jnp.float32) * score_scale
    )
    return jnp.where(allowed_mask[None], scores, MASKED)


def mp_total(size):
    def kernel(part, out, near, mine, far, core_send, core_recv, y_send, y_recv, back_send, back_recv):
        dp, mp = lax.axis_index("dp"), lax.axis_index("mp")
        side = lax.rem(mp, 2)
        core = (dp, mp + 1 - 2 * side)
        other = (dp, lax.rem(mp + 2, 4))
        half = part.shape[0] // 2
        pieces = near.shape[0]
        width = part.shape[1] // pieces
        own = pl.ds(pl.multiple_of(side * half, half), half)
        theirs = pl.ds(pl.multiple_of((1 - side) * half, half), half)

        def columns(i):
            return pl.ds(i * width, width)

        barrier = pltpu.get_barrier_semaphore()
        for device in (core, other):
            pl.semaphore_signal(barrier, inc=1, device_id=device, device_id_type=MESH)
        pl.semaphore_wait(barrier, 2)
        first = [
            pltpu.make_async_remote_copy(
                part.at[theirs, columns(i)], near.at[i], core_send.at[i], core_recv.at[i],
                device_id=core, device_id_type=MESH,
            )
            for i in range(pieces)
        ]
        second = [
            pltpu.make_async_remote_copy(
                mine.at[i], far.at[i], y_send.at[i], y_recv.at[i],
                device_id=other, device_id_type=MESH,
            )
            for i in range(pieces)
        ]
        third = [
            pltpu.make_async_remote_copy(
                out.at[own, columns(i)], out.at[own, columns(i)], back_send.at[i], back_recv.at[i],
                device_id=core, device_id_type=MESH,
            )
            for i in range(pieces)
        ]
        for copy in first:
            copy.start()
        for i in range(pieces):
            first[i].wait_recv()
            mine[i] = part[own, columns(i)] + near[i]
            second[i].start()
        for i in range(pieces):
            second[i].wait_recv()
            out[own, columns(i)] = mine[i] + far[i]
            third[i].start()
        for copy in third:
            copy.wait_recv()
        for copy in first + second + third:
            copy.wait_send()

    def total(identity, *parts):
        if size != 4:
            return lax.psum(parts, "mp")
        joined = jnp.concatenate(parts, axis=1)
        tokens_here, columns_here = joined.shape
        pieces = 1
        for count in (5, 4, 3, 2):
            if columns_here % (128 * count) == 0:
                pieces = count
                break
        half = (pieces, tokens_here // 2, columns_here // pieces)
        summed = pl.pallas_call(
            kernel,
            out_shape=jax.ShapeDtypeStruct(joined.shape, jnp.float32),
            in_specs=[pl.BlockSpec(memory_space=pltpu.VMEM)],
            out_specs=pl.BlockSpec(memory_space=pltpu.VMEM),
            scratch_shapes=[pltpu.VMEM(half, jnp.float32)] * 3
            + [pltpu.SemaphoreType.DMA((pieces,))] * 6,
            compiler_params=pltpu.CompilerParams(
                collective_id=identity, has_side_effects=True, vmem_limit_bytes=16 << 20
            ),
        )(joined)
        edges, start = [], 0
        for part in parts:
            edges.append(summed[:, start : start + part.shape[1]])
            start += part.shape[1]
        return tuple(edges)

    return total


def forward_loop(hidden_state, shared, adapters, tables, total, identity):
    (mixer_gain, feed_gain, query_matrix, pair_matrix, output_matrix, widen_matrix, down_matrix) = shared
    (q_in, q_out, kv_in, kv_out, o_in, o_out, w_in, w_out, d_in, d_out) = adapters
    cosine, sine, allowed = tables
    tokens_here, width = hidden_state.shape
    head = pair_matrix.shape[1] // 2
    heads = query_matrix.shape[1] // head
    rank = q_in.shape[1]
    hidden = down_matrix.shape[0]
    kept = SimpleNamespace(h=hidden_state)
    normed, kept.mixer_factor = normalize(hidden_state, mixer_gain)
    normed = normed.astype(jnp.bfloat16)
    query_rank = product(normed, q_in).astype(jnp.bfloat16)
    query_linear = product(normed, query_matrix) + product(query_rank, q_out)
    pair_rank = product(normed, kv_in.reshape(width, 2 * rank)).astype(jnp.bfloat16)
    pair_linear = product(normed, pair_matrix) + jnp.concatenate(
        [product(pair_rank[:, :rank], kv_out[0]), product(pair_rank[:, rank:], kv_out[1])], axis=1
    )
    queries = rotate(
        query_linear.reshape(tokens_here, heads, head), cosine[:, None], sine[:, None]
    ).astype(jnp.bfloat16)
    keys = rotate(pair_linear[:, :head], cosine, sine).astype(jnp.bfloat16)
    values = pair_linear[:, head:].astype(jnp.bfloat16)
    masked = attention_probs(queries, keys, allowed, 1.0 / math.sqrt(head))
    expo = jnp.exp(masked - jnp.max(masked, axis=-1, keepdims=True))
    probs = expo / jnp.sum(expo, axis=-1, keepdims=True)
    mixed = jnp.einsum(
        "hij,jd->ihd", probs.astype(jnp.bfloat16), values, preferred_element_type=jnp.float32
    )
    mixed = mixed.reshape(tokens_here, heads * head).astype(jnp.bfloat16)
    summed, output_rank = total(identity, product(mixed, output_matrix), product(mixed, o_in))
    middle = hidden_state + summed + exact_product(output_rank, o_out.astype(jnp.float32))
    fed, kept.feed_factor = normalize(middle, feed_gain)
    fed = fed.astype(jnp.bfloat16)
    widen_rank = product(fed, w_in.reshape(width, 2 * rank)).astype(jnp.bfloat16)
    gate = product(fed, widen_matrix[:, 0]) + product(widen_rank[:, :rank], w_out[0])
    up = product(fed, widen_matrix[:, 1]) + product(widen_rank[:, rank:], w_out[1])
    activated = (gelu_tanh(gate) * up).astype(jnp.bfloat16)
    shrunk, shrink_rank = total(identity + 1, product(activated, down_matrix), product(activated, d_in))
    result = middle + shrunk + exact_product(shrink_rank, d_out.astype(jnp.float32))
    vars(kept).update(
        normed=normed, query_rank=query_rank, pair_rank=pair_rank, queries=queries, keys=keys,
        values=values, probs=probs, mixed=mixed, output_rank=output_rank, middle=middle, fed=fed,
        widen_rank=widen_rank, gate=gate, up=up, activated=activated, shrink_rank=shrink_rank,
    )
    return result, kept


def reverse_loop(upstream, kept, shared, adapters, tables, total, identity):
    (mixer_gain, feed_gain, query_matrix, pair_matrix, output_matrix, widen_matrix, down_matrix) = shared
    (q_in, q_out, kv_in, kv_out, o_in, o_out, w_in, w_out, d_in, d_out) = adapters
    cosine, sine, allowed = tables
    tokens_here, width = upstream.shape
    head = pair_matrix.shape[1] // 2
    heads = query_matrix.shape[1] // head
    rank = q_in.shape[1]
    scale = 1.0 / math.sqrt(head)
    grad_feed = upstream.astype(jnp.bfloat16)
    grad_shrink_rank = product_t(grad_feed, d_out).astype(jnp.bfloat16)
    grad_activated = product_t(grad_feed, down_matrix) + product_t(grad_shrink_rank, d_in)
    gelu_value, gelu_pullback = jax.vjp(gelu_tanh, kept.gate)
    grad_gate = gelu_pullback(grad_activated * kept.up)[0].astype(jnp.bfloat16)
    grad_up = (grad_activated * gelu_value).astype(jnp.bfloat16)
    grad_fed, grad_widen_rank = total(
        identity,
        product_t(grad_gate, widen_matrix[:, 0]) + product_t(grad_up, widen_matrix[:, 1]),
        jnp.concatenate([product_t(grad_gate, w_out[0]), product_t(grad_up, w_out[1])], axis=1),
    )
    grad_widen_rank = grad_widen_rank.astype(jnp.bfloat16)
    grad_fed = grad_fed + product_t(grad_widen_rank, w_in.reshape(width, 2 * rank))
    grad_norm, feed_gain_grad = normalize_back(kept.middle, kept.feed_factor, feed_gain, grad_fed)
    grad_middle = upstream + grad_norm
    grad_attend = grad_middle.astype(jnp.bfloat16)
    grad_output_rank = product_t(grad_attend, o_out).astype(jnp.bfloat16)
    grad_mixed = product_t(grad_attend, output_matrix) + product_t(grad_output_rank, o_in)
    grad_mixed = grad_mixed.astype(jnp.bfloat16).reshape(tokens_here, heads, head)
    queries, keys, values, probs = kept.queries, kept.keys, kept.values, kept.probs
    grad_probs = jnp.einsum("ihd,jd->hij", grad_mixed, values, preferred_element_type=jnp.float32)
    delta = jnp.sum(grad_probs * probs, axis=-1, keepdims=True)
    grad_scores = (probs * (grad_probs - delta)).astype(jnp.bfloat16)
    grad_queries = scale * jnp.einsum(
        "hij,jd->ihd", grad_scores, keys, preferred_element_type=jnp.float32
    )
    grad_keys = scale * jnp.einsum(
        "hij,ihd->jd", grad_scores, queries, preferred_element_type=jnp.float32
    )
    grad_values = jnp.einsum(
        "hij,ihd->jd", probs.astype(jnp.bfloat16), grad_mixed, preferred_element_type=jnp.float32
    )
    grad_query = rotate(grad_queries, cosine[:, None], -sine[:, None])
    grad_query = grad_query.reshape(tokens_here, heads * head).astype(jnp.bfloat16)
    grad_normed, grad_query_rank, grad_pair = total(
        identity + 1,
        product_t(grad_query, query_matrix),
        product_t(grad_query, q_out),
        jnp.concatenate([rotate(grad_keys, cosine, -sine), grad_values], axis=1),
    )
    grad_query_rank = grad_query_rank.astype(jnp.bfloat16)
    grad_pair = grad_pair.astype(jnp.bfloat16)
    grad_pair_rank = jnp.concatenate(
        [product_t(grad_pair[:, :head], kv_out[0]), product_t(grad_pair[:, head:], kv_out[1])], axis=1
    ).astype(jnp.bfloat16)
    grad_normed = (
        grad_normed
        + product_t(grad_query_rank, q_in)
        + product_t(grad_pair, pair_matrix)
        + product_t(grad_pair_rank, kv_in.reshape(width, 2 * rank))
    )
    grad_norm, mixer_gain_grad = normalize_back(
        kept.h, kept.mixer_factor, mixer_gain, grad_normed
    )
    vars(kept).update(
        grad_feed=grad_feed, grad_shrink_rank=grad_shrink_rank, grad_gate=grad_gate, grad_up=grad_up,
        grad_widen_rank=grad_widen_rank, grad_attend=grad_attend, grad_output_rank=grad_output_rank,
        grad_query=grad_query, grad_query_rank=grad_query_rank, grad_pair=grad_pair,
        grad_pair_rank=grad_pair_rank, feed_gain_grad=feed_gain_grad, mixer_gain_grad=mixer_gain_grad,
    )
    return grad_middle + grad_norm


def scattered_gradients(kept, dp_size, mp_size):
    def scatter(value, axis):
        return lax.psum_scatter(value, "dp", scatter_dimension=axis, tiled=True)

    def shared_of(factors):
        return sum(product_tn(*factors(k)) for k in kept)

    def each(function):
        return jnp.stack([function(k) for k in kept], axis=0)

    def quarter(value, axis):
        block = scatter(value, axis)
        size = block.shape[axis] // mp_size
        return lax.dynamic_slice_in_dim(block, lax.axis_index("mp") * size, size, axis)

    width = kept[0].normed.shape[1]
    rank = kept[0].query_rank.shape[1]
    head = kept[0].grad_pair.shape[1] // 2

    def pair_outer(k):
        left, right = k.pair_rank, k.grad_pair
        return jnp.stack(
            [product_tn(left[:, :rank], right[:, :head]), product_tn(left[:, rank:], right[:, head:])]
        )

    def expand_outer(k):
        left = k.widen_rank
        return jnp.stack(
            [product_tn(left[:, :rank], k.grad_gate), product_tn(left[:, rank:], k.grad_up)]
        )

    return (
        scatter(sum(k.mixer_gain_grad for k in kept), 0),
        scatter(sum(k.feed_gain_grad for k in kept), 0),
        scatter(shared_of(lambda k: (k.normed, k.grad_query)), 0),
        quarter(shared_of(lambda k: (k.normed, k.grad_pair)), 0),
        scatter(shared_of(lambda k: (k.mixed, k.grad_attend)), 1),
        scatter(jnp.stack([shared_of(lambda k: (k.fed, k.grad_gate)), shared_of(lambda k: (k.fed, k.grad_up))], axis=1), 0),
        scatter(shared_of(lambda k: (k.activated, k.grad_feed)), 1),
        quarter(each(lambda k: product_tn(k.normed, k.grad_query_rank)), 1),
        scatter(each(lambda k: product_tn(k.query_rank, k.grad_query)), 1),
        quarter(
            each(lambda k: product_tn(k.normed, k.grad_pair_rank).reshape(width, 2, rank)), 1
        ),
        quarter(each(pair_outer), 2),
        scatter(each(lambda k: product_tn(k.mixed, k.grad_output_rank)), 2),
        scatter(
            each(lambda k: exact_tn(k.output_rank, k.grad_attend.astype(jnp.float32))), 2
        ),
        quarter(
            each(lambda k: product_tn(k.fed, k.grad_widen_rank).reshape(width, 2, rank)), 1
        ),
        scatter(each(expand_outer), 2),
        scatter(each(lambda k: product_tn(k.activated, k.grad_shrink_rank)), 2),
        scatter(each(lambda k: exact_tn(k.shrink_rank, k.grad_feed.astype(jnp.float32))), 2),
    )


WIDE = 896


def split3(value):
    high = value.astype(jnp.bfloat16)
    rest = value - high.astype(jnp.float32)
    middle = rest.astype(jnp.bfloat16)
    low = (rest - middle.astype(jnp.float32)).astype(jnp.bfloat16)
    return high, middle, low


WEIGHTS = (
    "q_in", "query", "q_out", "kv_in", "pair", "kv_out", "output", "o_in", "o_out",
    "w_in", "gate", "up", "w_out", "down", "d_in", "d_out",
)
SUM_STEP = 384


def block_kernel(*refs):
    (h_in, cot, cosine_ref, sine_ref, mask_ref, mixer_gain, feed_gain), refs = refs[:7], refs[7:]
    count = len(WEIGHTS)
    sources, refs = refs[:count], refs[count:]
    (
        out_ref, grad_ref, raw_ref, x_all, r_all, b_all, q_all, x_got, r_got, b_got, x_end, r_end, b_end,
    ), refs = refs[:13], refs[13:]
    weights, refs = refs[:count], refs[count:]
    (
        h_s, mid_s, normed_s, qr_s, kvr_s, q_s, k_s, v_s, probs_s, mixed_s, or_s, fed_s, er_s,
        gate_s, up_s, act_s, sr_s, gg_s, gu_s, g_s, gain_s, select,
        part, total, near, mine, far, xs, rs, bs, qs,
        load_sems, c_s, c_r, y_s, y_r, e_s, e_r,
        xl, rl, bl, ql, x_s, x_r, r_s, r_r, b_s, b_r, xe_s, xe_r, re_s, re_r, be_s, be_r,
    ) = refs
    W = SimpleNamespace(**dict(zip(WEIGHTS, weights)))
    dp, mp = lax.axis_index("dp"), lax.axis_index("mp")
    side = lax.rem(mp, 2)
    core = (dp, mp + 1 - 2 * side)
    other = (dp, lax.rem(mp + 2, 4))
    loads = [
        pltpu.make_async_copy(source, target, load_sems.at[i])
        for i, (source, target) in enumerate(zip(sources, weights))
    ]
    load = SimpleNamespace(**dict(zip(WEIGHTS, loads)))
    for copy in loads:
        copy.start()
    x = lax.rem(dp, 2)
    z = dp // 2
    pair = (dp + 1 - 2 * x, mp)
    near_end = (dp + 2 - 4 * lax.rem(z, 2), mp)
    is_end = jnp.logical_or(z == 0, z == 3)
    barrier = pltpu.get_barrier_semaphore()
    for device in (core, other, pair, near_end):
        pl.semaphore_signal(barrier, inc=1, device_id=device, device_id_type=MESH)
    pl.semaphore_wait(barrier, 4)

    tokens, width = h_in.shape
    half = tokens // 2
    head = W.query.shape[1]
    rank = W.q_in.shape[2]
    hidden = W.down.shape[0]
    loops = W.q_in.shape[0]
    scale = 1.0 / math.sqrt(head)
    own = pl.ds(pl.multiple_of(side * half, half), half)
    theirs = pl.ds(pl.multiple_of((1 - side) * half, half), half)
    blocks = x_all.shape[1] * x_all.shape[2]
    block = width // blocks
    quarter = block // 4
    rank_quarter = rank // (4 * blocks)
    chunks = [(0, WIDE), (WIDE, hidden - WIDE)]

    def remote(source, target, send, recv, device):
        return pltpu.make_async_remote_copy(
            source, target, send, recv, device_id=device, device_id_type=MESH
        )

    def span(l):
        return pl.ds(pl.multiple_of(l * tokens, tokens), tokens)

    def end_span(l, is_far):
        return pl.ds(pl.multiple_of((2 * l + is_far) * tokens, tokens), tokens)

    def x_copies(i, l):
        across = onward = None
        if i < 2:
            across = remote(
                xs.at[i, 1 - x], x_got.at[i, :, :, span(l)], x_s.at[i, l], x_r.at[i, l], pair
            )
        if i == 1:
            onward = remote(
                xs.at[i, x], x_end.at[:, :, end_span(l, 0)], xe_s.at[0, l], xe_r.at[0, l], near_end
            )
        return pltpu.make_async_copy(xs.at[i], x_all.at[i, :, :, :, span(l)], xl.at[i, l]), across, onward

    def r_copies(i, l):
        across = onward = None
        if i < 3:
            across = remote(
                rs.at[i, 1 - x], r_got.at[i, :, :, span(l)], r_s.at[i, l], r_r.at[i, l], pair
            )
        if i == 2:
            onward = remote(
                rs.at[i, x], r_end.at[:, :, end_span(l, 0)], re_s.at[0, l], re_r.at[0, l], near_end
            )
        return pltpu.make_async_copy(rs.at[i], r_all.at[i, :, :, :, span(l)], rl.at[i, l]), across, onward

    def b_copies(i, l):
        across = onward = None
        if i in (0, 4, 5):
            k = max(0, i - 3)
            across = remote(bs.at[i], b_got.at[k, span(l)], b_s.at[k, l], b_r.at[k, l], pair)
        if i >= 4:
            onward = remote(
                bs.at[i], b_end.at[i - 4, end_span(l, 0)],
                be_s.at[i - 4, 0, l], be_r.at[i - 4, 0, l], near_end,
            )
        return pltpu.make_async_copy(bs.at[i], b_all.at[i, span(l)], bl.at[i, l]), across, onward

    def q_copies(i, l):
        return pltpu.make_async_copy(qs.at[i], q_all.at[i, span(l)], ql.at[i, l]), None, None

    def launch(copies):
        local, across, onward = copies
        local.start()
        if across is not None:
            across.start()
        if onward is not None:

            @pl.when(is_end)
            def _():
                onward.start()

    def finish(copies):
        local, across, onward = copies
        local.wait()
        if across is not None:
            across.wait_send()
        if onward is not None:

            @pl.when(is_end)
            def _():
                onward.wait_send()

    def far_feed(l):
        return [
            remote(
                x_got.at[1, :, :, span(l)], x_end.at[:, :, end_span(l, 1)],
                xe_s.at[1, l], xe_r.at[1, l], near_end,
            ),
            remote(
                r_got.at[2, :, :, span(l)], r_end.at[:, :, end_span(l, 1)],
                re_s.at[1, l], re_r.at[1, l], near_end,
            ),
        ]

    def far_act(l):
        return [
            remote(
                b_got.at[1 + k, span(l)], b_end.at[k, end_span(l, 1)],
                be_s.at[k, 1, l], be_r.at[k, 1, l], near_end,
            )
            for k in range(2)
        ]

    def pass_act(l):
        for i in (4, 5):
            b_copies(i, l)[1].wait_recv()

        @pl.when(is_end)
        def _():
            for copy in far_act(l):
                copy.start()

    def pass_feed(l):
        x_copies(1, l)[1].wait_recv()
        r_copies(2, l)[1].wait_recv()

        @pl.when(is_end)
        def _():
            for copy in far_feed(l):
                copy.start()

    def ship_x(i, l, value, again, before):
        @pl.when(again)
        def _():
            finish(x_copies(i, before))

        turned = value.astype(jnp.float32).T
        for b in range(blocks):
            xs[i, b % 2, b // 2] = turned[b * block : (b + 1) * block]
        launch(x_copies(i, l))

    def ship_r(i, l, value, again, before):
        @pl.when(again)
        def _():
            finish(r_copies(i, before))

        turned = value.astype(jnp.float32).T
        size = rank // blocks
        for b in range(blocks):
            rs[i, b % 2, b // 2] = turned[b * size : (b + 1) * size]
        launch(r_copies(i, l))

    def ship_b(i, l, value, again, before):
        @pl.when(again)
        def _():
            finish(b_copies(i, before))

        n = value.shape[1]
        bs[i, :, :n] = value.astype(jnp.float32)
        if n < WIDE:
            bs[i, :, n:] = jnp.zeros((tokens, WIDE - n), jnp.float32)
        launch(b_copies(i, l))

    def ship_q(i, l, value, again, before):
        @pl.when(again)
        def _():
            finish(q_copies(i, before))

        qs[i] = value.astype(jnp.float32)
        launch(q_copies(i, l))

    def columns_of(size):
        return [(at, min(SUM_STEP, size - at)) for at in range(0, size, SUM_STEP)]

    def sum_over_mp(size, fill, turn, idle):
        def pieces_of(make):
            return [make(i, pl.ds(at, n)) for i, (at, n) in enumerate(columns_of(size))]

        first = pieces_of(
            lambda i, c: remote(part.at[theirs, c], near.at[:, c], c_s.at[i], c_r.at[i], core)
        )
        second = pieces_of(
            lambda i, c: remote(
                mine.at[:, c], far.at[turn, :, c], y_s.at[turn, i], y_r.at[turn, i], other
            )
        )
        third = pieces_of(
            lambda i, c: remote(total.at[own, c], total.at[own, c], e_s.at[i], e_r.at[i], core)
        )

        def middle(i):
            at, n = columns_of(size)[i]
            first[i].wait_recv()
            mine[:, at : at + n] = part[own, at : at + n] + near[:, at : at + n]
            second[i].start()

        for i, (at, n) in enumerate(columns_of(size)):
            fill(at, n)
            first[i].start()
            if i:
                middle(i - 1)
        middle(len(first) - 1)
        idle()
        for i, (at, n) in enumerate(columns_of(size)):
            second[i].wait_recv()
            total[own, at : at + n] = mine[:, at : at + n] + far[turn, :, at : at + n]
            third[i].start()
        for copy in third:
            copy.wait_recv()
        for copy in first + second + third:
            copy.wait_send()

    def dot(left, right):
        return jnp.dot(left, right, preferred_element_type=jnp.float32)

    def low(value):
        return value.astype(jnp.bfloat16)

    def spin(value, sign):
        a, b = value[:, : head // 2], value[:, head // 2 :]
        cosine, sine = cosine_ref[...], sign * sine_ref[...]
        return jnp.concatenate([a * cosine - b * sine, b * cosine + a * sine], axis=1)

    def factor_of(value):
        return lax.rsqrt(jnp.mean(value * value, axis=-1, keepdims=True) + EPSILON)

    def gelu_parts(value):
        c = math.sqrt(2.0 / math.pi)
        square = value * value
        t = jnp.tanh(c * value * (1.0 + 0.044715 * square))
        gelu = 0.5 * value * (1.0 + t)
        slope = 0.5 * (1.0 + t) + 0.5 * value * (1.0 - t * t) * c * (1.0 + 3 * 0.044715 * square)
        return gelu, slope

    h_s[0] = h_in[...].astype(jnp.float32)
    mixer, feed = mixer_gain[...], feed_gain[...]

    def forward(l, carry):
        def need(*copies):
            @pl.when(l == 0)
            def _():
                for copy in copies:
                    copy.wait()

        h = h_s[l]
        normed = low(h * factor_of(h) * mixer)
        normed_s[l] = normed
        need(load.q_in, load.query, load.q_out, load.kv_in, load.pair, load.kv_out)
        query_rank = low(dot(normed, W.q_in[l]))
        qr_s[l] = query_rank
        queries = dot(normed, W.query[...]) + dot(query_rank, W.q_out[l])
        q_s[l] = low(spin(queries, 1.0))
        pair_rank = low(dot(normed, W.kv_in[l]))
        kvr_s[l] = pair_rank
        keys = dot(normed, W.pair[:, :head]) + dot(pair_rank[:, :rank], W.kv_out[l, 0])
        k_s[l] = low(spin(keys, 1.0))
        values = dot(normed, W.pair[:, head:]) + dot(pair_rank[:, rank:], W.kv_out[l, 1])
        v_s[l] = low(values)
        scores = product_t(q_s[l], k_s[l]) * scale
        scores = jnp.where(mask_ref[...] > 0, scores, MASKED)
        expo = jnp.exp(scores - jnp.max(scores, axis=-1, keepdims=True))
        probs = expo / jnp.sum(expo, axis=-1, keepdims=True)
        probs_s[l] = probs
        mixed = low(dot(low(probs), v_s[l]))
        mixed_s[l] = mixed
        need(load.output, load.o_in, load.o_out)

        def fill_attend(at, n):
            cut = min(n, max(0, width - at))
            if cut:
                part[:, at : at + cut] = dot(mixed, W.output[:, at : at + cut])
            if cut < n:
                start = at + cut - width
                part[:, at + cut : at + n] = dot(mixed, W.o_in[l, :, start : start + n - cut])

        again = l > 0

        def idle_attend():
            ship_x(2, l, normed, again, 0)
            ship_r(3, l, query_rank, again, 0)
            ship_q(1, l, mixed, again, 0)

        sum_over_mp(width + rank, fill_attend, 0, idle_attend)
        output_rank = total[:, width : width + rank]
        or_s[l] = output_rank
        middle = h_s[l] + total[:, :width]
        for piece in split3(output_rank):
            middle = middle + dot(piece, W.o_out[l])
        mid_s[l] = middle
        fed = low(middle * factor_of(middle) * feed)
        fed_s[l] = fed
        need(load.w_in, load.gate, load.up, load.w_out)
        widen_rank = low(dot(fed, W.w_in[l]))
        er_s[l] = widen_rank
        for at, n in chunks:
            gate = dot(fed, W.gate[:, at : at + n]) + dot(
                widen_rank[:, :rank], W.w_out[l, 0, :, at : at + n]
            )
            gate_s[l, :, at : at + n] = gate
            up = dot(fed, W.up[:, at : at + n]) + dot(
                widen_rank[:, rank:], W.w_out[l, 1, :, at : at + n]
            )
            up_s[l, :, at : at + n] = up
            act_s[:, at : at + n] = low(gelu_parts(gate)[0] * up)
            ship_b(4 + at // WIDE, l, act_s[:, at : at + n], again, 0)
        need(load.down, load.d_in, load.d_out)

        def fill_feed(at, n):
            cut = min(n, max(0, width - at))
            if cut:
                part[:, at : at + cut] = dot(act_s[...], W.down[:, at : at + cut])
            if cut < n:
                start = at + cut - width
                part[:, at + cut : at + n] = dot(act_s[...], W.d_in[l, :, start : start + n - cut])

        def idle_feed():
            ship_x(0, l, fed, again, 0)
            ship_r(0, l, widen_rank[:, :rank], again, 0)
            ship_r(1, l, widen_rank[:, rank:], again, 0)

            @pl.when(again)
            def _():
                pass_act(0)

        sum_over_mp(width + rank, fill_feed, 1, idle_feed)
        shrink_rank = total[:, width : width + rank]
        sr_s[l] = shrink_rank
        result = mid_s[l] + total[:, :width]
        for piece in split3(shrink_rank):
            result = result + dot(piece, W.d_out[l])
        h_s[l + 1] = result
        return carry

    lax.fori_loop(0, loops, forward, 0)
    out_ref[...] = low(h_s[loops])

    g_s[...] = cot[...].astype(jnp.float32)
    gain_s[...] = jnp.zeros_like(gain_s)
    padded_quarter = select.shape[0] // blocks
    row = lax.broadcasted_iota(jnp.int32, (padded_quarter, width), 0)
    column = lax.broadcasted_iota(jnp.int32, (padded_quarter, width), 1)
    for b in range(blocks):
        hit = jnp.logical_and(column == row + (b * 4 + mp) * quarter, row < quarter)
        select[b * padded_quarter : (b + 1) * padded_quarter] = low(
            jnp.where(hit, 1.0, 0.0)
        )
    small_row = lax.broadcasted_iota(jnp.int32, (rank_quarter, rank), 0)
    small_column = lax.broadcasted_iota(jnp.int32, (rank_quarter, rank), 1)
    rank_select = low(
        jnp.concatenate(
            [
                jnp.where(small_column == small_row + (b * 4 + mp) * rank_quarter, 1.0, 0.0)
                for b in range(blocks)
            ],
            axis=0,
        )
    )
    raw_rows = raw_layout(quarter, rank_quarter, loops)

    def back(step, carry):
        l = loops - 1 - step
        again = step > 0
        before = loops - 1

        upstream = g_s[...]
        grad_feed = low(upstream)
        grad_shrink = low(product_t(grad_feed, W.d_out[l]))
        for i, (at, n) in enumerate(chunks):
            grad_act = product_t(grad_feed, W.down[at : at + n]) + product_t(
                grad_shrink, W.d_in[l, at : at + n]
            )
            gelu, slope = gelu_parts(gate_s[l, :, at : at + n])
            grad_gate = low(grad_act * up_s[l, :, at : at + n] * slope)
            grad_up = low(grad_act * gelu)
            gg_s[:, at : at + n] = grad_gate
            gu_s[:, at : at + n] = grad_up
            ship_b(i, l, grad_gate, again, before)
            ship_b(2 + i, l, grad_up, again, before)

        def fill_fed(at, n):
            cut = min(n, max(0, width - at))
            if cut:
                part[:, at : at + cut] = product_t(
                    gg_s[...], W.gate[at : at + cut]
                ) + product_t(gu_s[...], W.up[at : at + cut])
            while cut < n:
                start = at + cut - width
                j, offset = divmod(start, rank)
                size = min(n - cut, rank - offset)
                value = (gg_s, gu_s)[j][...]
                part[:, at + cut : at + cut + size] = product_t(
                    value, W.w_out[l, j, offset : offset + size]
                )
                cut += size

        def idle_fed():
            ship_x(1, l, grad_feed, again, before)
            ship_r(2, l, grad_shrink, again, before)

            @pl.when(step == 0)
            def _():
                pass_act(loops - 1)

        sum_over_mp(width + 2 * rank, fill_fed, 0, idle_fed)
        grad_widen = low(total[:, width : width + 2 * rank])
        grad_fed = total[:, :width] + product_t(grad_widen, W.w_in[l])
        middle = mid_s[l]
        factor = factor_of(middle)
        unit = middle * factor
        scaled = grad_fed * feed
        grad_middle = upstream + factor * (
            scaled - unit * jnp.mean(scaled * unit, axis=-1, keepdims=True)
        )
        gain_s[1:2] += jnp.sum(grad_fed * unit, axis=0, keepdims=True)
        g_s[...] = grad_middle
        grad_attend = low(grad_middle)
        grad_output = low(product_t(grad_attend, W.o_out[l]))
        grad_mixed = low(
            product_t(grad_attend, W.output[...]) + product_t(grad_output, W.o_in[l])
        )
        probs = probs_s[l]
        grad_probs = product_t(grad_mixed, v_s[l])
        delta = jnp.sum(grad_probs * probs, axis=-1, keepdims=True)
        grad_scores = low(probs * (grad_probs - delta))
        grad_query = low(spin(dot(grad_scores, k_s[l]) * scale, -1.0))

        def fill_normed(at, n):
            if at == columns_of(width + rank + 2 * head)[0][0]:
                part[:, width + rank : width + rank + head] = spin(
                    product_tn(grad_scores, q_s[l]) * scale, -1.0
                )
                part[:, width + rank + head :] = product_tn(low(probs), grad_mixed)
            cut = min(n, max(0, width - at))
            if cut:
                part[:, at : at + cut] = product_t(grad_query, W.query[at : at + cut])
            end = min(at + n, width + rank)
            if at + cut < end:
                start = at + cut - width
                part[:, at + cut : end] = product_t(
                    grad_query, W.q_out[l, start : end - width]
                )

        def idle_normed():
            ship_q(0, l, grad_query, again, before)
            ship_x(3, l, grad_attend, again, before)
            ship_r(4, l, grad_output, again, before)
            pass_feed(l)

        sum_over_mp(width + rank + 2 * head, fill_normed, 1, idle_normed)
        grad_rank = low(total[:, width : width + rank])
        grad_pair = low(total[:, width + rank : width + rank + 2 * head])
        grad_pair_rank = low(
            jnp.concatenate(
                [
                    product_t(grad_pair[:, :head], W.kv_out[l, 0]),
                    product_t(grad_pair[:, head:], W.kv_out[l, 1]),
                ],
                axis=1,
            )
        )
        grad_normed = (
            total[:, :width]
            + product_t(grad_rank, W.q_in[l])
            + product_t(grad_pair, W.pair[...])
            + product_t(grad_pair_rank, W.kv_in[l])
        )
        h = h_s[l]
        factor = factor_of(h)
        unit = h * factor
        scaled = grad_normed * mixer
        g_s[...] += factor * (scaled - unit * jnp.mean(scaled * unit, axis=-1, keepdims=True))
        gain_s[0:1] += jnp.sum(grad_normed * unit, axis=0, keepdims=True)

        def put(start, size, stride, value, add=False):
            for b in range(blocks):
                piece = value[b * stride : b * stride + size]
                at = pl.ds(start, size)
                if add:
                    raw_ref[b % 2, b // 2, at] += piece
                else:
                    raw_ref[b % 2, b // 2, at] = piece

        tall = raw_rows.tall
        normed_own = low(product_t(select[...], normed_s[l]))
        pair_weight = dot(normed_own, grad_pair)

        @pl.when(step == 0)
        def _():
            for j in range(2):
                put(j * tall, tall, padded_quarter, pair_weight[:, j * head : (j + 1) * head])

        @pl.when(step > 0)
        def _():
            for j in range(2):
                put(j * tall, tall, padded_quarter, pair_weight[:, j * head : (j + 1) * head], True)

        base = 2 * tall + l * raw_rows.loop

        def put_loop(i, value):
            put(pl.multiple_of(base + i * tall, 8), tall, padded_quarter, value)

        put_loop(0, dot(normed_own, grad_rank))
        for j in range(2):
            put_loop(1 + j, dot(normed_own, grad_pair_rank[:, j * rank : (j + 1) * rank]))
        fed_own = low(product_t(select[...], fed_s[l]))
        for j in range(2):
            put_loop(3 + j, dot(fed_own, grad_widen[:, j * rank : (j + 1) * rank]))
        attend_own = low(product_t(select[...], grad_attend))
        put_loop(5, sum(dot(attend_own, piece) for piece in split3(or_s[l])))
        feed_own = low(product_t(select[...], grad_feed))
        put_loop(6, sum(dot(feed_own, piece) for piece in split3(sr_s[l])))
        for j in range(2):
            rank_own = low(product_t(rank_select, kvr_s[l, :, j * rank : (j + 1) * rank]))
            put(
                pl.multiple_of(base + 7 * tall + j * rank_quarter, 8), rank_quarter, rank_quarter,
                dot(rank_own, grad_pair[:, j * head : (j + 1) * head]),
            )
        return carry

    lax.fori_loop(0, loops, back, 0)
    last = loops - 1
    for copies in (
        x_copies(0, last), x_copies(2, last), r_copies(0, last), r_copies(1, last), r_copies(3, last),
        b_copies(4, last), b_copies(5, last), q_copies(1, last),
        x_copies(1, 0), x_copies(3, 0), r_copies(2, 0), r_copies(4, 0),
        b_copies(0, 0), b_copies(1, 0), b_copies(2, 0), b_copies(3, 0), q_copies(0, 0),
    ):
        finish(copies)
    for l in range(loops):
        for copies in (x_copies(0, l), r_copies(0, l), r_copies(1, l), b_copies(0, l)):
            copies[1].wait_recv()

        @pl.when(is_end)
        def _():
            for copy in far_feed(l) + far_act(l):
                copy.wait_send()

        @pl.when(jnp.logical_not(is_end))
        def _():
            onward = [x_copies(1, l)[2], r_copies(2, l)[2], b_copies(4, l)[2], b_copies(5, l)[2]]
            for copy in onward + far_feed(l) + far_act(l):
                copy.wait_recv()

    grad_ref[...] = g_s[...]
    for b in range(blocks):
        ends = jnp.zeros((8, head), jnp.float32)
        raw_ref[b % 2, b // 2, raw_rows.gains :] = ends
        raw_ref[b % 2, b // 2, raw_rows.gains : raw_rows.gains + 2, :block] = gain_s[
            :2, b * block : (b + 1) * block
        ]


def raw_layout(quarter, rank_quarter, loops):
    tall = -(-quarter // 8) * 8
    loop = 7 * tall + 2 * rank_quarter
    gains = 2 * tall + loops * loop
    return SimpleNamespace(tall=tall, loop=loop, gains=gains, all=gains + 8)


def block_and_factors(block_input, cotangent, segments, shared, stacked, dp_size):
    (mixer_gain, feed_gain, query, pair, output, widen, down) = shared
    (q_in, q_out, kv_in, kv_out, o_in, o_out, w_in, w_out, d_in, d_out) = stacked
    tokens, width = block_input.shape
    head = query.shape[1]
    loops, _, rank = q_in.shape
    hidden = down.shape[0]
    cosine, sine, allowed = rotary_tables(segments[0], head)
    weights = (
        q_in, query, q_out, kv_in.reshape(loops, width, 2 * rank), pair, kv_out, output, o_in, o_out,
        w_in.reshape(loops, width, 2 * rank), widen[:, 0], widen[:, 1], w_out, down, d_in, d_out,
    )
    layout = raw_layout(width // (4 * dp_size), rank // (4 * dp_size), loops)
    line = dp_size // 2
    f32, bf16 = jnp.float32, jnp.bfloat16
    shape = jax.ShapeDtypeStruct
    block, rank_block, both = width // dp_size, rank // dp_size, loops * tokens
    out_shape = (
        shape((tokens, width), bf16),
        shape((tokens, width), f32),
        shape((2, line, layout.all, head), f32),
        shape((4, 2, line, block, both), f32),
        shape((5, 2, line, rank_block, both), f32),
        shape((6, both, WIDE), f32),
        shape((2, both, head), f32),
        shape((2, line, block, both), f32),
        shape((3, line, rank_block, both), f32),
        shape((3, both, WIDE), f32),
        shape((line, block, 2 * both), f32),
        shape((line, rank_block, 2 * both), f32),
        shape((2, 2 * both, WIDE), f32),
    )
    vmem = pl.BlockSpec(memory_space=pltpu.VMEM)
    hbm = pl.BlockSpec(memory_space=pl.ANY)
    widest = width + rank + 2 * head
    pieces = -(-widest // SUM_STEP)
    dma = pltpu.SemaphoreType.DMA

    def kept(columns, dtype, count=loops):
        return pltpu.VMEM((count, tokens, columns), dtype)

    scratch = [pltpu.VMEM(w.shape, bf16) for w in weights] + [
        kept(width, f32, loops + 1), kept(width, f32), kept(width, bf16), kept(rank, bf16),
        kept(2 * rank, bf16), kept(head, bf16), kept(head, bf16), kept(head, bf16), kept(tokens, f32),
        kept(head, bf16), kept(rank, f32), kept(width, bf16), kept(2 * rank, bf16),
        kept(hidden, f32), kept(hidden, f32), pltpu.VMEM((tokens, hidden), bf16), kept(rank, f32),
        pltpu.VMEM((tokens, hidden), bf16), pltpu.VMEM((tokens, hidden), bf16),
        pltpu.VMEM((tokens, width), f32), pltpu.VMEM((8, width), f32),
        pltpu.VMEM((dp_size * 48, width), bf16),
        pltpu.VMEM((tokens, widest), f32), pltpu.VMEM((tokens, widest), f32),
        pltpu.VMEM((tokens // 2, widest), f32), pltpu.VMEM((tokens // 2, widest), f32),
        pltpu.VMEM((2, tokens // 2, widest), f32),
        pltpu.VMEM((4, 2, line, block, tokens), f32), pltpu.VMEM((5, 2, line, rank_block, tokens), f32),
        pltpu.VMEM((6, tokens, WIDE), f32), pltpu.VMEM((2, tokens, head), f32),
        dma((len(weights),)), dma((pieces,)), dma((pieces,)), dma((2, pieces)), dma((2, pieces)),
        dma((pieces,)), dma((pieces,)),
        dma((4, loops)), dma((5, loops)), dma((6, loops)), dma((2, loops)),
    ]
    scratch += [dma((2, loops))] * 2 + [dma((3, loops))] * 4
    scratch += [dma((2, loops))] * 4 + [dma((2, 2, loops))] * 2
    return pl.pallas_call(
        block_kernel,
        out_shape=out_shape,
        in_specs=[vmem] * 7 + [hbm] * len(weights),
        out_specs=(vmem,) * 3 + (hbm,) * 10,
        scratch_shapes=scratch,
        compiler_params=pltpu.CompilerParams(
            collective_id=21, has_side_effects=True, vmem_limit_bytes=60 << 20
        ),
    )(
        block_input, cotangent, cosine, sine, allowed.astype(f32), mixer_gain[None], feed_gain[None],
        *weights,
    )


def line_kernel(
    raw_all, x_all, r_all, b_all, q_all, x_got, r_got, b_got, x_end_all, r_end_all, b_end_all,
    main_out, side_out, raw_out,
    x_own, r_own, b_own, q_own, x_far, r_far, b_far, q_far, x_end, r_end, b_end, raw_own, raw_far, product_ref,
    main_right, main_left, side_right, side_left, raw_right, raw_left,
    x_s, x_r, r_s, r_r, b_s, b_r, q_s, q_r, w_s, w_r, local_sems, step_sems,
    mr_s, mr_r, ml_s, ml_r, sr_s, sr_r, sl_s, sl_r, rr_s, rr_r, rl_s, rl_r,
    credit_right, credit_left,
):
    dp, mp = lax.axis_index("dp"), lax.axis_index("mp")
    x = lax.rem(dp, 2)
    z = dp // 2
    last = 3
    pair = (dp + 1 - 2 * x, mp)
    up, down = (dp + 2, mp), (dp - 2, mp)

    barrier = pltpu.get_barrier_semaphore()
    pl.semaphore_signal(barrier, inc=1, device_id=pair, device_id_type=MESH)

    @pl.when(z > 0)
    def _():
        pl.semaphore_signal(barrier, inc=1, device_id=down, device_id_type=MESH)

    @pl.when(z < last)
    def _():
        pl.semaphore_signal(barrier, inc=1, device_id=up, device_id_type=MESH)

    pl.semaphore_wait(barrier, 1 + jnp.minimum(z, 1) + jnp.minimum(last - z, 1))

    def across(source, target, send, recv):
        return pltpu.make_async_remote_copy(
            source, target, send, recv, device_id=pair, device_id_type=MESH
        )

    def x_copy(i):
        return across(x_all.at[i, 1 - x], x_far.at[i], x_s.at[i - 2], x_r.at[i - 2])

    def r_copy(i):
        return across(r_all.at[i, 1 - x], r_far.at[i], r_s.at[i - 3], r_r.at[i - 3])

    def b_copy(i):
        return across(b_all.at[i], b_far.at[i], b_s.at[i], b_r.at[i])

    q_copy = across(q_all, q_far, q_s, q_r)
    w_copy = across(raw_all.at[1 - x], raw_far, w_s, w_r)

    def here(source, target, i):
        return pltpu.make_async_copy(source, target, local_sems.at[i])

    at_start = [
        here(x_all.at[:, x], x_own, 0),
        here(r_all.at[:, x], r_own, 1),
        here(x_got, x_far.at[0:2], 2),
        here(r_got, r_far.at[0:3], 3),
        here(b_got.at[0], b_far.at[0], 4),
        here(b_got.at[1:3], b_far.at[4:6], 5),
        here(q_all, q_own, 6),
    ]
    for_ends = [here(x_end_all, x_end, 7), here(r_end_all, r_end, 8), here(b_end_all, b_end, 9)]
    own_copy = here(raw_all.at[x], raw_own, 10)
    inner = jnp.logical_and(z > 0, z < last)

    def chunk_of(step):
        return jnp.where(lax.rem(step, 3) == 1, 4 + step // 3, step - (step + 1) // 3)

    def b_load(step):
        slot = lax.rem(step, 2)
        return pltpu.make_async_copy(b_all.at[chunk_of(step)], b_own.at[slot], step_sems.at[slot])

    b_copy(1).start()
    b_load(0).start()
    for copy in at_start:
        copy.start()

    @pl.when(inner)
    def _():
        for copy in for_ends:
            copy.start()

    own_copy.start()
    for copy in at_start:
        copy.wait()

    @pl.when(inner)
    def _():
        for copy in for_ends:
            copy.wait()

    def chain(target, step, slot, steps, value, out, right, left, r_s, r_r, l_s, l_r, credits):
        def move(buffer, send, recv, i, s, device):
            return pltpu.make_async_remote_copy(
                buffer.at[i, s], buffer.at[i, s], send.at[i, s], recv.at[i, s],
                device_id=device, device_id_type=MESH,
            )

        def inside(at):
            return lax.rem(at, 3) == 1 if credits else at < 0

        def free(credit, i, source, at, from_end):
            @pl.when(
                jnp.logical_and(
                    at <= steps - 1,
                    jnp.logical_not(jnp.logical_and(from_end, inside(at))),
                )
            )
            def _():
                pl.semaphore_signal(credit.at[i], inc=1, device_id=source, device_id_type=MESH)

        def pass_on(i, buffer, send, recv, onward, source, at_end, next_to_end, credit):
            has_source = jnp.logical_not(
                jnp.logical_or(at_end, jnp.logical_and(next_to_end, inside(step)))
            )

            @pl.when(jnp.logical_not(jnp.logical_and(at_end, inside(step))))
            def _():
                if credits:

                    @pl.when(step >= 1)
                    def _():
                        skipped = jnp.logical_and(at_end, inside(step - 1))
                        before = jnp.where(skipped, slot, 1 - slot)
                        move(buffer, send, recv, i, before, onward).wait_send()

                        @pl.when(jnp.logical_not(at_end))
                        def _():
                            free(credit, i, source, step + 1, next_to_end)

                @pl.when(jnp.logical_not(has_source))
                def _():
                    buffer[i, slot] = value()

                @pl.when(has_source)
                def _():
                    product = value()
                    move(buffer, send, recv, i, slot, onward).wait_recv()
                    buffer[i, slot] += product

                if credits:

                    @pl.when(step >= 2)
                    def _():
                        pl.semaphore_wait(credit.at[i], 1)

                move(buffer, send, recv, i, slot, onward).start()

        @pl.when(target > z)
        def _():
            pass_on(target - 1, right, r_s, r_r, up, down, z == 0, z == 1, credit_right)

        @pl.when(target < z)
        def _():
            pass_on(target, left, l_s, l_r, down, up, z == last, z == last - 1, credit_left)

        @pl.when(target == z)
        def _():
            out[...] = value()

            @pl.when(z > 0)
            def _():
                @pl.when(jnp.logical_not(jnp.logical_and(z == 1, inside(step))))
                def _():
                    move(right, r_s, r_r, z - 1, slot, up).wait_recv()
                    out[...] += right[z - 1, slot]

                if credits:
                    free(credit_right, z - 1, down, step + 2, z == 1)

            @pl.when(z < last)
            def _():
                @pl.when(jnp.logical_not(jnp.logical_and(z == last - 1, inside(step))))
                def _():
                    move(left, l_s, l_r, z, slot, down).wait_recv()
                    out[...] += left[z, slot]

                if credits:
                    free(credit_left, z, up, step + 2, z == last - 1)

    def settle(slot, right, left, r_s, l_s):
        for target in range(4):

            @pl.when(target > z)
            def _():
                i = target - 1
                pltpu.make_async_remote_copy(
                    right.at[i, slot], right.at[i, slot], r_s.at[i, slot], r_s.at[i, slot],
                    device_id=up, device_id_type=MESH,
                ).wait_send()

            @pl.when(target < z)
            def _():
                pltpu.make_async_remote_copy(
                    left.at[target, slot], left.at[target, slot], l_s.at[target, slot], l_s.at[target, slot],
                    device_id=down, device_id_type=MESH,
                ).wait_send()

    def order(turn):
        def near(end):
            return jnp.where(
                end == 0,
                3 - turn,
                jnp.where(turn == 0, 3, jnp.where(turn == 1, 0, 4 - turn)),
            )

        return jnp.where(z < 2, near(z), 3 - near(3 - z))

    def dot(left, right):
        return jnp.dot(
            left.astype(jnp.bfloat16), right.astype(jnp.bfloat16), preferred_element_type=jnp.float32
        )

    steps = b_all.shape[0]

    def left_times(x_index, group, target, own, far):
        half = own.shape[0] // 2
        rank_own, rank_far = r_own[group, target], r_far[group, target]
        return [
            dot(x_own[x_index, target], own) + dot(x_far[x_index, target], far),
            dot(rank_own[:, :half], own[:half]) + dot(rank_far[:, :half], far[:half]),
            dot(rank_own[:, half:], own[half:]) + dot(rank_far[:, half:], far[half:]),
        ]

    def turn_body(at, carry):
        step, turn = at // 4, lax.rem(at, 4)
        slot = lax.rem(step, 2)
        chunk = chunk_of(step)
        group = chunk // 2
        target = order(turn)

        @pl.when(turn == 0)
        def _():
            b_load(step).wait()

            @pl.when(step < steps - 1)
            def _():
                b_load(step + 1).start()

            @pl.when(jnp.logical_and(chunk >= 1, chunk <= 3))
            def _():
                b_copy(chunk).wait_recv()

            @pl.when(step == 1)
            def _():
                b_copy(2).start()

            @pl.when(step == 2)
            def _():
                b_copy(3).start()

            @pl.when(step == 3)
            def _():
                x_copy(2).start()
                x_copy(3).start()
                r_copy(3).start()
                r_copy(4).start()
                q_copy.start()

            @pl.when(step == 4)
            def _():
                w_copy.start()

        def value():
            parts = left_times(
                group // 2, group, target,
                b_own[slot].astype(jnp.bfloat16), b_far[chunk].astype(jnp.bfloat16),
            )
            product_ref[...] = jnp.concatenate(parts, axis=0)
            beyond = jnp.logical_or(
                jnp.logical_and(z == 1, target >= 1),
                jnp.logical_and(z == last - 1, target <= last - 1),
            )

            @pl.when(jnp.logical_and(beyond, chunk >= 4))
            def _():
                end = b_end[jnp.maximum(chunk - 4, 0)].astype(jnp.bfloat16)
                middle = end.shape[0] // 2
                product_ref[...] += jnp.concatenate(
                    [
                        dot(x_end[target], end),
                        dot(r_end[target, :, :middle], end[:middle]),
                        dot(r_end[target, :, middle:], end[middle:]),
                    ],
                    axis=0,
                )

            return product_ref[...]

        chain(
            target, step, slot, steps, value, main_out.at[chunk], main_right, main_left,
            mr_s, mr_r, ml_s, ml_r, True,
        )
        return carry

    lax.fori_loop(0, 4 * steps, turn_body, 0)

    for i in (2, 3):
        x_copy(i).wait_recv()
    for i in (3, 4):
        r_copy(i).wait_recv()
    q_copy.wait_recv()

    def side_body(turn, carry):
        target = order(turn)

        def value():
            parts = [
                left_times(
                    2 + i, 3 + i, target, q_own[i].astype(jnp.bfloat16), q_far[i].astype(jnp.bfloat16)
                )
                for i in range(2)
            ]
            return jnp.concatenate([jnp.concatenate(p, axis=0) for p in parts], axis=1)

        chain(
            target, 0, 0, 1, value, side_out, side_right, side_left,
            sr_s, sr_r, sl_s, sl_r, False,
        )
        return carry

    lax.fori_loop(0, 4, side_body, 0)

    w_copy.wait_recv()
    own_copy.wait()

    def raw_body(turn, carry):
        target = order(turn)
        chain(
            target, 0, 0, 1, lambda: raw_own[target] + raw_far[target], raw_out, raw_right, raw_left,
            rr_s, rr_r, rl_s, rl_r, False,
        )
        return carry

    lax.fori_loop(0, 4, raw_body, 0)

    settle((steps - 1) % 2, main_right, main_left, mr_s, ml_s)
    settle(0, side_right, side_left, sr_s, sl_s)
    settle(0, raw_right, raw_left, rr_s, rl_s)
    for copy in (x_copy(2), x_copy(3), r_copy(3), r_copy(4), b_copy(1), b_copy(2), b_copy(3)):
        copy.wait_send()
    q_copy.wait_send()
    w_copy.wait_send()


def line_gradients(factors, loops, dp_size, mp_size, hidden):
    raw, x_all, r_all, b_all, q_all, x_got, r_got, b_got, x_end, r_end, b_end = factors
    block, rank_block, head = x_all.shape[3], r_all.shape[3], q_all.shape[2]
    quarter, rank_quarter = block // mp_size, rank_block // mp_size
    layout = raw_layout(quarter, rank_quarter, loops)
    rows = block + loops * rank_block
    steps = b_all.shape[0]
    vmem = pl.BlockSpec(memory_space=pltpu.VMEM)
    hbm = pl.BlockSpec(memory_space=pl.ANY)
    dma = pltpu.SemaphoreType.DMA
    f32 = jnp.float32
    line = dp_size // 2 - 1
    half_x = pltpu.VMEM((x_all.shape[0], *x_all.shape[2:]), f32)
    half_r = pltpu.VMEM((r_all.shape[0], *r_all.shape[2:]), f32)
    whole_b, whole_q = pltpu.VMEM(b_all.shape, f32), pltpu.VMEM(q_all.shape, f32)
    main, side, rest = pl.pallas_call(
        line_kernel,
        out_shape=(
            jax.ShapeDtypeStruct((steps, rows, WIDE), f32),
            jax.ShapeDtypeStruct((rows, 2 * head), f32),
            jax.ShapeDtypeStruct((layout.all, head), f32),
        ),
        in_specs=[hbm] * 11,
        out_specs=(vmem, vmem, vmem),
        scratch_shapes=[half_x, half_r, pltpu.VMEM((2, *b_all.shape[1:]), f32), whole_q]
        + [half_x, half_r, whole_b, whole_q]
        + [pltpu.VMEM(v.shape, f32) for v in (x_end, r_end, b_end)]
        + [pltpu.VMEM(raw.shape[1:], f32)] * 2
        + [pltpu.VMEM((rows, WIDE), f32)]
        + [pltpu.VMEM((line, 2, rows, WIDE), f32)] * 2
        + [pltpu.VMEM((line, 1, rows, 2 * head), f32)] * 2
        + [pltpu.VMEM((line, 1, layout.all, head), f32)] * 2
        + [dma((2,))] * 4 + [dma((steps,))] * 2 + [dma] * 4 + [dma((11,)), dma((2,))]
        + [dma((line, 2))] * 4 + [dma((line, 1))] * 8
        + [pltpu.SemaphoreType.REGULAR((line,))] * 2,
        compiler_params=pltpu.CompilerParams(
            collective_id=20, has_side_effects=True, vmem_limit_bytes=60 << 20
        ),
    )(*factors)

    wide = [
        jnp.concatenate([main[2 * i], main[2 * i + 1][:, : hidden - WIDE]], axis=1) for i in range(3)
    ]
    narrow = [side[:, :head], side[:, head:]]

    def shared_rows(value):
        return value[:block]

    def loop_rows(value, i):
        return value[block + i * rank_block : block + (i + 1) * rank_block]

    tall = layout.tall

    def raw_rows(start, size):
        return rest[start : start + size]

    pair_weight = jnp.concatenate([raw_rows(0, quarter), raw_rows(tall, quarter)], axis=1)
    query_inner, pair_inner, expand_inner, pair_outer, outers = [], [], [], [], []
    for i in range(loops):
        base = 2 * tall + i * layout.loop
        own = [raw_rows(base + j * tall, quarter) for j in range(7)]
        query_inner.append(own[0])
        pair_inner.append(jnp.stack(own[1:3], axis=1))
        expand_inner.append(jnp.stack(own[3:5], axis=1))
        outers += own[5:7]
        pair_outer.append(
            jnp.stack([raw_rows(base + 7 * tall + j * rank_quarter, rank_quarter) for j in range(2)])
        )
    outers = lax.all_gather(jnp.stack(outers), "mp")
    outers = jnp.swapaxes(outers, 0, 1).reshape(2 * loops, block, -1).swapaxes(1, 2)
    gains = rest[layout.gains : layout.gains + 2, :block]
    stack = jnp.stack
    return (
        gains[0],
        gains[1],
        shared_rows(narrow[0]),
        pair_weight,
        shared_rows(narrow[1]).T,
        stack([shared_rows(wide[0]), shared_rows(wide[1])], axis=1),
        shared_rows(wide[2]).T,
        stack(query_inner),
        stack([loop_rows(narrow[0], i) for i in range(loops)]),
        stack(pair_inner),
        stack(pair_outer),
        stack([loop_rows(narrow[1], i).T for i in range(loops)]),
        outers[0::2],
        stack(expand_inner),
        stack([stack([loop_rows(wide[j], i) for j in range(2)]) for i in range(loops)]),
        stack([loop_rows(wide[2], i).T for i in range(loops)]),
        outers[1::2],
    )


def per_device(dp_size, mp_size, block_input, cotangent, segments, *parameters):
    shared, stacked = parameters[:7], parameters[7:]
    loops = stacked[0].shape[0]
    if dp_size == 8 and mp_size == 4 and loops == 2:
        output, input_grad, *factors = block_and_factors(
            block_input, cotangent, segments, shared, stacked, dp_size
        )
        gradients = line_gradients(factors, loops, dp_size, mp_size, shared[6].shape[0])
        return (output, input_grad, *gradients)
    tables = rotary_tables(segments[0], shared[3].shape[1] // 2)
    total = mp_total(mp_size)
    state = block_input.astype(jnp.float32)
    kept_all = []
    for i in range(loops):
        state, kept = forward_loop(state, shared, [v[i] for v in stacked], tables, total, 1)
        kept_all.append(kept)
    upstream = cotangent.astype(jnp.float32)
    for i in reversed(range(loops)):
        upstream = reverse_loop(
            upstream, kept_all[i], shared, [v[i] for v in stacked], tables, total, 3
        )
    return (state.astype(jnp.bfloat16), upstream, *scattered_gradients(kept_all, dp_size, mp_size))


def solution(mesh):
    in_specs = (
        P("dp", None),
        P("dp", None),
        P("dp", None),
        P(),
        P(),
        P(None, "mp"),
        P(),
        P("mp", None),
        P(None, None, "mp"),
        P("mp", None),
        P(),
        P(None, None, "mp"),
        P(),
        P(),
        P(None, "mp", None),
        P(),
        P(),
        P(None, None, None, "mp"),
        P(None, "mp", None),
        P(),
    )
    out_specs = (
        P("dp", None),
        P("dp", None),
        P("dp"),
        P("dp"),
        P("dp", "mp"),
        P(("dp", "mp"), None),
        P("mp", "dp"),
        P("dp", None, "mp"),
        P("mp", "dp"),
        P(None, ("dp", "mp"), None),
        P(None, "dp", "mp"),
        P(None, ("dp", "mp"), None, None),
        P(None, None, ("dp", "mp"), None),
        P(None, "mp", "dp"),
        P(None, None, "dp"),
        P(None, ("dp", "mp"), None, None),
        P(None, None, "dp", "mp"),
        P(None, "mp", "dp"),
        P(None, None, "dp"),
    )
    return jax.shard_map(
        functools.partial(per_device, mesh.shape["dp"], mesh.shape["mp"]),
        mesh=mesh, in_specs=in_specs, out_specs=out_specs, check_vma=False
    )
```

```python
import functools
import math
from types import SimpleNamespace

import jax
import jax.numpy as jnp
from jax import lax
from jax.experimental import pallas as pl
from jax.experimental.pallas import tpu as pltpu
from jax.sharding import PartitionSpec as P

EPSILON = 1e-06
MASKED = -1e30
MESH = pl.DeviceIdType.MESH


def product(left, right):
    return jnp.dot(left, right, preferred_element_type=jnp.float32)


def product_t(left, right):
    return lax.dot_general(
        left, right, (((1,), (1,)), ((), ())), preferred_element_type=jnp.float32
    )


def product_tn(left, right):
    return lax.dot_general(
        left, right, (((0,), (0,)), ((), ())), preferred_element_type=jnp.float32
    )


def exact_product(left, right):
    return jnp.dot(left, right, precision=lax.Precision.HIGHEST, preferred_element_type=jnp.float32)


def exact_tn(left, right):
    return lax.dot_general(
        left,
        right,
        (((0,), (0,)), ((), ())),
        precision=lax.Precision.HIGHEST,
        preferred_element_type=jnp.float32,
    )


def normalize(hidden_state, gain):
    factor = lax.rsqrt(jnp.mean(hidden_state * hidden_state, axis=-1, keepdims=True) + EPSILON)
    return (hidden_state * factor * gain, factor)


def normalize_back(hidden_state, factor, gain, upstream_gradient):
    unit = hidden_state * factor
    scaled = upstream_gradient * gain
    downstream = factor * (scaled - unit * jnp.mean(scaled * unit, axis=-1, keepdims=True))
    return (downstream, jnp.sum(upstream_gradient * unit, axis=0))


def rotate(values, cosine_table, sine_table):
    half_width = values.shape[-1] // 2
    first = values[..., :half_width]
    second = values[..., half_width:]
    return jnp.concatenate(
        [first * cosine_table - second * sine_table, second * cosine_table + first * sine_table],
        axis=-1,
    )


def rotary_tables(segment_row, head_size):
    length_value = segment_row.shape[0]
    earlier = jnp.sum((segment_row[None, :] < segment_row[:, None]).astype(jnp.int32), axis=1)
    position = (jnp.arange(length_value, dtype=jnp.int32) - earlier).astype(jnp.float32)
    steps_half = jnp.arange(head_size // 2, dtype=jnp.float32)
    frequency = 10000.0 ** (-2.0 * steps_half / head_size)
    angles = position[:, None] * frequency[None, :]
    same_segment = segment_row[:, None] == segment_row[None, :]
    ordinal = jnp.arange(length_value, dtype=jnp.int32)
    allowed_mask = same_segment & (ordinal[:, None] >= ordinal[None, :])
    return (jnp.cos(angles), jnp.sin(angles), allowed_mask)


def gelu_tanh(values):
    return jax.nn.gelu(values, approximate=True)


def attention_probs(queries, keys, allowed_mask, score_scale):
    scores = (
        jnp.einsum("ihd,jd->hij", queries, keys, preferred_element_type=jnp.float32) * score_scale
    )
    return jnp.where(allowed_mask[None], scores, MASKED)


def mp_total(size):
    def kernel(part, out, near, mine, far, core_send, core_recv, y_send, y_recv, back_send, back_recv):
        dp, mp = lax.axis_index("dp"), lax.axis_index("mp")
        side = lax.rem(mp, 2)
        core = (dp, mp + 1 - 2 * side)
        other = (dp, lax.rem(mp + 2, 4))
        half = part.shape[0] // 2
        pieces = near.shape[0]
        width = part.shape[1] // pieces
        own = pl.ds(pl.multiple_of(side * half, half), half)
        theirs = pl.ds(pl.multiple_of((1 - side) * half, half), half)

        def columns(i):
            return pl.ds(i * width, width)

        barrier = pltpu.get_barrier_semaphore()
        for device in (core, other):
            pl.semaphore_signal(barrier, inc=1, device_id=device, device_id_type=MESH)
        pl.semaphore_wait(barrier, 2)
        first = [
            pltpu.make_async_remote_copy(
                part.at[theirs, columns(i)], near.at[i], core_send.at[i], core_recv.at[i],
                device_id=core, device_id_type=MESH,
            )
            for i in range(pieces)
        ]
        second = [
            pltpu.make_async_remote_copy(
                mine.at[i], far.at[i], y_send.at[i], y_recv.at[i],
                device_id=other, device_id_type=MESH,
            )
            for i in range(pieces)
        ]
        third = [
            pltpu.make_async_remote_copy(
                out.at[own, columns(i)], out.at[own, columns(i)], back_send.at[i], back_recv.at[i],
                device_id=core, device_id_type=MESH,
            )
            for i in range(pieces)
        ]
        for copy in first:
            copy.start()
        for i in range(pieces):
            first[i].wait_recv()
            mine[i] = part[own, columns(i)] + near[i]
            second[i].start()
        for i in range(pieces):
            second[i].wait_recv()
            out[own, columns(i)] = mine[i] + far[i]
            third[i].start()
        for copy in third:
            copy.wait_recv()
        for copy in first + second + third:
            copy.wait_send()

    def total(identity, *parts):
        if size != 4:
            return lax.psum(parts, "mp")
        joined = jnp.concatenate(parts, axis=1)
        tokens_here, columns_here = joined.shape
        pieces = 1
        for count in (5, 4, 3, 2):
            if columns_here % (128 * count) == 0:
                pieces = count
                break
        half = (pieces, tokens_here // 2, columns_here // pieces)
        summed = pl.pallas_call(
            kernel,
            out_shape=jax.ShapeDtypeStruct(joined.shape, jnp.float32),
            in_specs=[pl.BlockSpec(memory_space=pltpu.VMEM)],
            out_specs=pl.BlockSpec(memory_space=pltpu.VMEM),
            scratch_shapes=[pltpu.VMEM(half, jnp.float32)] * 3
            + [pltpu.SemaphoreType.DMA((pieces,))] * 6,
            compiler_params=pltpu.CompilerParams(
                collective_id=identity, has_side_effects=True, vmem_limit_bytes=16 << 20
            ),
        )(joined)
        edges, start = [], 0
        for part in parts:
            edges.append(summed[:, start : start + part.shape[1]])
            start += part.shape[1]
        return tuple(edges)

    return total


def forward_loop(hidden_state, shared, adapters, tables, total, identity):
    (mixer_gain, feed_gain, query_matrix, pair_matrix, output_matrix, widen_matrix, down_matrix) = shared
    (q_in, q_out, kv_in, kv_out, o_in, o_out, w_in, w_out, d_in, d_out) = adapters
    cosine, sine, allowed = tables
    tokens_here, width = hidden_state.shape
    head = pair_matrix.shape[1] // 2
    heads = query_matrix.shape[1] // head
    rank = q_in.shape[1]
    hidden = down_matrix.shape[0]
    kept = SimpleNamespace(h=hidden_state)
    normed, kept.mixer_factor = normalize(hidden_state, mixer_gain)
    normed = normed.astype(jnp.bfloat16)
    query_rank = product(normed, q_in).astype(jnp.bfloat16)
    query_linear = product(normed, query_matrix) + product(query_rank, q_out)
    pair_rank = product(normed, kv_in.reshape(width, 2 * rank)).astype(jnp.bfloat16)
    pair_linear = product(normed, pair_matrix) + jnp.concatenate(
        [product(pair_rank[:, :rank], kv_out[0]), product(pair_rank[:, rank:], kv_out[1])], axis=1
    )
    queries = rotate(
        query_linear.reshape(tokens_here, heads, head), cosine[:, None], sine[:, None]
    ).astype(jnp.bfloat16)
    keys = rotate(pair_linear[:, :head], cosine, sine).astype(jnp.bfloat16)
    values = pair_linear[:, head:].astype(jnp.bfloat16)
    masked = attention_probs(queries, keys, allowed, 1.0 / math.sqrt(head))
    expo = jnp.exp(masked - jnp.max(masked, axis=-1, keepdims=True))
    probs = expo / jnp.sum(expo, axis=-1, keepdims=True)
    mixed = jnp.einsum(
        "hij,jd->ihd", probs.astype(jnp.bfloat16), values, preferred_element_type=jnp.float32
    )
    mixed = mixed.reshape(tokens_here, heads * head).astype(jnp.bfloat16)
    summed, output_rank = total(identity, product(mixed, output_matrix), product(mixed, o_in))
    middle = hidden_state + summed + exact_product(output_rank, o_out.astype(jnp.float32))
    fed, kept.feed_factor = normalize(middle, feed_gain)
    fed = fed.astype(jnp.bfloat16)
    widen_rank = product(fed, w_in.reshape(width, 2 * rank)).astype(jnp.bfloat16)
    gate = product(fed, widen_matrix[:, 0]) + product(widen_rank[:, :rank], w_out[0])
    up = product(fed, widen_matrix[:, 1]) + product(widen_rank[:, rank:], w_out[1])
    activated = (gelu_tanh(gate) * up).astype(jnp.bfloat16)
    shrunk, shrink_rank = total(identity + 1, product(activated, down_matrix), product(activated, d_in))
    result = middle + shrunk + exact_product(shrink_rank, d_out.astype(jnp.float32))
    vars(kept).update(
        normed=normed, query_rank=query_rank, pair_rank=pair_rank, queries=queries, keys=keys,
        values=values, probs=probs, mixed=mixed, output_rank=output_rank, middle=middle, fed=fed,
        widen_rank=widen_rank, gate=gate, up=up, activated=activated, shrink_rank=shrink_rank,
    )
    return result, kept


def reverse_loop(upstream, kept, shared, adapters, tables, total, identity):
    (mixer_gain, feed_gain, query_matrix, pair_matrix, output_matrix, widen_matrix, down_matrix) = shared
    (q_in, q_out, kv_in, kv_out, o_in, o_out, w_in, w_out, d_in, d_out) = adapters
    cosine, sine, allowed = tables
    tokens_here, width = upstream.shape
    head = pair_matrix.shape[1] // 2
    heads = query_matrix.shape[1] // head
    rank = q_in.shape[1]
    scale = 1.0 / math.sqrt(head)
    grad_feed = upstream.astype(jnp.bfloat16)
    grad_shrink_rank = product_t(grad_feed, d_out).astype(jnp.bfloat16)
    grad_activated = product_t(grad_feed, down_matrix) + product_t(grad_shrink_rank, d_in)
    gelu_value, gelu_pullback = jax.vjp(gelu_tanh, kept.gate)
    grad_gate = gelu_pullback(grad_activated * kept.up)[0].astype(jnp.bfloat16)
    grad_up = (grad_activated * gelu_value).astype(jnp.bfloat16)
    grad_fed, grad_widen_rank = total(
        identity,
        product_t(grad_gate, widen_matrix[:, 0]) + product_t(grad_up, widen_matrix[:, 1]),
        jnp.concatenate([product_t(grad_gate, w_out[0]), product_t(grad_up, w_out[1])], axis=1),
    )
    grad_widen_rank = grad_widen_rank.astype(jnp.bfloat16)
    grad_fed = grad_fed + product_t(grad_widen_rank, w_in.reshape(width, 2 * rank))
    grad_norm, feed_gain_grad = normalize_back(kept.middle, kept.feed_factor, feed_gain, grad_fed)
    grad_middle = upstream + grad_norm
    grad_attend = grad_middle.astype(jnp.bfloat16)
    grad_output_rank = product_t(grad_attend, o_out).astype(jnp.bfloat16)
    grad_mixed = product_t(grad_attend, output_matrix) + product_t(grad_output_rank, o_in)
    grad_mixed = grad_mixed.astype(jnp.bfloat16).reshape(tokens_here, heads, head)
    queries, keys, values, probs = kept.queries, kept.keys, kept.values, kept.probs
    grad_probs = jnp.einsum("ihd,jd->hij", grad_mixed, values, preferred_element_type=jnp.float32)
    delta = jnp.sum(grad_probs * probs, axis=-1, keepdims=True)
    grad_scores = (probs * (grad_probs - delta)).astype(jnp.bfloat16)
    grad_queries = scale * jnp.einsum(
        "hij,jd->ihd", grad_scores, keys, preferred_element_type=jnp.float32
    )
    grad_keys = scale * jnp.einsum(
        "hij,ihd->jd", grad_scores, queries, preferred_element_type=jnp.float32
    )
    grad_values = jnp.einsum(
        "hij,ihd->jd", probs.astype(jnp.bfloat16), grad_mixed, preferred_element_type=jnp.float32
    )
    grad_query = rotate(grad_queries, cosine[:, None], -sine[:, None])
    grad_query = grad_query.reshape(tokens_here, heads * head).astype(jnp.bfloat16)
    grad_normed, grad_query_rank, grad_pair = total(
        identity + 1,
        product_t(grad_query, query_matrix),
        product_t(grad_query, q_out),
        jnp.concatenate([rotate(grad_keys, cosine, -sine), grad_values], axis=1),
    )
    grad_query_rank = grad_query_rank.astype(jnp.bfloat16)
    grad_pair = grad_pair.astype(jnp.bfloat16)
    grad_pair_rank = jnp.concatenate(
        [product_t(grad_pair[:, :head], kv_out[0]), product_t(grad_pair[:, head:], kv_out[1])], axis=1
    ).astype(jnp.bfloat16)
    grad_normed = (
        grad_normed
        + product_t(grad_query_rank, q_in)
        + product_t(grad_pair, pair_matrix)
        + product_t(grad_pair_rank, kv_in.reshape(width, 2 * rank))
    )
    grad_norm, mixer_gain_grad = normalize_back(
        kept.h, kept.mixer_factor, mixer_gain, grad_normed
    )
    vars(kept).update(
        grad_feed=grad_feed, grad_shrink_rank=grad_shrink_rank, grad_gate=grad_gate, grad_up=grad_up,
        grad_widen_rank=grad_widen_rank, grad_attend=grad_attend, grad_output_rank=grad_output_rank,
        grad_query=grad_query, grad_query_rank=grad_query_rank, grad_pair=grad_pair,
        grad_pair_rank=grad_pair_rank, feed_gain_grad=feed_gain_grad, mixer_gain_grad=mixer_gain_grad,
    )
    return grad_middle + grad_norm


def scattered_gradients(kept, dp_size, mp_size):
    def scatter(value, axis):
        return lax.psum_scatter(value, "dp", scatter_dimension=axis, tiled=True)

    def shared_of(factors):
        return sum(product_tn(*factors(k)) for k in kept)

    def each(function):
        return jnp.stack([function(k) for k in kept], axis=0)

    def quarter(value, axis):
        block = scatter(value, axis)
        size = block.shape[axis] // mp_size
        return lax.dynamic_slice_in_dim(block, lax.axis_index("mp") * size, size, axis)

    width = kept[0].normed.shape[1]
    rank = kept[0].query_rank.shape[1]
    head = kept[0].grad_pair.shape[1] // 2

    def pair_outer(k):
        left, right = k.pair_rank, k.grad_pair
        return jnp.stack(
            [product_tn(left[:, :rank], right[:, :head]), product_tn(left[:, rank:], right[:, head:])]
        )

    def expand_outer(k):
        left = k.widen_rank
        return jnp.stack(
            [product_tn(left[:, :rank], k.grad_gate), product_tn(left[:, rank:], k.grad_up)]
        )

    return (
        scatter(sum(k.mixer_gain_grad for k in kept), 0),
        scatter(sum(k.feed_gain_grad for k in kept), 0),
        scatter(shared_of(lambda k: (k.normed, k.grad_query)), 0),
        quarter(shared_of(lambda k: (k.normed, k.grad_pair)), 0),
        scatter(shared_of(lambda k: (k.mixed, k.grad_attend)), 1),
        scatter(jnp.stack([shared_of(lambda k: (k.fed, k.grad_gate)), shared_of(lambda k: (k.fed, k.grad_up))], axis=1), 0),
        scatter(shared_of(lambda k: (k.activated, k.grad_feed)), 1),
        quarter(each(lambda k: product_tn(k.normed, k.grad_query_rank)), 1),
        scatter(each(lambda k: product_tn(k.query_rank, k.grad_query)), 1),
        quarter(
            each(lambda k: product_tn(k.normed, k.grad_pair_rank).reshape(width, 2, rank)), 1
        ),
        quarter(each(pair_outer), 2),
        scatter(each(lambda k: product_tn(k.mixed, k.grad_output_rank)), 2),
        scatter(
            each(lambda k: exact_tn(k.output_rank, k.grad_attend.astype(jnp.float32))), 2
        ),
        quarter(
            each(lambda k: product_tn(k.fed, k.grad_widen_rank).reshape(width, 2, rank)), 1
        ),
        scatter(each(expand_outer), 2),
        scatter(each(lambda k: product_tn(k.activated, k.grad_shrink_rank)), 2),
        scatter(each(lambda k: exact_tn(k.shrink_rank, k.grad_feed.astype(jnp.float32))), 2),
    )


WIDE = 896


def split3(value):
    high = value.astype(jnp.bfloat16)
    rest = value - high.astype(jnp.float32)
    middle = rest.astype(jnp.bfloat16)
    low = (rest - middle.astype(jnp.float32)).astype(jnp.bfloat16)
    return high, middle, low


WEIGHTS = (
    "q_in", "query", "q_out", "kv_in", "pair", "kv_out", "output", "o_in", "o_out",
    "w_in", "wide", "w_out", "down", "d_in", "d_out",
)
SUM_STEP = 384


def block_kernel(*refs):
    (h_in, cot, segments, mixer_gain, feed_gain), refs = refs[:5], refs[5:]
    count = len(WEIGHTS)
    sources, refs = refs[:count], refs[count:]
    (
        out_ref, grad_ref, raw_ref, x_all, r_all, b_all, q_all, x_got, r_got, b_got, x_end, r_end, b_end,
    ), refs = refs[:13], refs[13:]
    weights, refs = refs[:count], refs[count:]
    (
        h_s, mid_s, normed_s, qr_s, kvr_s, q_s, k_s, v_s, probs_s, mixed_s, or_s, fed_s, er_s,
        gate_s, up_s, act_s, sr_s, gg_s, gu_s, g_s, gain_s, select,
        part, total, near, mine, far, xs, rs, bs, qs, kv_flat, w_flat, cosine_ref, sine_ref, mask_ref,
        load_sems, c_s, c_r, y_s, y_r, e_s, e_r,
        xl, rl, bl, ql, x_s, x_r, r_s, r_r, b_s, b_r, xe_s, xe_r, re_s, re_r, be_s, be_r,
    ) = refs
    W = SimpleNamespace(**dict(zip(WEIGHTS, weights)))
    dp, mp = lax.axis_index("dp"), lax.axis_index("mp")
    side = lax.rem(mp, 2)
    core = (dp, mp + 1 - 2 * side)
    other = (dp, lax.rem(mp + 2, 4))
    loads = [
        pltpu.make_async_copy(source, target, load_sems.at[i])
        for i, (source, target) in enumerate(zip(sources, weights))
    ]
    load = SimpleNamespace(**dict(zip(WEIGHTS, loads)))
    for copy in loads:
        copy.start()
    x = lax.rem(dp, 2)
    z = dp // 2
    pair = (dp + 1 - 2 * x, mp)
    near_end = (dp + 2 - 4 * lax.rem(z, 2), mp)
    is_end = jnp.logical_or(z == 0, z == 3)
    barrier = pltpu.get_barrier_semaphore()
    for device in (core, other, pair, near_end):
        pl.semaphore_signal(barrier, inc=1, device_id=device, device_id_type=MESH)
    pl.semaphore_wait(barrier, 4)

    tokens, width = h_in.shape
    half = tokens // 2
    head = W.query.shape[1]
    rank = W.q_in.shape[2]
    hidden = W.down.shape[0]
    loops = W.q_in.shape[0]
    scale = 1.0 / math.sqrt(head)
    own = pl.ds(pl.multiple_of(side * half, half), half)
    theirs = pl.ds(pl.multiple_of((1 - side) * half, half), half)
    blocks = x_all.shape[1] * x_all.shape[2]
    block = width // blocks
    quarter = block // 4
    rank_quarter = rank // (4 * blocks)
    chunks = [(0, WIDE), (WIDE, hidden - WIDE)]

    def remote(source, target, send, recv, device):
        return pltpu.make_async_remote_copy(
            source, target, send, recv, device_id=device, device_id_type=MESH
        )

    def span(l):
        return pl.ds(pl.multiple_of(l * tokens, tokens), tokens)

    def end_span(l, is_far):
        return pl.ds(pl.multiple_of((2 * l + is_far) * tokens, tokens), tokens)

    def x_copies(i, l):
        across = onward = None
        if i < 2:
            across = remote(
                xs.at[i, 1 - x], x_got.at[i, :, :, span(l)], x_s.at[i, l], x_r.at[i, l], pair
            )
        if i == 1:
            onward = remote(
                xs.at[i, x], x_end.at[:, :, end_span(l, 0)], xe_s.at[0, l], xe_r.at[0, l], near_end
            )
        return pltpu.make_async_copy(xs.at[i], x_all.at[i, :, :, :, span(l)], xl.at[i, l]), across, onward

    def r_copies(i, l):
        across = onward = None
        if i < 3:
            across = remote(
                rs.at[i, 1 - x], r_got.at[i, :, :, span(l)], r_s.at[i, l], r_r.at[i, l], pair
            )
        if i == 2:
            onward = remote(
                rs.at[i, x], r_end.at[:, :, end_span(l, 0)], re_s.at[0, l], re_r.at[0, l], near_end
            )
        return pltpu.make_async_copy(rs.at[i], r_all.at[i, :, :, :, span(l)], rl.at[i, l]), across, onward

    def b_copies(i, l):
        across = onward = None
        if i in (0, 4, 5):
            k = max(0, i - 3)
            across = remote(bs.at[i], b_got.at[k, span(l)], b_s.at[k, l], b_r.at[k, l], pair)
        if i >= 4:
            onward = remote(
                bs.at[i], b_end.at[i - 4, end_span(l, 0)],
                be_s.at[i - 4, 0, l], be_r.at[i - 4, 0, l], near_end,
            )
        return pltpu.make_async_copy(bs.at[i], b_all.at[i, span(l)], bl.at[i, l]), across, onward

    def q_copies(i, l):
        return pltpu.make_async_copy(qs.at[i], q_all.at[i, span(l)], ql.at[i, l]), None, None

    def launch(copies):
        local, across, onward = copies
        local.start()
        if across is not None:
            across.start()
        if onward is not None:

            @pl.when(is_end)
            def _():
                onward.start()

    def finish(copies):
        local, across, onward = copies
        local.wait()
        if across is not None:
            across.wait_send()
        if onward is not None:

            @pl.when(is_end)
            def _():
                onward.wait_send()

    def far_feed(l):
        return [
            remote(
                x_got.at[1, :, :, span(l)], x_end.at[:, :, end_span(l, 1)],
                xe_s.at[1, l], xe_r.at[1, l], near_end,
            ),
            remote(
                r_got.at[2, :, :, span(l)], r_end.at[:, :, end_span(l, 1)],
                re_s.at[1, l], re_r.at[1, l], near_end,
            ),
        ]

    def far_act(l):
        return [
            remote(
                b_got.at[1 + k, span(l)], b_end.at[k, end_span(l, 1)],
                be_s.at[k, 1, l], be_r.at[k, 1, l], near_end,
            )
            for k in range(2)
        ]

    def pass_act(l):
        for i in (4, 5):
            b_copies(i, l)[1].wait_recv()

        @pl.when(is_end)
        def _():
            for copy in far_act(l):
                copy.start()

    def pass_feed(l):
        x_copies(1, l)[1].wait_recv()
        r_copies(2, l)[1].wait_recv()

        @pl.when(is_end)
        def _():
            for copy in far_feed(l):
                copy.start()

    def ship_x(i, l, value, again, before):
        @pl.when(again)
        def _():
            finish(x_copies(i, before))

        turned = value.astype(jnp.float32).T
        for b in range(blocks):
            xs[i, b % 2, b // 2] = turned[b * block : (b + 1) * block]
        launch(x_copies(i, l))

    def ship_r(i, l, value, again, before):
        @pl.when(again)
        def _():
            finish(r_copies(i, before))

        turned = value.astype(jnp.float32).T
        size = rank // blocks
        for b in range(blocks):
            rs[i, b % 2, b // 2] = turned[b * size : (b + 1) * size]
        launch(r_copies(i, l))

    def ship_b(i, l, value, again, before):
        @pl.when(again)
        def _():
            finish(b_copies(i, before))

        n = value.shape[1]
        bs[i, :, :n] = value.astype(jnp.float32)
        if n < WIDE:
            bs[i, :, n:] = jnp.zeros((tokens, WIDE - n), jnp.float32)
        launch(b_copies(i, l))

    def ship_q(i, l, value, again, before):
        @pl.when(again)
        def _():
            finish(q_copies(i, before))

        qs[i] = value.astype(jnp.float32)
        launch(q_copies(i, l))

    def columns_of(size):
        return [(at, min(SUM_STEP, size - at)) for at in range(0, size, SUM_STEP)]

    def sum_over_mp(size, fill, turn, idle):
        def pieces_of(make):
            return [make(i, pl.ds(at, n)) for i, (at, n) in enumerate(columns_of(size))]

        first = pieces_of(
            lambda i, c: remote(part.at[theirs, c], near.at[:, c], c_s.at[i], c_r.at[i], core)
        )
        second = pieces_of(
            lambda i, c: remote(
                mine.at[:, c], far.at[turn, :, c], y_s.at[turn, i], y_r.at[turn, i], other
            )
        )
        third = pieces_of(
            lambda i, c: remote(total.at[own, c], total.at[own, c], e_s.at[i], e_r.at[i], core)
        )

        def middle(i):
            at, n = columns_of(size)[i]
            first[i].wait_recv()
            mine[:, at : at + n] = part[own, at : at + n] + near[:, at : at + n]
            second[i].start()

        for i, (at, n) in enumerate(columns_of(size)):
            fill(at, n)
            first[i].start()
            if i:
                middle(i - 1)
        middle(len(first) - 1)
        idle()
        for i, (at, n) in enumerate(columns_of(size)):
            second[i].wait_recv()
            total[own, at : at + n] = mine[:, at : at + n] + far[turn, :, at : at + n]
            third[i].start()
        for copy in third:
            copy.wait_recv()
        for copy in first + second + third:
            copy.wait_send()

    def dot(left, right):
        return jnp.dot(left, right, preferred_element_type=jnp.float32)

    def low(value):
        return value.astype(jnp.bfloat16)

    def spin(value, sign):
        a, b = value[:, : head // 2], value[:, head // 2 :]
        cosine, sine = cosine_ref[...], sign * sine_ref[...]
        return jnp.concatenate([a * cosine - b * sine, b * cosine + a * sine], axis=1)

    def factor_of(value):
        return lax.rsqrt(jnp.mean(value * value, axis=-1, keepdims=True) + EPSILON)

    def gelu_parts(value):
        c = math.sqrt(2.0 / math.pi)
        square = value * value
        t = jnp.tanh(c * value * (1.0 + 0.044715 * square))
        gelu = 0.5 * value * (1.0 + t)
        slope = 0.5 * (1.0 + t) + 0.5 * value * (1.0 - t * t) * c * (1.0 + 3 * 0.044715 * square)
        return gelu, slope

    across_row = jnp.broadcast_to(segments[...].astype(jnp.float32), (tokens, tokens))
    down_row = across_row.T
    at_row = lax.broadcasted_iota(jnp.int32, (tokens, tokens), 0)
    at_column = lax.broadcasted_iota(jnp.int32, (tokens, tokens), 1)
    earlier = jnp.sum(jnp.where(across_row < down_row, 1.0, 0.0), axis=1, keepdims=True)
    position = at_row[:, : head // 2].astype(jnp.float32) - earlier
    exponent = at_column[:, : head // 2].astype(jnp.float32) * (-2.0 / head)
    angles = position * jnp.exp(exponent * math.log(10000.0))
    cosine_ref[...] = jnp.cos(angles)
    sine_ref[...] = jnp.sin(angles)
    mask_ref[...] = jnp.where(
        jnp.logical_and(across_row == down_row, at_row >= at_column), 1.0, 0.0
    )
    h_s[0] = h_in[...].astype(jnp.float32)
    mixer, feed = mixer_gain[...], feed_gain[...]

    def forward(l, carry):
        def need(*copies):
            @pl.when(l == 0)
            def _():
                for copy in copies:
                    copy.wait()

        h = h_s[l]
        normed = low(h * factor_of(h) * mixer)
        normed_s[l] = normed
        need(load.q_in, load.query, load.q_out, load.kv_in, load.pair, load.kv_out)

        @pl.when(l == 0)
        def _():
            kv_flat[0] = W.kv_in[0].reshape(width, 2 * rank)

        query_rank = low(dot(normed, W.q_in[l]))
        qr_s[l] = query_rank
        queries = dot(normed, W.query[...]) + dot(query_rank, W.q_out[l])
        q_s[l] = low(spin(queries, 1.0))
        pair_rank = low(dot(normed, kv_flat[l]))
        kvr_s[l] = pair_rank
        keys = dot(normed, W.pair[:, :head]) + dot(pair_rank[:, :rank], W.kv_out[l, 0])
        k_s[l] = low(spin(keys, 1.0))
        values = dot(normed, W.pair[:, head:]) + dot(pair_rank[:, rank:], W.kv_out[l, 1])
        v_s[l] = low(values)
        scores = product_t(q_s[l], k_s[l]) * scale
        scores = jnp.where(mask_ref[...] > 0, scores, MASKED)
        expo = jnp.exp(scores - jnp.max(scores, axis=-1, keepdims=True))
        probs = expo / jnp.sum(expo, axis=-1, keepdims=True)
        probs_s[l] = probs
        mixed = low(dot(low(probs), v_s[l]))
        mixed_s[l] = mixed
        need(load.output, load.o_in, load.o_out)

        def fill_attend(at, n):
            cut = min(n, max(0, width - at))
            if cut:
                part[:, at : at + cut] = dot(mixed, W.output[:, at : at + cut])
            if cut < n:
                start = at + cut - width
                part[:, at + cut : at + n] = dot(mixed, W.o_in[l, :, start : start + n - cut])

        again = l > 0

        def idle_attend():
            ship_x(2, l, normed, again, 0)
            ship_r(3, l, query_rank, again, 0)
            ship_q(1, l, mixed, again, 0)

            @pl.when(l == 0)
            def _():
                load.w_in.wait()
                for i in range(loops):
                    w_flat[i] = W.w_in[i].reshape(width, 2 * rank)
                for i in range(1, loops):
                    kv_flat[i] = W.kv_in[i].reshape(width, 2 * rank)

        sum_over_mp(width + rank, fill_attend, 0, idle_attend)
        output_rank = total[:, width : width + rank]
        or_s[l] = output_rank
        middle = h_s[l] + total[:, :width]
        for piece in split3(output_rank):
            middle = middle + dot(piece, W.o_out[l])
        mid_s[l] = middle
        fed = low(middle * factor_of(middle) * feed)
        fed_s[l] = fed
        need(load.wide, load.w_out)
        widen_rank = low(dot(fed, w_flat[l]))
        er_s[l] = widen_rank
        for at, n in chunks:
            gate = product_t(fed, W.wide[0, at : at + n]) + product_t(
                widen_rank[:, :rank], W.w_out[l, 0, at : at + n]
            )
            gate_s[l, :, at : at + n] = gate
            up = product_t(fed, W.wide[1, at : at + n]) + product_t(
                widen_rank[:, rank:], W.w_out[l, 1, at : at + n]
            )
            up_s[l, :, at : at + n] = up
            act_s[:, at : at + n] = low(gelu_parts(gate)[0] * up)
            ship_b(4 + at // WIDE, l, act_s[:, at : at + n], again, 0)
        need(load.down, load.d_in, load.d_out)

        def fill_feed(at, n):
            cut = min(n, max(0, width - at))
            if cut:
                part[:, at : at + cut] = dot(act_s[...], W.down[:, at : at + cut])
            if cut < n:
                start = at + cut - width
                part[:, at + cut : at + n] = dot(act_s[...], W.d_in[l, :, start : start + n - cut])

        def idle_feed():
            ship_x(0, l, fed, again, 0)
            ship_r(0, l, widen_rank[:, :rank], again, 0)
            ship_r(1, l, widen_rank[:, rank:], again, 0)

            @pl.when(again)
            def _():
                pass_act(0)

        sum_over_mp(width + rank, fill_feed, 1, idle_feed)
        shrink_rank = total[:, width : width + rank]
        sr_s[l] = shrink_rank
        result = mid_s[l] + total[:, :width]
        for piece in split3(shrink_rank):
            result = result + dot(piece, W.d_out[l])
        h_s[l + 1] = result
        return carry

    lax.fori_loop(0, loops, forward, 0)
    out_ref[...] = low(h_s[loops])

    g_s[...] = cot[...].astype(jnp.float32)
    gain_s[...] = jnp.zeros_like(gain_s)
    padded_quarter = select.shape[0] // blocks
    row = lax.broadcasted_iota(jnp.int32, (padded_quarter, width), 0)
    column = lax.broadcasted_iota(jnp.int32, (padded_quarter, width), 1)
    for b in range(blocks):
        hit = jnp.logical_and(column == row + (b * 4 + mp) * quarter, row < quarter)
        select[b * padded_quarter : (b + 1) * padded_quarter] = low(
            jnp.where(hit, 1.0, 0.0)
        )
    small_row = lax.broadcasted_iota(jnp.int32, (rank_quarter, rank), 0)
    small_column = lax.broadcasted_iota(jnp.int32, (rank_quarter, rank), 1)
    rank_select = low(
        jnp.concatenate(
            [
                jnp.where(small_column == small_row + (b * 4 + mp) * rank_quarter, 1.0, 0.0)
                for b in range(blocks)
            ],
            axis=0,
        )
    )
    raw_rows = raw_layout(quarter, rank_quarter, loops)

    def back(step, carry):
        l = loops - 1 - step
        again = step > 0
        before = loops - 1

        upstream = g_s[...]
        grad_feed = low(upstream)
        grad_shrink = low(product_t(grad_feed, W.d_out[l]))
        for i, (at, n) in enumerate(chunks):
            grad_act = product_t(grad_feed, W.down[at : at + n]) + product_t(
                grad_shrink, W.d_in[l, at : at + n]
            )
            gelu, slope = gelu_parts(gate_s[l, :, at : at + n])
            grad_gate = low(grad_act * up_s[l, :, at : at + n] * slope)
            grad_up = low(grad_act * gelu)
            gg_s[:, at : at + n] = grad_gate
            gu_s[:, at : at + n] = grad_up
            ship_b(i, l, grad_gate, again, before)
            ship_b(2 + i, l, grad_up, again, before)

        def fill_fed(at, n):
            cut = min(n, max(0, width - at))
            if cut:
                part[:, at : at + cut] = dot(gg_s[...], W.wide[0, :, at : at + cut]) + dot(
                    gu_s[...], W.wide[1, :, at : at + cut]
                )
            while cut < n:
                start = at + cut - width
                j, offset = divmod(start, rank)
                size = min(n - cut, rank - offset)
                value = (gg_s, gu_s)[j][...]
                part[:, at + cut : at + cut + size] = dot(
                    value, W.w_out[l, j, :, offset : offset + size]
                )
                cut += size

        def idle_fed():
            ship_x(1, l, grad_feed, again, before)
            ship_r(2, l, grad_shrink, again, before)

            @pl.when(step == 0)
            def _():
                pass_act(loops - 1)

        sum_over_mp(width + 2 * rank, fill_fed, 0, idle_fed)
        grad_widen = low(total[:, width : width + 2 * rank])
        grad_fed = total[:, :width] + product_t(grad_widen, w_flat[l])
        middle = mid_s[l]
        factor = factor_of(middle)
        unit = middle * factor
        scaled = grad_fed * feed
        grad_middle = upstream + factor * (
            scaled - unit * jnp.mean(scaled * unit, axis=-1, keepdims=True)
        )
        gain_s[1:2] += jnp.sum(grad_fed * unit, axis=0, keepdims=True)
        g_s[...] = grad_middle
        grad_attend = low(grad_middle)
        grad_output = low(product_t(grad_attend, W.o_out[l]))
        grad_mixed = low(
            product_t(grad_attend, W.output[...]) + product_t(grad_output, W.o_in[l])
        )
        probs = probs_s[l]
        grad_probs = product_t(grad_mixed, v_s[l])
        delta = jnp.sum(grad_probs * probs, axis=-1, keepdims=True)
        grad_scores = low(probs * (grad_probs - delta))
        grad_query = low(spin(dot(grad_scores, k_s[l]) * scale, -1.0))

        def fill_normed(at, n):
            if at == columns_of(width + rank + 2 * head)[0][0]:
                part[:, width + rank : width + rank + head] = spin(
                    product_tn(grad_scores, q_s[l]) * scale, -1.0
                )
                part[:, width + rank + head :] = product_tn(low(probs), grad_mixed)
            cut = min(n, max(0, width - at))
            if cut:
                part[:, at : at + cut] = product_t(grad_query, W.query[at : at + cut])
            end = min(at + n, width + rank)
            if at + cut < end:
                start = at + cut - width
                part[:, at + cut : end] = product_t(
                    grad_query, W.q_out[l, start : end - width]
                )

        def idle_normed():
            ship_q(0, l, grad_query, again, before)
            ship_x(3, l, grad_attend, again, before)
            ship_r(4, l, grad_output, again, before)
            pass_feed(l)

        sum_over_mp(width + rank + 2 * head, fill_normed, 1, idle_normed)
        grad_rank = low(total[:, width : width + rank])
        grad_pair = low(total[:, width + rank : width + rank + 2 * head])
        grad_pair_rank = low(
            jnp.concatenate(
                [
                    product_t(grad_pair[:, :head], W.kv_out[l, 0]),
                    product_t(grad_pair[:, head:], W.kv_out[l, 1]),
                ],
                axis=1,
            )
        )
        grad_normed = (
            total[:, :width]
            + product_t(grad_rank, W.q_in[l])
            + product_t(grad_pair, W.pair[...])
            + product_t(grad_pair_rank, kv_flat[l])
        )
        h = h_s[l]
        factor = factor_of(h)
        unit = h * factor
        scaled = grad_normed * mixer
        g_s[...] += factor * (scaled - unit * jnp.mean(scaled * unit, axis=-1, keepdims=True))
        gain_s[0:1] += jnp.sum(grad_normed * unit, axis=0, keepdims=True)

        def put(start, size, stride, value, add=False):
            for b in range(blocks):
                piece = value[b * stride : b * stride + size]
                at = pl.ds(start, size)
                if add:
                    raw_ref[b % 2, b // 2, at] += piece
                else:
                    raw_ref[b % 2, b // 2, at] = piece

        tall = raw_rows.tall
        normed_own = low(product_t(select[...], normed_s[l]))
        pair_weight = dot(normed_own, grad_pair)

        @pl.when(step == 0)
        def _():
            for j in range(2):
                put(j * tall, tall, padded_quarter, pair_weight[:, j * head : (j + 1) * head])

        @pl.when(step > 0)
        def _():
            for j in range(2):
                put(j * tall, tall, padded_quarter, pair_weight[:, j * head : (j + 1) * head], True)

        base = 2 * tall + l * raw_rows.loop

        def put_loop(i, value):
            put(pl.multiple_of(base + i * tall, 8), tall, padded_quarter, value)

        put_loop(0, dot(normed_own, grad_rank))
        for j in range(2):
            put_loop(1 + j, dot(normed_own, grad_pair_rank[:, j * rank : (j + 1) * rank]))
        fed_own = low(product_t(select[...], fed_s[l]))
        for j in range(2):
            put_loop(3 + j, dot(fed_own, grad_widen[:, j * rank : (j + 1) * rank]))
        attend_own = low(product_t(select[...], grad_attend))
        put_loop(5, sum(dot(attend_own, piece) for piece in split3(or_s[l])))
        feed_own = low(product_t(select[...], grad_feed))
        put_loop(6, sum(dot(feed_own, piece) for piece in split3(sr_s[l])))
        for j in range(2):
            rank_own = low(product_t(rank_select, kvr_s[l, :, j * rank : (j + 1) * rank]))
            put(
                pl.multiple_of(base + 7 * tall + j * rank_quarter, 8), rank_quarter, rank_quarter,
                dot(rank_own, grad_pair[:, j * head : (j + 1) * head]),
            )
        return carry

    lax.fori_loop(0, loops, back, 0)
    last = loops - 1
    for copies in (
        x_copies(0, last), x_copies(2, last), r_copies(0, last), r_copies(1, last), r_copies(3, last),
        b_copies(4, last), b_copies(5, last), q_copies(1, last),
        x_copies(1, 0), x_copies(3, 0), r_copies(2, 0), r_copies(4, 0),
        b_copies(0, 0), b_copies(1, 0), b_copies(2, 0), b_copies(3, 0), q_copies(0, 0),
    ):
        finish(copies)
    for l in range(loops):
        for copies in (x_copies(0, l), r_copies(0, l), r_copies(1, l), b_copies(0, l)):
            copies[1].wait_recv()

        @pl.when(is_end)
        def _():
            for copy in far_feed(l) + far_act(l):
                copy.wait_send()

        @pl.when(jnp.logical_not(is_end))
        def _():
            onward = [x_copies(1, l)[2], r_copies(2, l)[2], b_copies(4, l)[2], b_copies(5, l)[2]]
            for copy in onward + far_feed(l) + far_act(l):
                copy.wait_recv()

    grad_ref[...] = g_s[...]
    for b in range(blocks):
        ends = jnp.zeros((8, head), jnp.float32)
        raw_ref[b % 2, b // 2, raw_rows.gains :] = ends
        raw_ref[b % 2, b // 2, raw_rows.gains : raw_rows.gains + 2, :block] = gain_s[
            :2, b * block : (b + 1) * block
        ]


def raw_layout(quarter, rank_quarter, loops):
    tall = -(-quarter // 8) * 8
    loop = 7 * tall + 2 * rank_quarter
    gains = 2 * tall + loops * loop
    return SimpleNamespace(tall=tall, loop=loop, gains=gains, all=gains + 8)


def block_and_factors(block_input, cotangent, segments, shared, stacked, dp_size):
    (mixer_gain, feed_gain, query, pair, output, widen, down) = shared
    (q_in, q_out, kv_in, kv_out, o_in, o_out, w_in, w_out, d_in, d_out) = stacked
    tokens, width = block_input.shape
    head = query.shape[1]
    loops, _, rank = q_in.shape
    hidden = down.shape[0]
    weights = (
        q_in, query, q_out, kv_in, pair, kv_out, output, o_in, o_out,
        w_in, widen.transpose(1, 2, 0), w_out.swapaxes(2, 3), down, d_in, d_out,
    )
    layout = raw_layout(width // (4 * dp_size), rank // (4 * dp_size), loops)
    line = dp_size // 2
    f32, bf16 = jnp.float32, jnp.bfloat16
    shape = jax.ShapeDtypeStruct
    block, rank_block, both = width // dp_size, rank // dp_size, loops * tokens
    out_shape = (
        shape((tokens, width), bf16),
        shape((tokens, width), f32),
        shape((2, line, layout.all, head), f32),
        shape((4, 2, line, block, both), f32),
        shape((5, 2, line, rank_block, both), f32),
        shape((6, both, WIDE), f32),
        shape((2, both, head), f32),
        shape((2, line, block, both), f32),
        shape((3, line, rank_block, both), f32),
        shape((3, both, WIDE), f32),
        shape((line, block, 2 * both), f32),
        shape((line, rank_block, 2 * both), f32),
        shape((2, 2 * both, WIDE), f32),
    )
    vmem = pl.BlockSpec(memory_space=pltpu.VMEM)
    hbm = pl.BlockSpec(memory_space=pl.ANY)
    widest = width + rank + 2 * head
    pieces = -(-widest // SUM_STEP)
    dma = pltpu.SemaphoreType.DMA

    def kept(columns, dtype, count=loops):
        return pltpu.VMEM((count, tokens, columns), dtype)

    scratch = [pltpu.VMEM(w.shape, bf16) for w in weights] + [
        kept(width, f32, loops + 1), kept(width, f32), kept(width, bf16), kept(rank, bf16),
        kept(2 * rank, bf16), kept(head, bf16), kept(head, bf16), kept(head, bf16), kept(tokens, f32),
        kept(head, bf16), kept(rank, f32), kept(width, bf16), kept(2 * rank, bf16),
        kept(hidden, f32), kept(hidden, f32), pltpu.VMEM((tokens, hidden), bf16), kept(rank, f32),
        pltpu.VMEM((tokens, hidden), bf16), pltpu.VMEM((tokens, hidden), bf16),
        pltpu.VMEM((tokens, width), f32), pltpu.VMEM((8, width), f32),
        pltpu.VMEM((dp_size * 48, width), bf16),
        pltpu.VMEM((tokens, widest), f32), pltpu.VMEM((tokens, widest), f32),
        pltpu.VMEM((tokens // 2, widest), f32), pltpu.VMEM((tokens // 2, widest), f32),
        pltpu.VMEM((2, tokens // 2, widest), f32),
        pltpu.VMEM((4, 2, line, block, tokens), f32), pltpu.VMEM((5, 2, line, rank_block, tokens), f32),
        pltpu.VMEM((6, tokens, WIDE), f32), pltpu.VMEM((2, tokens, head), f32),
        pltpu.VMEM((loops, width, 2 * rank), bf16), pltpu.VMEM((loops, width, 2 * rank), bf16),
        pltpu.VMEM((tokens, head // 2), f32), pltpu.VMEM((tokens, head // 2), f32),
        pltpu.VMEM((tokens, tokens), f32),
        dma((len(weights),)), dma((pieces,)), dma((pieces,)), dma((2, pieces)), dma((2, pieces)),
        dma((pieces,)), dma((pieces,)),
        dma((4, loops)), dma((5, loops)), dma((6, loops)), dma((2, loops)),
    ]
    scratch += [dma((2, loops))] * 2 + [dma((3, loops))] * 4
    scratch += [dma((2, loops))] * 4 + [dma((2, 2, loops))] * 2
    return pl.pallas_call(
        block_kernel,
        out_shape=out_shape,
        in_specs=[vmem] * 5 + [hbm] * len(weights),
        out_specs=(vmem,) * 3 + (hbm,) * 10,
        scratch_shapes=scratch,
        compiler_params=pltpu.CompilerParams(
            collective_id=21, has_side_effects=True, vmem_limit_bytes=63 << 20
        ),
    )(
        block_input, cotangent, segments, mixer_gain[None], feed_gain[None],
        *weights,
    )


def line_kernel(
    raw_all, x_all, r_all, b_all, q_all, x_got, r_got, b_got, x_end_all, r_end_all, b_end_all,
    gains_out, q_w, pair_w, o_w, e_w, s_w, q_i, q_o, p_i, p_o, o_i, o_o, e_i, e_o, s_i, s_o,
    main_out, side_out, raw_out, around,
    x_own, r_own, b_own, q_own, x_far, r_far, b_far, q_far, x_end, r_end, b_end, raw_own, raw_far, product_ref,
    main_right, main_left, side_right, side_left, raw_right, raw_left,
    x_s, x_r, r_s, r_r, b_s, b_r, q_s, q_r, w_s, w_r, local_sems, step_sems, around_s, around_r,
    mr_s, mr_r, ml_s, ml_r, sr_s, sr_r, sl_s, sl_r, rr_s, rr_r, rl_s, rl_r,
    credit_right, credit_left,
):
    dp, mp = lax.axis_index("dp"), lax.axis_index("mp")
    x = lax.rem(dp, 2)
    z = dp // 2
    last = 3
    pair = (dp + 1 - 2 * x, mp)
    up, down = (dp + 2, mp), (dp - 2, mp)

    core, other = (dp, mp + 1 - 2 * lax.rem(mp, 2)), (dp, lax.rem(mp + 2, 4))
    hidden = s_w.shape[1]
    block, rank_block, quarter = s_w.shape[0], s_i.shape[1], pair_w.shape[0]
    loops, head = s_i.shape[0], q_w.shape[1]
    layout = raw_layout(quarter, rank_block // 4, loops)
    tall = layout.tall

    barrier = pltpu.get_barrier_semaphore()
    for device in (pair, core, other):
        pl.semaphore_signal(barrier, inc=1, device_id=device, device_id_type=MESH)

    @pl.when(z > 0)
    def _():
        pl.semaphore_signal(barrier, inc=1, device_id=down, device_id_type=MESH)

    @pl.when(z < last)
    def _():
        pl.semaphore_signal(barrier, inc=1, device_id=up, device_id_type=MESH)

    pl.semaphore_wait(barrier, 3 + jnp.minimum(z, 1) + jnp.minimum(last - z, 1))

    def across(source, target, send, recv):
        return pltpu.make_async_remote_copy(
            source, target, send, recv, device_id=pair, device_id_type=MESH
        )

    def x_copy(i):
        return across(x_all.at[i, 1 - x], x_far.at[i], x_s.at[i - 2], x_r.at[i - 2])

    def r_copy(i):
        return across(r_all.at[i, 1 - x], r_far.at[i], r_s.at[i - 3], r_r.at[i - 3])

    def b_copy(i):
        return across(b_all.at[i], b_far.at[i], b_s.at[i], b_r.at[i])

    q_copy = across(q_all, q_far, q_s, q_r)
    w_copy = across(raw_all.at[1 - x], raw_far, w_s, w_r)

    def here(source, target, i):
        return pltpu.make_async_copy(source, target, local_sems.at[i])

    at_start = [
        here(x_all.at[:, x], x_own, 0),
        here(r_all.at[:, x], r_own, 1),
        here(x_got, x_far.at[0:2], 2),
        here(r_got, r_far.at[0:3], 3),
        here(b_got.at[0], b_far.at[0], 4),
        here(b_got.at[1:3], b_far.at[4:6], 5),
        here(q_all, q_own, 6),
    ]
    for_ends = [here(x_end_all, x_end, 7), here(r_end_all, r_end, 8), here(b_end_all, b_end, 9)]
    own_copy = here(raw_all.at[x], raw_own, 10)
    inner = jnp.logical_and(z > 0, z < last)

    def chunk_of(step):
        return jnp.where(lax.rem(step, 3) == 1, 4 + step // 3, step - (step + 1) // 3)

    def b_load(step):
        slot = lax.rem(step, 2)
        return pltpu.make_async_copy(b_all.at[chunk_of(step)], b_own.at[slot], step_sems.at[slot])

    b_copy(1).start()
    b_load(0).start()
    for copy in at_start:
        copy.start()

    @pl.when(inner)
    def _():
        for copy in for_ends:
            copy.start()

    own_copy.start()
    for copy in at_start:
        copy.wait()

    @pl.when(inner)
    def _():
        for copy in for_ends:
            copy.wait()

    def chain(target, step, slot, steps, value, out, right, left, r_s, r_r, l_s, l_r, credits):
        def move(buffer, send, recv, i, s, device):
            return pltpu.make_async_remote_copy(
                buffer.at[i, s], buffer.at[i, s], send.at[i, s], recv.at[i, s],
                device_id=device, device_id_type=MESH,
            )

        def inside(at):
            return lax.rem(at, 3) == 1 if credits else at < 0

        def free(credit, i, source, at, from_end):
            @pl.when(
                jnp.logical_and(
                    at <= steps - 1,
                    jnp.logical_not(jnp.logical_and(from_end, inside(at))),
                )
            )
            def _():
                pl.semaphore_signal(credit.at[i], inc=1, device_id=source, device_id_type=MESH)

        def pass_on(i, place, buffer, send, recv, onward, source, at_end, next_to_end, credit):
            def here(i, s):
                return move(buffer, send, recv, i, s, onward)

            def begin():
                if credits:

                    @pl.when(step >= 3)
                    def _():
                        pl.semaphore_wait(credit.at[i], 1)

                here(i, slot).start()

            @pl.when(jnp.logical_and(at_end, jnp.logical_not(inside(step))))
            def _():
                buffer[i, slot] = value()
                if credits:
                    before = lax.rem(step + 2 - inside(step - 1).astype(jnp.int32), 3)
                    after = jnp.where(onward[0] > dp, i - 1, i + 1)

                    @pl.when(jnp.logical_and(place < 2, step >= 1))
                    def _():
                        here(after, before).wait_send()

                    @pl.when(place == 2)
                    def _():
                        here(2 - i, slot).wait_send()

                    begin()
                else:
                    begin()
                    here(i, slot).wait_send()

            @pl.when(jnp.logical_not(at_end))
            def _():
                if credits:

                    @pl.when(step >= 1)
                    def _():
                        here(i, lax.rem(step + 2, 3)).wait_send()
                        free(credit, i, source, step + 2, next_to_end)

                has_source = jnp.logical_not(jnp.logical_and(next_to_end, inside(step)))

                @pl.when(jnp.logical_not(has_source))
                def _():
                    buffer[i, slot] = value()

                @pl.when(has_source)
                def _():
                    product = value()
                    here(i, slot).wait_recv()
                    buffer[i, slot] += product

                begin()

        @pl.when(target > z)
        def _():
            pass_on(target - 1, 3 - target, right, r_s, r_r, up, down, z == 0, z == 1, credit_right)

        @pl.when(target < z)
        def _():
            pass_on(target, target, left, l_s, l_r, down, up, z == last, z == last - 1, credit_left)

        @pl.when(target == z)
        def _():
            out[...] = value()

    def arrive(step, slot, steps, out, right, left, r_s, r_r, l_s, l_r, credits):
        def came(buffer, send, recv, i):
            return pltpu.make_async_remote_copy(
                buffer.at[i, slot], buffer.at[i, slot], send.at[i, slot], recv.at[i, slot],
                device_id=pair, device_id_type=MESH,
            )

        started_inside = lax.rem(step, 3) == 1 if credits else step < 0

        def side_of(there, from_end, buffer, send, recv, i, credit, source):
            @pl.when(there)
            def _():
                quiet = jnp.logical_and(from_end, started_inside)

                @pl.when(jnp.logical_not(quiet))
                def _():
                    came(buffer, send, recv, i).wait_recv()
                    out[...] += buffer[i, slot]

                if credits:
                    skip = jnp.logical_and(from_end, lax.rem(step + 3, 3) == 1)

                    @pl.when(jnp.logical_and(step + 3 <= steps - 1, jnp.logical_not(skip)))
                    def _():
                        pl.semaphore_signal(
                            credit.at[i], inc=1, device_id=source, device_id_type=MESH
                        )

        side_of(z > 0, z == 1, right, r_s, r_r, jnp.maximum(z - 1, 0), credit_right, down)
        side_of(z < last, z == last - 1, left, l_s, l_r, jnp.minimum(z, last - 1), credit_left, up)

    def settle(slot, right, left, r_s, l_s, main):
        def wait(buffer, send, i, device):
            pltpu.make_async_remote_copy(
                buffer.at[i, slot], buffer.at[i, slot], send.at[i, slot], send.at[i, slot],
                device_id=device, device_id_type=MESH,
            ).wait_send()

        for target in range(4):
            rightmost, leftmost = target == 3, target == 0

            @pl.when(jnp.logical_and(target > z, jnp.logical_or(z > 0, main and not rightmost)))
            def _():
                wait(right, r_s, target - 1, up)

            @pl.when(jnp.logical_and(target < z, jnp.logical_or(z < last, main and not leftmost)))
            def _():
                wait(left, l_s, target, down)

    def order(turn):
        def near(end):
            return jnp.where(end == 0, 3 - turn, jnp.where(turn < 2, 3 - turn, turn - 2))

        return jnp.where(z < 2, near(z), 3 - near(3 - z))

    def dot(left, right):
        return jnp.dot(
            left.astype(jnp.bfloat16), right.astype(jnp.bfloat16), preferred_element_type=jnp.float32
        )

    steps = b_all.shape[0]

    def left_times(x_index, group, target, own, far):
        half = own.shape[0] // 2
        rank_own, rank_far = r_own[group, target], r_far[group, target]
        return [
            dot(x_own[x_index, target], own) + dot(x_far[x_index, target], far),
            dot(rank_own[:, :half], own[:half]) + dot(rank_far[:, :half], far[:half]),
            dot(rank_own[:, half:], own[half:]) + dot(rank_far[:, half:], far[half:]),
        ]

    def main_arrive(step):
        slot = lax.rem(step, 3)
        chunk = chunk_of(step)
        arrive(
            step, slot, steps, main_out.at[slot], main_right, main_left, mr_s, mr_r, ml_s, ml_r, True,
        )
        for part, (at, n) in enumerate(((0, WIDE), (WIDE, hidden - WIDE))):
            for j in range(2):

                @pl.when(chunk == 2 * j + part)
                def _():
                    e_w[:, j, at : at + n] = main_out[slot, :block, :n]
                    for l in range(loops):
                        start = block + l * rank_block
                        e_o[l, j, :, at : at + n] = main_out[slot, start : start + rank_block, :n]

            @pl.when(chunk == 4 + part)
            def _():
                s_w[:, at : at + n] = main_out[slot, :block, :n]
                for l in range(loops):
                    start = block + l * rank_block
                    s_i[l, :, at : at + n] = main_out[slot, start : start + rank_block, :n]

    def turn_body(at, carry):
        step, turn = at // 4, lax.rem(at, 4)
        slot = lax.rem(step, 3)
        chunk = chunk_of(step)
        group = chunk // 2
        target = order(turn)

        @pl.when(turn == 0)
        def _():
            b_load(step).wait()

            @pl.when(step < steps - 1)
            def _():
                b_load(step + 1).start()

            @pl.when(jnp.logical_and(chunk >= 1, chunk <= 3))
            def _():
                b_copy(chunk).wait_recv()

            @pl.when(step == 1)
            def _():
                b_copy(2).start()

            @pl.when(step == 2)
            def _():
                b_copy(3).start()

            @pl.when(step == 3)
            def _():
                w_copy.start()

            @pl.when(step == 4)
            def _():
                x_copy(2).start()
                x_copy(3).start()
                r_copy(3).start()
                r_copy(4).start()
                q_copy.start()

        def value():
            parts = left_times(
                group // 2, group, target,
                b_own[lax.rem(step, 2)].astype(jnp.bfloat16), b_far[chunk].astype(jnp.bfloat16),
            )
            product_ref[...] = jnp.concatenate(parts, axis=0)
            beyond = jnp.logical_or(
                jnp.logical_and(z == 1, target >= 1),
                jnp.logical_and(z == last - 1, target <= last - 1),
            )

            @pl.when(jnp.logical_and(beyond, chunk >= 4))
            def _():
                end = b_end[jnp.maximum(chunk - 4, 0)].astype(jnp.bfloat16)
                middle = end.shape[0] // 2
                product_ref[...] += jnp.concatenate(
                    [
                        dot(x_end[target], end),
                        dot(r_end[target, :, :middle], end[:middle]),
                        dot(r_end[target, :, middle:], end[middle:]),
                    ],
                    axis=0,
                )

            return product_ref[...]

        chain(
            target, step, slot, steps, value, main_out.at[slot], main_right, main_left,
            mr_s, mr_r, ml_s, ml_r, True,
        )

        @pl.when(jnp.logical_and(turn == 3, step >= 2))
        def _():
            main_arrive(step - 2)

        return carry

    lax.fori_loop(0, 4 * steps, turn_body, 0)

    w_copy.wait_recv()
    own_copy.wait()

    def raw_body(turn, carry):
        target = order(turn)
        chain(
            target, 0, 0, 1, lambda: raw_own[target] + raw_far[target], raw_out, raw_right, raw_left,
            rr_s, rr_r, rl_s, rl_r, False,
        )
        return carry

    lax.fori_loop(0, 4, raw_body, 0)
    main_arrive(jnp.int32(steps - 2))

    for i in (2, 3):
        x_copy(i).wait_recv()
    for i in (3, 4):
        r_copy(i).wait_recv()
    q_copy.wait_recv()

    def side_body(turn, carry):
        target = order(turn)

        def value():
            parts = [
                left_times(
                    2 + i, 3 + i, target, q_own[i].astype(jnp.bfloat16), q_far[i].astype(jnp.bfloat16)
                )
                for i in range(2)
            ]
            return jnp.concatenate([jnp.concatenate(p, axis=0) for p in parts], axis=1)

        chain(
            target, 0, 0, 1, value, side_out, side_right, side_left,
            sr_s, sr_r, sl_s, sl_r, False,
        )
        return carry

    lax.fori_loop(0, 4, side_body, 0)
    main_arrive(jnp.int32(steps - 1))
    arrive(0, 0, 1, raw_out, raw_right, raw_left, rr_s, rr_r, rl_s, rl_r, False)

    def share(device, owner, i):
        return pltpu.make_async_remote_copy(
            around.at[owner], around.at[owner], around_s.at[i], around_r.at[i],
            device_id=device, device_id_type=MESH,
        )

    far_owner = lax.rem(mp + 2, 4)
    for l in range(loops):
        start = 2 * tall + l * layout.loop + 5 * tall
        around[mp, l] = raw_out[start : start + 2 * tall]
    along, same, passed = share(other, mp, 0), share(core, mp, 1), share(core, far_owner, 2)
    along.start()
    same.start()
    arrive(0, 0, 1, side_out, side_right, side_left, sr_s, sr_r, sl_s, sl_r, False)
    along.wait_recv()
    passed.start()
    q_w[...] = side_out[:block, :head]
    o_w[...] = side_out[:block, head:]
    for l in range(loops):
        start = block + l * rank_block
        q_o[l] = side_out[start : start + rank_block, :head]
        o_i[l] = side_out[start : start + rank_block, head:]
    gains_out[...] = raw_out[layout.gains : layout.gains + 2, :block]
    for j in range(2):
        pair_w[:, j * head : (j + 1) * head] = raw_out[j * tall : j * tall + quarter]
    for l in range(loops):
        base = 2 * tall + l * layout.loop
        q_i[:, l] = raw_out[base : base + quarter]
        for j in range(2):
            start = base + (1 + j) * tall
            p_i[l, :, j] = raw_out[start : start + quarter]
            e_i[l, :, j] = raw_out[start + 2 * tall : start + 2 * tall + quarter]
            start = base + 7 * tall + j * (rank_block // 4)
            p_o[l, j] = raw_out[start : start + rank_block // 4]
    same.wait_recv()
    passed.wait_recv()
    for l in range(loops):
        for m in range(4):
            o_o[l, m * quarter : (m + 1) * quarter] = around[m, l, :quarter]
            s_o[l, m * quarter : (m + 1) * quarter] = around[m, l, tall : tall + quarter]
    for copy in (along, same, passed):
        copy.wait_send()

    settle((steps - 1) % 3, main_right, main_left, mr_s, ml_s, True)
    settle(0, side_right, side_left, sr_s, sl_s, False)
    settle(0, raw_right, raw_left, rr_s, rl_s, False)
    for copy in (x_copy(2), x_copy(3), r_copy(3), r_copy(4), b_copy(1), b_copy(2), b_copy(3)):
        copy.wait_send()
    q_copy.wait_send()
    w_copy.wait_send()


def line_gradients(factors, loops, dp_size, mp_size, hidden):
    raw, x_all, r_all, b_all, q_all, x_got, r_got, b_got, x_end, r_end, b_end = factors
    block, rank_block, head = x_all.shape[3], r_all.shape[3], q_all.shape[2]
    quarter, rank_quarter = block // mp_size, rank_block // mp_size
    layout = raw_layout(quarter, rank_quarter, loops)
    rows = block + loops * rank_block
    steps = b_all.shape[0]
    vmem = pl.BlockSpec(memory_space=pltpu.VMEM)
    hbm = pl.BlockSpec(memory_space=pl.ANY)
    dma = pltpu.SemaphoreType.DMA
    f32 = jnp.float32
    line = dp_size // 2 - 1
    half_x = pltpu.VMEM((x_all.shape[0], *x_all.shape[2:]), f32)
    half_r = pltpu.VMEM((r_all.shape[0], *r_all.shape[2:]), f32)
    whole_b, whole_q = pltpu.VMEM(b_all.shape, f32), pltpu.VMEM(q_all.shape, f32)
    shapes = (
        (2, block), (block, head), (quarter, 2 * head), (block, head), (block, 2, hidden),
        (block, hidden), (quarter, loops, head), (loops, rank_block, head), (loops, quarter, 2, head),
        (loops, 2, rank_quarter, head), (loops, rank_block, head), (loops, block, head),
        (loops, quarter, 2, head), (loops, 2, rank_block, hidden), (loops, rank_block, hidden),
        (loops, block, head),
    )
    gains, q_w, pair_w, o_w, e_w, s_w, q_i, q_o, p_i, p_o, o_i, o_o, e_i, e_o, s_i, s_o = pl.pallas_call(
        line_kernel,
        out_shape=tuple(jax.ShapeDtypeStruct(v, f32) for v in shapes),
        in_specs=[hbm] * 11,
        out_specs=(vmem,) * len(shapes),
        scratch_shapes=[
            pltpu.VMEM((3, rows, WIDE), f32), pltpu.VMEM((rows, 2 * head), f32),
            pltpu.VMEM((layout.all, head), f32), pltpu.VMEM((4, loops, 2 * layout.tall, head), f32),
        ]
        + [half_x, half_r, pltpu.VMEM((2, *b_all.shape[1:]), f32), whole_q]
        + [half_x, half_r, whole_b, whole_q]
        + [pltpu.VMEM(v.shape, f32) for v in (x_end, r_end, b_end)]
        + [pltpu.VMEM(raw.shape[1:], f32)] * 2
        + [pltpu.VMEM((rows, WIDE), f32)]
        + [pltpu.VMEM((line, 3, rows, WIDE), f32)] * 2
        + [pltpu.VMEM((line, 1, rows, 2 * head), f32)] * 2
        + [pltpu.VMEM((line, 1, layout.all, head), f32)] * 2
        + [dma((2,))] * 4 + [dma((steps,))] * 2 + [dma] * 4 + [dma((11,)), dma((2,)), dma((3,)), dma((3,))]
        + [dma((line, 3))] * 4 + [dma((line, 1))] * 8
        + [pltpu.SemaphoreType.REGULAR((line,))] * 2,
        compiler_params=pltpu.CompilerParams(
            collective_id=20, has_side_effects=True, vmem_limit_bytes=63 << 20
        ),
    )(*factors)

    return (
        gains[0], gains[1], q_w, pair_w, o_w.T, e_w, s_w.T, q_i.swapaxes(0, 1), q_o, p_i, p_o,
        o_i.swapaxes(1, 2), o_o.swapaxes(1, 2), e_i, e_o, s_i.swapaxes(1, 2), s_o.swapaxes(1, 2),
    )


def per_device(dp_size, mp_size, block_input, cotangent, segments, *parameters):
    shared, stacked = parameters[:7], parameters[7:]
    loops = stacked[0].shape[0]
    if dp_size == 8 and mp_size == 4 and loops == 2:
        output, input_grad, *factors = block_and_factors(
            block_input, cotangent, segments, shared, stacked, dp_size
        )
        gradients = line_gradients(factors, loops, dp_size, mp_size, shared[6].shape[0])
        return (output, input_grad, *gradients)
    tables = rotary_tables(segments[0], shared[3].shape[1] // 2)
    total = mp_total(mp_size)
    state = block_input.astype(jnp.float32)
    kept_all = []
    for i in range(loops):
        state, kept = forward_loop(state, shared, [v[i] for v in stacked], tables, total, 1)
        kept_all.append(kept)
    upstream = cotangent.astype(jnp.float32)
    for i in reversed(range(loops)):
        upstream = reverse_loop(
            upstream, kept_all[i], shared, [v[i] for v in stacked], tables, total, 3
        )
    return (state.astype(jnp.bfloat16), upstream, *scattered_gradients(kept_all, dp_size, mp_size))


def solution(mesh):
    in_specs = (
        P("dp", None),
        P("dp", None),
        P("dp", None),
        P(),
        P(),
        P(None, "mp"),
        P(),
        P("mp", None),
        P(None, None, "mp"),
        P("mp", None),
        P(),
        P(None, None, "mp"),
        P(),
        P(),
        P(None, "mp", None),
        P(),
        P(),
        P(None, None, None, "mp"),
        P(None, "mp", None),
        P(),
    )
    out_specs = (
        P("dp", None),
        P("dp", None),
        P("dp"),
        P("dp"),
        P("dp", "mp"),
        P(("dp", "mp"), None),
        P("mp", "dp"),
        P("dp", None, "mp"),
        P("mp", "dp"),
        P(None, ("dp", "mp"), None),
        P(None, "dp", "mp"),
        P(None, ("dp", "mp"), None, None),
        P(None, None, ("dp", "mp"), None),
        P(None, "mp", "dp"),
        P(None, None, "dp"),
        P(None, ("dp", "mp"), None, None),
        P(None, None, "dp", "mp"),
        P(None, "mp", "dp"),
        P(None, None, "dp"),
    )
    return jax.shard_map(
        functools.partial(per_device, mesh.shape["dp"], mesh.shape["mp"]),
        mesh=mesh, in_specs=in_specs, out_specs=out_specs, check_vma=False
    )
```

```python
import functools
import math
from types import SimpleNamespace

import jax
import jax.numpy as jnp
from jax import lax
from jax.experimental import pallas as pl
from jax.experimental.pallas import tpu as pltpu
from jax.sharding import PartitionSpec as P

EPSILON = 1e-06
MASKED = -1e30
MESH = pl.DeviceIdType.MESH


def product(left, right):
    return jnp.dot(left, right, preferred_element_type=jnp.float32)


def product_t(left, right):
    return lax.dot_general(
        left, right, (((1,), (1,)), ((), ())), preferred_element_type=jnp.float32
    )


def product_tn(left, right):
    return lax.dot_general(
        left, right, (((0,), (0,)), ((), ())), preferred_element_type=jnp.float32
    )


def exact_product(left, right):
    return jnp.dot(left, right, precision=lax.Precision.HIGHEST, preferred_element_type=jnp.float32)


def exact_tn(left, right):
    return lax.dot_general(
        left,
        right,
        (((0,), (0,)), ((), ())),
        precision=lax.Precision.HIGHEST,
        preferred_element_type=jnp.float32,
    )


def normalize(hidden_state, gain):
    factor = lax.rsqrt(jnp.mean(hidden_state * hidden_state, axis=-1, keepdims=True) + EPSILON)
    return (hidden_state * factor * gain, factor)


def normalize_back(hidden_state, factor, gain, upstream_gradient):
    unit = hidden_state * factor
    scaled = upstream_gradient * gain
    downstream = factor * (scaled - unit * jnp.mean(scaled * unit, axis=-1, keepdims=True))
    return (downstream, jnp.sum(upstream_gradient * unit, axis=0))


def rotate(values, cosine_table, sine_table):
    half_width = values.shape[-1] // 2
    first = values[..., :half_width]
    second = values[..., half_width:]
    return jnp.concatenate(
        [first * cosine_table - second * sine_table, second * cosine_table + first * sine_table],
        axis=-1,
    )


def rotary_tables(segment_row, head_size):
    length_value = segment_row.shape[0]
    earlier = jnp.sum((segment_row[None, :] < segment_row[:, None]).astype(jnp.int32), axis=1)
    position = (jnp.arange(length_value, dtype=jnp.int32) - earlier).astype(jnp.float32)
    steps_half = jnp.arange(head_size // 2, dtype=jnp.float32)
    frequency = 10000.0 ** (-2.0 * steps_half / head_size)
    angles = position[:, None] * frequency[None, :]
    same_segment = segment_row[:, None] == segment_row[None, :]
    ordinal = jnp.arange(length_value, dtype=jnp.int32)
    allowed_mask = same_segment & (ordinal[:, None] >= ordinal[None, :])
    return (jnp.cos(angles), jnp.sin(angles), allowed_mask)


def gelu_tanh(values):
    return jax.nn.gelu(values, approximate=True)


def attention_probs(queries, keys, allowed_mask, score_scale):
    scores = (
        jnp.einsum("ihd,jd->hij", queries, keys, preferred_element_type=jnp.float32) * score_scale
    )
    return jnp.where(allowed_mask[None], scores, MASKED)


def mp_total(size):
    def kernel(part, out, near, mine, far, core_send, core_recv, y_send, y_recv, back_send, back_recv):
        dp, mp = lax.axis_index("dp"), lax.axis_index("mp")
        side = lax.rem(mp, 2)
        core = (dp, mp + 1 - 2 * side)
        other = (dp, lax.rem(mp + 2, 4))
        half = part.shape[0] // 2
        pieces = near.shape[0]
        width = part.shape[1] // pieces
        own = pl.ds(pl.multiple_of(side * half, half), half)
        theirs = pl.ds(pl.multiple_of((1 - side) * half, half), half)

        def columns(i):
            return pl.ds(i * width, width)

        barrier = pltpu.get_barrier_semaphore()
        for device in (core, other):
            pl.semaphore_signal(barrier, inc=1, device_id=device, device_id_type=MESH)
        pl.semaphore_wait(barrier, 2)
        first = [
            pltpu.make_async_remote_copy(
                part.at[theirs, columns(i)], near.at[i], core_send.at[i], core_recv.at[i],
                device_id=core, device_id_type=MESH,
            )
            for i in range(pieces)
        ]
        second = [
            pltpu.make_async_remote_copy(
                mine.at[i], far.at[i], y_send.at[i], y_recv.at[i],
                device_id=other, device_id_type=MESH,
            )
            for i in range(pieces)
        ]
        third = [
            pltpu.make_async_remote_copy(
                out.at[own, columns(i)], out.at[own, columns(i)], back_send.at[i], back_recv.at[i],
                device_id=core, device_id_type=MESH,
            )
            for i in range(pieces)
        ]
        for copy in first:
            copy.start()
        for i in range(pieces):
            first[i].wait_recv()
            mine[i] = part[own, columns(i)] + near[i]
            second[i].start()
        for i in range(pieces):
            second[i].wait_recv()
            out[own, columns(i)] = mine[i] + far[i]
            third[i].start()
        for copy in third:
            copy.wait_recv()
        for copy in first + second + third:
            copy.wait_send()

    def total(identity, *parts):
        if size != 4:
            return lax.psum(parts, "mp")
        joined = jnp.concatenate(parts, axis=1)
        tokens_here, columns_here = joined.shape
        pieces = 1
        for count in (5, 4, 3, 2):
            if columns_here % (128 * count) == 0:
                pieces = count
                break
        half = (pieces, tokens_here // 2, columns_here // pieces)
        summed = pl.pallas_call(
            kernel,
            out_shape=jax.ShapeDtypeStruct(joined.shape, jnp.float32),
            in_specs=[pl.BlockSpec(memory_space=pltpu.VMEM)],
            out_specs=pl.BlockSpec(memory_space=pltpu.VMEM),
            scratch_shapes=[pltpu.VMEM(half, jnp.float32)] * 3
            + [pltpu.SemaphoreType.DMA((pieces,))] * 6,
            compiler_params=pltpu.CompilerParams(
                collective_id=identity, has_side_effects=True, vmem_limit_bytes=16 << 20
            ),
        )(joined)
        edges, start = [], 0
        for part in parts:
            edges.append(summed[:, start : start + part.shape[1]])
            start += part.shape[1]
        return tuple(edges)

    return total


def forward_loop(hidden_state, shared, adapters, tables, total, identity):
    (mixer_gain, feed_gain, query_matrix, pair_matrix, output_matrix, widen_matrix, down_matrix) = shared
    (q_in, q_out, kv_in, kv_out, o_in, o_out, w_in, w_out, d_in, d_out) = adapters
    cosine, sine, allowed = tables
    tokens_here, width = hidden_state.shape
    head = pair_matrix.shape[1] // 2
    heads = query_matrix.shape[1] // head
    rank = q_in.shape[1]
    hidden = down_matrix.shape[0]
    kept = SimpleNamespace(h=hidden_state)
    normed, kept.mixer_factor = normalize(hidden_state, mixer_gain)
    normed = normed.astype(jnp.bfloat16)
    query_rank = product(normed, q_in).astype(jnp.bfloat16)
    query_linear = product(normed, query_matrix) + product(query_rank, q_out)
    pair_rank = product(normed, kv_in.reshape(width, 2 * rank)).astype(jnp.bfloat16)
    pair_linear = product(normed, pair_matrix) + jnp.concatenate(
        [product(pair_rank[:, :rank], kv_out[0]), product(pair_rank[:, rank:], kv_out[1])], axis=1
    )
    queries = rotate(
        query_linear.reshape(tokens_here, heads, head), cosine[:, None], sine[:, None]
    ).astype(jnp.bfloat16)
    keys = rotate(pair_linear[:, :head], cosine, sine).astype(jnp.bfloat16)
    values = pair_linear[:, head:].astype(jnp.bfloat16)
    masked = attention_probs(queries, keys, allowed, 1.0 / math.sqrt(head))
    expo = jnp.exp(masked - jnp.max(masked, axis=-1, keepdims=True))
    probs = expo / jnp.sum(expo, axis=-1, keepdims=True)
    mixed = jnp.einsum(
        "hij,jd->ihd", probs.astype(jnp.bfloat16), values, preferred_element_type=jnp.float32
    )
    mixed = mixed.reshape(tokens_here, heads * head).astype(jnp.bfloat16)
    summed, output_rank = total(identity, product(mixed, output_matrix), product(mixed, o_in))
    middle = hidden_state + summed + exact_product(output_rank, o_out.astype(jnp.float32))
    fed, kept.feed_factor = normalize(middle, feed_gain)
    fed = fed.astype(jnp.bfloat16)
    widen_rank = product(fed, w_in.reshape(width, 2 * rank)).astype(jnp.bfloat16)
    gate = product(fed, widen_matrix[:, 0]) + product(widen_rank[:, :rank], w_out[0])
    up = product(fed, widen_matrix[:, 1]) + product(widen_rank[:, rank:], w_out[1])
    activated = (gelu_tanh(gate) * up).astype(jnp.bfloat16)
    shrunk, shrink_rank = total(identity + 1, product(activated, down_matrix), product(activated, d_in))
    result = middle + shrunk + exact_product(shrink_rank, d_out.astype(jnp.float32))
    vars(kept).update(
        normed=normed, query_rank=query_rank, pair_rank=pair_rank, queries=queries, keys=keys,
        values=values, probs=probs, mixed=mixed, output_rank=output_rank, middle=middle, fed=fed,
        widen_rank=widen_rank, gate=gate, up=up, activated=activated, shrink_rank=shrink_rank,
    )
    return result, kept


def reverse_loop(upstream, kept, shared, adapters, tables, total, identity):
    (mixer_gain, feed_gain, query_matrix, pair_matrix, output_matrix, widen_matrix, down_matrix) = shared
    (q_in, q_out, kv_in, kv_out, o_in, o_out, w_in, w_out, d_in, d_out) = adapters
    cosine, sine, allowed = tables
    tokens_here, width = upstream.shape
    head = pair_matrix.shape[1] // 2
    heads = query_matrix.shape[1] // head
    rank = q_in.shape[1]
    scale = 1.0 / math.sqrt(head)
    grad_feed = upstream.astype(jnp.bfloat16)
    grad_shrink_rank = product_t(grad_feed, d_out).astype(jnp.bfloat16)
    grad_activated = product_t(grad_feed, down_matrix) + product_t(grad_shrink_rank, d_in)
    gelu_value, gelu_pullback = jax.vjp(gelu_tanh, kept.gate)
    grad_gate = gelu_pullback(grad_activated * kept.up)[0].astype(jnp.bfloat16)
    grad_up = (grad_activated * gelu_value).astype(jnp.bfloat16)
    grad_fed, grad_widen_rank = total(
        identity,
        product_t(grad_gate, widen_matrix[:, 0]) + product_t(grad_up, widen_matrix[:, 1]),
        jnp.concatenate([product_t(grad_gate, w_out[0]), product_t(grad_up, w_out[1])], axis=1),
    )
    grad_widen_rank = grad_widen_rank.astype(jnp.bfloat16)
    grad_fed = grad_fed + product_t(grad_widen_rank, w_in.reshape(width, 2 * rank))
    grad_norm, feed_gain_grad = normalize_back(kept.middle, kept.feed_factor, feed_gain, grad_fed)
    grad_middle = upstream + grad_norm
    grad_attend = grad_middle.astype(jnp.bfloat16)
    grad_output_rank = product_t(grad_attend, o_out).astype(jnp.bfloat16)
    grad_mixed = product_t(grad_attend, output_matrix) + product_t(grad_output_rank, o_in)
    grad_mixed = grad_mixed.astype(jnp.bfloat16).reshape(tokens_here, heads, head)
    queries, keys, values, probs = kept.queries, kept.keys, kept.values, kept.probs
    grad_probs = jnp.einsum("ihd,jd->hij", grad_mixed, values, preferred_element_type=jnp.float32)
    delta = jnp.sum(grad_probs * probs, axis=-1, keepdims=True)
    grad_scores = (probs * (grad_probs - delta)).astype(jnp.bfloat16)
    grad_queries = scale * jnp.einsum(
        "hij,jd->ihd", grad_scores, keys, preferred_element_type=jnp.float32
    )
    grad_keys = scale * jnp.einsum(
        "hij,ihd->jd", grad_scores, queries, preferred_element_type=jnp.float32
    )
    grad_values = jnp.einsum(
        "hij,ihd->jd", probs.astype(jnp.bfloat16), grad_mixed, preferred_element_type=jnp.float32
    )
    grad_query = rotate(grad_queries, cosine[:, None], -sine[:, None])
    grad_query = grad_query.reshape(tokens_here, heads * head).astype(jnp.bfloat16)
    grad_normed, grad_query_rank, grad_pair = total(
        identity + 1,
        product_t(grad_query, query_matrix),
        product_t(grad_query, q_out),
        jnp.concatenate([rotate(grad_keys, cosine, -sine), grad_values], axis=1),
    )
    grad_query_rank = grad_query_rank.astype(jnp.bfloat16)
    grad_pair = grad_pair.astype(jnp.bfloat16)
    grad_pair_rank = jnp.concatenate(
        [product_t(grad_pair[:, :head], kv_out[0]), product_t(grad_pair[:, head:], kv_out[1])], axis=1
    ).astype(jnp.bfloat16)
    grad_normed = (
        grad_normed
        + product_t(grad_query_rank, q_in)
        + product_t(grad_pair, pair_matrix)
        + product_t(grad_pair_rank, kv_in.reshape(width, 2 * rank))
    )
    grad_norm, mixer_gain_grad = normalize_back(
        kept.h, kept.mixer_factor, mixer_gain, grad_normed
    )
    vars(kept).update(
        grad_feed=grad_feed, grad_shrink_rank=grad_shrink_rank, grad_gate=grad_gate, grad_up=grad_up,
        grad_widen_rank=grad_widen_rank, grad_attend=grad_attend, grad_output_rank=grad_output_rank,
        grad_query=grad_query, grad_query_rank=grad_query_rank, grad_pair=grad_pair,
        grad_pair_rank=grad_pair_rank, feed_gain_grad=feed_gain_grad, mixer_gain_grad=mixer_gain_grad,
    )
    return grad_middle + grad_norm


def scattered_gradients(kept, dp_size, mp_size):
    def scatter(value, axis):
        return lax.psum_scatter(value, "dp", scatter_dimension=axis, tiled=True)

    def shared_of(factors):
        return sum(product_tn(*factors(k)) for k in kept)

    def each(function):
        return jnp.stack([function(k) for k in kept], axis=0)

    def quarter(value, axis):
        block = scatter(value, axis)
        size = block.shape[axis] // mp_size
        return lax.dynamic_slice_in_dim(block, lax.axis_index("mp") * size, size, axis)

    width = kept[0].normed.shape[1]
    rank = kept[0].query_rank.shape[1]
    head = kept[0].grad_pair.shape[1] // 2

    def pair_outer(k):
        left, right = k.pair_rank, k.grad_pair
        return jnp.stack(
            [product_tn(left[:, :rank], right[:, :head]), product_tn(left[:, rank:], right[:, head:])]
        )

    def expand_outer(k):
        left = k.widen_rank
        return jnp.stack(
            [product_tn(left[:, :rank], k.grad_gate), product_tn(left[:, rank:], k.grad_up)]
        )

    return (
        scatter(sum(k.mixer_gain_grad for k in kept), 0),
        scatter(sum(k.feed_gain_grad for k in kept), 0),
        scatter(shared_of(lambda k: (k.normed, k.grad_query)), 0),
        quarter(shared_of(lambda k: (k.normed, k.grad_pair)), 0),
        scatter(shared_of(lambda k: (k.mixed, k.grad_attend)), 1),
        scatter(jnp.stack([shared_of(lambda k: (k.fed, k.grad_gate)), shared_of(lambda k: (k.fed, k.grad_up))], axis=1), 0),
        scatter(shared_of(lambda k: (k.activated, k.grad_feed)), 1),
        quarter(each(lambda k: product_tn(k.normed, k.grad_query_rank)), 1),
        scatter(each(lambda k: product_tn(k.query_rank, k.grad_query)), 1),
        quarter(
            each(lambda k: product_tn(k.normed, k.grad_pair_rank).reshape(width, 2, rank)), 1
        ),
        quarter(each(pair_outer), 2),
        scatter(each(lambda k: product_tn(k.mixed, k.grad_output_rank)), 2),
        scatter(
            each(lambda k: exact_tn(k.output_rank, k.grad_attend.astype(jnp.float32))), 2
        ),
        quarter(
            each(lambda k: product_tn(k.fed, k.grad_widen_rank).reshape(width, 2, rank)), 1
        ),
        scatter(each(expand_outer), 2),
        scatter(each(lambda k: product_tn(k.activated, k.grad_shrink_rank)), 2),
        scatter(each(lambda k: exact_tn(k.shrink_rank, k.grad_feed.astype(jnp.float32))), 2),
    )


WIDE = 896


def split3(value):
    high = value.astype(jnp.bfloat16)
    rest = value - high.astype(jnp.float32)
    middle = rest.astype(jnp.bfloat16)
    low = (rest - middle.astype(jnp.float32)).astype(jnp.bfloat16)
    return high, middle, low


WEIGHTS = (
    "q_in", "query", "q_out", "kv_in", "pair", "kv_out", "output", "o_in", "o_out",
    "wide", "w_out", "down", "d_in", "d_out", "w_in",
)
SUM_STEP = 384


def block_kernel(*refs):
    (h_in, cot, segments, mixer_gain, feed_gain), refs = refs[:5], refs[5:]
    count = len(WEIGHTS)
    sources, refs = refs[:count], refs[count:]
    (
        out_ref, grad_ref, raw_ref, x_all, r_all, b_all, q_all, x_got, r_got, b_got, x_end, r_end, b_end,
    ), refs = refs[:13], refs[13:]
    weights, refs = (*refs[: count - 1], refs[WEIGHTS.index("kv_in")]), refs[count - 1 :]
    (
        h_s, mid_s, normed_s, qr_s, kvr_s, q_s, k_s, v_s, probs_s, mixed_s, or_s, fed_s, er_s,
        gate_s, up_s, act_s, sr_s, gg_s, gu_s, g_s, gain_s, select,
        part, total, near, mine, far, side_part, side_near, side_mine, side_far, side_total,
        late_s, er_grad_s, chosen_s, xs, rs, bs, qs, kv_flat, w_flat, cosine_ref, sine_ref, mask_ref,
        load_sems, c_s, c_r, y_s, y_r, e_s, e_r,
        xl, rl, bl, ql, x_s, x_r, r_s, r_r, b_s, b_r, xe_s, xe_r, re_s, re_r, be_s, be_r,
        sc_s, sc_r, sy_s, sy_r, se_s, se_r, xc_s, xc_r, rc_s, rc_r,
    ) = refs
    W = SimpleNamespace(**dict(zip(WEIGHTS, weights)))
    dp, mp = lax.axis_index("dp"), lax.axis_index("mp")
    side = lax.rem(mp, 2)
    core = (dp, mp + 1 - 2 * side)
    other = (dp, lax.rem(mp + 2, 4))
    loads = [
        pltpu.make_async_copy(source, target, load_sems.at[i])
        for i, (source, target) in enumerate(zip(sources, weights))
    ]
    load = SimpleNamespace(**dict(zip(WEIGHTS, loads)))
    for copy in loads[:-1]:
        copy.start()
    x = lax.rem(dp, 2)
    z = dp // 2
    pair = (dp + 1 - 2 * x, mp)
    near_end = (dp + 2 - 4 * lax.rem(z, 2), mp)
    is_end = jnp.logical_or(z == 0, z == 3)
    barrier = pltpu.get_barrier_semaphore()
    for device in (core, other, pair, near_end):
        pl.semaphore_signal(barrier, inc=1, device_id=device, device_id_type=MESH)
    pl.semaphore_wait(barrier, 4)

    tokens, width = h_in.shape
    half = tokens // 2
    head = W.query.shape[1]
    rank = W.q_in.shape[2]
    hidden = W.down.shape[0]
    loops = W.q_in.shape[0]
    scale = 1.0 / math.sqrt(head)
    own = pl.ds(pl.multiple_of(side * half, half), half)
    theirs = pl.ds(pl.multiple_of((1 - side) * half, half), half)
    blocks = x_all.shape[1] * x_all.shape[2]
    block = width // blocks
    quarter = block // 4
    rank_quarter = rank // (4 * blocks)
    chunks = [(0, WIDE), (WIDE, hidden - WIDE)]

    def remote(source, target, send, recv, device):
        return pltpu.make_async_remote_copy(
            source, target, send, recv, device_id=device, device_id_type=MESH
        )

    def span(l):
        return pl.ds(pl.multiple_of(l * tokens, tokens), tokens)

    def end_span(l, is_far):
        return pl.ds(pl.multiple_of((2 * l + is_far) * tokens, tokens), tokens)

    def x_copies(i, l):
        across = onward = None
        if i < 2:
            across = remote(
                xs.at[i, 1 - x], x_got.at[i, :, :, span(l)], x_s.at[i, l], x_r.at[i, l], pair
            )
        if i == 1:
            onward = remote(
                xs.at[i, x], x_end.at[:, :, end_span(l, 0)], xe_s.at[0, l], xe_r.at[0, l], near_end
            )
        return pltpu.make_async_copy(xs.at[i], x_all.at[i, :, :, :, span(l)], xl.at[i, l]), across, onward

    def r_copies(i, l):
        across = onward = None
        if i < 3:
            across = remote(
                rs.at[i, 1 - x], r_got.at[i, :, :, span(l)], r_s.at[i, l], r_r.at[i, l], pair
            )
        if i == 2:
            onward = remote(
                rs.at[i, x], r_end.at[:, :, end_span(l, 0)], re_s.at[0, l], re_r.at[0, l], near_end
            )
        return pltpu.make_async_copy(rs.at[i], r_all.at[i, :, :, :, span(l)], rl.at[i, l]), across, onward

    def b_copies(i, l):
        across = onward = None
        if i in (0, 4, 5):
            k = max(0, i - 3)
            across = remote(bs.at[i], b_got.at[k, span(l)], b_s.at[k, l], b_r.at[k, l], pair)
        if i >= 4:
            onward = remote(
                bs.at[i], b_end.at[i - 4, end_span(l, 0)],
                be_s.at[i - 4, 0, l], be_r.at[i - 4, 0, l], near_end,
            )
        return pltpu.make_async_copy(bs.at[i], b_all.at[i, span(l)], bl.at[i, l]), across, onward

    def q_copies(i, l):
        return pltpu.make_async_copy(qs.at[i], q_all.at[i, span(l)], ql.at[i, l]), None, None

    def launch(copies, whole=True):
        local, across, onward = copies
        local.start()
        if across is not None:
            across.start()
        if onward is not None:

            @pl.when(is_end if whole else jnp.logical_and(is_end, side == 0))
            def _():
                onward.start()

    def finish(copies, whole=True):
        local, across, onward = copies
        local.wait()
        if across is not None:
            across.wait_send()
        if onward is not None:

            @pl.when(is_end if whole else jnp.logical_and(is_end, side == 0))
            def _():
                onward.wait_send()

    def far_feed(l):
        return [
            remote(
                x_got.at[1, :, :, span(l)], x_end.at[:, :, end_span(l, 1)],
                xe_s.at[1, l], xe_r.at[1, l], near_end,
            ),
            remote(
                r_got.at[2, :, :, span(l)], r_end.at[:, :, end_span(l, 1)],
                re_s.at[1, l], re_r.at[1, l], near_end,
            ),
        ]

    def far_act(l):
        return [
            remote(
                b_got.at[1 + k, span(l)], b_end.at[k, end_span(l, 1)],
                be_s.at[k, 1, l], be_r.at[k, 1, l], near_end,
            )
            for k in range(2)
        ]

    def pass_act(l):
        for i in (4, 5):
            b_copies(i, l)[1].wait_recv()

        @pl.when(is_end)
        def _():
            for copy in far_act(l):
                copy.start()

    def pass_feed(l):
        x_copies(1, l)[1].wait_recv()
        r_copies(2, l)[1].wait_recv()

        @pl.when(jnp.logical_and(is_end, side == 1))
        def _():
            for copy in far_feed(l):
                copy.start()

    def ship_x(i, l, value, again, before):
        @pl.when(again)
        def _():
            finish(x_copies(i, before), False)

        turned = value.astype(jnp.float32).T
        for b in range(blocks):
            xs[i, b % 2, b // 2] = turned[b * block : (b + 1) * block]
        launch(x_copies(i, l), False)

    def ship_r(i, l, value, again, before):
        @pl.when(again)
        def _():
            finish(r_copies(i, before), False)

        turned = value.astype(jnp.float32).T
        size = rank // blocks
        for b in range(blocks):
            rs[i, b % 2, b // 2] = turned[b * size : (b + 1) * size]
        launch(r_copies(i, l), False)

    def ship_b(i, l, value, again, before):
        @pl.when(again)
        def _():
            finish(b_copies(i, before))

        n = value.shape[1]
        bs[i, :, :n] = value.astype(jnp.float32)
        if n < WIDE:
            bs[i, :, n:] = jnp.zeros((tokens, WIDE - n), jnp.float32)
        launch(b_copies(i, l))

    def ship_q(i, l, value, again, before):
        @pl.when(again)
        def _():
            finish(q_copies(i, before))

        qs[i] = value.astype(jnp.float32)
        launch(q_copies(i, l))

    def columns_of(size):
        return [(at, min(SUM_STEP, size - at)) for at in range(0, size, SUM_STEP)]

    def side_copies(turn, size):
        columns = pl.ds(0, size)
        return (
            remote(
                side_part.at[turn, theirs, columns], side_near.at[turn, :, columns],
                sc_s.at[turn], sc_r.at[turn], core,
            ),
            remote(
                side_mine.at[turn, :, columns], side_far.at[turn, :, columns],
                sy_s.at[turn], sy_r.at[turn], other,
            ),
            remote(
                side_total.at[turn, own, columns], side_total.at[turn, own, columns],
                se_s.at[turn], se_r.at[turn], core,
            ),
        )

    def finish_side(turn, size):
        first, second, third = side_copies(turn, size)
        second.wait_recv()
        side_total[turn, own, :size] = side_mine[turn, :, :size] + side_far[turn, :, :size]
        third.start()
        third.wait_recv()
        for copy in (first, second, third):
            copy.wait_send()
        return side_total[turn, :, :size]

    def sum_over_mp(fill, turn, side_size, finish_previous, idle):
        pieces = columns_of(width)

        def pieces_of(make):
            return [make(i, pl.ds(at, n)) for i, (at, n) in enumerate(pieces)]

        first = pieces_of(
            lambda i, c: remote(part.at[theirs, c], near.at[:, c], c_s.at[i], c_r.at[i], core)
        )
        second = pieces_of(
            lambda i, c: remote(
                mine.at[:, c], far.at[turn, :, c], y_s.at[turn, i], y_r.at[turn, i], other
            )
        )
        third = pieces_of(
            lambda i, c: remote(total.at[own, c], total.at[own, c], e_s.at[i], e_r.at[i], core)
        )
        side_first, side_second, _ = side_copies(turn, side_size)

        def middle(i):
            at, n = pieces[i]
            first[i].wait_recv()
            mine[:, at : at + n] = part[own, at : at + n] + near[:, at : at + n]
            second[i].start()

        for i, (at, n) in enumerate(pieces):
            fill(at, n)
            first[i].start()
            if i:
                middle(i - 1)
        side_first.start()
        middle(len(first) - 1)
        side_first.wait_recv()
        side_mine[turn, :, :side_size] = (
            side_part[turn, own, :side_size] + side_near[turn, :, :side_size]
        )
        finish_previous()
        side_second.start()
        idle()
        for i, (at, n) in enumerate(pieces):
            second[i].wait_recv()
            total[own, at : at + n] = mine[:, at : at + n] + far[turn, :, at : at + n]
            third[i].start()
        for copy in third:
            copy.wait_recv()
        for copy in first + second + third:
            copy.wait_send()

    def dot(left, right):
        return jnp.dot(left, right, preferred_element_type=jnp.float32)

    def low(value):
        return value.astype(jnp.bfloat16)

    def spin(value, sign):
        a, b = value[:, : head // 2], value[:, head // 2 :]
        cosine, sine = cosine_ref[...], sign * sine_ref[...]
        return jnp.concatenate([a * cosine - b * sine, b * cosine + a * sine], axis=1)

    def factor_of(value):
        return lax.rsqrt(jnp.mean(value * value, axis=-1, keepdims=True) + EPSILON)

    def gelu_parts(value):
        c = math.sqrt(2.0 / math.pi)
        square = value * value
        t = jnp.tanh(c * value * (1.0 + 0.044715 * square))
        gelu = 0.5 * value * (1.0 + t)
        slope = 0.5 * (1.0 + t) + 0.5 * value * (1.0 - t * t) * c * (1.0 + 3 * 0.044715 * square)
        return gelu, slope

    across_row = jnp.broadcast_to(segments[...].astype(jnp.float32), (tokens, tokens))
    down_row = across_row.T
    at_row = lax.broadcasted_iota(jnp.int32, (tokens, tokens), 0)
    at_column = lax.broadcasted_iota(jnp.int32, (tokens, tokens), 1)
    earlier = jnp.sum(jnp.where(across_row < down_row, 1.0, 0.0), axis=1, keepdims=True)
    position = at_row[:, : head // 2].astype(jnp.float32) - earlier
    exponent = at_column[:, : head // 2].astype(jnp.float32) * (-2.0 / head)
    angles = position * jnp.exp(exponent * math.log(10000.0))
    cosine_ref[...] = jnp.cos(angles)
    sine_ref[...] = jnp.sin(angles)
    mask_ref[...] = jnp.where(
        jnp.logical_and(across_row == down_row, at_row >= at_column), 1.0, 0.0
    )
    h_s[0] = h_in[...].astype(jnp.float32)
    mixer, feed = mixer_gain[...], feed_gain[...]

    def forward(l, carry):
        def need(*copies):
            @pl.when(l == 0)
            def _():
                for copy in copies:
                    copy.wait()

        h = h_s[l]
        normed = low(h * factor_of(h) * mixer)
        normed_s[l] = normed
        need(load.q_in, load.query, load.q_out, load.kv_in, load.pair, load.kv_out)

        @pl.when(l == 0)
        def _():
            kv_flat[0] = W.kv_in[0].reshape(width, 2 * rank)

        query_rank = low(dot(normed, W.q_in[l]))
        qr_s[l] = query_rank
        queries = dot(normed, W.query[...]) + dot(query_rank, W.q_out[l])
        q_s[l] = low(spin(queries, 1.0))
        pair_rank = low(dot(normed, kv_flat[l]))
        kvr_s[l] = pair_rank
        keys = dot(normed, W.pair[:, :head]) + dot(pair_rank[:, :rank], W.kv_out[l, 0])
        k_s[l] = low(spin(keys, 1.0))
        values = dot(normed, W.pair[:, head:]) + dot(pair_rank[:, rank:], W.kv_out[l, 1])
        v_s[l] = low(values)
        scores = product_t(q_s[l], k_s[l]) * scale
        scores = jnp.where(mask_ref[...] > 0, scores, MASKED)
        expo = jnp.exp(scores - jnp.max(scores, axis=-1, keepdims=True))
        probs = expo / jnp.sum(expo, axis=-1, keepdims=True)
        probs_s[l] = probs
        mixed = low(dot(low(probs), v_s[l]))
        mixed_s[l] = mixed
        need(load.output, load.o_in, load.o_out)

        output_rank = dot(mixed, W.o_in[l])
        side_part[0, :, :rank] = output_rank
        output_parts = split3(output_rank)

        def fill_attend(at, n):
            value = dot(mixed, W.output[:, at : at + n])
            for piece in output_parts:
                value = value + dot(piece, W.o_out[l, :, at : at + n])
            part[:, at : at + n] = value

        again = l > 0

        def idle_attend():
            ship_x(2, l, normed, again, 0)
            ship_r(3, l, query_rank, again, 0)
            ship_q(1, l, mixed, again, 0)

            @pl.when(l == 0)
            def _():
                for i in range(1, loops):
                    kv_flat[i] = W.kv_in[i].reshape(width, 2 * rank)
                load.w_in.start()
                load.w_in.wait()
                for i in range(loops):
                    w_flat[i] = W.w_in[i].reshape(width, 2 * rank)

            @pl.when(again)
            def _():
                pass_act(0)

        def finish_before_attend():
            @pl.when(again)
            def _():
                sr_s[jnp.maximum(l - 1, 0)] = finish_side(1, rank)

        sum_over_mp(fill_attend, 0, rank, finish_before_attend, idle_attend)
        middle = h_s[l] + total[...]
        mid_s[l] = middle
        fed = low(middle * factor_of(middle) * feed)
        fed_s[l] = fed
        need(load.wide, load.w_out)
        widen_rank = low(dot(fed, w_flat[l]))
        er_s[l] = widen_rank
        for at, n in chunks:
            gate = product_t(fed, W.wide[0, at : at + n]) + product_t(
                widen_rank[:, :rank], W.w_out[l, 0, at : at + n]
            )
            gate_s[l, :, at : at + n] = gate
            up = product_t(fed, W.wide[1, at : at + n]) + product_t(
                widen_rank[:, rank:], W.w_out[l, 1, at : at + n]
            )
            up_s[l, :, at : at + n] = up
            act_s[:, at : at + n] = low(gelu_parts(gate)[0] * up)
            ship_b(4 + at // WIDE, l, act_s[:, at : at + n], again, 0)
        need(load.down, load.d_in, load.d_out)

        shrink_rank = dot(act_s[...], W.d_in[l])
        side_part[1, :, :rank] = shrink_rank
        shrink_parts = split3(shrink_rank)

        def fill_feed(at, n):
            value = dot(act_s[...], W.down[:, at : at + n])
            for piece in shrink_parts:
                value = value + dot(piece, W.d_out[l, :, at : at + n])
            part[:, at : at + n] = value

        def idle_feed():
            ship_x(0, l, fed, again, 0)
            ship_r(0, l, widen_rank[:, :rank], again, 0)
            ship_r(1, l, widen_rank[:, rank:], again, 0)

        def finish_before_feed():
            or_s[l] = finish_side(0, rank)

        sum_over_mp(fill_feed, 1, rank, finish_before_feed, idle_feed)
        h_s[l + 1] = mid_s[l] + total[...]
        return carry

    lax.fori_loop(0, loops, forward, 0)
    out_ref[...] = low(h_s[loops])

    g_s[...] = cot[...].astype(jnp.float32)
    gain_s[...] = jnp.zeros_like(gain_s)
    padded_quarter = select.shape[0] // blocks
    row = lax.broadcasted_iota(jnp.int32, (padded_quarter, width), 0)
    column = lax.broadcasted_iota(jnp.int32, (padded_quarter, width), 1)
    for b in range(blocks):
        hit = jnp.logical_and(column == row + (b * 4 + mp) * quarter, row < quarter)
        select[b * padded_quarter : (b + 1) * padded_quarter] = low(
            jnp.where(hit, 1.0, 0.0)
        )
    small_row = lax.broadcasted_iota(jnp.int32, (rank_quarter, rank), 0)
    small_column = lax.broadcasted_iota(jnp.int32, (rank_quarter, rank), 1)
    rank_select = low(
        jnp.concatenate(
            [
                jnp.where(small_column == small_row + (b * 4 + mp) * rank_quarter, 1.0, 0.0)
                for b in range(blocks)
            ],
            axis=0,
        )
    )
    raw_rows = raw_layout(quarter, rank_quarter, loops)

    tall = raw_rows.tall

    def put(start, size, stride, value, add=False):
        for b in range(blocks):
            piece = value[b * stride : b * stride + size]
            if add:
                raw_ref[b % 2, b // 2, start : start + size] += piece
            else:
                raw_ref[b % 2, b // 2, start : start + size] = piece

    def pair_ranks(l, grad_keys, grad_values):
        return low(
            jnp.concatenate(
                [product_t(grad_keys, W.kv_out[l, 0]), product_t(grad_values, W.kv_out[l, 1])], axis=1
            )
        )

    def raw_of(l):
        grad_rank = late_s[l, :, :rank]
        grad_pair = late_s[l, :, rank:]
        grad_pair_rank = pair_ranks(l, grad_pair[:, :head], grad_pair[:, head:])
        grad_widen = er_grad_s[l]
        normed_own = low(product_t(select[...], normed_s[l]))
        pair_weight = dot(normed_own, grad_pair)
        for j in range(2):
            value = pair_weight[:, j * head : (j + 1) * head]
            put(j * tall, tall, padded_quarter, value, l < loops - 1)
        base = 2 * tall + l * raw_rows.loop

        def put_loop(i, value):
            put(base + i * tall, tall, padded_quarter, value)

        put_loop(0, dot(normed_own, grad_rank))
        for j in range(2):
            put_loop(1 + j, dot(normed_own, grad_pair_rank[:, j * rank : (j + 1) * rank]))
        fed_own = low(product_t(select[...], fed_s[l]))
        for j in range(2):
            put_loop(3 + j, dot(fed_own, grad_widen[:, j * rank : (j + 1) * rank]))
        put_loop(5, sum(dot(chosen_s[l, 1], piece) for piece in split3(or_s[l])))
        put_loop(6, sum(dot(chosen_s[l, 0], piece) for piece in split3(sr_s[l])))
        for j in range(2):
            rank_own = low(product_t(rank_select, kvr_s[l, :, j * rank : (j + 1) * rank]))
            put(
                base + 7 * tall + j * rank_quarter, rank_quarter, rank_quarter,
                dot(rank_own, grad_pair[:, j * head : (j + 1) * head]),
            )

    def back(step, carry):
        l = loops - 1 - step
        again = step > 0
        before = loops - 1

        upstream = g_s[...]
        grad_feed = low(upstream)
        grad_shrink = low(product_t(grad_feed, W.d_out[l]))
        for i, (at, n) in enumerate(chunks):
            grad_act = product_t(grad_feed, W.down[at : at + n]) + product_t(
                grad_shrink, W.d_in[l, at : at + n]
            )
            gelu, slope = gelu_parts(gate_s[l, :, at : at + n])
            grad_gate = low(grad_act * up_s[l, :, at : at + n] * slope)
            grad_up = low(grad_act * gelu)
            gg_s[:, at : at + n] = grad_gate
            gu_s[:, at : at + n] = grad_up
            ship_b(i, l, grad_gate, again, before)
            ship_b(2 + i, l, grad_up, again, before)

        for j, value in enumerate((gg_s, gu_s)):
            side_part[0, :, j * rank : (j + 1) * rank] = dot(value[...], W.w_out[l, j])
        grad_widen = low(side_part[0, :, : 2 * rank])

        def fill_fed(at, n):
            part[:, at : at + n] = (
                dot(gg_s[...], W.wide[0, :, at : at + n])
                + dot(gu_s[...], W.wide[1, :, at : at + n])
                + product_t(grad_widen, w_flat[l, at : at + n])
            )

        def finish_before_fed():
            @pl.when(step == 0)
            def _():
                sr_s[loops - 1] = finish_side(1, rank)

            @pl.when(again)
            def _():
                late_s[loops - 1] = low(finish_side(1, rank + 2 * head))

        def idle_fed():
            ship_x(1, l, grad_feed, again, before)
            ship_r(2, l, grad_shrink, again, before)
            chosen_s[l, 0] = low(product_t(select[...], grad_feed))

            @pl.when(again)
            def _():
                raw_of(loops - 1)

        sum_over_mp(fill_fed, 0, 2 * rank, finish_before_fed, idle_fed)
        grad_fed = total[...]
        middle = mid_s[l]
        factor = factor_of(middle)
        unit = middle * factor
        scaled = grad_fed * feed
        grad_middle = upstream + factor * (
            scaled - unit * jnp.mean(scaled * unit, axis=-1, keepdims=True)
        )
        gain_s[1:2] += jnp.sum(grad_fed * unit, axis=0, keepdims=True)
        g_s[...] = grad_middle
        grad_attend = low(grad_middle)
        grad_output = low(product_t(grad_attend, W.o_out[l]))
        grad_mixed = low(
            product_t(grad_attend, W.output[...]) + product_t(grad_output, W.o_in[l])
        )
        probs = probs_s[l]
        grad_probs = product_t(grad_mixed, v_s[l])
        delta = jnp.sum(grad_probs * probs, axis=-1, keepdims=True)
        grad_scores = low(probs * (grad_probs - delta))
        grad_query = low(spin(dot(grad_scores, k_s[l]) * scale, -1.0))

        grad_rank = product_t(grad_query, W.q_out[l])
        grad_keys = spin(product_tn(grad_scores, q_s[l]) * scale, -1.0)
        grad_values = product_tn(low(probs), grad_mixed)
        side_part[1, :, :rank] = grad_rank
        side_part[1, :, rank : rank + head] = grad_keys
        side_part[1, :, rank + head :] = grad_values
        grad_rank, grad_keys, grad_values = low(grad_rank), low(grad_keys), low(grad_values)
        grad_pair = jnp.concatenate([grad_keys, grad_values], axis=1)
        grad_pair_rank = pair_ranks(l, grad_keys, grad_values)

        def fill_normed(at, n):
            part[:, at : at + n] = (
                product_t(grad_query, W.query[at : at + n])
                + product_t(grad_rank, W.q_in[l, at : at + n])
                + product_t(grad_pair, W.pair[at : at + n])
                + product_t(grad_pair_rank, kv_flat[l, at : at + n])
            )

        def finish_before_normed():
            er_grad_s[l] = low(finish_side(0, 2 * rank))

        def idle_normed():
            ship_q(0, l, grad_query, again, before)
            ship_x(3, l, grad_attend, again, before)
            ship_r(4, l, grad_output, again, before)
            chosen_s[l, 1] = low(product_t(select[...], grad_attend))

            @pl.when(step == 0)
            def _():
                pass_act(loops - 1)

            pass_feed(l)

        sum_over_mp(fill_normed, 1, rank + 2 * head, finish_before_normed, idle_normed)
        grad_normed = total[...]
        h = h_s[l]
        factor = factor_of(h)
        unit = h * factor
        scaled = grad_normed * mixer
        g_s[...] += factor * (scaled - unit * jnp.mean(scaled * unit, axis=-1, keepdims=True))
        gain_s[0:1] += jnp.sum(grad_normed * unit, axis=0, keepdims=True)

        return carry

    lax.fori_loop(0, loops, back, 0)
    late_s[0] = low(finish_side(1, rank + 2 * head))
    raw_of(0)
    grad_ref[...] = g_s[...]
    for b in range(blocks):
        ends = jnp.zeros((8, head), jnp.float32)
        raw_ref[b % 2, b // 2, raw_rows.gains :] = ends
        raw_ref[b % 2, b // 2, raw_rows.gains : raw_rows.gains + 2, :block] = gain_s[
            :2, b * block : (b + 1) * block
        ]
    last = loops - 1
    for copies in (
        x_copies(0, last), x_copies(2, last), r_copies(0, last), r_copies(1, last), r_copies(3, last),
        q_copies(1, last), x_copies(1, 0), x_copies(3, 0), r_copies(2, 0), r_copies(4, 0),
        q_copies(0, 0),
    ):
        finish(copies, False)
    for copies in (
        b_copies(4, last), b_copies(5, last), b_copies(0, 0), b_copies(1, 0), b_copies(2, 0),
        b_copies(3, 0),
    ):
        finish(copies)

    def to_core(l, half):
        lanes = end_span(l, half)
        return [
            remote(x_end.at[:, :, lanes], x_end.at[:, :, lanes], xc_s.at[l], xc_r.at[l], core),
            remote(r_end.at[:, :, lanes], r_end.at[:, :, lanes], rc_s.at[l], rc_r.at[l], core),
        ]

    for l in range(loops):
        for copies in (x_copies(0, l), r_copies(0, l), r_copies(1, l), b_copies(0, l)):
            copies[1].wait_recv()

        @pl.when(is_end)
        def _():
            for copy in far_act(l):
                copy.wait_send()

        @pl.when(jnp.logical_and(is_end, side == 1))
        def _():
            for copy in far_feed(l):
                copy.wait_send()

        for half in range(2):

            @pl.when(jnp.logical_and(jnp.logical_not(is_end), side == half))
            def _():
                came = far_feed(l) if half else [x_copies(1, l)[2], r_copies(2, l)[2]]
                for copy, onward in zip(came, to_core(l, half)):
                    copy.wait_recv()
                    onward.start()

    @pl.when(jnp.logical_not(is_end))
    def _():
        for l in range(loops):
            for copy in [b_copies(4, l)[2], b_copies(5, l)[2]] + far_act(l):
                copy.wait_recv()
            for copy in to_core(l, 0):
                copy.wait_send()
                copy.wait_recv()


def raw_layout(quarter, rank_quarter, loops):
    tall = -(-quarter // 8) * 8
    loop = 7 * tall + 2 * rank_quarter
    gains = 2 * tall + loops * loop
    return SimpleNamespace(tall=tall, loop=loop, gains=gains, all=gains + 8)


def block_and_factors(block_input, cotangent, segments, shared, stacked, dp_size):
    (mixer_gain, feed_gain, query, pair, output, widen, down) = shared
    (q_in, q_out, kv_in, kv_out, o_in, o_out, w_in, w_out, d_in, d_out) = stacked
    tokens, width = block_input.shape
    head = query.shape[1]
    loops, _, rank = q_in.shape
    hidden = down.shape[0]
    weights = (
        q_in, query, q_out, kv_in, pair, kv_out, output, o_in, o_out,
        widen.transpose(1, 2, 0), w_out.swapaxes(2, 3), down, d_in, d_out, w_in,
    )
    layout = raw_layout(width // (4 * dp_size), rank // (4 * dp_size), loops)
    line = dp_size // 2
    f32, bf16 = jnp.float32, jnp.bfloat16
    shape = jax.ShapeDtypeStruct
    block, rank_block, both = width // dp_size, rank // dp_size, loops * tokens
    out_shape = (
        shape((tokens, width), bf16),
        shape((tokens, width), f32),
        shape((2, line, layout.all, head), f32),
        shape((4, 2, line, block, both), f32),
        shape((5, 2, line, rank_block, both), f32),
        shape((6, both, WIDE), f32),
        shape((2, both, head), f32),
        shape((2, line, block, both), f32),
        shape((3, line, rank_block, both), f32),
        shape((3, both, WIDE), f32),
        shape((line, block, 2 * both), f32),
        shape((line, rank_block, 2 * both), f32),
        shape((2, 2 * both, WIDE), f32),
    )
    vmem = pl.BlockSpec(memory_space=pltpu.VMEM)
    hbm = pl.BlockSpec(memory_space=pl.ANY)
    widest = rank + 2 * head
    pieces = -(-width // SUM_STEP)
    dma = pltpu.SemaphoreType.DMA

    def kept(columns, dtype, count=loops):
        return pltpu.VMEM((count, tokens, columns), dtype)

    scratch = [pltpu.VMEM(w.shape, bf16) for w in weights[:-1]] + [
        kept(width, f32, loops + 1), kept(width, f32), kept(width, bf16), kept(rank, bf16),
        kept(2 * rank, bf16), kept(head, bf16), kept(head, bf16), kept(head, bf16), kept(tokens, f32),
        kept(head, bf16), kept(rank, f32), kept(width, bf16), kept(2 * rank, bf16),
        kept(hidden, f32), kept(hidden, f32), pltpu.VMEM((tokens, hidden), bf16), kept(rank, f32),
        pltpu.VMEM((tokens, hidden), bf16), pltpu.VMEM((tokens, hidden), bf16),
        pltpu.VMEM((tokens, width), f32), pltpu.VMEM((8, width), f32),
        pltpu.VMEM((dp_size * 48, width), bf16),
        pltpu.VMEM((tokens, width), f32), pltpu.VMEM((tokens, width), f32),
        pltpu.VMEM((tokens // 2, width), f32), pltpu.VMEM((tokens // 2, width), f32),
        pltpu.VMEM((2, tokens // 2, width), f32),
        pltpu.VMEM((2, tokens, widest), f32), pltpu.VMEM((2, tokens // 2, widest), f32),
        pltpu.VMEM((2, tokens // 2, widest), f32), pltpu.VMEM((2, tokens // 2, widest), f32),
        pltpu.VMEM((2, tokens, widest), f32),
        kept(widest, bf16), kept(2 * rank, bf16), pltpu.VMEM((loops, 2, dp_size * 48, tokens), bf16),
        pltpu.VMEM((4, 2, line, block, tokens), f32), pltpu.VMEM((5, 2, line, rank_block, tokens), f32),
        pltpu.VMEM((6, tokens, WIDE), f32), pltpu.VMEM((2, tokens, head), f32),
        pltpu.VMEM((loops, width, 2 * rank), bf16), pltpu.VMEM((loops, width, 2 * rank), bf16),
        pltpu.VMEM((tokens, head // 2), f32), pltpu.VMEM((tokens, head // 2), f32),
        pltpu.VMEM((tokens, tokens), f32),
        dma((len(weights),)), dma((pieces,)), dma((pieces,)), dma((2, pieces)), dma((2, pieces)),
        dma((pieces,)), dma((pieces,)),
        dma((4, loops)), dma((5, loops)), dma((6, loops)), dma((2, loops)),
    ]
    scratch += [dma((2, loops))] * 2 + [dma((3, loops))] * 4
    scratch += [dma((2, loops))] * 4 + [dma((2, 2, loops))] * 2
    scratch += [dma((2,))] * 6 + [dma((loops,))] * 4
    return pl.pallas_call(
        block_kernel,
        out_shape=out_shape,
        in_specs=[vmem] * 5 + [hbm] * len(weights),
        out_specs=(vmem,) * 3 + (hbm,) * 10,
        scratch_shapes=scratch,
        compiler_params=pltpu.CompilerParams(
            collective_id=21, has_side_effects=True, vmem_limit_bytes=63 << 20
        ),
    )(
        block_input, cotangent, segments, mixer_gain[None], feed_gain[None],
        *weights,
    )


def line_kernel(
    raw_all, x_all, r_all, b_all, q_all, x_got, r_got, b_got, x_end_all, r_end_all, b_end_all,
    gains_out, q_w, pair_w, o_w, e_w, s_w, q_i, q_o, p_i, p_o, o_i, o_o, e_i, e_o, s_i, s_o,
    main_out, side_out, raw_out, around,
    x_own, r_own, b_own, q_own, x_far, r_far, b_far, q_far, x_end, r_end, b_end, raw_own, raw_far, product_ref,
    main_right, main_left, side_right, side_left, raw_right, raw_left,
    x_s, x_r, r_s, r_r, b_s, b_r, q_s, q_r, w_s, w_r, local_sems, step_sems, around_s, around_r,
    mr_s, mr_r, ml_s, ml_r, sr_s, sr_r, sl_s, sl_r, rr_s, rr_r, rl_s, rl_r,
    credit_right, credit_left,
):
    dp, mp = lax.axis_index("dp"), lax.axis_index("mp")
    x = lax.rem(dp, 2)
    z = dp // 2
    last = 3
    pair = (dp + 1 - 2 * x, mp)
    up, down = (dp + 2, mp), (dp - 2, mp)

    core, other = (dp, mp + 1 - 2 * lax.rem(mp, 2)), (dp, lax.rem(mp + 2, 4))
    hidden = s_w.shape[1]
    block, rank_block, quarter = s_w.shape[0], s_i.shape[1], pair_w.shape[0]
    loops, head = s_i.shape[0], q_w.shape[1]
    layout = raw_layout(quarter, rank_block // 4, loops)
    tall = layout.tall

    barrier = pltpu.get_barrier_semaphore()
    for device in (pair, core, other):
        pl.semaphore_signal(barrier, inc=1, device_id=device, device_id_type=MESH)

    @pl.when(z > 0)
    def _():
        pl.semaphore_signal(barrier, inc=1, device_id=down, device_id_type=MESH)

    @pl.when(z < last)
    def _():
        pl.semaphore_signal(barrier, inc=1, device_id=up, device_id_type=MESH)

    pl.semaphore_wait(barrier, 3 + jnp.minimum(z, 1) + jnp.minimum(last - z, 1))

    def across(source, target, send, recv):
        return pltpu.make_async_remote_copy(
            source, target, send, recv, device_id=pair, device_id_type=MESH
        )

    def x_copy(i):
        return across(x_all.at[i, 1 - x], x_far.at[i], x_s.at[i - 2], x_r.at[i - 2])

    def r_copy(i):
        return across(r_all.at[i, 1 - x], r_far.at[i], r_s.at[i - 3], r_r.at[i - 3])

    def b_copy(i):
        return across(b_all.at[i], b_far.at[i], b_s.at[i], b_r.at[i])

    q_copy = across(q_all, q_far, q_s, q_r)
    w_copy = across(raw_all.at[1 - x], raw_far, w_s, w_r)

    def here(source, target, i):
        return pltpu.make_async_copy(source, target, local_sems.at[i])

    at_start = [
        here(x_all.at[:, x], x_own, 0),
        here(r_all.at[:, x], r_own, 1),
        here(x_got, x_far.at[0:2], 2),
        here(r_got, r_far.at[0:3], 3),
        here(b_got.at[0], b_far.at[0], 4),
        here(b_got.at[1:3], b_far.at[4:6], 5),
        here(q_all, q_own, 6),
    ]
    for_ends = [here(x_end_all, x_end, 7), here(r_end_all, r_end, 8), here(b_end_all, b_end, 9)]
    own_copy = here(raw_all.at[x], raw_own, 10)
    inner = jnp.logical_and(z > 0, z < last)

    def chunk_of(step):
        return jnp.where(lax.rem(step, 3) == 1, 4 + step // 3, step - (step + 1) // 3)

    def b_load(step):
        slot = lax.rem(step, 2)
        return pltpu.make_async_copy(b_all.at[chunk_of(step)], b_own.at[slot], step_sems.at[slot])

    b_copy(1).start()
    b_load(0).start()
    for copy in at_start:
        copy.start()

    @pl.when(inner)
    def _():
        for copy in for_ends:
            copy.start()

    own_copy.start()
    for copy in at_start:
        copy.wait()

    @pl.when(inner)
    def _():
        for copy in for_ends:
            copy.wait()

    def chain(target, step, slot, steps, value, out, right, left, r_s, r_r, l_s, l_r, credits):
        def move(buffer, send, recv, i, s, device):
            return pltpu.make_async_remote_copy(
                buffer.at[i, s], buffer.at[i, s], send.at[i, s], recv.at[i, s],
                device_id=device, device_id_type=MESH,
            )

        def inside(at):
            return lax.rem(at, 3) == 1 if credits else at < 0

        def free(credit, i, source, at, from_end):
            @pl.when(
                jnp.logical_and(
                    at <= steps - 1,
                    jnp.logical_not(jnp.logical_and(from_end, inside(at))),
                )
            )
            def _():
                pl.semaphore_signal(credit.at[i], inc=1, device_id=source, device_id_type=MESH)

        def pass_on(i, place, buffer, send, recv, onward, source, at_end, next_to_end, credit):
            def here(i, s):
                return move(buffer, send, recv, i, s, onward)

            def begin():
                if credits:

                    @pl.when(step >= 3)
                    def _():
                        pl.semaphore_wait(credit.at[i], 1)

                here(i, slot).start()

            @pl.when(jnp.logical_and(at_end, jnp.logical_not(inside(step))))
            def _():
                buffer[i, slot] = value()
                if credits:
                    before = lax.rem(step + 2 - inside(step - 1).astype(jnp.int32), 3)
                    after = jnp.where(onward[0] > dp, i - 1, i + 1)

                    @pl.when(jnp.logical_and(place < 2, step >= 1))
                    def _():
                        here(after, before).wait_send()

                    @pl.when(place == 2)
                    def _():
                        here(2 - i, slot).wait_send()

                    begin()
                else:
                    begin()
                    here(i, slot).wait_send()

            @pl.when(jnp.logical_not(at_end))
            def _():
                if credits:

                    @pl.when(step >= 1)
                    def _():
                        here(i, lax.rem(step + 2, 3)).wait_send()
                        free(credit, i, source, step + 2, next_to_end)

                has_source = jnp.logical_not(jnp.logical_and(next_to_end, inside(step)))

                @pl.when(jnp.logical_not(has_source))
                def _():
                    buffer[i, slot] = value()

                @pl.when(has_source)
                def _():
                    product = value()
                    here(i, slot).wait_recv()
                    buffer[i, slot] += product

                begin()

        @pl.when(target > z)
        def _():
            pass_on(target - 1, 3 - target, right, r_s, r_r, up, down, z == 0, z == 1, credit_right)

        @pl.when(target < z)
        def _():
            pass_on(target, target, left, l_s, l_r, down, up, z == last, z == last - 1, credit_left)

        @pl.when(target == z)
        def _():
            out[...] = value()

    def arrive(step, slot, steps, out, right, left, r_s, r_r, l_s, l_r, credits):
        def came(buffer, send, recv, i):
            return pltpu.make_async_remote_copy(
                buffer.at[i, slot], buffer.at[i, slot], send.at[i, slot], recv.at[i, slot],
                device_id=pair, device_id_type=MESH,
            )

        started_inside = lax.rem(step, 3) == 1 if credits else step < 0

        def side_of(there, from_end, buffer, send, recv, i, credit, source):
            @pl.when(there)
            def _():
                quiet = jnp.logical_and(from_end, started_inside)

                @pl.when(jnp.logical_not(quiet))
                def _():
                    came(buffer, send, recv, i).wait_recv()
                    out[...] += buffer[i, slot]

                if credits:
                    skip = jnp.logical_and(from_end, lax.rem(step + 3, 3) == 1)

                    @pl.when(jnp.logical_and(step + 3 <= steps - 1, jnp.logical_not(skip)))
                    def _():
                        pl.semaphore_signal(
                            credit.at[i], inc=1, device_id=source, device_id_type=MESH
                        )

        side_of(z > 0, z == 1, right, r_s, r_r, jnp.maximum(z - 1, 0), credit_right, down)
        side_of(z < last, z == last - 1, left, l_s, l_r, jnp.minimum(z, last - 1), credit_left, up)

    def settle(slot, right, left, r_s, l_s, main):
        def wait(buffer, send, i, device):
            pltpu.make_async_remote_copy(
                buffer.at[i, slot], buffer.at[i, slot], send.at[i, slot], send.at[i, slot],
                device_id=device, device_id_type=MESH,
            ).wait_send()

        for target in range(4):
            rightmost, leftmost = target == 3, target == 0

            @pl.when(jnp.logical_and(target > z, jnp.logical_or(z > 0, main and not rightmost)))
            def _():
                wait(right, r_s, target - 1, up)

            @pl.when(jnp.logical_and(target < z, jnp.logical_or(z < last, main and not leftmost)))
            def _():
                wait(left, l_s, target, down)

    def order(turn):
        def near(end):
            return jnp.where(end == 0, 3 - turn, jnp.where(turn < 2, 3 - turn, turn - 2))

        return jnp.where(z < 2, near(z), 3 - near(3 - z))

    def dot(left, right):
        return jnp.dot(
            left.astype(jnp.bfloat16), right.astype(jnp.bfloat16), preferred_element_type=jnp.float32
        )

    steps = b_all.shape[0]

    def left_times(x_index, group, target, own, far):
        half = own.shape[0] // 2
        rank_own, rank_far = r_own[group, target], r_far[group, target]
        return [
            dot(x_own[x_index, target], own) + dot(x_far[x_index, target], far),
            dot(rank_own[:, :half], own[:half]) + dot(rank_far[:, :half], far[:half]),
            dot(rank_own[:, half:], own[half:]) + dot(rank_far[:, half:], far[half:]),
        ]

    def main_arrive(step):
        slot = lax.rem(step, 3)
        chunk = chunk_of(step)
        arrive(
            step, slot, steps, main_out.at[slot], main_right, main_left, mr_s, mr_r, ml_s, ml_r, True,
        )
        for part, (at, n) in enumerate(((0, WIDE), (WIDE, hidden - WIDE))):
            for j in range(2):

                @pl.when(chunk == 2 * j + part)
                def _():
                    e_w[:, j, at : at + n] = main_out[slot, :block, :n]
                    for l in range(loops):
                        start = block + l * rank_block
                        e_o[l, j, :, at : at + n] = main_out[slot, start : start + rank_block, :n]

            @pl.when(chunk == 4 + part)
            def _():
                s_w[:, at : at + n] = main_out[slot, :block, :n]
                for l in range(loops):
                    start = block + l * rank_block
                    s_i[l, :, at : at + n] = main_out[slot, start : start + rank_block, :n]

    def turn_body(at, carry):
        step, turn = at // 4, lax.rem(at, 4)
        slot = lax.rem(step, 3)
        chunk = chunk_of(step)
        group = chunk // 2
        target = order(turn)

        @pl.when(turn == 0)
        def _():
            b_load(step).wait()

            @pl.when(step < steps - 1)
            def _():
                b_load(step + 1).start()

            @pl.when(jnp.logical_and(chunk >= 1, chunk <= 3))
            def _():
                b_copy(chunk).wait_recv()

            @pl.when(step == 1)
            def _():
                b_copy(2).start()

            @pl.when(step == 2)
            def _():
                b_copy(3).start()

            @pl.when(step == 3)
            def _():
                w_copy.start()

            @pl.when(step == 4)
            def _():
                x_copy(2).start()
                x_copy(3).start()
                r_copy(3).start()
                r_copy(4).start()
                q_copy.start()

        def value():
            parts = left_times(
                group // 2, group, target,
                b_own[lax.rem(step, 2)].astype(jnp.bfloat16), b_far[chunk].astype(jnp.bfloat16),
            )
            product_ref[...] = jnp.concatenate(parts, axis=0)
            beyond = jnp.logical_or(
                jnp.logical_and(z == 1, target >= 1),
                jnp.logical_and(z == last - 1, target <= last - 1),
            )

            @pl.when(jnp.logical_and(beyond, chunk >= 4))
            def _():
                end = b_end[jnp.maximum(chunk - 4, 0)].astype(jnp.bfloat16)
                middle = end.shape[0] // 2
                product_ref[...] += jnp.concatenate(
                    [
                        dot(x_end[target], end),
                        dot(r_end[target, :, :middle], end[:middle]),
                        dot(r_end[target, :, middle:], end[middle:]),
                    ],
                    axis=0,
                )

            return product_ref[...]

        chain(
            target, step, slot, steps, value, main_out.at[slot], main_right, main_left,
            mr_s, mr_r, ml_s, ml_r, True,
        )

        @pl.when(jnp.logical_and(turn == 3, step >= 2))
        def _():
            main_arrive(step - 2)

        return carry

    lax.fori_loop(0, 4 * steps, turn_body, 0)

    w_copy.wait_recv()
    own_copy.wait()

    def raw_body(turn, carry):
        target = order(turn)
        chain(
            target, 0, 0, 1, lambda: raw_own[target] + raw_far[target], raw_out, raw_right, raw_left,
            rr_s, rr_r, rl_s, rl_r, False,
        )
        return carry

    lax.fori_loop(0, 4, raw_body, 0)
    main_arrive(jnp.int32(steps - 2))

    for i in (2, 3):
        x_copy(i).wait_recv()
    for i in (3, 4):
        r_copy(i).wait_recv()
    q_copy.wait_recv()

    def side_body(turn, carry):
        target = order(turn)

        def value():
            parts = [
                left_times(
                    2 + i, 3 + i, target, q_own[i].astype(jnp.bfloat16), q_far[i].astype(jnp.bfloat16)
                )
                for i in range(2)
            ]
            return jnp.concatenate([jnp.concatenate(p, axis=0) for p in parts], axis=1)

        chain(
            target, 0, 0, 1, value, side_out, side_right, side_left,
            sr_s, sr_r, sl_s, sl_r, False,
        )
        return carry

    lax.fori_loop(0, 4, side_body, 0)
    main_arrive(jnp.int32(steps - 1))
    arrive(0, 0, 1, raw_out, raw_right, raw_left, rr_s, rr_r, rl_s, rl_r, False)

    def share(device, owner, i):
        return pltpu.make_async_remote_copy(
            around.at[owner], around.at[owner], around_s.at[i], around_r.at[i],
            device_id=device, device_id_type=MESH,
        )

    far_owner = lax.rem(mp + 2, 4)
    for l in range(loops):
        start = 2 * tall + l * layout.loop + 5 * tall
        around[mp, l] = raw_out[start : start + 2 * tall]
    along, same, passed = share(other, mp, 0), share(core, mp, 1), share(core, far_owner, 2)
    along.start()
    same.start()
    arrive(0, 0, 1, side_out, side_right, side_left, sr_s, sr_r, sl_s, sl_r, False)
    along.wait_recv()
    passed.start()
    q_w[...] = side_out[:block, :head]
    o_w[...] = side_out[:block, head:]
    for l in range(loops):
        start = block + l * rank_block
        q_o[l] = side_out[start : start + rank_block, :head]
        o_i[l] = side_out[start : start + rank_block, head:]
    gains_out[...] = raw_out[layout.gains : layout.gains + 2, :block]
    for j in range(2):
        pair_w[:, j * head : (j + 1) * head] = raw_out[j * tall : j * tall + quarter]
    for l in range(loops):
        base = 2 * tall + l * layout.loop
        q_i[:, l] = raw_out[base : base + quarter]
        for j in range(2):
            start = base + (1 + j) * tall
            p_i[l, :, j] = raw_out[start : start + quarter]
            e_i[l, :, j] = raw_out[start + 2 * tall : start + 2 * tall + quarter]
            start = base + 7 * tall + j * (rank_block // 4)
            p_o[l, j] = raw_out[start : start + rank_block // 4]
    same.wait_recv()
    passed.wait_recv()
    for l in range(loops):
        for m in range(4):
            o_o[l, m * quarter : (m + 1) * quarter] = around[m, l, :quarter]
            s_o[l, m * quarter : (m + 1) * quarter] = around[m, l, tall : tall + quarter]
    for copy in (along, same, passed):
        copy.wait_send()

    settle((steps - 1) % 3, main_right, main_left, mr_s, ml_s, True)
    settle(0, side_right, side_left, sr_s, sl_s, False)
    settle(0, raw_right, raw_left, rr_s, rl_s, False)
    for copy in (x_copy(2), x_copy(3), r_copy(3), r_copy(4), b_copy(1), b_copy(2), b_copy(3)):
        copy.wait_send()
    q_copy.wait_send()
    w_copy.wait_send()


def line_gradients(factors, loops, dp_size, mp_size, hidden):
    raw, x_all, r_all, b_all, q_all, x_got, r_got, b_got, x_end, r_end, b_end = factors
    block, rank_block, head = x_all.shape[3], r_all.shape[3], q_all.shape[2]
    quarter, rank_quarter = block // mp_size, rank_block // mp_size
    layout = raw_layout(quarter, rank_quarter, loops)
    rows = block + loops * rank_block
    steps = b_all.shape[0]
    vmem = pl.BlockSpec(memory_space=pltpu.VMEM)
    hbm = pl.BlockSpec(memory_space=pl.ANY)
    dma = pltpu.SemaphoreType.DMA
    f32 = jnp.float32
    line = dp_size // 2 - 1
    half_x = pltpu.VMEM((x_all.shape[0], *x_all.shape[2:]), f32)
    half_r = pltpu.VMEM((r_all.shape[0], *r_all.shape[2:]), f32)
    whole_b, whole_q = pltpu.VMEM(b_all.shape, f32), pltpu.VMEM(q_all.shape, f32)
    shapes = (
        (2, block), (block, head), (quarter, 2 * head), (block, head), (block, 2, hidden),
        (block, hidden), (quarter, loops, head), (loops, rank_block, head), (loops, quarter, 2, head),
        (loops, 2, rank_quarter, head), (loops, rank_block, head), (loops, block, head),
        (loops, quarter, 2, head), (loops, 2, rank_block, hidden), (loops, rank_block, hidden),
        (loops, block, head),
    )
    gains, q_w, pair_w, o_w, e_w, s_w, q_i, q_o, p_i, p_o, o_i, o_o, e_i, e_o, s_i, s_o = pl.pallas_call(
        line_kernel,
        out_shape=tuple(jax.ShapeDtypeStruct(v, f32) for v in shapes),
        in_specs=[hbm] * 11,
        out_specs=(vmem,) * len(shapes),
        scratch_shapes=[
            pltpu.VMEM((3, rows, WIDE), f32), pltpu.VMEM((rows, 2 * head), f32),
            pltpu.VMEM((layout.all, head), f32), pltpu.VMEM((4, loops, 2 * layout.tall, head), f32),
        ]
        + [half_x, half_r, pltpu.VMEM((2, *b_all.shape[1:]), f32), whole_q]
        + [half_x, half_r, whole_b, whole_q]
        + [pltpu.VMEM(v.shape, f32) for v in (x_end, r_end, b_end)]
        + [pltpu.VMEM(raw.shape[1:], f32)] * 2
        + [pltpu.VMEM((rows, WIDE), f32)]
        + [pltpu.VMEM((line, 3, rows, WIDE), f32)] * 2
        + [pltpu.VMEM((line, 1, rows, 2 * head), f32)] * 2
        + [pltpu.VMEM((line, 1, layout.all, head), f32)] * 2
        + [dma((2,))] * 4 + [dma((steps,))] * 2 + [dma] * 4 + [dma((11,)), dma((2,)), dma((3,)), dma((3,))]
        + [dma((line, 3))] * 4 + [dma((line, 1))] * 8
        + [pltpu.SemaphoreType.REGULAR((line,))] * 2,
        compiler_params=pltpu.CompilerParams(
            collective_id=20, has_side_effects=True, vmem_limit_bytes=63 << 20
        ),
    )(*factors)

    return (
        gains, q_w, pair_w, o_w, e_w, s_w, q_i, q_o, p_i, p_o, o_i, o_o, e_i, e_o, s_i, s_o
    )


def in_place(results):
    gains, q_w, pair_w, o_w, e_w, s_w, q_i, q_o, p_i, p_o, o_i, o_o, e_i, e_o, s_i, s_o = results
    return (
        gains[0], gains[1], q_w, pair_w, o_w.T, e_w, s_w.T, q_i.swapaxes(0, 1), q_o, p_i, p_o,
        o_i.swapaxes(1, 2), o_o.swapaxes(1, 2), e_i, e_o, s_i.swapaxes(1, 2), s_o.swapaxes(1, 2),
    )


def copy_kernel(*refs):
    count = (len(refs) - 2) // 3
    sources, targets, rooms = refs[:count], refs[count : 2 * count], refs[2 * count : 3 * count]
    come = [pltpu.make_async_copy(v, room, refs[-2].at[i]) for i, (v, room) in enumerate(zip(sources, rooms))]
    go = [pltpu.make_async_copy(room, v, refs[-1].at[i]) for i, (v, room) in enumerate(zip(targets, rooms))]
    for copy in come:
        copy.start()
    for first, second in zip(come, go):
        first.wait()
        second.start()
    for copy in go:
        copy.wait()


def placed(values):
    hbm = pl.BlockSpec(memory_space=pl.ANY)
    sems = pltpu.SemaphoreType.DMA((len(values),))
    return pl.pallas_call(
        copy_kernel,
        out_shape=tuple(jax.ShapeDtypeStruct(v.shape, v.dtype) for v in values),
        in_specs=[hbm] * len(values),
        out_specs=(hbm,) * len(values),
        scratch_shapes=[pltpu.VMEM(v.shape, v.dtype) for v in values] + [sems, sems],
        compiler_params=pltpu.CompilerParams(vmem_limit_bytes=60 << 20),
    )(*values)


def per_device(dp_size, mp_size, block_input, cotangent, segments, *parameters):
    shared, stacked = parameters[:7], parameters[7:]
    loops = stacked[0].shape[0]
    if dp_size == 8 and mp_size == 4 and loops == 2:
        output, input_grad, *factors = block_and_factors(
            block_input, cotangent, segments, shared, stacked, dp_size
        )
        gradients = line_gradients(factors, loops, dp_size, mp_size, shared[6].shape[0])
        output, input_grad, *gradients = placed((output, input_grad, *gradients))
        gradients = in_place(gradients)
        return (output, input_grad, *gradients)
    tables = rotary_tables(segments[0], shared[3].shape[1] // 2)
    total = mp_total(mp_size)
    state = block_input.astype(jnp.float32)
    kept_all = []
    for i in range(loops):
        state, kept = forward_loop(state, shared, [v[i] for v in stacked], tables, total, 1)
        kept_all.append(kept)
    upstream = cotangent.astype(jnp.float32)
    for i in reversed(range(loops)):
        upstream = reverse_loop(
            upstream, kept_all[i], shared, [v[i] for v in stacked], tables, total, 3
        )
    return (state.astype(jnp.bfloat16), upstream, *scattered_gradients(kept_all, dp_size, mp_size))


def solution(mesh):
    in_specs = (
        P("dp", None),
        P("dp", None),
        P("dp", None),
        P(),
        P(),
        P(None, "mp"),
        P(),
        P("mp", None),
        P(None, None, "mp"),
        P("mp", None),
        P(),
        P(None, None, "mp"),
        P(),
        P(),
        P(None, "mp", None),
        P(),
        P(),
        P(None, None, None, "mp"),
        P(None, "mp", None),
        P(),
    )
    out_specs = (
        P("dp", None),
        P("dp", None),
        P("dp"),
        P("dp"),
        P("dp", "mp"),
        P(("dp", "mp"), None),
        P("mp", "dp"),
        P("dp", None, "mp"),
        P("mp", "dp"),
        P(None, ("dp", "mp"), None),
        P(None, "dp", "mp"),
        P(None, ("dp", "mp"), None, None),
        P(None, None, ("dp", "mp"), None),
        P(None, "mp", "dp"),
        P(None, None, "dp"),
        P(None, ("dp", "mp"), None, None),
        P(None, None, "dp", "mp"),
        P(None, "mp", "dp"),
        P(None, None, "dp"),
    )
    return jax.shard_map(
        functools.partial(per_device, mesh.shape["dp"], mesh.shape["mp"]),
        mesh=mesh, in_specs=in_specs, out_specs=out_specs, check_vma=False
    )
```

```python
import functools
import math
from types import SimpleNamespace

import jax
import jax.numpy as jnp
from jax import lax
from jax.experimental import pallas as pl
from jax.experimental.pallas import tpu as pltpu
from jax.sharding import PartitionSpec as P

EPSILON = 1e-06
MASKED = -1e30
MESH = pl.DeviceIdType.MESH


def product(left, right):
    return jnp.dot(left, right, preferred_element_type=jnp.float32)


def product_t(left, right):
    return lax.dot_general(
        left, right, (((1,), (1,)), ((), ())), preferred_element_type=jnp.float32
    )


def product_tn(left, right):
    return lax.dot_general(
        left, right, (((0,), (0,)), ((), ())), preferred_element_type=jnp.float32
    )


def exact_product(left, right):
    return jnp.dot(left, right, precision=lax.Precision.HIGHEST, preferred_element_type=jnp.float32)


def exact_tn(left, right):
    return lax.dot_general(
        left,
        right,
        (((0,), (0,)), ((), ())),
        precision=lax.Precision.HIGHEST,
        preferred_element_type=jnp.float32,
    )


def normalize(hidden_state, gain):
    factor = lax.rsqrt(jnp.mean(hidden_state * hidden_state, axis=-1, keepdims=True) + EPSILON)
    return (hidden_state * factor * gain, factor)


def normalize_back(hidden_state, factor, gain, upstream_gradient):
    unit = hidden_state * factor
    scaled = upstream_gradient * gain
    downstream = factor * (scaled - unit * jnp.mean(scaled * unit, axis=-1, keepdims=True))
    return (downstream, jnp.sum(upstream_gradient * unit, axis=0))


def rotate(values, cosine_table, sine_table):
    half_width = values.shape[-1] // 2
    first = values[..., :half_width]
    second = values[..., half_width:]
    return jnp.concatenate(
        [first * cosine_table - second * sine_table, second * cosine_table + first * sine_table],
        axis=-1,
    )


def rotary_tables(segment_row, head_size):
    length_value = segment_row.shape[0]
    earlier = jnp.sum((segment_row[None, :] < segment_row[:, None]).astype(jnp.int32), axis=1)
    position = (jnp.arange(length_value, dtype=jnp.int32) - earlier).astype(jnp.float32)
    steps_half = jnp.arange(head_size // 2, dtype=jnp.float32)
    frequency = 10000.0 ** (-2.0 * steps_half / head_size)
    angles = position[:, None] * frequency[None, :]
    same_segment = segment_row[:, None] == segment_row[None, :]
    ordinal = jnp.arange(length_value, dtype=jnp.int32)
    allowed_mask = same_segment & (ordinal[:, None] >= ordinal[None, :])
    return (jnp.cos(angles), jnp.sin(angles), allowed_mask)


def gelu_tanh(values):
    return jax.nn.gelu(values, approximate=True)


def attention_probs(queries, keys, allowed_mask, score_scale):
    scores = (
        jnp.einsum("ihd,jd->hij", queries, keys, preferred_element_type=jnp.float32) * score_scale
    )
    return jnp.where(allowed_mask[None], scores, MASKED)


def mp_total(size):
    def kernel(part, out, near, mine, far, core_send, core_recv, y_send, y_recv, back_send, back_recv):
        dp, mp = lax.axis_index("dp"), lax.axis_index("mp")
        side = lax.rem(mp, 2)
        core = (dp, mp + 1 - 2 * side)
        other = (dp, lax.rem(mp + 2, 4))
        half = part.shape[0] // 2
        pieces = near.shape[0]
        width = part.shape[1] // pieces
        own = pl.ds(pl.multiple_of(side * half, half), half)
        theirs = pl.ds(pl.multiple_of((1 - side) * half, half), half)

        def columns(i):
            return pl.ds(i * width, width)

        barrier = pltpu.get_barrier_semaphore()
        for device in (core, other):
            pl.semaphore_signal(barrier, inc=1, device_id=device, device_id_type=MESH)
        pl.semaphore_wait(barrier, 2)
        first = [
            pltpu.make_async_remote_copy(
                part.at[theirs, columns(i)], near.at[i], core_send.at[i], core_recv.at[i],
                device_id=core, device_id_type=MESH,
            )
            for i in range(pieces)
        ]
        second = [
            pltpu.make_async_remote_copy(
                mine.at[i], far.at[i], y_send.at[i], y_recv.at[i],
                device_id=other, device_id_type=MESH,
            )
            for i in range(pieces)
        ]
        third = [
            pltpu.make_async_remote_copy(
                out.at[own, columns(i)], out.at[own, columns(i)], back_send.at[i], back_recv.at[i],
                device_id=core, device_id_type=MESH,
            )
            for i in range(pieces)
        ]
        for copy in first:
            copy.start()
        for i in range(pieces):
            first[i].wait_recv()
            mine[i] = part[own, columns(i)] + near[i]
            second[i].start()
        for i in range(pieces):
            second[i].wait_recv()
            out[own, columns(i)] = mine[i] + far[i]
            third[i].start()
        for copy in third:
            copy.wait_recv()
        for copy in first + second + third:
            copy.wait_send()

    def total(identity, *parts):
        if size != 4:
            return lax.psum(parts, "mp")
        joined = jnp.concatenate(parts, axis=1)
        tokens_here, columns_here = joined.shape
        pieces = 1
        for count in (5, 4, 3, 2):
            if columns_here % (128 * count) == 0:
                pieces = count
                break
        half = (pieces, tokens_here // 2, columns_here // pieces)
        summed = pl.pallas_call(
            kernel,
            out_shape=jax.ShapeDtypeStruct(joined.shape, jnp.float32),
            in_specs=[pl.BlockSpec(memory_space=pltpu.VMEM)],
            out_specs=pl.BlockSpec(memory_space=pltpu.VMEM),
            scratch_shapes=[pltpu.VMEM(half, jnp.float32)] * 3
            + [pltpu.SemaphoreType.DMA((pieces,))] * 6,
            compiler_params=pltpu.CompilerParams(
                collective_id=identity, has_side_effects=True, vmem_limit_bytes=16 << 20
            ),
        )(joined)
        edges, start = [], 0
        for part in parts:
            edges.append(summed[:, start : start + part.shape[1]])
            start += part.shape[1]
        return tuple(edges)

    return total


def forward_loop(hidden_state, shared, adapters, tables, total, identity):
    (mixer_gain, feed_gain, query_matrix, pair_matrix, output_matrix, widen_matrix, down_matrix) = shared
    (q_in, q_out, kv_in, kv_out, o_in, o_out, w_in, w_out, d_in, d_out) = adapters
    cosine, sine, allowed = tables
    tokens_here, width = hidden_state.shape
    head = pair_matrix.shape[1] // 2
    heads = query_matrix.shape[1] // head
    rank = q_in.shape[1]
    hidden = down_matrix.shape[0]
    kept = SimpleNamespace(h=hidden_state)
    normed, kept.mixer_factor = normalize(hidden_state, mixer_gain)
    normed = normed.astype(jnp.bfloat16)
    query_rank = product(normed, q_in).astype(jnp.bfloat16)
    query_linear = product(normed, query_matrix) + product(query_rank, q_out)
    pair_rank = product(normed, kv_in.reshape(width, 2 * rank)).astype(jnp.bfloat16)
    pair_linear = product(normed, pair_matrix) + jnp.concatenate(
        [product(pair_rank[:, :rank], kv_out[0]), product(pair_rank[:, rank:], kv_out[1])], axis=1
    )
    queries = rotate(
        query_linear.reshape(tokens_here, heads, head), cosine[:, None], sine[:, None]
    ).astype(jnp.bfloat16)
    keys = rotate(pair_linear[:, :head], cosine, sine).astype(jnp.bfloat16)
    values = pair_linear[:, head:].astype(jnp.bfloat16)
    masked = attention_probs(queries, keys, allowed, 1.0 / math.sqrt(head))
    expo = jnp.exp(masked - jnp.max(masked, axis=-1, keepdims=True))
    probs = expo / jnp.sum(expo, axis=-1, keepdims=True)
    mixed = jnp.einsum(
        "hij,jd->ihd", probs.astype(jnp.bfloat16), values, preferred_element_type=jnp.float32
    )
    mixed = mixed.reshape(tokens_here, heads * head).astype(jnp.bfloat16)
    summed, output_rank = total(identity, product(mixed, output_matrix), product(mixed, o_in))
    middle = hidden_state + summed + exact_product(output_rank, o_out.astype(jnp.float32))
    fed, kept.feed_factor = normalize(middle, feed_gain)
    fed = fed.astype(jnp.bfloat16)
    widen_rank = product(fed, w_in.reshape(width, 2 * rank)).astype(jnp.bfloat16)
    gate = product(fed, widen_matrix[:, 0]) + product(widen_rank[:, :rank], w_out[0])
    up = product(fed, widen_matrix[:, 1]) + product(widen_rank[:, rank:], w_out[1])
    activated = (gelu_tanh(gate) * up).astype(jnp.bfloat16)
    shrunk, shrink_rank = total(identity + 1, product(activated, down_matrix), product(activated, d_in))
    result = middle + shrunk + exact_product(shrink_rank, d_out.astype(jnp.float32))
    vars(kept).update(
        normed=normed, query_rank=query_rank, pair_rank=pair_rank, queries=queries, keys=keys,
        values=values, probs=probs, mixed=mixed, output_rank=output_rank, middle=middle, fed=fed,
        widen_rank=widen_rank, gate=gate, up=up, activated=activated, shrink_rank=shrink_rank,
    )
    return result, kept


def reverse_loop(upstream, kept, shared, adapters, tables, total, identity):
    (mixer_gain, feed_gain, query_matrix, pair_matrix, output_matrix, widen_matrix, down_matrix) = shared
    (q_in, q_out, kv_in, kv_out, o_in, o_out, w_in, w_out, d_in, d_out) = adapters
    cosine, sine, allowed = tables
    tokens_here, width = upstream.shape
    head = pair_matrix.shape[1] // 2
    heads = query_matrix.shape[1] // head
    rank = q_in.shape[1]
    scale = 1.0 / math.sqrt(head)
    grad_feed = upstream.astype(jnp.bfloat16)
    grad_shrink_rank = product_t(grad_feed, d_out).astype(jnp.bfloat16)
    grad_activated = product_t(grad_feed, down_matrix) + product_t(grad_shrink_rank, d_in)
    gelu_value, gelu_pullback = jax.vjp(gelu_tanh, kept.gate)
    grad_gate = gelu_pullback(grad_activated * kept.up)[0].astype(jnp.bfloat16)
    grad_up = (grad_activated * gelu_value).astype(jnp.bfloat16)
    grad_fed, grad_widen_rank = total(
        identity,
        product_t(grad_gate, widen_matrix[:, 0]) + product_t(grad_up, widen_matrix[:, 1]),
        jnp.concatenate([product_t(grad_gate, w_out[0]), product_t(grad_up, w_out[1])], axis=1),
    )
    grad_widen_rank = grad_widen_rank.astype(jnp.bfloat16)
    grad_fed = grad_fed + product_t(grad_widen_rank, w_in.reshape(width, 2 * rank))
    grad_norm, feed_gain_grad = normalize_back(kept.middle, kept.feed_factor, feed_gain, grad_fed)
    grad_middle = upstream + grad_norm
    grad_attend = grad_middle.astype(jnp.bfloat16)
    grad_output_rank = product_t(grad_attend, o_out).astype(jnp.bfloat16)
    grad_mixed = product_t(grad_attend, output_matrix) + product_t(grad_output_rank, o_in)
    grad_mixed = grad_mixed.astype(jnp.bfloat16).reshape(tokens_here, heads, head)
    queries, keys, values, probs = kept.queries, kept.keys, kept.values, kept.probs
    grad_probs = jnp.einsum("ihd,jd->hij", grad_mixed, values, preferred_element_type=jnp.float32)
    delta = jnp.sum(grad_probs * probs, axis=-1, keepdims=True)
    grad_scores = (probs * (grad_probs - delta)).astype(jnp.bfloat16)
    grad_queries = scale * jnp.einsum(
        "hij,jd->ihd", grad_scores, keys, preferred_element_type=jnp.float32
    )
    grad_keys = scale * jnp.einsum(
        "hij,ihd->jd", grad_scores, queries, preferred_element_type=jnp.float32
    )
    grad_values = jnp.einsum(
        "hij,ihd->jd", probs.astype(jnp.bfloat16), grad_mixed, preferred_element_type=jnp.float32
    )
    grad_query = rotate(grad_queries, cosine[:, None], -sine[:, None])
    grad_query = grad_query.reshape(tokens_here, heads * head).astype(jnp.bfloat16)
    grad_normed, grad_query_rank, grad_pair = total(
        identity + 1,
        product_t(grad_query, query_matrix),
        product_t(grad_query, q_out),
        jnp.concatenate([rotate(grad_keys, cosine, -sine), grad_values], axis=1),
    )
    grad_query_rank = grad_query_rank.astype(jnp.bfloat16)
    grad_pair = grad_pair.astype(jnp.bfloat16)
    grad_pair_rank = jnp.concatenate(
        [product_t(grad_pair[:, :head], kv_out[0]), product_t(grad_pair[:, head:], kv_out[1])], axis=1
    ).astype(jnp.bfloat16)
    grad_normed = (
        grad_normed
        + product_t(grad_query_rank, q_in)
        + product_t(grad_pair, pair_matrix)
        + product_t(grad_pair_rank, kv_in.reshape(width, 2 * rank))
    )
    grad_norm, mixer_gain_grad = normalize_back(
        kept.h, kept.mixer_factor, mixer_gain, grad_normed
    )
    vars(kept).update(
        grad_feed=grad_feed, grad_shrink_rank=grad_shrink_rank, grad_gate=grad_gate, grad_up=grad_up,
        grad_widen_rank=grad_widen_rank, grad_attend=grad_attend, grad_output_rank=grad_output_rank,
        grad_query=grad_query, grad_query_rank=grad_query_rank, grad_pair=grad_pair,
        grad_pair_rank=grad_pair_rank, feed_gain_grad=feed_gain_grad, mixer_gain_grad=mixer_gain_grad,
    )
    return grad_middle + grad_norm


def scattered_gradients(kept, dp_size, mp_size):
    def scatter(value, axis):
        return lax.psum_scatter(value, "dp", scatter_dimension=axis, tiled=True)

    def shared_of(factors):
        return sum(product_tn(*factors(k)) for k in kept)

    def each(function):
        return jnp.stack([function(k) for k in kept], axis=0)

    def quarter(value, axis):
        block = scatter(value, axis)
        size = block.shape[axis] // mp_size
        return lax.dynamic_slice_in_dim(block, lax.axis_index("mp") * size, size, axis)

    width = kept[0].normed.shape[1]
    rank = kept[0].query_rank.shape[1]
    head = kept[0].grad_pair.shape[1] // 2

    def pair_outer(k):
        left, right = k.pair_rank, k.grad_pair
        return jnp.stack(
            [product_tn(left[:, :rank], right[:, :head]), product_tn(left[:, rank:], right[:, head:])]
        )

    def expand_outer(k):
        left = k.widen_rank
        return jnp.stack(
            [product_tn(left[:, :rank], k.grad_gate), product_tn(left[:, rank:], k.grad_up)]
        )

    return (
        scatter(sum(k.mixer_gain_grad for k in kept), 0),
        scatter(sum(k.feed_gain_grad for k in kept), 0),
        scatter(shared_of(lambda k: (k.normed, k.grad_query)), 0),
        quarter(shared_of(lambda k: (k.normed, k.grad_pair)), 0),
        scatter(shared_of(lambda k: (k.mixed, k.grad_attend)), 1),
        scatter(jnp.stack([shared_of(lambda k: (k.fed, k.grad_gate)), shared_of(lambda k: (k.fed, k.grad_up))], axis=1), 0),
        scatter(shared_of(lambda k: (k.activated, k.grad_feed)), 1),
        quarter(each(lambda k: product_tn(k.normed, k.grad_query_rank)), 1),
        scatter(each(lambda k: product_tn(k.query_rank, k.grad_query)), 1),
        quarter(
            each(lambda k: product_tn(k.normed, k.grad_pair_rank).reshape(width, 2, rank)), 1
        ),
        quarter(each(pair_outer), 2),
        scatter(each(lambda k: product_tn(k.mixed, k.grad_output_rank)), 2),
        scatter(
            each(lambda k: exact_tn(k.output_rank, k.grad_attend.astype(jnp.float32))), 2
        ),
        quarter(
            each(lambda k: product_tn(k.fed, k.grad_widen_rank).reshape(width, 2, rank)), 1
        ),
        scatter(each(expand_outer), 2),
        scatter(each(lambda k: product_tn(k.activated, k.grad_shrink_rank)), 2),
        scatter(each(lambda k: exact_tn(k.shrink_rank, k.grad_feed.astype(jnp.float32))), 2),
    )


WIDE = 896


def split3(value):
    high = value.astype(jnp.bfloat16)
    rest = value - high.astype(jnp.float32)
    middle = rest.astype(jnp.bfloat16)
    low = (rest - middle.astype(jnp.float32)).astype(jnp.bfloat16)
    return high, middle, low


WEIGHTS = (
    "q_in", "query", "q_out", "kv_in", "pair", "kv_out", "output", "o_in", "o_out",
    "wide", "w_out", "down", "d_in", "d_out", "w_in",
)
SUM_STEP = 384


def block_kernel(*refs):
    (h_in, cot, segments, mixer_gain, feed_gain), refs = refs[:5], refs[5:]
    count = len(WEIGHTS)
    sources, refs = refs[:count], refs[count:]
    (
        out_ref, grad_ref, raw_ref, x_all, r_all, b_all, q_all, x_got, r_got, b_got, x_end, r_end, b_end,
    ), refs = refs[:13], refs[13:]
    weights, refs = (*refs[: count - 1], refs[WEIGHTS.index("kv_in")]), refs[count - 1 :]
    (
        h_s, mid_s, normed_s, qr_s, kvr_s, q_s, k_s, v_s, probs_s, mixed_s, or_s, fed_s, er_s,
        gate_s, up_s, act_s, sr_s, gg_s, gu_s, g_s, gain_s, select,
        part, total, near, mine, far, side_part, side_near, side_mine, side_far, side_total,
        late_s, er_grad_s, chosen_s, xs, rs, bs, qs, kv_flat, w_flat, cosine_ref, sine_ref, mask_ref,
        load_sems, c_s, c_r, y_s, y_r, e_s, e_r,
        xl, rl, bl, ql, x_s, x_r, r_s, r_r, b_s, b_r, xe_s, xe_r, re_s, re_r, be_s, be_r,
        sc_s, sc_r, sy_s, sy_r, se_s, se_r, xc_s, xc_r, rc_s, rc_r,
    ) = refs
    W = SimpleNamespace(**dict(zip(WEIGHTS, weights)))
    dp, mp = lax.axis_index("dp"), lax.axis_index("mp")
    side = lax.rem(mp, 2)
    core = (dp, mp + 1 - 2 * side)
    other = (dp, lax.rem(mp + 2, 4))
    loads = [
        pltpu.make_async_copy(source, target, load_sems.at[i])
        for i, (source, target) in enumerate(zip(sources, weights))
    ]
    load = SimpleNamespace(**dict(zip(WEIGHTS, loads)))
    for copy in loads[:-1]:
        copy.start()
    x = lax.rem(dp, 2)
    z = dp // 2
    pair = (dp + 1 - 2 * x, mp)
    near_end = (dp + 2 - 4 * lax.rem(z, 2), mp)
    is_end = jnp.logical_or(z == 0, z == 3)
    barrier = pltpu.get_barrier_semaphore()
    for device in (core, other, pair, near_end):
        pl.semaphore_signal(barrier, inc=1, device_id=device, device_id_type=MESH)
    pl.semaphore_wait(barrier, 4)

    tokens, width = h_in.shape
    half = tokens // 2
    head = W.query.shape[1]
    rank = W.q_in.shape[2]
    hidden = W.down.shape[0]
    loops = W.q_in.shape[0]
    scale = 1.0 / math.sqrt(head)
    own = pl.ds(pl.multiple_of(side * half, half), half)
    theirs = pl.ds(pl.multiple_of((1 - side) * half, half), half)
    blocks = x_all.shape[1] * x_all.shape[2]
    block = width // blocks
    quarter = block // 4
    rank_quarter = rank // (4 * blocks)
    chunks = [(0, WIDE), (WIDE, hidden - WIDE)]

    def remote(source, target, send, recv, device):
        return pltpu.make_async_remote_copy(
            source, target, send, recv, device_id=device, device_id_type=MESH
        )

    def span(l):
        return pl.ds(pl.multiple_of(l * tokens, tokens), tokens)

    def end_span(l, is_far):
        return pl.ds(pl.multiple_of((2 * l + is_far) * tokens, tokens), tokens)

    def x_copies(i, l):
        across = onward = None
        if i < 2:
            across = remote(
                xs.at[i, 1 - x], x_got.at[i, :, :, span(l)], x_s.at[i, l], x_r.at[i, l], pair
            )
        if i == 1:
            onward = remote(
                xs.at[i, x], x_end.at[:, :, end_span(l, 0)], xe_s.at[0, l], xe_r.at[0, l], near_end
            )
        return pltpu.make_async_copy(xs.at[i], x_all.at[i, :, :, :, span(l)], xl.at[i, l]), across, onward

    def r_copies(i, l):
        across = onward = None
        if i < 3:
            across = remote(
                rs.at[i, 1 - x], r_got.at[i, :, :, span(l)], r_s.at[i, l], r_r.at[i, l], pair
            )
        if i == 2:
            onward = remote(
                rs.at[i, x], r_end.at[:, :, end_span(l, 0)], re_s.at[0, l], re_r.at[0, l], near_end
            )
        return pltpu.make_async_copy(rs.at[i], r_all.at[i, :, :, :, span(l)], rl.at[i, l]), across, onward

    def b_copies(i, l):
        across = onward = None
        if i in (0, 4, 5):
            k = max(0, i - 3)
            across = remote(bs.at[i], b_got.at[k, span(l)], b_s.at[k, l], b_r.at[k, l], pair)
        if i >= 4:
            onward = remote(
                bs.at[i], b_end.at[i - 4, end_span(l, 0)],
                be_s.at[i - 4, 0, l], be_r.at[i - 4, 0, l], near_end,
            )
        return pltpu.make_async_copy(bs.at[i], b_all.at[i, span(l)], bl.at[i, l]), across, onward

    def q_copies(i, l):
        return pltpu.make_async_copy(qs.at[i], q_all.at[i, span(l)], ql.at[i, l]), None, None

    def launch(copies, whole=True):
        local, across, onward = copies
        local.start()
        if across is not None:
            across.start()
        if onward is not None:

            @pl.when(is_end if whole else jnp.logical_and(is_end, side == 0))
            def _():
                onward.start()

    def finish(copies, whole=True):
        local, across, onward = copies
        local.wait()
        if across is not None:
            across.wait_send()
        if onward is not None:

            @pl.when(is_end if whole else jnp.logical_and(is_end, side == 0))
            def _():
                onward.wait_send()

    def far_feed(l):
        return [
            remote(
                x_got.at[1, :, :, span(l)], x_end.at[:, :, end_span(l, 1)],
                xe_s.at[1, l], xe_r.at[1, l], near_end,
            ),
            remote(
                r_got.at[2, :, :, span(l)], r_end.at[:, :, end_span(l, 1)],
                re_s.at[1, l], re_r.at[1, l], near_end,
            ),
        ]

    def far_act(l):
        return [
            remote(
                b_got.at[1 + k, span(l)], b_end.at[k, end_span(l, 1)],
                be_s.at[k, 1, l], be_r.at[k, 1, l], near_end,
            )
            for k in range(2)
        ]

    def pass_act(l):
        for i in (4, 5):
            b_copies(i, l)[1].wait_recv()

        @pl.when(is_end)
        def _():
            for copy in far_act(l):
                copy.start()

    def pass_feed(l):
        x_copies(1, l)[1].wait_recv()
        r_copies(2, l)[1].wait_recv()

        @pl.when(jnp.logical_and(is_end, side == 1))
        def _():
            for copy in far_feed(l):
                copy.start()

    def ship_x(i, l, value, again, before):
        @pl.when(again)
        def _():
            finish(x_copies(i, before), False)

        turned = value.astype(jnp.float32).T
        for b in range(blocks):
            xs[i, b % 2, b // 2] = turned[b * block : (b + 1) * block]
        launch(x_copies(i, l), False)

    def ship_r(i, l, value, again, before):
        @pl.when(again)
        def _():
            finish(r_copies(i, before), False)

        turned = value.astype(jnp.float32).T
        size = rank // blocks
        for b in range(blocks):
            rs[i, b % 2, b // 2] = turned[b * size : (b + 1) * size]
        launch(r_copies(i, l), False)

    def ship_b(i, l, values, again, before):
        @pl.when(again)
        def _():
            finish(b_copies(i, before))

        filled = 0
        for value in values:
            n = value.shape[1]
            bs[i, :, filled : filled + n] = value.astype(jnp.float32)
            filled += n
        if filled < WIDE:
            bs[i, :, filled:] = jnp.zeros((tokens, WIDE - filled), jnp.float32)
        launch(b_copies(i, l))

    def ship_q(i, l, value, again, before):
        @pl.when(again)
        def _():
            finish(q_copies(i, before))

        qs[i] = value.astype(jnp.float32)
        launch(q_copies(i, l))

    def columns_of(size):
        return [(at, min(SUM_STEP, size - at)) for at in range(0, size, SUM_STEP)]

    def side_copies(turn, size):
        columns = pl.ds(0, size)
        return (
            remote(
                side_part.at[turn, theirs, columns], side_near.at[turn, :, columns],
                sc_s.at[turn], sc_r.at[turn], core,
            ),
            remote(
                side_mine.at[turn, :, columns], side_far.at[turn, :, columns],
                sy_s.at[turn], sy_r.at[turn], other,
            ),
            remote(
                side_total.at[turn, own, columns], side_total.at[turn, own, columns],
                se_s.at[turn], se_r.at[turn], core,
            ),
        )

    def finish_side(turn, size):
        first, second, third = side_copies(turn, size)
        second.wait_recv()
        side_total[turn, own, :size] = side_mine[turn, :, :size] + side_far[turn, :, :size]
        third.start()
        third.wait_recv()
        for copy in (first, second, third):
            copy.wait_send()
        return side_total[turn, :, :size]

    def sum_over_mp(fill, turn, side_size, finish_previous, idle):
        pieces = columns_of(width)

        def pieces_of(make):
            return [make(i, pl.ds(at, n)) for i, (at, n) in enumerate(pieces)]

        first = pieces_of(
            lambda i, c: remote(part.at[theirs, c], near.at[:, c], c_s.at[i], c_r.at[i], core)
        )
        second = pieces_of(
            lambda i, c: remote(
                mine.at[:, c], far.at[turn, :, c], y_s.at[turn, i], y_r.at[turn, i], other
            )
        )
        third = pieces_of(
            lambda i, c: remote(total.at[own, c], total.at[own, c], e_s.at[i], e_r.at[i], core)
        )
        side_first, side_second, _ = side_copies(turn, side_size)

        def middle(i):
            at, n = pieces[i]
            first[i].wait_recv()
            mine[:, at : at + n] = part[own, at : at + n] + near[:, at : at + n]
            second[i].start()

        for i, (at, n) in enumerate(pieces):
            fill(at, n)
            first[i].start()
            if i:
                middle(i - 1)
        side_first.start()
        middle(len(first) - 1)
        side_first.wait_recv()
        side_mine[turn, :, :side_size] = (
            side_part[turn, own, :side_size] + side_near[turn, :, :side_size]
        )
        finish_previous()
        side_second.start()
        idle()
        for i, (at, n) in enumerate(pieces):
            second[i].wait_recv()
            total[own, at : at + n] = mine[:, at : at + n] + far[turn, :, at : at + n]
            third[i].start()
        for copy in third:
            copy.wait_recv()
        for copy in first + second + third:
            copy.wait_send()

    def dot(left, right):
        return jnp.dot(left, right, preferred_element_type=jnp.float32)

    def low(value):
        return value.astype(jnp.bfloat16)

    def spin(value, sign):
        a, b = value[:, : head // 2], value[:, head // 2 :]
        cosine, sine = cosine_ref[...], sign * sine_ref[...]
        return jnp.concatenate([a * cosine - b * sine, b * cosine + a * sine], axis=1)

    def factor_of(value):
        return lax.rsqrt(jnp.mean(value * value, axis=-1, keepdims=True) + EPSILON)

    def gelu_parts(value):
        c = math.sqrt(2.0 / math.pi)
        square = value * value
        t = jnp.tanh(c * value * (1.0 + 0.044715 * square))
        gelu = 0.5 * value * (1.0 + t)
        slope = 0.5 * (1.0 + t) + 0.5 * value * (1.0 - t * t) * c * (1.0 + 3 * 0.044715 * square)
        return gelu, slope

    across_row = jnp.broadcast_to(segments[...].astype(jnp.float32), (tokens, tokens))
    down_row = across_row.T
    at_row = lax.broadcasted_iota(jnp.int32, (tokens, tokens), 0)
    at_column = lax.broadcasted_iota(jnp.int32, (tokens, tokens), 1)
    earlier = jnp.sum(jnp.where(across_row < down_row, 1.0, 0.0), axis=1, keepdims=True)
    position = at_row[:, : head // 2].astype(jnp.float32) - earlier
    exponent = at_column[:, : head // 2].astype(jnp.float32) * (-2.0 / head)
    angles = position * jnp.exp(exponent * math.log(10000.0))
    cosine_ref[...] = jnp.cos(angles)
    sine_ref[...] = jnp.sin(angles)
    mask_ref[...] = jnp.where(
        jnp.logical_and(across_row == down_row, at_row >= at_column), 1.0, 0.0
    )
    h_s[0] = h_in[...].astype(jnp.float32)
    mixer, feed = mixer_gain[...].reshape(1, width), feed_gain[...].reshape(1, width)

    def forward(l, carry):
        def need(*copies):
            @pl.when(l == 0)
            def _():
                for copy in copies:
                    copy.wait()

        h = h_s[l]
        normed = low(h * factor_of(h) * mixer)
        normed_s[l] = normed
        need(load.q_in, load.query, load.q_out, load.kv_in, load.pair, load.kv_out)

        @pl.when(l == 0)
        def _():
            kv_flat[0] = W.kv_in[0].reshape(width, 2 * rank)

        query_rank = low(dot(normed, W.q_in[l]))
        qr_s[l] = query_rank
        queries = dot(normed, W.query[...]) + dot(query_rank, W.q_out[l])
        q_s[l] = low(spin(queries, 1.0))
        pair_rank = low(dot(normed, kv_flat[l]))
        kvr_s[l] = pair_rank
        keys = dot(normed, W.pair[:, :head]) + dot(pair_rank[:, :rank], W.kv_out[l, 0])
        k_s[l] = low(spin(keys, 1.0))
        values = dot(normed, W.pair[:, head:]) + dot(pair_rank[:, rank:], W.kv_out[l, 1])
        v_s[l] = low(values)
        scores = product_t(q_s[l], k_s[l]) * scale
        scores = jnp.where(mask_ref[...] > 0, scores, MASKED)
        expo = jnp.exp(scores - jnp.max(scores, axis=-1, keepdims=True))
        probs = expo / jnp.sum(expo, axis=-1, keepdims=True)
        probs_s[l] = probs
        mixed = low(dot(low(probs), v_s[l]))
        mixed_s[l] = mixed
        need(load.output, load.o_in, load.o_out)

        output_rank = dot(mixed, W.o_in[l])
        side_part[0, :, :rank] = output_rank
        output_parts = split3(output_rank)

        def fill_attend(at, n):
            value = dot(mixed, W.output[:, at : at + n])
            for piece in output_parts:
                value = value + dot(piece, W.o_out[l, :, at : at + n])
            part[:, at : at + n] = value

        again = l > 0

        def idle_attend():
            ship_x(2, l, normed, again, 0)
            ship_r(3, l, query_rank, again, 0)
            ship_q(1, l, mixed, again, 0)

            @pl.when(l == 0)
            def _():
                for i in range(1, loops):
                    kv_flat[i] = W.kv_in[i].reshape(width, 2 * rank)
                load.w_in.start()
                load.w_in.wait()
                for i in range(loops):
                    w_flat[i] = W.w_in[i].reshape(width, 2 * rank)

            @pl.when(again)
            def _():
                pass_act(0)

        def finish_before_attend():
            @pl.when(again)
            def _():
                sr_s[jnp.maximum(l - 1, 0)] = finish_side(1, rank)

        sum_over_mp(fill_attend, 0, rank, finish_before_attend, idle_attend)
        middle = h_s[l] + total[...]
        mid_s[l] = middle
        fed = low(middle * factor_of(middle) * feed)
        fed_s[l] = fed
        need(load.wide, load.w_out)
        widen_rank = low(dot(fed, w_flat[l]))
        er_s[l] = widen_rank
        for at, n in chunks:
            gate = product_t(fed, W.wide[0, at : at + n]) + product_t(
                widen_rank[:, :rank], W.w_out[l, 0, at : at + n]
            )
            gate_s[l, :, at : at + n] = gate
            up = product_t(fed, W.wide[1, at : at + n]) + product_t(
                widen_rank[:, rank:], W.w_out[l, 1, at : at + n]
            )
            up_s[l, :, at : at + n] = up
            act_s[:, at : at + n] = low(gelu_parts(gate)[0] * up)
            ship_b(4 + at // WIDE, l, [act_s[:, at : at + n]], again, 0)
        need(load.down, load.d_in, load.d_out)

        shrink_rank = dot(act_s[...], W.d_in[l])
        side_part[1, :, :rank] = shrink_rank
        shrink_parts = split3(shrink_rank)

        def fill_feed(at, n):
            value = dot(act_s[...], W.down[:, at : at + n])
            for piece in shrink_parts:
                value = value + dot(piece, W.d_out[l, :, at : at + n])
            part[:, at : at + n] = value

        def idle_feed():
            ship_x(0, l, fed, again, 0)
            ship_r(0, l, widen_rank[:, :rank], again, 0)
            ship_r(1, l, widen_rank[:, rank:], again, 0)

        def finish_before_feed():
            or_s[l] = finish_side(0, rank)

        sum_over_mp(fill_feed, 1, rank, finish_before_feed, idle_feed)
        h_s[l + 1] = mid_s[l] + total[...]
        return carry

    lax.fori_loop(0, loops, forward, 0)
    out_ref[...] = low(h_s[loops])

    g_s[...] = cot[...].astype(jnp.float32)
    gain_s[...] = jnp.zeros_like(gain_s)
    padded_quarter = select.shape[0] // blocks
    row = lax.broadcasted_iota(jnp.int32, (padded_quarter, width), 0)
    column = lax.broadcasted_iota(jnp.int32, (padded_quarter, width), 1)
    for b in range(blocks):
        hit = jnp.logical_and(column == row + (b * 4 + mp) * quarter, row < quarter)
        select[b * padded_quarter : (b + 1) * padded_quarter] = low(
            jnp.where(hit, 1.0, 0.0)
        )
    small_row = lax.broadcasted_iota(jnp.int32, (rank_quarter, rank), 0)
    small_column = lax.broadcasted_iota(jnp.int32, (rank_quarter, rank), 1)
    rank_select = low(
        jnp.concatenate(
            [
                jnp.where(small_column == small_row + (b * 4 + mp) * rank_quarter, 1.0, 0.0)
                for b in range(blocks)
            ],
            axis=0,
        )
    )
    raw_rows = raw_layout(quarter, rank_quarter, loops)

    tall = raw_rows.tall

    def put(start, size, stride, value, add=False):
        for b in range(blocks):
            piece = value[b * stride : b * stride + size]
            if add:
                raw_ref[b % 2, b // 2, start : start + size] += piece
            else:
                raw_ref[b % 2, b // 2, start : start + size] = piece

    def pair_ranks(l, grad_keys, grad_values):
        return low(
            jnp.concatenate(
                [product_t(grad_keys, W.kv_out[l, 0]), product_t(grad_values, W.kv_out[l, 1])], axis=1
            )
        )

    def raw_of(l):
        grad_rank = late_s[l, :, :rank]
        grad_pair = late_s[l, :, rank:]
        grad_pair_rank = pair_ranks(l, grad_pair[:, :head], grad_pair[:, head:])
        grad_widen = er_grad_s[l]
        normed_own = low(product_t(select[...], normed_s[l]))
        pair_weight = dot(normed_own, grad_pair)
        for j in range(2):
            value = pair_weight[:, j * head : (j + 1) * head]
            put(j * tall, tall, padded_quarter, value, l < loops - 1)
        base = 2 * tall + l * raw_rows.loop

        def put_loop(i, value):
            put(base + i * tall, tall, padded_quarter, value)

        put_loop(0, dot(normed_own, grad_rank))
        for j in range(2):
            put_loop(1 + j, dot(normed_own, grad_pair_rank[:, j * rank : (j + 1) * rank]))
        fed_own = low(product_t(select[...], fed_s[l]))
        for j in range(2):
            put_loop(3 + j, dot(fed_own, grad_widen[:, j * rank : (j + 1) * rank]))
        put_loop(5, sum(dot(chosen_s[l, 1], piece) for piece in split3(or_s[l])))
        put_loop(6, sum(dot(chosen_s[l, 0], piece) for piece in split3(sr_s[l])))
        for j in range(2):
            rank_own = low(product_t(rank_select, kvr_s[l, :, j * rank : (j + 1) * rank]))
            put(
                base + 7 * tall + j * rank_quarter, rank_quarter, rank_quarter,
                dot(rank_own, grad_pair[:, j * head : (j + 1) * head]),
            )

    def back(step, carry):
        l = loops - 1 - step
        again = step > 0
        before = loops - 1

        upstream = g_s[...]
        grad_feed = low(upstream)
        grad_shrink = low(product_t(grad_feed, W.d_out[l]))
        for i, (at, n) in enumerate(chunks):
            grad_act = product_t(grad_feed, W.down[at : at + n]) + product_t(
                grad_shrink, W.d_in[l, at : at + n]
            )
            gelu, slope = gelu_parts(gate_s[l, :, at : at + n])
            grad_gate = low(grad_act * up_s[l, :, at : at + n] * slope)
            grad_up = low(grad_act * gelu)
            gg_s[:, at : at + n] = grad_gate
            gu_s[:, at : at + n] = grad_up
            if i == 0:
                ship_b(0, l, [grad_gate], again, before)
                ship_b(2, l, [grad_up], again, before)
            else:
                ahead = WIDE - n
                grad_up = grad_up.astype(jnp.float32)
                ship_b(1, l, [grad_gate, grad_up[:, :ahead]], again, before)
                ship_b(3, l, [grad_up[:, ahead:]], again, before)

        for j, value in enumerate((gg_s, gu_s)):
            side_part[0, :, j * rank : (j + 1) * rank] = dot(value[...], W.w_out[l, j])
        grad_widen = low(side_part[0, :, : 2 * rank])

        def fill_fed(at, n):
            part[:, at : at + n] = (
                dot(gg_s[...], W.wide[0, :, at : at + n])
                + dot(gu_s[...], W.wide[1, :, at : at + n])
                + product_t(grad_widen, w_flat[l, at : at + n])
            )

        def finish_before_fed():
            @pl.when(step == 0)
            def _():
                sr_s[loops - 1] = finish_side(1, rank)

            @pl.when(again)
            def _():
                late_s[loops - 1] = low(finish_side(1, rank + 2 * head))

        def idle_fed():
            ship_x(1, l, grad_feed, again, before)
            ship_r(2, l, grad_shrink, again, before)
            chosen_s[l, 0] = low(product_t(select[...], grad_feed))

            @pl.when(again)
            def _():
                pass_feed(loops - 1)
                raw_of(loops - 1)

        sum_over_mp(fill_fed, 0, 2 * rank, finish_before_fed, idle_fed)
        grad_fed = total[...]
        middle = mid_s[l]
        factor = factor_of(middle)
        unit = middle * factor
        scaled = grad_fed * feed
        grad_middle = upstream + factor * (
            scaled - unit * jnp.mean(scaled * unit, axis=-1, keepdims=True)
        )
        gain_s[1:2] += jnp.sum(grad_fed * unit, axis=0, keepdims=True)
        g_s[...] = grad_middle
        grad_attend = low(grad_middle)
        grad_output = low(product_t(grad_attend, W.o_out[l]))
        grad_mixed = low(
            product_t(grad_attend, W.output[...]) + product_t(grad_output, W.o_in[l])
        )
        probs = probs_s[l]
        grad_probs = product_t(grad_mixed, v_s[l])
        delta = jnp.sum(grad_probs * probs, axis=-1, keepdims=True)
        grad_scores = low(probs * (grad_probs - delta))
        grad_query = low(spin(dot(grad_scores, k_s[l]) * scale, -1.0))

        grad_rank = product_t(grad_query, W.q_out[l])
        grad_keys = spin(product_tn(grad_scores, q_s[l]) * scale, -1.0)
        grad_values = product_tn(low(probs), grad_mixed)
        side_part[1, :, :rank] = grad_rank
        side_part[1, :, rank : rank + head] = grad_keys
        side_part[1, :, rank + head :] = grad_values
        grad_rank, grad_keys, grad_values = low(grad_rank), low(grad_keys), low(grad_values)
        grad_pair = jnp.concatenate([grad_keys, grad_values], axis=1)
        grad_pair_rank = pair_ranks(l, grad_keys, grad_values)

        def fill_normed(at, n):
            part[:, at : at + n] = (
                product_t(grad_query, W.query[at : at + n])
                + product_t(grad_rank, W.q_in[l, at : at + n])
                + product_t(grad_pair, W.pair[at : at + n])
                + product_t(grad_pair_rank, kv_flat[l, at : at + n])
            )

        def finish_before_normed():
            er_grad_s[l] = low(finish_side(0, 2 * rank))

        def idle_normed():
            ship_q(0, l, grad_query, again, before)
            ship_x(3, l, grad_attend, again, before)
            ship_r(4, l, grad_output, again, before)
            chosen_s[l, 1] = low(product_t(select[...], grad_attend))

            @pl.when(step == 0)
            def _():
                pass_act(loops - 1)

            @pl.when(again)
            def _():
                pass_feed(0)

        sum_over_mp(fill_normed, 1, rank + 2 * head, finish_before_normed, idle_normed)
        grad_normed = total[...]
        h = h_s[l]
        factor = factor_of(h)
        unit = h * factor
        scaled = grad_normed * mixer
        g_s[...] += factor * (scaled - unit * jnp.mean(scaled * unit, axis=-1, keepdims=True))
        gain_s[0:1] += jnp.sum(grad_normed * unit, axis=0, keepdims=True)

        return carry

    lax.fori_loop(0, loops, back, 0)
    late_s[0] = low(finish_side(1, rank + 2 * head))
    raw_of(0)
    grad_ref[...] = g_s[...]
    for b in range(blocks):
        ends = jnp.zeros((8, head), jnp.float32)
        raw_ref[b % 2, b // 2, raw_rows.gains :] = ends
        raw_ref[b % 2, b // 2, raw_rows.gains : raw_rows.gains + 2, :block] = gain_s[
            :2, b * block : (b + 1) * block
        ]
    last = loops - 1
    for copies in (
        x_copies(0, last), x_copies(2, last), r_copies(0, last), r_copies(1, last), r_copies(3, last),
        q_copies(1, last), x_copies(1, 0), x_copies(3, 0), r_copies(2, 0), r_copies(4, 0),
        q_copies(0, 0),
    ):
        finish(copies, False)
    for copies in (
        b_copies(4, last), b_copies(5, last), b_copies(0, 0), b_copies(1, 0), b_copies(2, 0),
        b_copies(3, 0),
    ):
        finish(copies)

    def to_core(l, half):
        lanes = end_span(l, half)
        return [
            remote(x_end.at[:, :, lanes], x_end.at[:, :, lanes], xc_s.at[l], xc_r.at[l], core),
            remote(r_end.at[:, :, lanes], r_end.at[:, :, lanes], rc_s.at[l], rc_r.at[l], core),
        ]

    for l in range(loops):
        for copies in (x_copies(0, l), r_copies(0, l), r_copies(1, l), b_copies(0, l)):
            copies[1].wait_recv()

        @pl.when(is_end)
        def _():
            for copy in far_act(l):
                copy.wait_send()

        @pl.when(jnp.logical_and(is_end, side == 1))
        def _():
            for copy in far_feed(l):
                copy.wait_send()

        for half in range(2):

            @pl.when(jnp.logical_and(jnp.logical_not(is_end), side == half))
            def _():
                came = far_feed(l) if half else [x_copies(1, l)[2], r_copies(2, l)[2]]
                for copy, onward in zip(came, to_core(l, half)):
                    copy.wait_recv()
                    onward.start()

    @pl.when(jnp.logical_not(is_end))
    def _():
        for l in range(loops):
            for copy in [b_copies(4, l)[2], b_copies(5, l)[2]] + far_act(l):
                copy.wait_recv()
            for copy in to_core(l, 0):
                copy.wait_send()
                copy.wait_recv()


def raw_layout(quarter, rank_quarter, loops):
    tall = quarter
    loop = 7 * tall + 2 * rank_quarter
    gains = 2 * tall + loops * loop
    return SimpleNamespace(tall=tall, loop=loop, gains=gains, all=gains + 8)


def block_and_factors(block_input, cotangent, segments, shared, stacked, dp_size):
    (mixer_gain, feed_gain, query, pair, output, widen, down) = shared
    (q_in, q_out, kv_in, kv_out, o_in, o_out, w_in, w_out, d_in, d_out) = stacked
    tokens, width = block_input.shape
    head = query.shape[1]
    loops, _, rank = q_in.shape
    hidden = down.shape[0]
    weights = (
        q_in, query, q_out, kv_in, pair, kv_out, output, o_in, o_out,
        widen.transpose(1, 2, 0), w_out.swapaxes(2, 3), down, d_in, d_out, w_in,
    )
    layout = raw_layout(width // (4 * dp_size), rank // (4 * dp_size), loops)
    line = dp_size // 2
    f32, bf16 = jnp.float32, jnp.bfloat16
    shape = jax.ShapeDtypeStruct
    block, rank_block, both = width // dp_size, rank // dp_size, loops * tokens
    out_shape = (
        shape((tokens, width), bf16),
        shape((tokens, width), f32),
        shape((2, line, layout.all, head), f32),
        shape((4, 2, line, block, both), f32),
        shape((5, 2, line, rank_block, both), f32),
        shape((6, both, WIDE), f32),
        shape((2, both, head), f32),
        shape((2, line, block, both), f32),
        shape((3, line, rank_block, both), f32),
        shape((3, both, WIDE), f32),
        shape((line, block, 2 * both), f32),
        shape((line, rank_block, 2 * both), f32),
        shape((2, 2 * both, WIDE), f32),
    )
    vmem = pl.BlockSpec(memory_space=pltpu.VMEM)
    hbm = pl.BlockSpec(memory_space=pl.ANY)
    widest = rank + 2 * head
    pieces = -(-width // SUM_STEP)
    dma = pltpu.SemaphoreType.DMA

    def kept(columns, dtype, count=loops):
        return pltpu.VMEM((count, tokens, columns), dtype)

    scratch = [pltpu.VMEM(w.shape, bf16) for w in weights[:-1]] + [
        kept(width, f32, loops + 1), kept(width, f32), kept(width, bf16), kept(rank, bf16),
        kept(2 * rank, bf16), kept(head, bf16), kept(head, bf16), kept(head, bf16), kept(tokens, f32),
        kept(head, bf16), kept(rank, f32), kept(width, bf16), kept(2 * rank, bf16),
        kept(hidden, f32), kept(hidden, f32), pltpu.VMEM((tokens, hidden), bf16), kept(rank, f32),
        pltpu.VMEM((tokens, hidden), bf16), pltpu.VMEM((tokens, hidden), bf16),
        pltpu.VMEM((tokens, width), f32), pltpu.VMEM((8, width), f32),
        pltpu.VMEM((dp_size * 48, width), bf16),
        pltpu.VMEM((tokens, width), f32), pltpu.VMEM((tokens, width), f32),
        pltpu.VMEM((tokens // 2, width), f32), pltpu.VMEM((tokens // 2, width), f32),
        pltpu.VMEM((2, tokens // 2, width), f32),
        pltpu.VMEM((2, tokens, widest), f32), pltpu.VMEM((2, tokens // 2, widest), f32),
        pltpu.VMEM((2, tokens // 2, widest), f32), pltpu.VMEM((2, tokens // 2, widest), f32),
        pltpu.VMEM((2, tokens, widest), f32),
        kept(widest, bf16), kept(2 * rank, bf16), pltpu.VMEM((loops, 2, dp_size * 48, tokens), bf16),
        pltpu.VMEM((4, 2, line, block, tokens), f32), pltpu.VMEM((5, 2, line, rank_block, tokens), f32),
        pltpu.VMEM((6, tokens, WIDE), f32), pltpu.VMEM((2, tokens, head), f32),
        pltpu.VMEM((loops, width, 2 * rank), bf16), pltpu.VMEM((loops, width, 2 * rank), bf16),
        pltpu.VMEM((tokens, head // 2), f32), pltpu.VMEM((tokens, head // 2), f32),
        pltpu.VMEM((tokens, tokens), f32),
        dma((len(weights),)), dma((pieces,)), dma((pieces,)), dma((2, pieces)), dma((2, pieces)),
        dma((pieces,)), dma((pieces,)),
        dma((4, loops)), dma((5, loops)), dma((6, loops)), dma((2, loops)),
    ]
    scratch += [dma((2, loops))] * 2 + [dma((3, loops))] * 4
    scratch += [dma((2, loops))] * 4 + [dma((2, 2, loops))] * 2
    scratch += [dma((2,))] * 6 + [dma((loops,))] * 4
    return pl.pallas_call(
        block_kernel,
        out_shape=out_shape,
        in_specs=[vmem] * 5 + [hbm] * len(weights),
        out_specs=(vmem,) * 3 + (hbm,) * 10,
        scratch_shapes=scratch,
        compiler_params=pltpu.CompilerParams(
            collective_id=21, has_side_effects=True, vmem_limit_bytes=63 << 20
        ),
    )(
        block_input, cotangent, segments, mixer_gain, feed_gain,
        *weights,
    )


def line_kernel(
    raw_all, x_all, r_all, b_all, q_all, x_got, r_got, b_got, x_end_all, r_end_all, b_end_all,
    mixer_out, feed_out, q_w, pair_w, o_w, e_w, s_w, q_i, q_o, p_i, p_o, o_i, o_o, e_i, e_o, s_i, s_o,
    main_out, side_out, raw_out, around,
    x_own, r_own, b_own, q_own, x_far, r_far, b_far, q_far, x_end, r_end, b_end, raw_own, raw_far, product_ref,
    main_right, main_left, side_right, side_left, raw_right, raw_left,
    x_s, x_r, r_s, r_r, b_s, b_r, q_s, q_r, w_s, w_r, local_sems, step_sems, around_s, around_r,
    mr_s, mr_r, ml_s, ml_r, sr_s, sr_r, sl_s, sl_r, rr_s, rr_r, rl_s, rl_r,
    credit_right, credit_left,
):
    dp, mp = lax.axis_index("dp"), lax.axis_index("mp")
    x = lax.rem(dp, 2)
    z = dp // 2
    last = 3
    pair = (dp + 1 - 2 * x, mp)
    up, down = (dp + 2, mp), (dp - 2, mp)

    core, other = (dp, mp + 1 - 2 * lax.rem(mp, 2)), (dp, lax.rem(mp + 2, 4))
    hidden = s_w.shape[1]
    block, rank_block, quarter = s_w.shape[0], s_i.shape[1], pair_w.shape[0]
    loops, head = s_i.shape[0], q_w.shape[1]
    layout = raw_layout(quarter, rank_block // 4, loops)
    tall = layout.tall
    tail = hidden - WIDE
    short = 2 * hidden - 3 * WIDE

    barrier = pltpu.get_barrier_semaphore()
    for device in (pair, core, other):
        pl.semaphore_signal(barrier, inc=1, device_id=device, device_id_type=MESH)

    @pl.when(z > 0)
    def _():
        pl.semaphore_signal(barrier, inc=1, device_id=down, device_id_type=MESH)

    @pl.when(z < last)
    def _():
        pl.semaphore_signal(barrier, inc=1, device_id=up, device_id_type=MESH)

    pl.semaphore_wait(barrier, 3 + jnp.minimum(z, 1) + jnp.minimum(last - z, 1))

    def across(source, target, send, recv):
        return pltpu.make_async_remote_copy(
            source, target, send, recv, device_id=pair, device_id_type=MESH
        )

    def x_copy(i):
        return across(x_all.at[i, 1 - x], x_far.at[i], x_s.at[i - 2], x_r.at[i - 2])

    def r_copy(i):
        return across(r_all.at[i, 1 - x], r_far.at[i], r_s.at[i - 3], r_r.at[i - 3])

    def b_copy(i):
        return across(b_all.at[i], b_far.at[i], b_s.at[i], b_r.at[i])

    q_copy = across(q_all, q_far, q_s, q_r)
    w_copy = across(raw_all.at[1 - x], raw_far, w_s, w_r)

    def here(source, target, i):
        return pltpu.make_async_copy(source, target, local_sems.at[i])

    at_start = [
        here(x_all.at[:, x], x_own, 0),
        here(r_all.at[:, x], r_own, 1),
        here(x_got, x_far.at[0:2], 2),
        here(r_got, r_far.at[0:3], 3),
        here(b_got.at[0], b_far.at[0], 4),
        here(b_got.at[1:3], b_far.at[4:6], 5),
        here(q_all, q_own, 6),
    ]
    for_ends = [here(x_end_all, x_end, 7), here(r_end_all, r_end, 8), here(b_end_all, b_end, 9)]
    own_copy = here(raw_all.at[x], raw_own, 10)
    inner = jnp.logical_and(z > 0, z < last)

    def chunk_of(step):
        return jnp.where(lax.rem(step, 3) == 1, 4 + step // 3, step - (step + 1) // 3)

    def b_load(step):
        slot = lax.rem(step, 2)
        return pltpu.make_async_copy(b_all.at[chunk_of(step)], b_own.at[slot], step_sems.at[slot])

    b_copy(1).start()
    b_load(0).start()
    for copy in at_start:
        copy.start()

    @pl.when(inner)
    def _():
        for copy in for_ends:
            copy.start()

    own_copy.start()
    for copy in at_start[:5]:
        copy.wait()

    def chain(target, step, slot, steps, value, out, right, left, r_s, r_r, l_s, l_r, credits):
        def move(buffer, send, recv, i, s, device, size):
            piece = buffer.at[i, s, :, pl.ds(0, size)]
            return pltpu.make_async_remote_copy(
                piece, piece, send.at[i, s], recv.at[i, s], device_id=device, device_id_type=MESH
            )

        def at_size(act):
            full = right.shape[3]
            if credits:
                pl.when(step < steps - 1)(lambda: act(full))
                pl.when(step == steps - 1)(lambda: act(short))
            else:
                act(full)

        def inside(at):
            return lax.rem(at, 3) == 1 if credits else at < 0

        def free(credit, i, source, at, from_end):
            @pl.when(
                jnp.logical_and(
                    at <= steps - 1,
                    jnp.logical_not(jnp.logical_and(from_end, inside(at))),
                )
            )
            def _():
                pl.semaphore_signal(credit.at[i], inc=1, device_id=source, device_id_type=MESH)

        def pass_on(i, place, buffer, send, recv, onward, source, at_end, next_to_end, credit):
            def here(i, s, size=right.shape[3]):
                return move(buffer, send, recv, i, s, onward, size)

            def begin():
                if credits:

                    @pl.when(step >= 3)
                    def _():
                        pl.semaphore_wait(credit.at[i], 1)

                at_size(lambda size: here(i, slot, size).start())

            @pl.when(jnp.logical_and(at_end, jnp.logical_not(inside(step))))
            def _():
                buffer[i, slot] = value()
                if credits:
                    before = lax.rem(step + 2 - inside(step - 1).astype(jnp.int32), 3)
                    after = jnp.where(onward[0] > dp, i - 1, i + 1)

                    @pl.when(jnp.logical_and(place < 2, step >= 1))
                    def _():
                        here(after, before).wait_send()

                    @pl.when(place == 2)
                    def _():
                        at_size(lambda size: here(2 - i, slot, size).wait_send())

                    begin()
                else:
                    begin()
                    here(i, slot).wait_send()

            @pl.when(jnp.logical_not(at_end))
            def _():
                if credits:

                    @pl.when(step >= 1)
                    def _():
                        here(i, lax.rem(step + 2, 3)).wait_send()
                        free(credit, i, source, step + 2, next_to_end)

                has_source = jnp.logical_not(jnp.logical_and(next_to_end, inside(step)))

                @pl.when(jnp.logical_not(has_source))
                def _():
                    buffer[i, slot] = value()

                @pl.when(has_source)
                def _():
                    product = value()
                    at_size(lambda size: here(i, slot, size).wait_recv())
                    buffer[i, slot] += product

                begin()

        @pl.when(target > z)
        def _():
            pass_on(target - 1, 3 - target, right, r_s, r_r, up, down, z == 0, z == 1, credit_right)

        @pl.when(target < z)
        def _():
            pass_on(target, target, left, l_s, l_r, down, up, z == last, z == last - 1, credit_left)

        @pl.when(target == z)
        def _():
            out[...] = value()

    def arrive(step, slot, steps, out, right, left, r_s, r_r, l_s, l_r, credits):
        def take(buffer, send, recv, i, size):
            piece = buffer.at[i, slot, :, pl.ds(0, size)]
            pltpu.make_async_remote_copy(
                piece, piece, send.at[i, slot], recv.at[i, slot], device_id=pair, device_id_type=MESH
            ).wait_recv()
            out[:, :size] += buffer[i, slot, :, :size]

        started_inside = lax.rem(step, 3) == 1 if credits else step < 0

        def side_of(there, from_end, buffer, send, recv, i, credit, source):
            @pl.when(there)
            def _():
                quiet = jnp.logical_and(from_end, started_inside)

                @pl.when(jnp.logical_not(quiet))
                def _():
                    full = buffer.shape[3]
                    if credits:
                        pl.when(step < steps - 1)(lambda: take(buffer, send, recv, i, full))
                        pl.when(step == steps - 1)(lambda: take(buffer, send, recv, i, short))
                    else:
                        take(buffer, send, recv, i, full)

                if credits:
                    skip = jnp.logical_and(from_end, lax.rem(step + 3, 3) == 1)

                    @pl.when(jnp.logical_and(step + 3 <= steps - 1, jnp.logical_not(skip)))
                    def _():
                        pl.semaphore_signal(
                            credit.at[i], inc=1, device_id=source, device_id_type=MESH
                        )

        side_of(z > 0, z == 1, right, r_s, r_r, jnp.maximum(z - 1, 0), credit_right, down)
        side_of(z < last, z == last - 1, left, l_s, l_r, jnp.minimum(z, last - 1), credit_left, up)

    def settle(slot, right, left, r_s, l_s, main):
        def wait(buffer, send, i, device):
            piece = buffer.at[i, slot, :, pl.ds(0, short if main else buffer.shape[3])]
            pltpu.make_async_remote_copy(
                piece, piece, send.at[i, slot], send.at[i, slot], device_id=device, device_id_type=MESH
            ).wait_send()

        for target in range(4):
            rightmost, leftmost = target == 3, target == 0

            @pl.when(jnp.logical_and(target > z, jnp.logical_or(z > 0, main and not rightmost)))
            def _():
                wait(right, r_s, target - 1, up)

            @pl.when(jnp.logical_and(target < z, jnp.logical_or(z < last, main and not leftmost)))
            def _():
                wait(left, l_s, target, down)

    def order(turn):
        def near(end):
            return jnp.where(end == 0, 3 - turn, jnp.where(turn < 2, 3 - turn, turn - 2))

        return jnp.where(z < 2, near(z), 3 - near(3 - z))

    def dot(left, right):
        return jnp.dot(
            left.astype(jnp.bfloat16), right.astype(jnp.bfloat16), preferred_element_type=jnp.float32
        )

    steps = b_all.shape[0]

    def left_times(x_index, group, target, own, far):
        shared = dot(x_own[x_index, target], own) + dot(x_far[x_index, target], far)
        return [shared, *rank_times(group, target, own, far)]

    def rank_times(group, target, own, far):
        half = own.shape[0] // 2
        rank_own, rank_far = r_own[group, target], r_far[group, target]
        return [
            dot(rank_own[:, :half], own[:half]) + dot(rank_far[:, :half], far[:half]),
            dot(rank_own[:, half:], own[half:]) + dot(rank_far[:, half:], far[half:]),
        ]

    def main_arrive(step):
        slot = lax.rem(step, 3)
        chunk = chunk_of(step)
        arrive(
            step, slot, steps, main_out.at[slot], main_right, main_left, mr_s, mr_r, ml_s, ml_r, True,
        )
        parts = (
            (0, 0, 0, 0, WIDE), (1, 0, 0, WIDE, tail), (1, tail, 1, WIDE, WIDE - tail),
            (2, 0, 1, 0, WIDE), (3, 0, 1, 2 * WIDE - tail, short),
        )
        for which, start, j, at, n in parts:

            @pl.when(chunk == which)
            def _():
                e_w[:, j, at : at + n] = main_out[slot, :block, start : start + n]
                for l in range(loops):
                    first = block + l * rank_block
                    e_o[l, j, :, at : at + n] = main_out[
                        slot, first : first + rank_block, start : start + n
                    ]

        for part, (at, n) in enumerate(((0, WIDE), (WIDE, tail))):

            @pl.when(chunk == 4 + part)
            def _():
                s_w[:, at : at + n] = main_out[slot, :block, :n]
                for l in range(loops):
                    first = block + l * rank_block
                    s_i[l, :, at : at + n] = main_out[slot, first : first + rank_block, :n]

    def turn_body(at, carry):
        step, turn = at // 4, lax.rem(at, 4)
        slot = lax.rem(step, 3)
        chunk = chunk_of(step)
        group = chunk // 2
        target = order(turn)

        @pl.when(turn == 0)
        def _():
            b_load(step).wait()

            @pl.when(step < steps - 1)
            def _():
                b_load(step + 1).start()

            @pl.when(jnp.logical_and(chunk >= 1, chunk <= 3))
            def _():
                b_copy(chunk).wait_recv()

            @pl.when(step == 1)
            def _():
                b_copy(2).start()
                for copy in at_start[5:]:
                    copy.wait()

                @pl.when(inner)
                def _():
                    for copy in for_ends:
                        copy.wait()

            @pl.when(step == 2)
            def _():
                b_copy(3).start()

            @pl.when(step == 3)
            def _():
                w_copy.start()

            @pl.when(step == 4)
            def _():
                x_copy(2).start()
                x_copy(3).start()
                r_copy(3).start()
                r_copy(4).start()
                q_copy.start()

        def value():
            parts = left_times(
                group // 2, group, target,
                b_own[lax.rem(step, 2)].astype(jnp.bfloat16), b_far[chunk].astype(jnp.bfloat16),
            )
            product_ref[...] = jnp.concatenate(parts, axis=0)

            @pl.when(chunk == 1)
            def _():
                other_rank = rank_times(
                    1, target, b_own[lax.rem(step, 2)].astype(jnp.bfloat16),
                    b_far[1].astype(jnp.bfloat16),
                )
                kept = product_ref[block:]
                column = lax.broadcasted_iota(jnp.int32, kept.shape, 1)
                product_ref[block:] = jnp.where(
                    column < tail, kept, jnp.concatenate(other_rank, axis=0)
                )

            beyond = jnp.logical_or(
                jnp.logical_and(z == 1, target >= 1),
                jnp.logical_and(z == last - 1, target <= last - 1),
            )

            @pl.when(jnp.logical_and(beyond, chunk >= 4))
            def _():
                end = b_end[jnp.maximum(chunk - 4, 0)].astype(jnp.bfloat16)
                middle = end.shape[0] // 2
                product_ref[...] += jnp.concatenate(
                    [
                        dot(x_end[target], end),
                        dot(r_end[target, :, :middle], end[:middle]),
                        dot(r_end[target, :, middle:], end[middle:]),
                    ],
                    axis=0,
                )

            return product_ref[...]

        chain(
            target, step, slot, steps, value, main_out.at[slot], main_right, main_left,
            mr_s, mr_r, ml_s, ml_r, True,
        )

        @pl.when(jnp.logical_and(turn == 3, step >= 2))
        def _():
            main_arrive(step - 2)

        return carry

    lax.fori_loop(0, 4 * steps, turn_body, 0)

    w_copy.wait_recv()
    own_copy.wait()

    def raw_body(turn, carry):
        target = order(turn)
        chain(
            target, 0, 0, 1, lambda: raw_own[target] + raw_far[target], raw_out, raw_right, raw_left,
            rr_s, rr_r, rl_s, rl_r, False,
        )
        return carry

    lax.fori_loop(0, 4, raw_body, 0)
    main_arrive(jnp.int32(steps - 2))

    for i in (2, 3):
        x_copy(i).wait_recv()
    for i in (3, 4):
        r_copy(i).wait_recv()
    q_copy.wait_recv()

    def side_body(turn, carry):
        target = order(turn)

        def value():
            parts = [
                left_times(
                    2 + i, 3 + i, target, q_own[i].astype(jnp.bfloat16), q_far[i].astype(jnp.bfloat16)
                )
                for i in range(2)
            ]
            return jnp.concatenate([jnp.concatenate(p, axis=0) for p in parts], axis=1)

        chain(
            target, 0, 0, 1, value, side_out, side_right, side_left,
            sr_s, sr_r, sl_s, sl_r, False,
        )
        return carry

    lax.fori_loop(0, 4, side_body, 0)
    main_arrive(jnp.int32(steps - 1))
    arrive(0, 0, 1, raw_out, raw_right, raw_left, rr_s, rr_r, rl_s, rl_r, False)

    def share(device, owner, i):
        return pltpu.make_async_remote_copy(
            around.at[owner], around.at[owner], around_s.at[i], around_r.at[i],
            device_id=device, device_id_type=MESH,
        )

    far_owner = lax.rem(mp + 2, 4)
    for l in range(loops):
        start = 2 * tall + l * layout.loop + 5 * tall
        around[mp, l] = raw_out[start : start + 2 * tall]
    along, same, passed = share(other, mp, 0), share(core, mp, 1), share(core, far_owner, 2)
    along.start()
    same.start()
    arrive(0, 0, 1, side_out, side_right, side_left, sr_s, sr_r, sl_s, sl_r, False)
    along.wait_recv()
    passed.start()
    q_w[...] = side_out[:block, :head]
    o_w[...] = side_out[:block, head:]
    for l in range(loops):
        start = block + l * rank_block
        q_o[l] = side_out[start : start + rank_block, :head]
        o_i[l] = side_out[start : start + rank_block, head:]
    mixer_out[...] = raw_out[layout.gains, :block]
    feed_out[...] = raw_out[layout.gains + 1, :block]
    for j in range(2):
        pair_w[:, j * head : (j + 1) * head] = raw_out[j * tall : j * tall + quarter]
    for l in range(loops):
        base = 2 * tall + l * layout.loop
        q_i[:, l] = raw_out[base : base + quarter]
        for j in range(2):
            start = base + (1 + j) * tall
            p_i[l, :, j] = raw_out[start : start + quarter]
            e_i[l, :, j] = raw_out[start + 2 * tall : start + 2 * tall + quarter]
            start = base + 7 * tall + j * (rank_block // 4)
            p_o[l, j] = raw_out[start : start + rank_block // 4]
    same.wait_recv()
    passed.wait_recv()
    for l in range(loops):
        for m in range(4):
            o_o[l, m * quarter : (m + 1) * quarter] = around[m, l, :quarter]
            s_o[l, m * quarter : (m + 1) * quarter] = around[m, l, tall : tall + quarter]
    for copy in (along, same, passed):
        copy.wait_send()

    settle((steps - 1) % 3, main_right, main_left, mr_s, ml_s, True)
    settle(0, side_right, side_left, sr_s, sl_s, False)
    settle(0, raw_right, raw_left, rr_s, rl_s, False)
    for copy in (x_copy(2), x_copy(3), r_copy(3), r_copy(4), b_copy(1), b_copy(2), b_copy(3)):
        copy.wait_send()
    q_copy.wait_send()
    w_copy.wait_send()


def line_gradients(factors, loops, dp_size, mp_size, hidden):
    raw, x_all, r_all, b_all, q_all, x_got, r_got, b_got, x_end, r_end, b_end = factors
    block, rank_block, head = x_all.shape[3], r_all.shape[3], q_all.shape[2]
    quarter, rank_quarter = block // mp_size, rank_block // mp_size
    layout = raw_layout(quarter, rank_quarter, loops)
    rows = block + loops * rank_block
    steps = b_all.shape[0]
    vmem = pl.BlockSpec(memory_space=pltpu.VMEM)
    hbm = pl.BlockSpec(memory_space=pl.ANY)
    dma = pltpu.SemaphoreType.DMA
    f32 = jnp.float32
    line = dp_size // 2 - 1
    half_x = pltpu.VMEM((x_all.shape[0], *x_all.shape[2:]), f32)
    half_r = pltpu.VMEM((r_all.shape[0], *r_all.shape[2:]), f32)
    whole_b, whole_q = pltpu.VMEM(b_all.shape, f32), pltpu.VMEM(q_all.shape, f32)
    shapes = (
        (block,), (block,), (block, head), (quarter, 2 * head), (block, head), (block, 2, hidden),
        (block, hidden), (quarter, loops, head), (loops, rank_block, head), (loops, quarter, 2, head),
        (loops, 2, rank_quarter, head), (loops, rank_block, head), (loops, block, head),
        (loops, quarter, 2, head), (loops, 2, rank_block, hidden), (loops, rank_block, hidden),
        (loops, block, head),
    )
    return pl.pallas_call(
        line_kernel,
        out_shape=tuple(jax.ShapeDtypeStruct(v, f32) for v in shapes),
        in_specs=[hbm] * 11,
        out_specs=(vmem,) * len(shapes),
        scratch_shapes=[
            pltpu.VMEM((3, rows, WIDE), f32), pltpu.VMEM((rows, 2 * head), f32),
            pltpu.VMEM((layout.all, head), f32), pltpu.VMEM((4, loops, 2 * layout.tall, head), f32),
        ]
        + [half_x, half_r, pltpu.VMEM((2, *b_all.shape[1:]), f32), whole_q]
        + [half_x, half_r, whole_b, whole_q]
        + [pltpu.VMEM(v.shape, f32) for v in (x_end, r_end, b_end)]
        + [pltpu.VMEM(raw.shape[1:], f32)] * 2
        + [pltpu.VMEM((rows, WIDE), f32)]
        + [pltpu.VMEM((line, 3, rows, WIDE), f32)] * 2
        + [pltpu.VMEM((line, 1, rows, 2 * head), f32)] * 2
        + [pltpu.VMEM((line, 1, layout.all, head), f32)] * 2
        + [dma((2,))] * 4 + [dma((steps,))] * 2 + [dma] * 4 + [dma((11,)), dma((2,)), dma((3,)), dma((3,))]
        + [dma((line, 3))] * 4 + [dma((line, 1))] * 8
        + [pltpu.SemaphoreType.REGULAR((line,))] * 2,
        compiler_params=pltpu.CompilerParams(
            collective_id=20, has_side_effects=True, vmem_limit_bytes=63 << 20
        ),
    )(*factors)


def in_place(results):
    mixer, feed, q_w, pair_w, o_w, e_w, s_w, q_i, q_o, p_i, p_o, o_i, o_o, e_i, e_o, s_i, s_o = results
    return (
        mixer, feed, q_w, pair_w, o_w.T, e_w, s_w.T, q_i.swapaxes(0, 1), q_o, p_i, p_o,
        o_i.swapaxes(1, 2), o_o.swapaxes(1, 2), e_i, e_o, s_i.swapaxes(1, 2), s_o.swapaxes(1, 2),
    )


def copy_kernel(*refs):
    count = (len(refs) - 2) // 3
    sources, targets, rooms = refs[:count], refs[count : 2 * count], refs[2 * count : 3 * count]
    come = [pltpu.make_async_copy(v, room, refs[-2].at[i]) for i, (v, room) in enumerate(zip(sources, rooms))]
    go = [pltpu.make_async_copy(room, v, refs[-1].at[i]) for i, (v, room) in enumerate(zip(targets, rooms))]
    for copy in come:
        copy.start()
    for first, second in zip(come, go):
        first.wait()
        second.start()
    for copy in go:
        copy.wait()


def placed(values):
    hbm = pl.BlockSpec(memory_space=pl.ANY)
    sems = pltpu.SemaphoreType.DMA((len(values),))
    return pl.pallas_call(
        copy_kernel,
        out_shape=tuple(jax.ShapeDtypeStruct(v.shape, v.dtype) for v in values),
        in_specs=[hbm] * len(values),
        out_specs=(hbm,) * len(values),
        scratch_shapes=[pltpu.VMEM(v.shape, v.dtype) for v in values] + [sems, sems],
        compiler_params=pltpu.CompilerParams(vmem_limit_bytes=60 << 20),
    )(*values)


def per_device(dp_size, mp_size, block_input, cotangent, segments, *parameters):
    shared, stacked = parameters[:7], parameters[7:]
    loops = stacked[0].shape[0]
    if dp_size == 8 and mp_size == 4 and loops == 2:
        output, input_grad, *factors = block_and_factors(
            block_input, cotangent, segments, shared, stacked, dp_size
        )
        gradients = line_gradients(factors, loops, dp_size, mp_size, shared[6].shape[0])
        output, input_grad, *gradients = placed((output, input_grad, *gradients))
        gradients = in_place(gradients)
        return (output, input_grad, *gradients)
    tables = rotary_tables(segments[0], shared[3].shape[1] // 2)
    total = mp_total(mp_size)
    state = block_input.astype(jnp.float32)
    kept_all = []
    for i in range(loops):
        state, kept = forward_loop(state, shared, [v[i] for v in stacked], tables, total, 1)
        kept_all.append(kept)
    upstream = cotangent.astype(jnp.float32)
    for i in reversed(range(loops)):
        upstream = reverse_loop(
            upstream, kept_all[i], shared, [v[i] for v in stacked], tables, total, 3
        )
    return (state.astype(jnp.bfloat16), upstream, *scattered_gradients(kept_all, dp_size, mp_size))


def solution(mesh):
    in_specs = (
        P("dp", None),
        P("dp", None),
        P("dp", None),
        P(),
        P(),
        P(None, "mp"),
        P(),
        P("mp", None),
        P(None, None, "mp"),
        P("mp", None),
        P(),
        P(None, None, "mp"),
        P(),
        P(),
        P(None, "mp", None),
        P(),
        P(),
        P(None, None, None, "mp"),
        P(None, "mp", None),
        P(),
    )
    out_specs = (
        P("dp", None),
        P("dp", None),
        P("dp"),
        P("dp"),
        P("dp", "mp"),
        P(("dp", "mp"), None),
        P("mp", "dp"),
        P("dp", None, "mp"),
        P("mp", "dp"),
        P(None, ("dp", "mp"), None),
        P(None, "dp", "mp"),
        P(None, ("dp", "mp"), None, None),
        P(None, None, ("dp", "mp"), None),
        P(None, "mp", "dp"),
        P(None, None, "dp"),
        P(None, ("dp", "mp"), None, None),
        P(None, None, "dp", "mp"),
        P(None, "mp", "dp"),
        P(None, None, "dp"),
    )
    return jax.shard_map(
        functools.partial(per_device, mesh.shape["dp"], mesh.shape["mp"]),
        mesh=mesh, in_specs=in_specs, out_specs=out_specs, check_vma=False
    )
```

```python
import functools
import math
from types import SimpleNamespace

import jax
import jax.numpy as jnp
from jax import lax
from jax.experimental import pallas as pl
from jax.experimental.pallas import tpu as pltpu
from jax.sharding import PartitionSpec as P

EPSILON = 1e-06
MASKED = -1e30
MESH = pl.DeviceIdType.MESH


def product(left, right):
    return jnp.dot(left, right, preferred_element_type=jnp.float32)


def product_t(left, right):
    return lax.dot_general(
        left, right, (((1,), (1,)), ((), ())), preferred_element_type=jnp.float32
    )


def product_tn(left, right):
    return lax.dot_general(
        left, right, (((0,), (0,)), ((), ())), preferred_element_type=jnp.float32
    )


def exact_product(left, right):
    return jnp.dot(left, right, precision=lax.Precision.HIGHEST, preferred_element_type=jnp.float32)


def exact_tn(left, right):
    return lax.dot_general(
        left,
        right,
        (((0,), (0,)), ((), ())),
        precision=lax.Precision.HIGHEST,
        preferred_element_type=jnp.float32,
    )


def normalize(hidden_state, gain):
    factor = lax.rsqrt(jnp.mean(hidden_state * hidden_state, axis=-1, keepdims=True) + EPSILON)
    return (hidden_state * factor * gain, factor)


def normalize_back(hidden_state, factor, gain, upstream_gradient):
    unit = hidden_state * factor
    scaled = upstream_gradient * gain
    downstream = factor * (scaled - unit * jnp.mean(scaled * unit, axis=-1, keepdims=True))
    return (downstream, jnp.sum(upstream_gradient * unit, axis=0))


def rotate(values, cosine_table, sine_table):
    half_width = values.shape[-1] // 2
    first = values[..., :half_width]
    second = values[..., half_width:]
    return jnp.concatenate(
        [first * cosine_table - second * sine_table, second * cosine_table + first * sine_table],
        axis=-1,
    )


def rotary_tables(segment_row, head_size):
    length_value = segment_row.shape[0]
    earlier = jnp.sum((segment_row[None, :] < segment_row[:, None]).astype(jnp.int32), axis=1)
    position = (jnp.arange(length_value, dtype=jnp.int32) - earlier).astype(jnp.float32)
    steps_half = jnp.arange(head_size // 2, dtype=jnp.float32)
    frequency = 10000.0 ** (-2.0 * steps_half / head_size)
    angles = position[:, None] * frequency[None, :]
    same_segment = segment_row[:, None] == segment_row[None, :]
    ordinal = jnp.arange(length_value, dtype=jnp.int32)
    allowed_mask = same_segment & (ordinal[:, None] >= ordinal[None, :])
    return (jnp.cos(angles), jnp.sin(angles), allowed_mask)


def gelu_tanh(values):
    return jax.nn.gelu(values, approximate=True)


def attention_probs(queries, keys, allowed_mask, score_scale):
    scores = (
        jnp.einsum("ihd,jd->hij", queries, keys, preferred_element_type=jnp.float32) * score_scale
    )
    return jnp.where(allowed_mask[None], scores, MASKED)


def mp_total(size):
    def kernel(part, out, near, mine, far, core_send, core_recv, y_send, y_recv, back_send, back_recv):
        dp, mp = lax.axis_index("dp"), lax.axis_index("mp")
        side = lax.rem(mp, 2)
        core = (dp, mp + 1 - 2 * side)
        other = (dp, lax.rem(mp + 2, 4))
        half = part.shape[0] // 2
        pieces = near.shape[0]
        width = part.shape[1] // pieces
        own = pl.ds(pl.multiple_of(side * half, half), half)
        theirs = pl.ds(pl.multiple_of((1 - side) * half, half), half)

        def columns(i):
            return pl.ds(i * width, width)

        barrier = pltpu.get_barrier_semaphore()
        for device in (core, other):
            pl.semaphore_signal(barrier, inc=1, device_id=device, device_id_type=MESH)
        pl.semaphore_wait(barrier, 2)
        first = [
            pltpu.make_async_remote_copy(
                part.at[theirs, columns(i)], near.at[i], core_send.at[i], core_recv.at[i],
                device_id=core, device_id_type=MESH,
            )
            for i in range(pieces)
        ]
        second = [
            pltpu.make_async_remote_copy(
                mine.at[i], far.at[i], y_send.at[i], y_recv.at[i],
                device_id=other, device_id_type=MESH,
            )
            for i in range(pieces)
        ]
        third = [
            pltpu.make_async_remote_copy(
                out.at[own, columns(i)], out.at[own, columns(i)], back_send.at[i], back_recv.at[i],
                device_id=core, device_id_type=MESH,
            )
            for i in range(pieces)
        ]
        for copy in first:
            copy.start()
        for i in range(pieces):
            first[i].wait_recv()
            mine[i] = part[own, columns(i)] + near[i]
            second[i].start()
        for i in range(pieces):
            second[i].wait_recv()
            out[own, columns(i)] = mine[i] + far[i]
            third[i].start()
        for copy in third:
            copy.wait_recv()
        for copy in first + second + third:
            copy.wait_send()

    def total(identity, *parts):
        if size != 4:
            return lax.psum(parts, "mp")
        joined = jnp.concatenate(parts, axis=1)
        tokens_here, columns_here = joined.shape
        pieces = 1
        for count in (5, 4, 3, 2):
            if columns_here % (128 * count) == 0:
                pieces = count
                break
        half = (pieces, tokens_here // 2, columns_here // pieces)
        summed = pl.pallas_call(
            kernel,
            out_shape=jax.ShapeDtypeStruct(joined.shape, jnp.float32),
            in_specs=[pl.BlockSpec(memory_space=pltpu.VMEM)],
            out_specs=pl.BlockSpec(memory_space=pltpu.VMEM),
            scratch_shapes=[pltpu.VMEM(half, jnp.float32)] * 3
            + [pltpu.SemaphoreType.DMA((pieces,))] * 6,
            compiler_params=pltpu.CompilerParams(
                collective_id=identity, has_side_effects=True, vmem_limit_bytes=16 << 20
            ),
        )(joined)
        edges, start = [], 0
        for part in parts:
            edges.append(summed[:, start : start + part.shape[1]])
            start += part.shape[1]
        return tuple(edges)

    return total


def forward_loop(hidden_state, shared, adapters, tables, total, identity):
    (mixer_gain, feed_gain, query_matrix, pair_matrix, output_matrix, widen_matrix, down_matrix) = shared
    (q_in, q_out, kv_in, kv_out, o_in, o_out, w_in, w_out, d_in, d_out) = adapters
    cosine, sine, allowed = tables
    tokens_here, width = hidden_state.shape
    head = pair_matrix.shape[1] // 2
    heads = query_matrix.shape[1] // head
    rank = q_in.shape[1]
    hidden = down_matrix.shape[0]
    kept = SimpleNamespace(h=hidden_state)
    normed, kept.mixer_factor = normalize(hidden_state, mixer_gain)
    normed = normed.astype(jnp.bfloat16)
    query_rank = product(normed, q_in).astype(jnp.bfloat16)
    query_linear = product(normed, query_matrix) + product(query_rank, q_out)
    pair_rank = product(normed, kv_in.reshape(width, 2 * rank)).astype(jnp.bfloat16)
    pair_linear = product(normed, pair_matrix) + jnp.concatenate(
        [product(pair_rank[:, :rank], kv_out[0]), product(pair_rank[:, rank:], kv_out[1])], axis=1
    )
    queries = rotate(
        query_linear.reshape(tokens_here, heads, head), cosine[:, None], sine[:, None]
    ).astype(jnp.bfloat16)
    keys = rotate(pair_linear[:, :head], cosine, sine).astype(jnp.bfloat16)
    values = pair_linear[:, head:].astype(jnp.bfloat16)
    masked = attention_probs(queries, keys, allowed, 1.0 / math.sqrt(head))
    expo = jnp.exp(masked - jnp.max(masked, axis=-1, keepdims=True))
    probs = expo / jnp.sum(expo, axis=-1, keepdims=True)
    mixed = jnp.einsum(
        "hij,jd->ihd", probs.astype(jnp.bfloat16), values, preferred_element_type=jnp.float32
    )
    mixed = mixed.reshape(tokens_here, heads * head).astype(jnp.bfloat16)
    summed, output_rank = total(identity, product(mixed, output_matrix), product(mixed, o_in))
    middle = hidden_state + summed + exact_product(output_rank, o_out.astype(jnp.float32))
    fed, kept.feed_factor = normalize(middle, feed_gain)
    fed = fed.astype(jnp.bfloat16)
    widen_rank = product(fed, w_in.reshape(width, 2 * rank)).astype(jnp.bfloat16)
    gate = product(fed, widen_matrix[:, 0]) + product(widen_rank[:, :rank], w_out[0])
    up = product(fed, widen_matrix[:, 1]) + product(widen_rank[:, rank:], w_out[1])
    activated = (gelu_tanh(gate) * up).astype(jnp.bfloat16)
    shrunk, shrink_rank = total(identity + 1, product(activated, down_matrix), product(activated, d_in))
    result = middle + shrunk + exact_product(shrink_rank, d_out.astype(jnp.float32))
    vars(kept).update(
        normed=normed, query_rank=query_rank, pair_rank=pair_rank, queries=queries, keys=keys,
        values=values, probs=probs, mixed=mixed, output_rank=output_rank, middle=middle, fed=fed,
        widen_rank=widen_rank, gate=gate, up=up, activated=activated, shrink_rank=shrink_rank,
    )
    return result, kept


def reverse_loop(upstream, kept, shared, adapters, tables, total, identity):
    (mixer_gain, feed_gain, query_matrix, pair_matrix, output_matrix, widen_matrix, down_matrix) = shared
    (q_in, q_out, kv_in, kv_out, o_in, o_out, w_in, w_out, d_in, d_out) = adapters
    cosine, sine, allowed = tables
    tokens_here, width = upstream.shape
    head = pair_matrix.shape[1] // 2
    heads = query_matrix.shape[1] // head
    rank = q_in.shape[1]
    scale = 1.0 / math.sqrt(head)
    grad_feed = upstream.astype(jnp.bfloat16)
    grad_shrink_rank = product_t(grad_feed, d_out).astype(jnp.bfloat16)
    grad_activated = product_t(grad_feed, down_matrix) + product_t(grad_shrink_rank, d_in)
    gelu_value, gelu_pullback = jax.vjp(gelu_tanh, kept.gate)
    grad_gate = gelu_pullback(grad_activated * kept.up)[0].astype(jnp.bfloat16)
    grad_up = (grad_activated * gelu_value).astype(jnp.bfloat16)
    grad_fed, grad_widen_rank = total(
        identity,
        product_t(grad_gate, widen_matrix[:, 0]) + product_t(grad_up, widen_matrix[:, 1]),
        jnp.concatenate([product_t(grad_gate, w_out[0]), product_t(grad_up, w_out[1])], axis=1),
    )
    grad_widen_rank = grad_widen_rank.astype(jnp.bfloat16)
    grad_fed = grad_fed + product_t(grad_widen_rank, w_in.reshape(width, 2 * rank))
    grad_norm, feed_gain_grad = normalize_back(kept.middle, kept.feed_factor, feed_gain, grad_fed)
    grad_middle = upstream + grad_norm
    grad_attend = grad_middle.astype(jnp.bfloat16)
    grad_output_rank = product_t(grad_attend, o_out).astype(jnp.bfloat16)
    grad_mixed = product_t(grad_attend, output_matrix) + product_t(grad_output_rank, o_in)
    grad_mixed = grad_mixed.astype(jnp.bfloat16).reshape(tokens_here, heads, head)
    queries, keys, values, probs = kept.queries, kept.keys, kept.values, kept.probs
    grad_probs = jnp.einsum("ihd,jd->hij", grad_mixed, values, preferred_element_type=jnp.float32)
    delta = jnp.sum(grad_probs * probs, axis=-1, keepdims=True)
    grad_scores = (probs * (grad_probs - delta)).astype(jnp.bfloat16)
    grad_queries = scale * jnp.einsum(
        "hij,jd->ihd", grad_scores, keys, preferred_element_type=jnp.float32
    )
    grad_keys = scale * jnp.einsum(
        "hij,ihd->jd", grad_scores, queries, preferred_element_type=jnp.float32
    )
    grad_values = jnp.einsum(
        "hij,ihd->jd", probs.astype(jnp.bfloat16), grad_mixed, preferred_element_type=jnp.float32
    )
    grad_query = rotate(grad_queries, cosine[:, None], -sine[:, None])
    grad_query = grad_query.reshape(tokens_here, heads * head).astype(jnp.bfloat16)
    grad_normed, grad_query_rank, grad_pair = total(
        identity + 1,
        product_t(grad_query, query_matrix),
        product_t(grad_query, q_out),
        jnp.concatenate([rotate(grad_keys, cosine, -sine), grad_values], axis=1),
    )
    grad_query_rank = grad_query_rank.astype(jnp.bfloat16)
    grad_pair = grad_pair.astype(jnp.bfloat16)
    grad_pair_rank = jnp.concatenate(
        [product_t(grad_pair[:, :head], kv_out[0]), product_t(grad_pair[:, head:], kv_out[1])], axis=1
    ).astype(jnp.bfloat16)
    grad_normed = (
        grad_normed
        + product_t(grad_query_rank, q_in)
        + product_t(grad_pair, pair_matrix)
        + product_t(grad_pair_rank, kv_in.reshape(width, 2 * rank))
    )
    grad_norm, mixer_gain_grad = normalize_back(
        kept.h, kept.mixer_factor, mixer_gain, grad_normed
    )
    vars(kept).update(
        grad_feed=grad_feed, grad_shrink_rank=grad_shrink_rank, grad_gate=grad_gate, grad_up=grad_up,
        grad_widen_rank=grad_widen_rank, grad_attend=grad_attend, grad_output_rank=grad_output_rank,
        grad_query=grad_query, grad_query_rank=grad_query_rank, grad_pair=grad_pair,
        grad_pair_rank=grad_pair_rank, feed_gain_grad=feed_gain_grad, mixer_gain_grad=mixer_gain_grad,
    )
    return grad_middle + grad_norm


def scattered_gradients(kept, dp_size, mp_size):
    def scatter(value, axis):
        return lax.psum_scatter(value, "dp", scatter_dimension=axis, tiled=True)

    def shared_of(factors):
        return sum(product_tn(*factors(k)) for k in kept)

    def each(function):
        return jnp.stack([function(k) for k in kept], axis=0)

    def quarter(value, axis):
        block = scatter(value, axis)
        size = block.shape[axis] // mp_size
        return lax.dynamic_slice_in_dim(block, lax.axis_index("mp") * size, size, axis)

    width = kept[0].normed.shape[1]
    rank = kept[0].query_rank.shape[1]
    head = kept[0].grad_pair.shape[1] // 2

    def pair_outer(k):
        left, right = k.pair_rank, k.grad_pair
        return jnp.stack(
            [product_tn(left[:, :rank], right[:, :head]), product_tn(left[:, rank:], right[:, head:])]
        )

    def expand_outer(k):
        left = k.widen_rank
        return jnp.stack(
            [product_tn(left[:, :rank], k.grad_gate), product_tn(left[:, rank:], k.grad_up)]
        )

    return (
        scatter(sum(k.mixer_gain_grad for k in kept), 0),
        scatter(sum(k.feed_gain_grad for k in kept), 0),
        scatter(shared_of(lambda k: (k.normed, k.grad_query)), 0),
        quarter(shared_of(lambda k: (k.normed, k.grad_pair)), 0),
        scatter(shared_of(lambda k: (k.mixed, k.grad_attend)), 1),
        scatter(jnp.stack([shared_of(lambda k: (k.fed, k.grad_gate)), shared_of(lambda k: (k.fed, k.grad_up))], axis=1), 0),
        scatter(shared_of(lambda k: (k.activated, k.grad_feed)), 1),
        quarter(each(lambda k: product_tn(k.normed, k.grad_query_rank)), 1),
        scatter(each(lambda k: product_tn(k.query_rank, k.grad_query)), 1),
        quarter(
            each(lambda k: product_tn(k.normed, k.grad_pair_rank).reshape(width, 2, rank)), 1
        ),
        quarter(each(pair_outer), 2),
        scatter(each(lambda k: product_tn(k.mixed, k.grad_output_rank)), 2),
        scatter(
            each(lambda k: exact_tn(k.output_rank, k.grad_attend.astype(jnp.float32))), 2
        ),
        quarter(
            each(lambda k: product_tn(k.fed, k.grad_widen_rank).reshape(width, 2, rank)), 1
        ),
        scatter(each(expand_outer), 2),
        scatter(each(lambda k: product_tn(k.activated, k.grad_shrink_rank)), 2),
        scatter(each(lambda k: exact_tn(k.shrink_rank, k.grad_feed.astype(jnp.float32))), 2),
    )


WIDE = 896


def split3(value):
    high = value.astype(jnp.bfloat16)
    rest = value - high.astype(jnp.float32)
    middle = rest.astype(jnp.bfloat16)
    low = (rest - middle.astype(jnp.float32)).astype(jnp.bfloat16)
    return high, middle, low


WEIGHTS = (
    "q_in", "query", "q_out", "kv_in", "pair", "kv_out", "output", "o_in", "o_out",
    "wide", "w_out", "down", "d_in", "d_out", "w_in",
)
SUM_STEP = 384


def block_kernel(*refs):
    (h_in, cot, segments, mixer_gain, feed_gain), refs = refs[:5], refs[5:]
    count = len(WEIGHTS)
    sources, refs = refs[:count], refs[count:]
    (
        out_ref, grad_ref, raw_ref, x_all, r_all, b_all, q_all, x_got, r_got, b_got, x_end, r_end, b_end,
    ), refs = refs[:13], refs[13:]
    weights, refs = (*refs[: count - 1], refs[WEIGHTS.index("kv_in")]), refs[count - 1 :]
    (
        h_s, mid_s, normed_s, qr_s, kvr_s, q_s, k_s, v_s, probs_s, mixed_s, or_s, fed_s, er_s,
        gate_s, up_s, act_s, sr_s, gg_s, gu_s, g_s, gain_s, select,
        part, total, near, mine, far, side_part, side_near, side_mine, side_far, side_total,
        late_s, er_grad_s, chosen_s, xs, rs, bs, qs, kv_flat, w_flat, cosine_ref, sine_ref, mask_ref,
        load_sems, c_s, c_r, y_s, y_r, e_s, e_r,
        xl, rl, bl, ql, x_s, x_r, r_s, r_r, b_s, b_r, xe_s, xe_r, re_s, re_r, be_s, be_r, bf_s, bf_r,
        sc_s, sc_r, sy_s, sy_r, se_s, se_r, xc_s, xc_r, rc_s, rc_r,
    ) = refs
    W = SimpleNamespace(**dict(zip(WEIGHTS, weights)))
    dp, mp = lax.axis_index("dp"), lax.axis_index("mp")
    side = lax.rem(mp, 2)
    core = (dp, mp + 1 - 2 * side)
    other = (dp, lax.rem(mp + 2, 4))
    loads = [
        pltpu.make_async_copy(source, target, load_sems.at[i])
        for i, (source, target) in enumerate(zip(sources, weights))
    ]
    load = SimpleNamespace(**dict(zip(WEIGHTS, loads)))
    for copy in loads[:-1]:
        copy.start()
    x = lax.rem(dp, 2)
    z = dp // 2
    pair = (dp + 1 - 2 * x, mp)
    near_end = (dp + 2 - 4 * lax.rem(z, 2), mp)
    is_end = jnp.logical_or(z == 0, z == 3)
    barrier = pltpu.get_barrier_semaphore()
    for device in (core, other, pair, near_end):
        pl.semaphore_signal(barrier, inc=1, device_id=device, device_id_type=MESH)
    pl.semaphore_wait(barrier, 4)

    tokens, width = h_in.shape
    half = tokens // 2
    head = W.query.shape[1]
    rank = W.q_in.shape[2]
    hidden = W.down.shape[0]
    loops = W.q_in.shape[0]
    scale = 1.0 / math.sqrt(head)
    own = pl.ds(pl.multiple_of(side * half, half), half)
    theirs = pl.ds(pl.multiple_of((1 - side) * half, half), half)
    blocks = x_all.shape[1] * x_all.shape[2]
    block = width // blocks
    quarter = block // 4
    rank_quarter = rank // (4 * blocks)
    chunks = [(0, WIDE), (WIDE, hidden - WIDE)]

    def remote(source, target, send, recv, device):
        return pltpu.make_async_remote_copy(
            source, target, send, recv, device_id=device, device_id_type=MESH
        )

    def span(l):
        return pl.ds(pl.multiple_of(l * tokens, tokens), tokens)

    def end_span(l, is_far):
        return pl.ds(pl.multiple_of((2 * l + is_far) * tokens, tokens), tokens)

    def x_copies(i, l):
        across = onward = None
        if i < 2:
            across = remote(
                xs.at[i, 1 - x], x_got.at[i, :, :, span(l)], x_s.at[i, l], x_r.at[i, l], pair
            )
            onward = remote(
                xs.at[i, x], x_end.at[i, :, :, end_span(l, 0)],
                xe_s.at[0, i, l], xe_r.at[0, i, l], near_end,
            )
        return pltpu.make_async_copy(xs.at[i], x_all.at[i, :, :, :, span(l)], xl.at[i, l]), across, onward

    def r_copies(i, l):
        across = onward = None
        if i < 3:
            across = remote(
                rs.at[i, 1 - x], r_got.at[i, :, :, span(l)], r_s.at[i, l], r_r.at[i, l], pair
            )
        if i in (1, 2):
            onward = remote(
                rs.at[i, x], r_end.at[i - 1, :, :, end_span(l, 0)],
                re_s.at[0, i - 1, l], re_r.at[0, i - 1, l], near_end,
            )
        return pltpu.make_async_copy(rs.at[i], r_all.at[i, :, :, :, span(l)], rl.at[i, l]), across, onward

    def b_copies(i, l):
        across = onward = None
        if i in (0, 4, 5):
            k = max(0, i - 3)
            across = remote(bs.at[i], b_got.at[k, span(l)], b_s.at[k, l], b_r.at[k, l], pair)
        if i >= 3:
            k = (i - 4) % 3
            onward = remote(
                bs.at[i], b_end.at[k, end_span(l, 0)], be_s.at[k, l], be_r.at[k, l], near_end
            )
        return pltpu.make_async_copy(bs.at[i], b_all.at[i, span(l)], bl.at[i, l]), across, onward

    def q_copies(i, l):
        return pltpu.make_async_copy(qs.at[i], q_all.at[i, span(l)], ql.at[i, l]), None, None

    def launch(copies, whole=True):
        local, across, onward = copies
        local.start()
        if across is not None:
            across.start()
        if onward is not None:

            @pl.when(is_end if whole else jnp.logical_and(is_end, side == 0))
            def _():
                onward.start()

    def finish(copies, whole=True):
        local, across, onward = copies
        local.wait()
        if across is not None:
            across.wait_send()
        if onward is not None:

            @pl.when(is_end if whole else jnp.logical_and(is_end, side == 0))
            def _():
                onward.wait_send()

    def far_rows(i, l):
        return [
            remote(
                x_got.at[i, :, :, span(l)], x_end.at[i, :, :, end_span(l, 1)],
                xe_s.at[1, i, l], xe_r.at[1, i, l], near_end,
            ),
            remote(
                r_got.at[i + 1, :, :, span(l)], r_end.at[i, :, :, end_span(l, 1)],
                re_s.at[1, i, l], re_r.at[1, i, l], near_end,
            ),
        ]

    def far_act(l):
        return remote(
            b_got.at[1, span(l)], b_end.at[0, end_span(l, 1)], bf_s.at[l], bf_r.at[l], near_end
        )

    def pass_act(l):
        for i in (4, 5):
            b_copies(i, l)[1].wait_recv()

        @pl.when(is_end)
        def _():
            far_act(l).start()

    def pass_rows(i, l):
        x_copies(i, l)[1].wait_recv()
        r_copies(i + 1, l)[1].wait_recv()

        @pl.when(jnp.logical_and(is_end, side == 1))
        def _():
            for copy in far_rows(i, l):
                copy.start()

    def ship_x(i, l, value, again, before):
        @pl.when(again)
        def _():
            finish(x_copies(i, before), False)

        turned = value.astype(jnp.float32).T
        for b in range(blocks):
            xs[i, b % 2, b // 2] = turned[b * block : (b + 1) * block]
        launch(x_copies(i, l), False)

    def ship_r(i, l, value, again, before):
        @pl.when(again)
        def _():
            finish(r_copies(i, before), False)

        turned = value.astype(jnp.float32).T
        size = rank // blocks
        for b in range(blocks):
            rs[i, b % 2, b // 2] = turned[b * size : (b + 1) * size]
        launch(r_copies(i, l), False)

    def ship_b(i, l, values, again, before):
        @pl.when(again)
        def _():
            finish(b_copies(i, before))

        filled = 0
        for value in values:
            n = value.shape[1]
            bs[i, :, filled : filled + n] = value.astype(jnp.float32)
            filled += n
        if filled < WIDE:
            bs[i, :, filled:] = jnp.zeros((tokens, WIDE - filled), jnp.float32)
        launch(b_copies(i, l))

    def ship_q(i, l, value, again, before):
        @pl.when(again)
        def _():
            finish(q_copies(i, before))

        qs[i] = value.astype(jnp.float32)
        launch(q_copies(i, l))

    def columns_of(size):
        return [(at, min(SUM_STEP, size - at)) for at in range(0, size, SUM_STEP)]

    def side_copies(turn, size):
        columns = pl.ds(0, size)
        return (
            remote(
                side_part.at[turn, theirs, columns], side_near.at[turn, :, columns],
                sc_s.at[turn], sc_r.at[turn], core,
            ),
            remote(
                side_mine.at[turn, :, columns], side_far.at[turn, :, columns],
                sy_s.at[turn], sy_r.at[turn], other,
            ),
            remote(
                side_total.at[turn, own, columns], side_total.at[turn, own, columns],
                se_s.at[turn], se_r.at[turn], core,
            ),
        )

    def finish_side(turn, size):
        first, second, third = side_copies(turn, size)
        second.wait_recv()
        side_total[turn, own, :size] = side_mine[turn, :, :size] + side_far[turn, :, :size]
        third.start()
        third.wait_recv()
        for copy in (first, second, third):
            copy.wait_send()
        return side_total[turn, :, :size]

    def sum_over_mp(fill, turn, side_size, finish_previous, idle):
        pieces = columns_of(width)

        def pieces_of(make):
            return [make(i, pl.ds(at, n)) for i, (at, n) in enumerate(pieces)]

        first = pieces_of(
            lambda i, c: remote(part.at[theirs, c], near.at[:, c], c_s.at[i], c_r.at[i], core)
        )
        second = pieces_of(
            lambda i, c: remote(
                mine.at[:, c], far.at[turn, :, c], y_s.at[turn, i], y_r.at[turn, i], other
            )
        )
        third = pieces_of(
            lambda i, c: remote(total.at[own, c], total.at[own, c], e_s.at[i], e_r.at[i], core)
        )
        side_first, side_second, _ = side_copies(turn, side_size)

        def middle(i):
            at, n = pieces[i]
            first[i].wait_recv()
            mine[:, at : at + n] = part[own, at : at + n] + near[:, at : at + n]
            second[i].start()

        for i, (at, n) in enumerate(pieces):
            fill(at, n)
            first[i].start()
            if i:
                middle(i - 1)
        side_first.start()
        middle(len(first) - 1)
        side_first.wait_recv()
        side_mine[turn, :, :side_size] = (
            side_part[turn, own, :side_size] + side_near[turn, :, :side_size]
        )
        finish_previous()
        side_second.start()
        idle()
        for i, (at, n) in enumerate(pieces):
            second[i].wait_recv()
            total[own, at : at + n] = mine[:, at : at + n] + far[turn, :, at : at + n]
            third[i].start()
        for copy in third:
            copy.wait_recv()
        for copy in first + second + third:
            copy.wait_send()

    def dot(left, right):
        return jnp.dot(left, right, preferred_element_type=jnp.float32)

    def low(value):
        return value.astype(jnp.bfloat16)

    def spin(value, sign):
        a, b = value[:, : head // 2], value[:, head // 2 :]
        cosine, sine = cosine_ref[...], sign * sine_ref[...]
        return jnp.concatenate([a * cosine - b * sine, b * cosine + a * sine], axis=1)

    def factor_of(value):
        return lax.rsqrt(jnp.mean(value * value, axis=-1, keepdims=True) + EPSILON)

    def gelu_parts(value):
        c = math.sqrt(2.0 / math.pi)
        square = value * value
        t = jnp.tanh(c * value * (1.0 + 0.044715 * square))
        gelu = 0.5 * value * (1.0 + t)
        slope = 0.5 * (1.0 + t) + 0.5 * value * (1.0 - t * t) * c * (1.0 + 3 * 0.044715 * square)
        return gelu, slope

    across_row = jnp.broadcast_to(segments[...].astype(jnp.float32), (tokens, tokens))
    down_row = across_row.T
    at_row = lax.broadcasted_iota(jnp.int32, (tokens, tokens), 0)
    at_column = lax.broadcasted_iota(jnp.int32, (tokens, tokens), 1)
    earlier = jnp.sum(jnp.where(across_row < down_row, 1.0, 0.0), axis=1, keepdims=True)
    position = at_row[:, : head // 2].astype(jnp.float32) - earlier
    exponent = at_column[:, : head // 2].astype(jnp.float32) * (-2.0 / head)
    angles = position * jnp.exp(exponent * math.log(10000.0))
    cosine_ref[...] = jnp.cos(angles)
    sine_ref[...] = jnp.sin(angles)
    mask_ref[...] = jnp.where(
        jnp.logical_and(across_row == down_row, at_row >= at_column), 1.0, 0.0
    )
    h_s[0] = h_in[...].astype(jnp.float32)
    mixer, feed = mixer_gain[...].reshape(1, width), feed_gain[...].reshape(1, width)

    def forward(l, carry):
        def need(*copies):
            @pl.when(l == 0)
            def _():
                for copy in copies:
                    copy.wait()

        h = h_s[l]
        normed = low(h * factor_of(h) * mixer)
        normed_s[l] = normed
        need(load.q_in, load.query, load.q_out, load.kv_in, load.pair, load.kv_out)

        @pl.when(l == 0)
        def _():
            kv_flat[0] = W.kv_in[0].reshape(width, 2 * rank)

        query_rank = low(dot(normed, W.q_in[l]))
        qr_s[l] = query_rank
        queries = dot(normed, W.query[...]) + dot(query_rank, W.q_out[l])
        q_s[l] = low(spin(queries, 1.0))
        pair_rank = low(dot(normed, kv_flat[l]))
        kvr_s[l] = pair_rank
        keys = dot(normed, W.pair[:, :head]) + dot(pair_rank[:, :rank], W.kv_out[l, 0])
        k_s[l] = low(spin(keys, 1.0))
        values = dot(normed, W.pair[:, head:]) + dot(pair_rank[:, rank:], W.kv_out[l, 1])
        v_s[l] = low(values)
        scores = product_t(q_s[l], k_s[l]) * scale
        scores = jnp.where(mask_ref[...] > 0, scores, MASKED)
        expo = jnp.exp(scores - jnp.max(scores, axis=-1, keepdims=True))
        probs = expo / jnp.sum(expo, axis=-1, keepdims=True)
        probs_s[l] = probs
        mixed = low(dot(low(probs), v_s[l]))
        mixed_s[l] = mixed
        need(load.output, load.o_in, load.o_out)

        output_rank = dot(mixed, W.o_in[l])
        side_part[0, :, :rank] = output_rank
        output_parts = split3(output_rank)

        def fill_attend(at, n):
            value = dot(mixed, W.output[:, at : at + n])
            for piece in output_parts:
                value = value + dot(piece, W.o_out[l, :, at : at + n])
            part[:, at : at + n] = value

        again = l > 0

        def idle_attend():
            ship_x(2, l, normed, again, 0)
            ship_r(3, l, query_rank, again, 0)
            ship_q(1, l, mixed, again, 0)

            @pl.when(l == 0)
            def _():
                for i in range(1, loops):
                    kv_flat[i] = W.kv_in[i].reshape(width, 2 * rank)
                load.w_in.start()
                load.w_in.wait()
                for i in range(loops):
                    w_flat[i] = W.w_in[i].reshape(width, 2 * rank)

            @pl.when(again)
            def _():
                pass_act(0)
                pass_rows(1, loops - 1)

            @pl.when(l == 0)
            def _():
                load.d_out.wait()
                shrink = product_t(cot[...], W.d_out[loops - 1])
                ship_x(1, loops - 1, cot[...], False, 0)
                ship_r(2, loops - 1, low(shrink), False, 0)

        def finish_before_attend():
            @pl.when(again)
            def _():
                sr_s[jnp.maximum(l - 1, 0)] = finish_side(1, rank)

        sum_over_mp(fill_attend, 0, rank, finish_before_attend, idle_attend)
        middle = h_s[l] + total[...]
        mid_s[l] = middle
        fed = low(middle * factor_of(middle) * feed)
        fed_s[l] = fed
        need(load.wide, load.w_out)
        widen_rank = low(dot(fed, w_flat[l]))
        er_s[l] = widen_rank
        for at, n in chunks:
            gate = product_t(fed, W.wide[0, at : at + n]) + product_t(
                widen_rank[:, :rank], W.w_out[l, 0, at : at + n]
            )
            gate_s[l, :, at : at + n] = gate
            up = product_t(fed, W.wide[1, at : at + n]) + product_t(
                widen_rank[:, rank:], W.w_out[l, 1, at : at + n]
            )
            up_s[l, :, at : at + n] = up
            act_s[:, at : at + n] = low(gelu_parts(gate)[0] * up)
            ship_b(4 + at // WIDE, l, [act_s[:, at : at + n]], again, 0)
        need(load.down, load.d_in)

        shrink_rank = dot(act_s[...], W.d_in[l])
        side_part[1, :, :rank] = shrink_rank
        shrink_parts = split3(shrink_rank)

        def fill_feed(at, n):
            value = dot(act_s[...], W.down[:, at : at + n])
            for piece in shrink_parts:
                value = value + dot(piece, W.d_out[l, :, at : at + n])
            part[:, at : at + n] = value

        def idle_feed():
            ship_x(0, l, fed, again, 0)
            ship_r(0, l, widen_rank[:, :rank], again, 0)
            ship_r(1, l, widen_rank[:, rank:], again, 0)

            @pl.when(again)
            def _():
                pass_rows(0, 0)

        def finish_before_feed():
            or_s[l] = finish_side(0, rank)

        sum_over_mp(fill_feed, 1, rank, finish_before_feed, idle_feed)
        h_s[l + 1] = mid_s[l] + total[...]
        return carry

    lax.fori_loop(0, loops, forward, 0)
    out_ref[...] = low(h_s[loops])

    g_s[...] = cot[...].astype(jnp.float32)
    gain_s[...] = jnp.zeros_like(gain_s)
    padded_quarter = select.shape[0] // blocks
    row = lax.broadcasted_iota(jnp.int32, (padded_quarter, width), 0)
    column = lax.broadcasted_iota(jnp.int32, (padded_quarter, width), 1)
    for b in range(blocks):
        hit = jnp.logical_and(column == row + (b * 4 + mp) * quarter, row < quarter)
        select[b * padded_quarter : (b + 1) * padded_quarter] = low(
            jnp.where(hit, 1.0, 0.0)
        )
    small_row = lax.broadcasted_iota(jnp.int32, (rank_quarter, rank), 0)
    small_column = lax.broadcasted_iota(jnp.int32, (rank_quarter, rank), 1)
    rank_select = low(
        jnp.concatenate(
            [
                jnp.where(small_column == small_row + (b * 4 + mp) * rank_quarter, 1.0, 0.0)
                for b in range(blocks)
            ],
            axis=0,
        )
    )
    raw_rows = raw_layout(quarter, rank_quarter, loops)

    tall = raw_rows.tall

    def put(start, size, stride, value, add=False):
        for b in range(blocks):
            piece = value[b * stride : b * stride + size]
            if add:
                raw_ref[b % 2, b // 2, start : start + size] += piece
            else:
                raw_ref[b % 2, b // 2, start : start + size] = piece

    def pair_ranks(l, grad_keys, grad_values):
        return low(
            jnp.concatenate(
                [product_t(grad_keys, W.kv_out[l, 0]), product_t(grad_values, W.kv_out[l, 1])], axis=1
            )
        )

    def raw_of(l):
        grad_rank = late_s[l, :, :rank]
        grad_pair = late_s[l, :, rank:]
        grad_pair_rank = pair_ranks(l, grad_pair[:, :head], grad_pair[:, head:])
        grad_widen = er_grad_s[l]
        normed_own = low(product_t(select[...], normed_s[l]))
        pair_weight = dot(normed_own, grad_pair)
        for j in range(2):
            value = pair_weight[:, j * head : (j + 1) * head]
            put(j * tall, tall, padded_quarter, value, l < loops - 1)
        base = 2 * tall + l * raw_rows.loop

        def put_loop(i, value):
            put(base + i * tall, tall, padded_quarter, value)

        put_loop(0, dot(normed_own, grad_rank))
        for j in range(2):
            put_loop(1 + j, dot(normed_own, grad_pair_rank[:, j * rank : (j + 1) * rank]))
        fed_own = low(product_t(select[...], fed_s[l]))
        for j in range(2):
            put_loop(3 + j, dot(fed_own, grad_widen[:, j * rank : (j + 1) * rank]))
        put_loop(5, sum(dot(chosen_s[l, 1], piece) for piece in split3(or_s[l])))
        put_loop(6, sum(dot(chosen_s[l, 0], piece) for piece in split3(sr_s[l])))
        for j in range(2):
            rank_own = low(product_t(rank_select, kvr_s[l, :, j * rank : (j + 1) * rank]))
            put(
                base + 7 * tall + j * rank_quarter, rank_quarter, rank_quarter,
                dot(rank_own, grad_pair[:, j * head : (j + 1) * head]),
            )

    def back(step, carry):
        l = loops - 1 - step
        again = step > 0
        before = loops - 1

        upstream = g_s[...]
        grad_feed = low(upstream)
        grad_shrink = low(product_t(grad_feed, W.d_out[l]))
        for i, (at, n) in enumerate(chunks):
            grad_act = product_t(grad_feed, W.down[at : at + n]) + product_t(
                grad_shrink, W.d_in[l, at : at + n]
            )
            gelu, slope = gelu_parts(gate_s[l, :, at : at + n])
            grad_gate = low(grad_act * up_s[l, :, at : at + n] * slope)
            grad_up = low(grad_act * gelu)
            gg_s[:, at : at + n] = grad_gate
            gu_s[:, at : at + n] = grad_up
            if i == 0:
                ship_b(0, l, [grad_gate], again, before)
                ship_b(2, l, [grad_up], again, before)
            else:
                ahead = WIDE - n
                grad_up = grad_up.astype(jnp.float32)
                ship_b(1, l, [grad_gate, grad_up[:, :ahead]], again, before)
                ship_b(3, l, [grad_up[:, ahead:]], again, before)

        for j, value in enumerate((gg_s, gu_s)):
            side_part[0, :, j * rank : (j + 1) * rank] = dot(value[...], W.w_out[l, j])
        grad_widen = low(side_part[0, :, : 2 * rank])

        def fill_fed(at, n):
            part[:, at : at + n] = (
                dot(gg_s[...], W.wide[0, :, at : at + n])
                + dot(gu_s[...], W.wide[1, :, at : at + n])
                + product_t(grad_widen, w_flat[l, at : at + n])
            )

        def finish_before_fed():
            @pl.when(step == 0)
            def _():
                sr_s[loops - 1] = finish_side(1, rank)

            @pl.when(again)
            def _():
                late_s[loops - 1] = low(finish_side(1, rank + 2 * head))

        def idle_fed():
            @pl.when(again)
            def _():
                ship_x(1, l, grad_feed, True, before)
                ship_r(2, l, grad_shrink, True, before)

            chosen_s[l, 0] = low(product_t(select[...], grad_feed))

            @pl.when(again)
            def _():
                raw_of(loops - 1)

        sum_over_mp(fill_fed, 0, 2 * rank, finish_before_fed, idle_fed)
        grad_fed = total[...]
        middle = mid_s[l]
        factor = factor_of(middle)
        unit = middle * factor
        scaled = grad_fed * feed
        grad_middle = upstream + factor * (
            scaled - unit * jnp.mean(scaled * unit, axis=-1, keepdims=True)
        )
        gain_s[1:2] += jnp.sum(grad_fed * unit, axis=0, keepdims=True)
        g_s[...] = grad_middle
        grad_attend = low(grad_middle)
        grad_output = low(product_t(grad_attend, W.o_out[l]))
        grad_mixed = low(
            product_t(grad_attend, W.output[...]) + product_t(grad_output, W.o_in[l])
        )
        probs = probs_s[l]
        grad_probs = product_t(grad_mixed, v_s[l])
        delta = jnp.sum(grad_probs * probs, axis=-1, keepdims=True)
        grad_scores = low(probs * (grad_probs - delta))
        grad_query = low(spin(dot(grad_scores, k_s[l]) * scale, -1.0))

        grad_rank = product_t(grad_query, W.q_out[l])
        grad_keys = spin(product_tn(grad_scores, q_s[l]) * scale, -1.0)
        grad_values = product_tn(low(probs), grad_mixed)
        side_part[1, :, :rank] = grad_rank
        side_part[1, :, rank : rank + head] = grad_keys
        side_part[1, :, rank + head :] = grad_values
        grad_rank, grad_keys, grad_values = low(grad_rank), low(grad_keys), low(grad_values)
        grad_pair = jnp.concatenate([grad_keys, grad_values], axis=1)
        grad_pair_rank = pair_ranks(l, grad_keys, grad_values)

        def fill_normed(at, n):
            part[:, at : at + n] = (
                product_t(grad_query, W.query[at : at + n])
                + product_t(grad_rank, W.q_in[l, at : at + n])
                + product_t(grad_pair, W.pair[at : at + n])
                + product_t(grad_pair_rank, kv_flat[l, at : at + n])
            )

        def finish_before_normed():
            er_grad_s[l] = low(finish_side(0, 2 * rank))

        def idle_normed():
            ship_q(0, l, grad_query, again, before)
            ship_x(3, l, grad_attend, again, before)
            ship_r(4, l, grad_output, again, before)
            chosen_s[l, 1] = low(product_t(select[...], grad_attend))

            @pl.when(step == 0)
            def _():
                pass_act(loops - 1)
                pass_rows(0, loops - 1)

            @pl.when(again)
            def _():
                pass_rows(1, 0)

        sum_over_mp(fill_normed, 1, rank + 2 * head, finish_before_normed, idle_normed)
        grad_normed = total[...]
        h = h_s[l]
        factor = factor_of(h)
        unit = h * factor
        scaled = grad_normed * mixer
        g_s[...] += factor * (scaled - unit * jnp.mean(scaled * unit, axis=-1, keepdims=True))
        gain_s[0:1] += jnp.sum(grad_normed * unit, axis=0, keepdims=True)

        return carry

    lax.fori_loop(0, loops, back, 0)
    late_s[0] = low(finish_side(1, rank + 2 * head))
    raw_of(0)
    grad_ref[...] = g_s[...]
    for b in range(blocks):
        ends = jnp.zeros((8, head), jnp.float32)
        raw_ref[b % 2, b // 2, raw_rows.gains :] = ends
        raw_ref[b % 2, b // 2, raw_rows.gains : raw_rows.gains + 2, :block] = gain_s[
            :2, b * block : (b + 1) * block
        ]
    last = loops - 1
    for copies in (
        x_copies(0, last), x_copies(2, last), r_copies(0, last), r_copies(1, last), r_copies(3, last),
        q_copies(1, last), x_copies(1, 0), x_copies(3, 0), r_copies(2, 0), r_copies(4, 0),
        q_copies(0, 0),
    ):
        finish(copies, False)
    for copies in (
        b_copies(4, last), b_copies(5, last), b_copies(0, 0), b_copies(1, 0), b_copies(2, 0),
        b_copies(3, 0),
    ):
        finish(copies)

    def to_core(i, l, half):
        lanes = end_span(l, half)
        x_part, r_part = x_end.at[i, :, :, lanes], r_end.at[i, :, :, lanes]
        return [
            remote(x_part, x_part, xc_s.at[i, l], xc_r.at[i, l], core),
            remote(r_part, r_part, rc_s.at[i, l], rc_r.at[i, l], core),
        ]

    both = [(i, l) for l in range(loops) for i in range(2)]
    for l in range(loops):
        for copies in (r_copies(0, l), b_copies(0, l)):
            copies[1].wait_recv()

    @pl.when(is_end)
    def _():
        for l in range(loops):
            far_act(l).wait_send()

    @pl.when(jnp.logical_and(is_end, side == 1))
    def _():
        for i, l in both:
            for copy in far_rows(i, l):
                copy.wait_send()

    for half in range(2):

        @pl.when(jnp.logical_and(jnp.logical_not(is_end), side == half))
        def _():
            for i, l in both:
                came = far_rows(i, l) if half else [x_copies(i, l)[2], r_copies(i + 1, l)[2]]
                for copy, onward in zip(came, to_core(i, l, half)):
                    copy.wait_recv()
                    onward.start()

    @pl.when(jnp.logical_not(is_end))
    def _():
        for l in range(loops):
            for copy in [b_copies(i, l)[2] for i in (3, 4, 5)] + [far_act(l)]:
                copy.wait_recv()
        for i, l in both:
            for copy in to_core(i, l, 0):
                copy.wait_send()
                copy.wait_recv()


def raw_layout(quarter, rank_quarter, loops):
    tall = quarter
    loop = 7 * tall + 2 * rank_quarter
    gains = 2 * tall + loops * loop
    return SimpleNamespace(tall=tall, loop=loop, gains=gains, all=gains + 8)


def block_and_factors(block_input, cotangent, segments, shared, stacked, dp_size):
    (mixer_gain, feed_gain, query, pair, output, widen, down) = shared
    (q_in, q_out, kv_in, kv_out, o_in, o_out, w_in, w_out, d_in, d_out) = stacked
    tokens, width = block_input.shape
    head = query.shape[1]
    loops, _, rank = q_in.shape
    hidden = down.shape[0]
    weights = (
        q_in, query, q_out, kv_in, pair, kv_out, output, o_in, o_out,
        widen.transpose(1, 2, 0), w_out.swapaxes(2, 3), down, d_in, d_out, w_in,
    )
    layout = raw_layout(width // (4 * dp_size), rank // (4 * dp_size), loops)
    line = dp_size // 2
    f32, bf16 = jnp.float32, jnp.bfloat16
    shape = jax.ShapeDtypeStruct
    block, rank_block, both = width // dp_size, rank // dp_size, loops * tokens
    out_shape = (
        shape((tokens, width), bf16),
        shape((tokens, width), f32),
        shape((2, line, layout.all, head), f32),
        shape((4, 2, line, block, both), f32),
        shape((5, 2, line, rank_block, both), f32),
        shape((6, both, WIDE), f32),
        shape((2, both, head), f32),
        shape((2, line, block, both), f32),
        shape((3, line, rank_block, both), f32),
        shape((3, both, WIDE), f32),
        shape((2, line, block, 2 * both), f32),
        shape((2, line, rank_block, 2 * both), f32),
        shape((3, 2 * both, WIDE), f32),
    )
    vmem = pl.BlockSpec(memory_space=pltpu.VMEM)
    hbm = pl.BlockSpec(memory_space=pl.ANY)
    widest = rank + 2 * head
    pieces = -(-width // SUM_STEP)
    dma = pltpu.SemaphoreType.DMA

    def kept(columns, dtype, count=loops):
        return pltpu.VMEM((count, tokens, columns), dtype)

    scratch = [pltpu.VMEM(w.shape, bf16) for w in weights[:-1]] + [
        kept(width, f32, loops + 1), kept(width, f32), kept(width, bf16), kept(rank, bf16),
        kept(2 * rank, bf16), kept(head, bf16), kept(head, bf16), kept(head, bf16), kept(tokens, f32),
        kept(head, bf16), kept(rank, f32), kept(width, bf16), kept(2 * rank, bf16),
        kept(hidden, f32), kept(hidden, f32), pltpu.VMEM((tokens, hidden), bf16), kept(rank, f32),
        pltpu.VMEM((tokens, hidden), bf16), pltpu.VMEM((tokens, hidden), bf16),
        pltpu.VMEM((tokens, width), f32), pltpu.VMEM((8, width), f32),
        pltpu.VMEM((dp_size * 48, width), bf16),
        pltpu.VMEM((tokens, width), f32), pltpu.VMEM((tokens, width), f32),
        pltpu.VMEM((tokens // 2, width), f32), pltpu.VMEM((tokens // 2, width), f32),
        pltpu.VMEM((2, tokens // 2, width), f32),
        pltpu.VMEM((2, tokens, widest), f32), pltpu.VMEM((2, tokens // 2, widest), f32),
        pltpu.VMEM((2, tokens // 2, widest), f32), pltpu.VMEM((2, tokens // 2, widest), f32),
        pltpu.VMEM((2, tokens, widest), f32),
        kept(widest, bf16), kept(2 * rank, bf16), pltpu.VMEM((loops, 2, dp_size * 48, tokens), bf16),
        pltpu.VMEM((4, 2, line, block, tokens), f32), pltpu.VMEM((5, 2, line, rank_block, tokens), f32),
        pltpu.VMEM((6, tokens, WIDE), f32), pltpu.VMEM((2, tokens, head), f32),
        pltpu.VMEM((loops, width, 2 * rank), bf16), pltpu.VMEM((loops, width, 2 * rank), bf16),
        pltpu.VMEM((tokens, head // 2), f32), pltpu.VMEM((tokens, head // 2), f32),
        pltpu.VMEM((tokens, tokens), f32),
        dma((len(weights),)), dma((pieces,)), dma((pieces,)), dma((2, pieces)), dma((2, pieces)),
        dma((pieces,)), dma((pieces,)),
        dma((4, loops)), dma((5, loops)), dma((6, loops)), dma((2, loops)),
    ]
    scratch += [dma((2, loops))] * 2 + [dma((3, loops))] * 4
    scratch += [dma((2, 2, loops))] * 4 + [dma((3, loops))] * 2 + [dma((loops,))] * 2
    scratch += [dma((2,))] * 6 + [dma((2, loops))] * 4
    return pl.pallas_call(
        block_kernel,
        out_shape=out_shape,
        in_specs=[vmem] * 5 + [hbm] * len(weights),
        out_specs=(vmem,) * 3 + (hbm,) * 10,
        scratch_shapes=scratch,
        compiler_params=pltpu.CompilerParams(
            collective_id=21, has_side_effects=True, vmem_limit_bytes=63 << 20
        ),
    )(
        block_input, cotangent, segments, mixer_gain, feed_gain,
        *weights,
    )


def line_kernel(
    raw_all, x_all, r_all, b_all, q_all, x_got, r_got, b_got, x_end_all, r_end_all, b_end_all,
    mixer_out, feed_out, q_w, pair_w, o_w, e_w, s_w, q_i, q_o, p_i, p_o, o_i, o_o, e_i, e_o, s_i, s_o,
    main_out, side_out, raw_out, around,
    x_own, r_own, b_own, q_own, x_far, r_far, b_far, q_far, x_end, r_end, b_end, raw_own, raw_far, product_ref,
    main_right, main_left, side_right, side_left, raw_right, raw_left,
    x_s, x_r, r_s, r_r, b_s, b_r, q_s, q_r, w_s, w_r, local_sems, step_sems, around_s, around_r, ee_s, ee_r,
    mr_s, mr_r, ml_s, ml_r, sr_s, sr_r, sl_s, sl_r, rr_s, rr_r, rl_s, rl_r,
    credit_right, credit_left,
):
    dp, mp = lax.axis_index("dp"), lax.axis_index("mp")
    x = lax.rem(dp, 2)
    z = dp // 2
    last = 3
    pair = (dp + 1 - 2 * x, mp)
    up, down = (dp + 2, mp), (dp - 2, mp)

    core, other = (dp, mp + 1 - 2 * lax.rem(mp, 2)), (dp, lax.rem(mp + 2, 4))
    hidden = s_w.shape[1]
    block, rank_block, quarter = s_w.shape[0], s_i.shape[1], pair_w.shape[0]
    loops, head = s_i.shape[0], q_w.shape[1]
    layout = raw_layout(quarter, rank_block // 4, loops)
    tall = layout.tall
    tail = hidden - WIDE
    short = 2 * hidden - 3 * WIDE

    barrier = pltpu.get_barrier_semaphore()
    for device in (pair, core, other):
        pl.semaphore_signal(barrier, inc=1, device_id=device, device_id_type=MESH)

    @pl.when(z > 0)
    def _():
        pl.semaphore_signal(barrier, inc=1, device_id=down, device_id_type=MESH)

    @pl.when(z < last)
    def _():
        pl.semaphore_signal(barrier, inc=1, device_id=up, device_id_type=MESH)

    pl.semaphore_wait(barrier, 3 + jnp.minimum(z, 1) + jnp.minimum(last - z, 1))

    def across(source, target, send, recv):
        return pltpu.make_async_remote_copy(
            source, target, send, recv, device_id=pair, device_id_type=MESH
        )

    def x_copy(i):
        return across(x_all.at[i, 1 - x], x_far.at[i], x_s.at[i - 2], x_r.at[i - 2])

    def r_copy(i):
        return across(r_all.at[i, 1 - x], r_far.at[i], r_s.at[i - 3], r_r.at[i - 3])

    def b_copy(i):
        return across(b_all.at[i], b_far.at[i], b_s.at[i], b_r.at[i])

    q_copy = across(q_all, q_far, q_s, q_r)
    w_copy = across(raw_all.at[1 - x], raw_far, w_s, w_r)

    def here(source, target, i):
        return pltpu.make_async_copy(source, target, local_sems.at[i])

    at_start = [
        here(x_all.at[:, x], x_own, 0),
        here(r_all.at[:, x], r_own, 1),
        here(x_got, x_far.at[0:2], 2),
        here(r_got, r_far.at[0:3], 3),
        here(b_got.at[0], b_far.at[0], 4),
        here(b_got.at[1:3], b_far.at[4:6], 5),
        here(q_all, q_own, 6),
    ]
    tokens = b_end.shape[1] // 4

    def end_rows(at):
        return pl.ds(at * tokens, tokens)

    for_ends = [
        here(x_end_all, x_end, 7), here(r_end_all, r_end, 8), here(b_end_all.at[0], b_end.at[0], 9)
    ] + [
        here(b_end_all.at[k, end_rows(2 * l)], b_end.at[k, end_rows(2 * l)], 9 + 2 * k + l)
        for k in (1, 2) for l in range(loops)
    ]

    def end_copies(k):
        return [
            across(
                b_end_all.at[k, end_rows(2 * l)], b_end.at[k, end_rows(2 * l + 1)],
                ee_s.at[k - 1, l], ee_r.at[k - 1, l],
            )
            for l in range(loops)
        ]

    own_copy = here(raw_all.at[x], raw_own, 10)
    inner = jnp.logical_and(z > 0, z < last)

    def chunk_of(step):
        return jnp.where(lax.rem(step, 3) == 0, 4 + step // 3, step - 1 - step // 3)

    def begins_inside(step):
        return jnp.logical_or(lax.rem(step, 3) == 0, step == 5)

    def b_load(step):
        slot = lax.rem(step, 2)
        return pltpu.make_async_copy(b_all.at[chunk_of(step)], b_own.at[slot], step_sems.at[slot])

    b_copy(1).start()
    b_load(0).start()
    for copy in at_start:
        copy.start()

    @pl.when(inner)
    def _():
        for copy in for_ends:
            copy.start()

    own_copy.start()
    for copy in at_start[:-1]:
        copy.wait()

    @pl.when(inner)
    def _():
        for copy in for_ends:
            copy.wait()

    def chain(target, step, slot, steps, value, out, right, left, r_s, r_r, l_s, l_r, credits):
        def move(buffer, send, recv, i, s, device, size):
            piece = buffer.at[i, s, :, pl.ds(0, size)]
            return pltpu.make_async_remote_copy(
                piece, piece, send.at[i, s], recv.at[i, s], device_id=device, device_id_type=MESH
            )

        def at_size(act):
            full = right.shape[3]
            if credits:
                pl.when(step < steps - 1)(lambda: act(full))
                pl.when(step == steps - 1)(lambda: act(short))
            else:
                act(full)

        def inside(at):
            return begins_inside(at) if credits else at < 0

        def free(credit, i, source, at, from_end):
            @pl.when(
                jnp.logical_and(
                    at <= steps - 1,
                    jnp.logical_not(jnp.logical_and(from_end, inside(at))),
                )
            )
            def _():
                pl.semaphore_signal(credit.at[i], inc=1, device_id=source, device_id_type=MESH)

        def pass_on(i, place, buffer, send, recv, onward, source, at_end, next_to_end, credit):
            def here(i, s, size=right.shape[3]):
                return move(buffer, send, recv, i, s, onward, size)

            def begin():
                if credits:

                    @pl.when(step >= 3)
                    def _():
                        pl.semaphore_wait(credit.at[i], 1)

                at_size(lambda size: here(i, slot, size).start())

            @pl.when(jnp.logical_and(at_end, jnp.logical_not(inside(step))))
            def _():
                buffer[i, slot] = value()
                if credits:
                    before = lax.rem(step + 2 - inside(step - 1).astype(jnp.int32), 3)
                    after = jnp.where(onward[0] > dp, i - 1, i + 1)

                    @pl.when(jnp.logical_and(place < 2, step >= 2))
                    def _():
                        here(after, before).wait_send()

                    @pl.when(place == 2)
                    def _():
                        at_size(lambda size: here(2 - i, slot, size).wait_send())

                    begin()
                else:
                    begin()
                    here(i, slot).wait_send()

            @pl.when(jnp.logical_not(at_end))
            def _():
                if credits:

                    @pl.when(step >= 1)
                    def _():
                        here(i, lax.rem(step + 2, 3)).wait_send()
                        free(credit, i, source, step + 2, next_to_end)

                has_source = jnp.logical_not(jnp.logical_and(next_to_end, inside(step)))

                @pl.when(jnp.logical_not(has_source))
                def _():
                    buffer[i, slot] = value()

                @pl.when(has_source)
                def _():
                    product = value()
                    at_size(lambda size: here(i, slot, size).wait_recv())
                    buffer[i, slot] += product

                begin()

        @pl.when(target > z)
        def _():
            pass_on(target - 1, 3 - target, right, r_s, r_r, up, down, z == 0, z == 1, credit_right)

        @pl.when(target < z)
        def _():
            pass_on(target, target, left, l_s, l_r, down, up, z == last, z == last - 1, credit_left)

        @pl.when(target == z)
        def _():
            out[...] = value()

    def arrive(step, slot, steps, out, right, left, r_s, r_r, l_s, l_r, credits):
        def take(buffer, send, recv, i, size):
            piece = buffer.at[i, slot, :, pl.ds(0, size)]
            pltpu.make_async_remote_copy(
                piece, piece, send.at[i, slot], recv.at[i, slot], device_id=pair, device_id_type=MESH
            ).wait_recv()
            out[:, :size] += buffer[i, slot, :, :size]

        started_inside = begins_inside(step) if credits else step < 0

        def side_of(there, from_end, buffer, send, recv, i, credit, source):
            @pl.when(there)
            def _():
                quiet = jnp.logical_and(from_end, started_inside)

                @pl.when(jnp.logical_not(quiet))
                def _():
                    full = buffer.shape[3]
                    if credits:
                        pl.when(step < steps - 1)(lambda: take(buffer, send, recv, i, full))
                        pl.when(step == steps - 1)(lambda: take(buffer, send, recv, i, short))
                    else:
                        take(buffer, send, recv, i, full)

                if credits:
                    skip = jnp.logical_and(from_end, begins_inside(step + 3))

                    @pl.when(jnp.logical_and(step + 3 <= steps - 1, jnp.logical_not(skip)))
                    def _():
                        pl.semaphore_signal(
                            credit.at[i], inc=1, device_id=source, device_id_type=MESH
                        )

        side_of(z > 0, z == 1, right, r_s, r_r, jnp.maximum(z - 1, 0), credit_right, down)
        side_of(z < last, z == last - 1, left, l_s, l_r, jnp.minimum(z, last - 1), credit_left, up)

    def settle(right, left, r_s, l_s, main):
        def wait(buffer, send, i, slot, size, device):
            piece = buffer.at[i, slot, :, pl.ds(0, size)]
            pltpu.make_async_remote_copy(
                piece, piece, send.at[i, slot], send.at[i, slot], device_id=device, device_id_type=MESH
            ).wait_send()

        full = right.shape[3]
        slot, size = (2, short) if main else (0, full)
        for target in range(1, 4):

            @pl.when(jnp.logical_and(target > z, z > 0))
            def _():
                wait(right, r_s, target - 1, slot, size, up)

        for target in range(3):

            @pl.when(jnp.logical_and(target < z, z < last))
            def _():
                wait(left, l_s, target, slot, size, down)

        if main:

            @pl.when(z == 0)
            def _():
                for i in (0, 1):
                    wait(right, r_s, i, 1, full, up)

            @pl.when(z == last)
            def _():
                for i in (1, 2):
                    wait(left, l_s, i, 1, full, down)

    def order(turn):
        def near(end):
            return jnp.where(end == 0, 3 - turn, jnp.where(turn < 2, 3 - turn, turn - 2))

        return jnp.where(z < 2, near(z), 3 - near(3 - z))

    def dot(left, right):
        return jnp.dot(
            left.astype(jnp.bfloat16), right.astype(jnp.bfloat16), preferred_element_type=jnp.float32
        )

    steps = b_all.shape[0]

    def left_times(x_index, group, target, own, far):
        shared = dot(x_own[x_index, target], own) + dot(x_far[x_index, target], far)
        return [shared, *rank_times(group, target, own, far)]

    def rank_times(group, target, own, far):
        half = own.shape[0] // 2
        rank_own, rank_far = r_own[group, target], r_far[group, target]
        return [
            dot(rank_own[:, :half], own[:half]) + dot(rank_far[:, :half], far[:half]),
            dot(rank_own[:, half:], own[half:]) + dot(rank_far[:, half:], far[half:]),
        ]

    def main_arrive(step):
        slot = lax.rem(step, 3)
        chunk = chunk_of(step)
        arrive(
            step, slot, steps, main_out.at[slot], main_right, main_left, mr_s, mr_r, ml_s, ml_r, True,
        )
        parts = (
            (0, 0, 0, 0, WIDE), (1, 0, 0, WIDE, tail), (1, tail, 1, WIDE, WIDE - tail),
            (2, 0, 1, 0, WIDE), (3, 0, 1, 2 * WIDE - tail, short),
        )
        for which, start, j, at, n in parts:

            @pl.when(chunk == which)
            def _():
                e_w[:, j, at : at + n] = main_out[slot, :block, start : start + n]
                for l in range(loops):
                    first = block + l * rank_block
                    e_o[l, j, :, at : at + n] = main_out[
                        slot, first : first + rank_block, start : start + n
                    ]

        for part, (at, n) in enumerate(((0, WIDE), (WIDE, tail))):

            @pl.when(chunk == 4 + part)
            def _():
                s_w[:, at : at + n] = main_out[slot, :block, :n]
                for l in range(loops):
                    first = block + l * rank_block
                    s_i[l, :, at : at + n] = main_out[slot, first : first + rank_block, :n]

    def turn_body(at, carry):
        step, turn = at // 4, lax.rem(at, 4)
        slot = lax.rem(step, 3)
        chunk = chunk_of(step)
        group = chunk // 2
        target = order(turn)

        @pl.when(turn == 0)
        def _():
            b_load(step).wait()

            @pl.when(step < steps - 1)
            def _():
                b_load(step + 1).start()

            @pl.when(jnp.logical_and(chunk >= 1, chunk <= 3))
            def _():
                b_copy(chunk).wait_recv()

            @pl.when(step == 1)
            def _():
                @pl.when(inner)
                def _():
                    for copy in end_copies(1):
                        copy.start()

                b_copy(2).start()

            @pl.when(step == 2)
            def _():
                @pl.when(inner)
                def _():
                    for copy in end_copies(2):
                        copy.start()

                b_copy(3).start()

            @pl.when(step == 3)
            def _():
                w_copy.start()

                @pl.when(inner)
                def _():
                    for copy in end_copies(1):
                        copy.wait_recv()

            @pl.when(step == 4)
            def _():
                x_copy(2).start()
                x_copy(3).start()
                r_copy(3).start()
                r_copy(4).start()
                q_copy.start()

            @pl.when(jnp.logical_and(step == 5, inner))
            def _():
                for copy in end_copies(2):
                    copy.wait_recv()

        def value():
            parts = left_times(
                group // 2, group, target,
                b_own[lax.rem(step, 2)].astype(jnp.bfloat16), b_far[chunk].astype(jnp.bfloat16),
            )
            product_ref[...] = jnp.concatenate(parts, axis=0)

            @pl.when(chunk == 1)
            def _():
                other_rank = rank_times(
                    1, target, b_own[lax.rem(step, 2)].astype(jnp.bfloat16),
                    b_far[1].astype(jnp.bfloat16),
                )
                kept = product_ref[block:]
                column = lax.broadcasted_iota(jnp.int32, kept.shape, 1)
                product_ref[block:] = jnp.where(
                    column < tail, kept, jnp.concatenate(other_rank, axis=0)
                )

            beyond = jnp.logical_or(
                jnp.logical_and(z == 1, target >= 1),
                jnp.logical_and(z == last - 1, target <= last - 1),
            )

            @pl.when(jnp.logical_and(beyond, chunk >= 3))
            def _():
                end = b_end[jnp.where(chunk == 3, 2, jnp.maximum(chunk - 4, 0))].astype(jnp.bfloat16)
                shared = jnp.where(chunk == 3, 0, 1)
                middle = end.shape[0] // 2
                product_ref[...] += jnp.concatenate(
                    [
                        dot(x_end[shared, target], end),
                        dot(r_end[shared, target, :, :middle], end[:middle]),
                        dot(r_end[shared, target, :, middle:], end[middle:]),
                    ],
                    axis=0,
                )

            return product_ref[...]

        chain(
            target, step, slot, steps, value, main_out.at[slot], main_right, main_left,
            mr_s, mr_r, ml_s, ml_r, True,
        )

        @pl.when(jnp.logical_and(turn == 3, step >= 2))
        def _():
            main_arrive(step - 2)

        return carry

    lax.fori_loop(0, 4 * steps, turn_body, 0)

    w_copy.wait_recv()
    own_copy.wait()
    at_start[-1].wait()

    def raw_body(turn, carry):
        target = order(turn)
        chain(
            target, 0, 0, 1, lambda: raw_own[target] + raw_far[target], raw_out, raw_right, raw_left,
            rr_s, rr_r, rl_s, rl_r, False,
        )
        return carry

    lax.fori_loop(0, 4, raw_body, 0)
    main_arrive(jnp.int32(steps - 2))

    for i in (2, 3):
        x_copy(i).wait_recv()
    for i in (3, 4):
        r_copy(i).wait_recv()
    q_copy.wait_recv()

    def side_body(turn, carry):
        target = order(turn)

        def value():
            parts = [
                left_times(
                    2 + i, 3 + i, target, q_own[i].astype(jnp.bfloat16), q_far[i].astype(jnp.bfloat16)
                )
                for i in range(2)
            ]
            return jnp.concatenate([jnp.concatenate(p, axis=0) for p in parts], axis=1)

        chain(
            target, 0, 0, 1, value, side_out, side_right, side_left,
            sr_s, sr_r, sl_s, sl_r, False,
        )
        return carry

    lax.fori_loop(0, 4, side_body, 0)
    main_arrive(jnp.int32(steps - 1))
    arrive(0, 0, 1, raw_out, raw_right, raw_left, rr_s, rr_r, rl_s, rl_r, False)

    def share(device, owner, i):
        return pltpu.make_async_remote_copy(
            around.at[owner], around.at[owner], around_s.at[i], around_r.at[i],
            device_id=device, device_id_type=MESH,
        )

    far_owner = lax.rem(mp + 2, 4)
    for l in range(loops):
        start = 2 * tall + l * layout.loop + 5 * tall
        around[mp, l] = raw_out[start : start + 2 * tall]
    along, same, passed = share(other, mp, 0), share(core, mp, 1), share(core, far_owner, 2)
    along.start()
    same.start()
    arrive(0, 0, 1, side_out, side_right, side_left, sr_s, sr_r, sl_s, sl_r, False)
    along.wait_recv()
    passed.start()
    q_w[...] = side_out[:block, :head]
    o_w[...] = side_out[:block, head:]
    for l in range(loops):
        start = block + l * rank_block
        q_o[l] = side_out[start : start + rank_block, :head]
        o_i[l] = side_out[start : start + rank_block, head:]
    mixer_out[...] = raw_out[layout.gains, :block]
    feed_out[...] = raw_out[layout.gains + 1, :block]
    for j in range(2):
        pair_w[:, j * head : (j + 1) * head] = raw_out[j * tall : j * tall + quarter]
    for l in range(loops):
        base = 2 * tall + l * layout.loop
        q_i[:, l] = raw_out[base : base + quarter]
        for j in range(2):
            start = base + (1 + j) * tall
            p_i[l, :, j] = raw_out[start : start + quarter]
            e_i[l, :, j] = raw_out[start + 2 * tall : start + 2 * tall + quarter]
            start = base + 7 * tall + j * (rank_block // 4)
            p_o[l, j] = raw_out[start : start + rank_block // 4]
    same.wait_recv()
    passed.wait_recv()
    for l in range(loops):
        for m in range(4):
            o_o[l, m * quarter : (m + 1) * quarter] = around[m, l, :quarter]
            s_o[l, m * quarter : (m + 1) * quarter] = around[m, l, tall : tall + quarter]
    for copy in (along, same, passed):
        copy.wait_send()

    settle(main_right, main_left, mr_s, ml_s, True)
    settle(side_right, side_left, sr_s, sl_s, False)
    settle(raw_right, raw_left, rr_s, rl_s, False)
    @pl.when(inner)
    def _():
        for copy in end_copies(1) + end_copies(2):
            copy.wait_send()

    for copy in (x_copy(2), x_copy(3), r_copy(3), r_copy(4), b_copy(1), b_copy(2), b_copy(3)):
        copy.wait_send()
    q_copy.wait_send()
    w_copy.wait_send()


def line_gradients(factors, loops, dp_size, mp_size, hidden):
    raw, x_all, r_all, b_all, q_all, x_got, r_got, b_got, x_end, r_end, b_end = factors
    block, rank_block, head = x_all.shape[3], r_all.shape[3], q_all.shape[2]
    quarter, rank_quarter = block // mp_size, rank_block // mp_size
    layout = raw_layout(quarter, rank_quarter, loops)
    rows = block + loops * rank_block
    steps = b_all.shape[0]
    vmem = pl.BlockSpec(memory_space=pltpu.VMEM)
    hbm = pl.BlockSpec(memory_space=pl.ANY)
    dma = pltpu.SemaphoreType.DMA
    f32 = jnp.float32
    line = dp_size // 2 - 1
    half_x = pltpu.VMEM((x_all.shape[0], *x_all.shape[2:]), f32)
    half_r = pltpu.VMEM((r_all.shape[0], *r_all.shape[2:]), f32)
    whole_b, whole_q = pltpu.VMEM(b_all.shape, f32), pltpu.VMEM(q_all.shape, f32)
    shapes = (
        (block,), (block,), (block, head), (quarter, 2 * head), (block, head), (block, 2, hidden),
        (block, hidden), (quarter, loops, head), (loops, rank_block, head), (loops, quarter, 2, head),
        (loops, 2, rank_quarter, head), (loops, rank_block, head), (loops, block, head),
        (loops, quarter, 2, head), (loops, 2, rank_block, hidden), (loops, rank_block, hidden),
        (loops, block, head),
    )
    return pl.pallas_call(
        line_kernel,
        out_shape=tuple(jax.ShapeDtypeStruct(v, f32) for v in shapes),
        in_specs=[hbm] * 11,
        out_specs=(vmem,) * len(shapes),
        scratch_shapes=[
            pltpu.VMEM((3, rows, WIDE), f32), pltpu.VMEM((rows, 2 * head), f32),
            pltpu.VMEM((layout.all, head), f32), pltpu.VMEM((4, loops, 2 * layout.tall, head), f32),
        ]
        + [half_x, half_r, pltpu.VMEM((2, *b_all.shape[1:]), f32), whole_q]
        + [half_x, half_r, whole_b, whole_q]
        + [pltpu.VMEM(v.shape, f32) for v in (x_end, r_end, b_end)]
        + [pltpu.VMEM(raw.shape[1:], f32)] * 2
        + [pltpu.VMEM((rows, WIDE), f32)]
        + [pltpu.VMEM((line, 3, rows, WIDE), f32)] * 2
        + [pltpu.VMEM((line, 1, rows, 2 * head), f32)] * 2
        + [pltpu.VMEM((line, 1, layout.all, head), f32)] * 2
        + [dma((2,))] * 4 + [dma((steps,))] * 2 + [dma] * 4 + [dma((15,)), dma((2,)), dma((3,)), dma((3,))]
        + [dma((2, loops))] * 2
        + [dma((line, 3))] * 4 + [dma((line, 1))] * 8
        + [pltpu.SemaphoreType.REGULAR((line,))] * 2,
        compiler_params=pltpu.CompilerParams(
            collective_id=20, has_side_effects=True, vmem_limit_bytes=63 << 20
        ),
    )(*factors)


def in_place(results):
    mixer, feed, q_w, pair_w, o_w, e_w, s_w, q_i, q_o, p_i, p_o, o_i, o_o, e_i, e_o, s_i, s_o = results
    return (
        mixer, feed, q_w, pair_w, o_w.T, e_w, s_w.T, q_i.swapaxes(0, 1), q_o, p_i, p_o,
        o_i.swapaxes(1, 2), o_o.swapaxes(1, 2), e_i, e_o, s_i.swapaxes(1, 2), s_o.swapaxes(1, 2),
    )


def copy_kernel(*refs):
    count = (len(refs) - 2) // 3
    sources, targets, rooms = refs[:count], refs[count : 2 * count], refs[2 * count : 3 * count]
    come = [pltpu.make_async_copy(v, room, refs[-2].at[i]) for i, (v, room) in enumerate(zip(sources, rooms))]
    go = [pltpu.make_async_copy(room, v, refs[-1].at[i]) for i, (v, room) in enumerate(zip(targets, rooms))]
    for copy in come:
        copy.start()
    for first, second in zip(come, go):
        first.wait()
        second.start()
    for copy in go:
        copy.wait()


def placed(values):
    hbm = pl.BlockSpec(memory_space=pl.ANY)
    sems = pltpu.SemaphoreType.DMA((len(values),))
    return pl.pallas_call(
        copy_kernel,
        out_shape=tuple(jax.ShapeDtypeStruct(v.shape, v.dtype) for v in values),
        in_specs=[hbm] * len(values),
        out_specs=(hbm,) * len(values),
        scratch_shapes=[pltpu.VMEM(v.shape, v.dtype) for v in values] + [sems, sems],
        compiler_params=pltpu.CompilerParams(vmem_limit_bytes=60 << 20),
    )(*values)


def per_device(dp_size, mp_size, block_input, cotangent, segments, *parameters):
    shared, stacked = parameters[:7], parameters[7:]
    loops = stacked[0].shape[0]
    if dp_size == 8 and mp_size == 4 and loops == 2:
        output, input_grad, *factors = block_and_factors(
            block_input, cotangent, segments, shared, stacked, dp_size
        )
        gradients = line_gradients(factors, loops, dp_size, mp_size, shared[6].shape[0])
        output, input_grad, *gradients = placed((output, input_grad, *gradients))
        gradients = in_place(gradients)
        return (output, input_grad, *gradients)
    tables = rotary_tables(segments[0], shared[3].shape[1] // 2)
    total = mp_total(mp_size)
    state = block_input.astype(jnp.float32)
    kept_all = []
    for i in range(loops):
        state, kept = forward_loop(state, shared, [v[i] for v in stacked], tables, total, 1)
        kept_all.append(kept)
    upstream = cotangent.astype(jnp.float32)
    for i in reversed(range(loops)):
        upstream = reverse_loop(
            upstream, kept_all[i], shared, [v[i] for v in stacked], tables, total, 3
        )
    return (state.astype(jnp.bfloat16), upstream, *scattered_gradients(kept_all, dp_size, mp_size))


def solution(mesh):
    in_specs = (
        P("dp", None),
        P("dp", None),
        P("dp", None),
        P(),
        P(),
        P(None, "mp"),
        P(),
        P("mp", None),
        P(None, None, "mp"),
        P("mp", None),
        P(),
        P(None, None, "mp"),
        P(),
        P(),
        P(None, "mp", None),
        P(),
        P(),
        P(None, None, None, "mp"),
        P(None, "mp", None),
        P(),
    )
    out_specs = (
        P("dp", None),
        P("dp", None),
        P("dp"),
        P("dp"),
        P("dp", "mp"),
        P(("dp", "mp"), None),
        P("mp", "dp"),
        P("dp", None, "mp"),
        P("mp", "dp"),
        P(None, ("dp", "mp"), None),
        P(None, "dp", "mp"),
        P(None, ("dp", "mp"), None, None),
        P(None, None, ("dp", "mp"), None),
        P(None, "mp", "dp"),
        P(None, None, "dp"),
        P(None, ("dp", "mp"), None, None),
        P(None, None, "dp", "mp"),
        P(None, "mp", "dp"),
        P(None, None, "dp"),
    )
    return jax.shard_map(
        functools.partial(per_device, mesh.shape["dp"], mesh.shape["mp"]),
        mesh=mesh, in_specs=in_specs, out_specs=out_specs, check_vma=False
    )
```

```python
import functools
import math
from types import SimpleNamespace

import jax
import jax.numpy as jnp
from jax import lax
from jax.experimental import pallas as pl
from jax.experimental.pallas import tpu as pltpu
from jax.sharding import PartitionSpec as P

EPSILON = 1e-06
MASKED = -1e30
MESH = pl.DeviceIdType.MESH


def product(left, right):
    return jnp.dot(left, right, preferred_element_type=jnp.float32)


def product_t(left, right):
    return lax.dot_general(
        left, right, (((1,), (1,)), ((), ())), preferred_element_type=jnp.float32
    )


def product_tn(left, right):
    return lax.dot_general(
        left, right, (((0,), (0,)), ((), ())), preferred_element_type=jnp.float32
    )


def exact_product(left, right):
    return jnp.dot(left, right, precision=lax.Precision.HIGHEST, preferred_element_type=jnp.float32)


def exact_tn(left, right):
    return lax.dot_general(
        left,
        right,
        (((0,), (0,)), ((), ())),
        precision=lax.Precision.HIGHEST,
        preferred_element_type=jnp.float32,
    )


def normalize(hidden_state, gain):
    factor = lax.rsqrt(jnp.mean(hidden_state * hidden_state, axis=-1, keepdims=True) + EPSILON)
    return (hidden_state * factor * gain, factor)


def normalize_back(hidden_state, factor, gain, upstream_gradient):
    unit = hidden_state * factor
    scaled = upstream_gradient * gain
    downstream = factor * (scaled - unit * jnp.mean(scaled * unit, axis=-1, keepdims=True))
    return (downstream, jnp.sum(upstream_gradient * unit, axis=0))


def rotate(values, cosine_table, sine_table):
    half_width = values.shape[-1] // 2
    first = values[..., :half_width]
    second = values[..., half_width:]
    return jnp.concatenate(
        [first * cosine_table - second * sine_table, second * cosine_table + first * sine_table],
        axis=-1,
    )


def rotary_tables(segment_row, head_size):
    length_value = segment_row.shape[0]
    earlier = jnp.sum((segment_row[None, :] < segment_row[:, None]).astype(jnp.int32), axis=1)
    position = (jnp.arange(length_value, dtype=jnp.int32) - earlier).astype(jnp.float32)
    steps_half = jnp.arange(head_size // 2, dtype=jnp.float32)
    frequency = 10000.0 ** (-2.0 * steps_half / head_size)
    angles = position[:, None] * frequency[None, :]
    same_segment = segment_row[:, None] == segment_row[None, :]
    ordinal = jnp.arange(length_value, dtype=jnp.int32)
    allowed_mask = same_segment & (ordinal[:, None] >= ordinal[None, :])
    return (jnp.cos(angles), jnp.sin(angles), allowed_mask)


def gelu_tanh(values):
    return jax.nn.gelu(values, approximate=True)


def attention_probs(queries, keys, allowed_mask, score_scale):
    scores = (
        jnp.einsum("ihd,jd->hij", queries, keys, preferred_element_type=jnp.float32) * score_scale
    )
    return jnp.where(allowed_mask[None], scores, MASKED)


def mp_total(size):
    def kernel(part, out, near, mine, far, core_send, core_recv, y_send, y_recv, back_send, back_recv):
        dp, mp = lax.axis_index("dp"), lax.axis_index("mp")
        side = lax.rem(mp, 2)
        core = (dp, mp + 1 - 2 * side)
        other = (dp, lax.rem(mp + 2, 4))
        half = part.shape[0] // 2
        pieces = near.shape[0]
        width = part.shape[1] // pieces
        own = pl.ds(pl.multiple_of(side * half, half), half)
        theirs = pl.ds(pl.multiple_of((1 - side) * half, half), half)

        def columns(i):
            return pl.ds(i * width, width)

        barrier = pltpu.get_barrier_semaphore()
        for device in (core, other):
            pl.semaphore_signal(barrier, inc=1, device_id=device, device_id_type=MESH)
        pl.semaphore_wait(barrier, 2)
        first = [
            pltpu.make_async_remote_copy(
                part.at[theirs, columns(i)], near.at[i], core_send.at[i], core_recv.at[i],
                device_id=core, device_id_type=MESH,
            )
            for i in range(pieces)
        ]
        second = [
            pltpu.make_async_remote_copy(
                mine.at[i], far.at[i], y_send.at[i], y_recv.at[i],
                device_id=other, device_id_type=MESH,
            )
            for i in range(pieces)
        ]
        third = [
            pltpu.make_async_remote_copy(
                out.at[own, columns(i)], out.at[own, columns(i)], back_send.at[i], back_recv.at[i],
                device_id=core, device_id_type=MESH,
            )
            for i in range(pieces)
        ]
        for copy in first:
            copy.start()
        for i in range(pieces):
            first[i].wait_recv()
            mine[i] = part[own, columns(i)] + near[i]
            second[i].start()
        for i in range(pieces):
            second[i].wait_recv()
            out[own, columns(i)] = mine[i] + far[i]
            third[i].start()
        for copy in third:
            copy.wait_recv()
        for copy in first + second + third:
            copy.wait_send()

    def total(identity, *parts):
        if size != 4:
            return lax.psum(parts, "mp")
        joined = jnp.concatenate(parts, axis=1)
        tokens_here, columns_here = joined.shape
        pieces = 1
        for count in (5, 4, 3, 2):
            if columns_here % (128 * count) == 0:
                pieces = count
                break
        half = (pieces, tokens_here // 2, columns_here // pieces)
        summed = pl.pallas_call(
            kernel,
            out_shape=jax.ShapeDtypeStruct(joined.shape, jnp.float32),
            in_specs=[pl.BlockSpec(memory_space=pltpu.VMEM)],
            out_specs=pl.BlockSpec(memory_space=pltpu.VMEM),
            scratch_shapes=[pltpu.VMEM(half, jnp.float32)] * 3
            + [pltpu.SemaphoreType.DMA((pieces,))] * 6,
            compiler_params=pltpu.CompilerParams(
                collective_id=identity, has_side_effects=True, vmem_limit_bytes=16 << 20
            ),
        )(joined)
        edges, start = [], 0
        for part in parts:
            edges.append(summed[:, start : start + part.shape[1]])
            start += part.shape[1]
        return tuple(edges)

    return total


def forward_loop(hidden_state, shared, adapters, tables, total, identity):
    (mixer_gain, feed_gain, query_matrix, pair_matrix, output_matrix, widen_matrix, down_matrix) = shared
    (q_in, q_out, kv_in, kv_out, o_in, o_out, w_in, w_out, d_in, d_out) = adapters
    cosine, sine, allowed = tables
    tokens_here, width = hidden_state.shape
    head = pair_matrix.shape[1] // 2
    heads = query_matrix.shape[1] // head
    rank = q_in.shape[1]
    hidden = down_matrix.shape[0]
    kept = SimpleNamespace(h=hidden_state)
    normed, kept.mixer_factor = normalize(hidden_state, mixer_gain)
    normed = normed.astype(jnp.bfloat16)
    query_rank = product(normed, q_in).astype(jnp.bfloat16)
    query_linear = product(normed, query_matrix) + product(query_rank, q_out)
    pair_rank = product(normed, kv_in.reshape(width, 2 * rank)).astype(jnp.bfloat16)
    pair_linear = product(normed, pair_matrix) + jnp.concatenate(
        [product(pair_rank[:, :rank], kv_out[0]), product(pair_rank[:, rank:], kv_out[1])], axis=1
    )
    queries = rotate(
        query_linear.reshape(tokens_here, heads, head), cosine[:, None], sine[:, None]
    ).astype(jnp.bfloat16)
    keys = rotate(pair_linear[:, :head], cosine, sine).astype(jnp.bfloat16)
    values = pair_linear[:, head:].astype(jnp.bfloat16)
    masked = attention_probs(queries, keys, allowed, 1.0 / math.sqrt(head))
    expo = jnp.exp(masked - jnp.max(masked, axis=-1, keepdims=True))
    probs = expo / jnp.sum(expo, axis=-1, keepdims=True)
    mixed = jnp.einsum(
        "hij,jd->ihd", probs.astype(jnp.bfloat16), values, preferred_element_type=jnp.float32
    )
    mixed = mixed.reshape(tokens_here, heads * head).astype(jnp.bfloat16)
    summed, output_rank = total(identity, product(mixed, output_matrix), product(mixed, o_in))
    middle = hidden_state + summed + exact_product(output_rank, o_out.astype(jnp.float32))
    fed, kept.feed_factor = normalize(middle, feed_gain)
    fed = fed.astype(jnp.bfloat16)
    widen_rank = product(fed, w_in.reshape(width, 2 * rank)).astype(jnp.bfloat16)
    gate = product(fed, widen_matrix[:, 0]) + product(widen_rank[:, :rank], w_out[0])
    up = product(fed, widen_matrix[:, 1]) + product(widen_rank[:, rank:], w_out[1])
    activated = (gelu_tanh(gate) * up).astype(jnp.bfloat16)
    shrunk, shrink_rank = total(identity + 1, product(activated, down_matrix), product(activated, d_in))
    result = middle + shrunk + exact_product(shrink_rank, d_out.astype(jnp.float32))
    vars(kept).update(
        normed=normed, query_rank=query_rank, pair_rank=pair_rank, queries=queries, keys=keys,
        values=values, probs=probs, mixed=mixed, output_rank=output_rank, middle=middle, fed=fed,
        widen_rank=widen_rank, gate=gate, up=up, activated=activated, shrink_rank=shrink_rank,
    )
    return result, kept


def reverse_loop(upstream, kept, shared, adapters, tables, total, identity):
    (mixer_gain, feed_gain, query_matrix, pair_matrix, output_matrix, widen_matrix, down_matrix) = shared
    (q_in, q_out, kv_in, kv_out, o_in, o_out, w_in, w_out, d_in, d_out) = adapters
    cosine, sine, allowed = tables
    tokens_here, width = upstream.shape
    head = pair_matrix.shape[1] // 2
    heads = query_matrix.shape[1] // head
    rank = q_in.shape[1]
    scale = 1.0 / math.sqrt(head)
    grad_feed = upstream.astype(jnp.bfloat16)
    grad_shrink_rank = product_t(grad_feed, d_out).astype(jnp.bfloat16)
    grad_activated = product_t(grad_feed, down_matrix) + product_t(grad_shrink_rank, d_in)
    gelu_value, gelu_pullback = jax.vjp(gelu_tanh, kept.gate)
    grad_gate = gelu_pullback(grad_activated * kept.up)[0].astype(jnp.bfloat16)
    grad_up = (grad_activated * gelu_value).astype(jnp.bfloat16)
    grad_fed, grad_widen_rank = total(
        identity,
        product_t(grad_gate, widen_matrix[:, 0]) + product_t(grad_up, widen_matrix[:, 1]),
        jnp.concatenate([product_t(grad_gate, w_out[0]), product_t(grad_up, w_out[1])], axis=1),
    )
    grad_widen_rank = grad_widen_rank.astype(jnp.bfloat16)
    grad_fed = grad_fed + product_t(grad_widen_rank, w_in.reshape(width, 2 * rank))
    grad_norm, feed_gain_grad = normalize_back(kept.middle, kept.feed_factor, feed_gain, grad_fed)
    grad_middle = upstream + grad_norm
    grad_attend = grad_middle.astype(jnp.bfloat16)
    grad_output_rank = product_t(grad_attend, o_out).astype(jnp.bfloat16)
    grad_mixed = product_t(grad_attend, output_matrix) + product_t(grad_output_rank, o_in)
    grad_mixed = grad_mixed.astype(jnp.bfloat16).reshape(tokens_here, heads, head)
    queries, keys, values, probs = kept.queries, kept.keys, kept.values, kept.probs
    grad_probs = jnp.einsum("ihd,jd->hij", grad_mixed, values, preferred_element_type=jnp.float32)
    delta = jnp.sum(grad_probs * probs, axis=-1, keepdims=True)
    grad_scores = (probs * (grad_probs - delta)).astype(jnp.bfloat16)
    grad_queries = scale * jnp.einsum(
        "hij,jd->ihd", grad_scores, keys, preferred_element_type=jnp.float32
    )
    grad_keys = scale * jnp.einsum(
        "hij,ihd->jd", grad_scores, queries, preferred_element_type=jnp.float32
    )
    grad_values = jnp.einsum(
        "hij,ihd->jd", probs.astype(jnp.bfloat16), grad_mixed, preferred_element_type=jnp.float32
    )
    grad_query = rotate(grad_queries, cosine[:, None], -sine[:, None])
    grad_query = grad_query.reshape(tokens_here, heads * head).astype(jnp.bfloat16)
    grad_normed, grad_query_rank, grad_pair = total(
        identity + 1,
        product_t(grad_query, query_matrix),
        product_t(grad_query, q_out),
        jnp.concatenate([rotate(grad_keys, cosine, -sine), grad_values], axis=1),
    )
    grad_query_rank = grad_query_rank.astype(jnp.bfloat16)
    grad_pair = grad_pair.astype(jnp.bfloat16)
    grad_pair_rank = jnp.concatenate(
        [product_t(grad_pair[:, :head], kv_out[0]), product_t(grad_pair[:, head:], kv_out[1])], axis=1
    ).astype(jnp.bfloat16)
    grad_normed = (
        grad_normed
        + product_t(grad_query_rank, q_in)
        + product_t(grad_pair, pair_matrix)
        + product_t(grad_pair_rank, kv_in.reshape(width, 2 * rank))
    )
    grad_norm, mixer_gain_grad = normalize_back(
        kept.h, kept.mixer_factor, mixer_gain, grad_normed
    )
    vars(kept).update(
        grad_feed=grad_feed, grad_shrink_rank=grad_shrink_rank, grad_gate=grad_gate, grad_up=grad_up,
        grad_widen_rank=grad_widen_rank, grad_attend=grad_attend, grad_output_rank=grad_output_rank,
        grad_query=grad_query, grad_query_rank=grad_query_rank, grad_pair=grad_pair,
        grad_pair_rank=grad_pair_rank, feed_gain_grad=feed_gain_grad, mixer_gain_grad=mixer_gain_grad,
    )
    return grad_middle + grad_norm


def scattered_gradients(kept, dp_size, mp_size):
    def scatter(value, axis):
        return lax.psum_scatter(value, "dp", scatter_dimension=axis, tiled=True)

    def shared_of(factors):
        return sum(product_tn(*factors(k)) for k in kept)

    def each(function):
        return jnp.stack([function(k) for k in kept], axis=0)

    def quarter(value, axis):
        block = scatter(value, axis)
        size = block.shape[axis] // mp_size
        return lax.dynamic_slice_in_dim(block, lax.axis_index("mp") * size, size, axis)

    width = kept[0].normed.shape[1]
    rank = kept[0].query_rank.shape[1]
    head = kept[0].grad_pair.shape[1] // 2

    def pair_outer(k):
        left, right = k.pair_rank, k.grad_pair
        return jnp.stack(
            [product_tn(left[:, :rank], right[:, :head]), product_tn(left[:, rank:], right[:, head:])]
        )

    def expand_outer(k):
        left = k.widen_rank
        return jnp.stack(
            [product_tn(left[:, :rank], k.grad_gate), product_tn(left[:, rank:], k.grad_up)]
        )

    return (
        scatter(sum(k.mixer_gain_grad for k in kept), 0),
        scatter(sum(k.feed_gain_grad for k in kept), 0),
        scatter(shared_of(lambda k: (k.normed, k.grad_query)), 0),
        quarter(shared_of(lambda k: (k.normed, k.grad_pair)), 0),
        scatter(shared_of(lambda k: (k.mixed, k.grad_attend)), 1),
        scatter(jnp.stack([shared_of(lambda k: (k.fed, k.grad_gate)), shared_of(lambda k: (k.fed, k.grad_up))], axis=1), 0),
        scatter(shared_of(lambda k: (k.activated, k.grad_feed)), 1),
        quarter(each(lambda k: product_tn(k.normed, k.grad_query_rank)), 1),
        scatter(each(lambda k: product_tn(k.query_rank, k.grad_query)), 1),
        quarter(
            each(lambda k: product_tn(k.normed, k.grad_pair_rank).reshape(width, 2, rank)), 1
        ),
        quarter(each(pair_outer), 2),
        scatter(each(lambda k: product_tn(k.mixed, k.grad_output_rank)), 2),
        scatter(
            each(lambda k: exact_tn(k.output_rank, k.grad_attend.astype(jnp.float32))), 2
        ),
        quarter(
            each(lambda k: product_tn(k.fed, k.grad_widen_rank).reshape(width, 2, rank)), 1
        ),
        scatter(each(expand_outer), 2),
        scatter(each(lambda k: product_tn(k.activated, k.grad_shrink_rank)), 2),
        scatter(each(lambda k: exact_tn(k.shrink_rank, k.grad_feed.astype(jnp.float32))), 2),
    )


WIDE = 896


def split3(value):
    high = value.astype(jnp.bfloat16)
    rest = value - high.astype(jnp.float32)
    middle = rest.astype(jnp.bfloat16)
    low = (rest - middle.astype(jnp.float32)).astype(jnp.bfloat16)
    return high, middle, low


WEIGHTS = (
    "q_in", "query", "q_out", "kv_in", "pair", "kv_out", "output", "o_in", "o_out",
    "wide", "w_out", "down", "d_in", "d_out", "w_in",
)
SUM_STEP = 384


def block_kernel(*refs):
    (h_in, cot, segments, mixer_gain, feed_gain), refs = refs[:5], refs[5:]
    count = len(WEIGHTS)
    sources, refs = refs[:count], refs[count:]
    (
        out_ref, grad_ref, raw_out, x_all, r_all, b_all, q_all, x_got, r_got, b_got, x_end, r_end, b_end,
    ), refs = refs[:13], refs[13:]
    weights, refs = (*refs[: count - 1], refs[WEIGHTS.index("kv_in")]), refs[count - 1 :]
    (
        h_s, mid_s, normed_s, qr_s, kvr_s, q_s, k_s, v_s, probs_s, mixed_s, or_s, fed_s, er_s,
        gate_s, up_s, act_s, sr_s, gg_s, gu_s, g_s, gain_s, select,
        part, total, near, mine, far, side_part, side_near, side_mine, side_far, side_total,
        late_s, er_grad_s, chosen_s, xs, rs, bs, qs, kv_flat, w_flat, cosine_ref, sine_ref, mask_ref,
        load_sems, c_s, c_r, y_s, y_r, e_s, e_r,
        xl, rl, bl, ql, x_s, x_r, r_s, r_r, b_s, b_r, xe_s, xe_r, re_s, re_r, be_s, be_r, bf_s, bf_r,
        sc_s, sc_r, sy_s, sy_r, se_s, se_r, xc_s, xc_r, rc_s, rc_r, raw_ref, raw_sems,
    ) = refs
    W = SimpleNamespace(**dict(zip(WEIGHTS, weights)))
    dp, mp = lax.axis_index("dp"), lax.axis_index("mp")
    side = lax.rem(mp, 2)
    core = (dp, mp + 1 - 2 * side)
    other = (dp, lax.rem(mp + 2, 4))
    loads = [
        pltpu.make_async_copy(source, target, load_sems.at[i])
        for i, (source, target) in enumerate(zip(sources, weights))
    ]
    load = SimpleNamespace(**dict(zip(WEIGHTS, loads)))
    for copy in loads[:-1]:
        copy.start()
    x = lax.rem(dp, 2)
    z = dp // 2
    pair = (dp + 1 - 2 * x, mp)
    near_end = (dp + 2 - 4 * lax.rem(z, 2), mp)
    is_end = jnp.logical_or(z == 0, z == 3)
    barrier = pltpu.get_barrier_semaphore()
    for device in (core, other, pair, near_end):
        pl.semaphore_signal(barrier, inc=1, device_id=device, device_id_type=MESH)
    pl.semaphore_wait(barrier, 4)

    tokens, width = h_in.shape
    half = tokens // 2
    head = W.query.shape[1]
    rank = W.q_in.shape[2]
    hidden = W.down.shape[0]
    loops = W.q_in.shape[0]
    scale = 1.0 / math.sqrt(head)
    own = pl.ds(pl.multiple_of(side * half, half), half)
    theirs = pl.ds(pl.multiple_of((1 - side) * half, half), half)
    blocks = x_all.shape[1] * x_all.shape[2]
    block = width // blocks
    quarter = block // 4
    rank_quarter = rank // (4 * blocks)
    chunks = [(0, WIDE), (WIDE, hidden - WIDE)]

    def remote(source, target, send, recv, device):
        return pltpu.make_async_remote_copy(
            source, target, send, recv, device_id=device, device_id_type=MESH
        )

    def span(l):
        return pl.ds(pl.multiple_of(l * tokens, tokens), tokens)

    def end_span(l, is_far):
        return pl.ds(pl.multiple_of((2 * l + is_far) * tokens, tokens), tokens)

    def x_copies(i, l):
        across = onward = None
        if i < 2:
            across = remote(
                xs.at[i, 1 - x], x_got.at[i, :, :, span(l)], x_s.at[i, l], x_r.at[i, l], pair
            )
            onward = remote(
                xs.at[i, x], x_end.at[i, :, :, end_span(l, 0)],
                xe_s.at[0, i, l], xe_r.at[0, i, l], near_end,
            )
        return pltpu.make_async_copy(xs.at[i], x_all.at[i, :, :, :, span(l)], xl.at[i, l]), across, onward

    def r_copies(i, l):
        across = onward = None
        if i < 3:
            across = remote(
                rs.at[i, 1 - x], r_got.at[i, :, :, span(l)], r_s.at[i, l], r_r.at[i, l], pair
            )
        if i in (1, 2):
            onward = remote(
                rs.at[i, x], r_end.at[i - 1, :, :, end_span(l, 0)],
                re_s.at[0, i - 1, l], re_r.at[0, i - 1, l], near_end,
            )
        return pltpu.make_async_copy(rs.at[i], r_all.at[i, :, :, :, span(l)], rl.at[i, l]), across, onward

    def b_copies(i, l):
        across = onward = None
        if i in (0, 4, 5):
            k = max(0, i - 3)
            across = remote(bs.at[i], b_got.at[k, span(l)], b_s.at[k, l], b_r.at[k, l], pair)
        if i >= 3:
            k = (i - 4) % 3
            onward = remote(
                bs.at[i], b_end.at[k, end_span(l, 0)], be_s.at[k, l], be_r.at[k, l], near_end
            )
        return pltpu.make_async_copy(bs.at[i], b_all.at[i, span(l)], bl.at[i, l]), across, onward

    def q_copies(i, l):
        return pltpu.make_async_copy(qs.at[i], q_all.at[i, span(l)], ql.at[i, l]), None, None

    def launch(copies, whole=True):
        local, across, onward = copies
        local.start()
        if across is not None:
            across.start()
        if onward is not None:

            @pl.when(is_end if whole else jnp.logical_and(is_end, side == 0))
            def _():
                onward.start()

    def finish(copies, whole=True):
        local, across, onward = copies
        local.wait()
        if across is not None:
            across.wait_send()
        if onward is not None:

            @pl.when(is_end if whole else jnp.logical_and(is_end, side == 0))
            def _():
                onward.wait_send()

    def far_rows(i, l):
        return [
            remote(
                x_got.at[i, :, :, span(l)], x_end.at[i, :, :, end_span(l, 1)],
                xe_s.at[1, i, l], xe_r.at[1, i, l], near_end,
            ),
            remote(
                r_got.at[i + 1, :, :, span(l)], r_end.at[i, :, :, end_span(l, 1)],
                re_s.at[1, i, l], re_r.at[1, i, l], near_end,
            ),
        ]

    def far_act(l):
        return remote(
            b_got.at[1, span(l)], b_end.at[0, end_span(l, 1)], bf_s.at[l], bf_r.at[l], near_end
        )

    def pass_act(l):
        for i in (4, 5):
            b_copies(i, l)[1].wait_recv()

        @pl.when(is_end)
        def _():
            far_act(l).start()

    def pass_rows(i, l):
        x_copies(i, l)[1].wait_recv()
        r_copies(i + 1, l)[1].wait_recv()

        @pl.when(jnp.logical_and(is_end, side == 1))
        def _():
            for copy in far_rows(i, l):
                copy.start()

    def ship_x(i, l, value, again, before):
        @pl.when(again)
        def _():
            finish(x_copies(i, before), False)

        turned = value.astype(jnp.float32).T
        for b in range(blocks):
            xs[i, b % 2, b // 2] = turned[b * block : (b + 1) * block]
        launch(x_copies(i, l), False)

    def ship_r(i, l, value, again, before):
        @pl.when(again)
        def _():
            finish(r_copies(i, before), False)

        turned = value.astype(jnp.float32).T
        size = rank // blocks
        for b in range(blocks):
            rs[i, b % 2, b // 2] = turned[b * size : (b + 1) * size]
        launch(r_copies(i, l), False)

    def ship_b(i, l, values, again, before):
        @pl.when(again)
        def _():
            finish(b_copies(i, before))

        filled = 0
        for value in values:
            n = value.shape[1]
            bs[i, :, filled : filled + n] = value.astype(jnp.float32)
            filled += n
        if filled < WIDE:
            bs[i, :, filled:] = jnp.zeros((tokens, WIDE - filled), jnp.float32)
        launch(b_copies(i, l))

    def ship_q(i, l, value, again, before):
        @pl.when(again)
        def _():
            finish(q_copies(i, before))

        qs[i] = value.astype(jnp.float32)
        launch(q_copies(i, l))

    def columns_of(size):
        return [(at, min(SUM_STEP, size - at)) for at in range(0, size, SUM_STEP)]

    def side_copies(turn, size):
        columns = pl.ds(0, size)
        return (
            remote(
                side_part.at[turn, theirs, columns], side_near.at[turn, :, columns],
                sc_s.at[turn], sc_r.at[turn], core,
            ),
            remote(
                side_mine.at[turn, :, columns], side_far.at[turn, :, columns],
                sy_s.at[turn], sy_r.at[turn], other,
            ),
            remote(
                side_total.at[turn, own, columns], side_total.at[turn, own, columns],
                se_s.at[turn], se_r.at[turn], core,
            ),
        )

    def finish_side(turn, size):
        first, second, third = side_copies(turn, size)
        second.wait_recv()
        side_total[turn, own, :size] = side_mine[turn, :, :size] + side_far[turn, :, :size]
        third.start()
        third.wait_recv()
        for copy in (first, second, third):
            copy.wait_send()
        return side_total[turn, :, :size]

    def sum_over_mp(fill, turn, side_size, finish_previous, idle, side_ahead=False):
        pieces = columns_of(width)

        def pieces_of(make):
            return [make(i, pl.ds(at, n)) for i, (at, n) in enumerate(pieces)]

        first = pieces_of(
            lambda i, c: remote(part.at[theirs, c], near.at[:, c], c_s.at[i], c_r.at[i], core)
        )
        second = pieces_of(
            lambda i, c: remote(
                mine.at[:, c], far.at[turn, :, c], y_s.at[turn, i], y_r.at[turn, i], other
            )
        )
        third = pieces_of(
            lambda i, c: remote(total.at[own, c], total.at[own, c], e_s.at[i], e_r.at[i], core)
        )
        side_first, side_second, _ = side_copies(turn, side_size)

        def middle(i):
            at, n = pieces[i]
            first[i].wait_recv()
            mine[:, at : at + n] = part[own, at : at + n] + near[:, at : at + n]
            second[i].start()

        def begin_side():
            side_first.wait_recv()
            side_mine[turn, :, :side_size] = (
                side_part[turn, own, :side_size] + side_near[turn, :, :side_size]
            )
            finish_previous()
            side_second.start()

        side_behind = jnp.logical_not(side_ahead)
        pl.when(side_ahead)(side_first.start)
        for i, (at, n) in enumerate(pieces):
            fill(at, n)
            first[i].start()
            if i:
                middle(i - 1)
            else:
                pl.when(side_ahead)(begin_side)
        pl.when(side_behind)(side_first.start)
        middle(len(first) - 1)
        pl.when(side_behind)(begin_side)
        idle()
        for i, (at, n) in enumerate(pieces):
            second[i].wait_recv()
            total[own, at : at + n] = mine[:, at : at + n] + far[turn, :, at : at + n]
            third[i].start()
        for copy in third:
            copy.wait_recv()
        for copy in first + second + third:
            copy.wait_send()

    def dot(left, right):
        return jnp.dot(left, right, preferred_element_type=jnp.float32)

    def low(value):
        return value.astype(jnp.bfloat16)

    def spin(value, sign):
        a, b = value[:, : head // 2], value[:, head // 2 :]
        cosine, sine = cosine_ref[...], sign * sine_ref[...]
        return jnp.concatenate([a * cosine - b * sine, b * cosine + a * sine], axis=1)

    def factor_of(value):
        return lax.rsqrt(jnp.mean(value * value, axis=-1, keepdims=True) + EPSILON)

    def gelu_parts(value):
        c = math.sqrt(2.0 / math.pi)
        square = value * value
        t = jnp.tanh(c * value * (1.0 + 0.044715 * square))
        gelu = 0.5 * value * (1.0 + t)
        slope = 0.5 * (1.0 + t) + 0.5 * value * (1.0 - t * t) * c * (1.0 + 3 * 0.044715 * square)
        return gelu, slope

    across_row = jnp.broadcast_to(segments[...].astype(jnp.float32), (tokens, tokens))
    down_row = across_row.T
    at_row = lax.broadcasted_iota(jnp.int32, (tokens, tokens), 0)
    at_column = lax.broadcasted_iota(jnp.int32, (tokens, tokens), 1)
    earlier = jnp.sum(jnp.where(across_row < down_row, 1.0, 0.0), axis=1, keepdims=True)
    position = at_row[:, : head // 2].astype(jnp.float32) - earlier
    exponent = at_column[:, : head // 2].astype(jnp.float32) * (-2.0 / head)
    angles = position * jnp.exp(exponent * math.log(10000.0))
    cosine_ref[...] = jnp.cos(angles)
    sine_ref[...] = jnp.sin(angles)
    mask_ref[...] = jnp.where(
        jnp.logical_and(across_row == down_row, at_row >= at_column), 1.0, 0.0
    )
    h_s[0] = h_in[...].astype(jnp.float32)
    mixer, feed = mixer_gain[...].reshape(1, width), feed_gain[...].reshape(1, width)

    def forward(l, carry):
        def need(*copies):
            @pl.when(l == 0)
            def _():
                for copy in copies:
                    copy.wait()

        h = h_s[l]
        normed = low(h * factor_of(h) * mixer)
        normed_s[l] = normed
        need(load.q_in, load.query, load.q_out, load.kv_in, load.pair, load.kv_out)

        @pl.when(l == 0)
        def _():
            kv_flat[0] = W.kv_in[0].reshape(width, 2 * rank)

        query_rank = low(dot(normed, W.q_in[l]))
        qr_s[l] = query_rank
        queries = dot(normed, W.query[...]) + dot(query_rank, W.q_out[l])
        q_s[l] = low(spin(queries, 1.0))
        pair_rank = low(dot(normed, kv_flat[l]))
        kvr_s[l] = pair_rank
        keys = dot(normed, W.pair[:, :head]) + dot(pair_rank[:, :rank], W.kv_out[l, 0])
        k_s[l] = low(spin(keys, 1.0))
        values = dot(normed, W.pair[:, head:]) + dot(pair_rank[:, rank:], W.kv_out[l, 1])
        v_s[l] = low(values)
        scores = product_t(q_s[l], k_s[l]) * scale
        scores = jnp.where(mask_ref[...] > 0, scores, MASKED)
        expo = jnp.exp(scores - jnp.max(scores, axis=-1, keepdims=True))
        probs = expo / jnp.sum(expo, axis=-1, keepdims=True)
        probs_s[l] = probs
        mixed = low(dot(low(probs), v_s[l]))
        mixed_s[l] = mixed
        need(load.output, load.o_in, load.o_out)

        output_rank = dot(mixed, W.o_in[l])
        side_part[0, :, :rank] = output_rank
        output_parts = split3(output_rank)

        def fill_attend(at, n):
            value = dot(mixed, W.output[:, at : at + n])
            for piece in output_parts:
                value = value + dot(piece, W.o_out[l, :, at : at + n])
            part[:, at : at + n] = value

        again = l > 0

        def idle_attend():
            ship_x(2, l, normed, again, 0)
            ship_r(3, l, query_rank, again, 0)
            ship_q(1, l, mixed, again, 0)

            @pl.when(l == 0)
            def _():
                for i in range(1, loops):
                    kv_flat[i] = W.kv_in[i].reshape(width, 2 * rank)
                load.w_in.start()
                load.w_in.wait()
                for i in range(loops):
                    w_flat[i] = W.w_in[i].reshape(width, 2 * rank)

            @pl.when(again)
            def _():
                pass_act(0)
                pass_rows(1, loops - 1)

            @pl.when(l == 0)
            def _():
                load.d_out.wait()
                shrink = product_t(cot[...], W.d_out[loops - 1])
                ship_x(1, loops - 1, cot[...], False, 0)
                ship_r(2, loops - 1, low(shrink), False, 0)

        def finish_before_attend():
            @pl.when(again)
            def _():
                sr_s[jnp.maximum(l - 1, 0)] = finish_side(1, rank)

        sum_over_mp(fill_attend, 0, rank, finish_before_attend, idle_attend)
        middle = h_s[l] + total[...]
        mid_s[l] = middle
        fed = low(middle * factor_of(middle) * feed)
        fed_s[l] = fed
        need(load.wide, load.w_out)
        widen_rank = low(dot(fed, w_flat[l]))
        er_s[l] = widen_rank
        for at, n in chunks:
            gate = product_t(fed, W.wide[0, at : at + n]) + product_t(
                widen_rank[:, :rank], W.w_out[l, 0, at : at + n]
            )
            gate_s[l, :, at : at + n] = gate
            up = product_t(fed, W.wide[1, at : at + n]) + product_t(
                widen_rank[:, rank:], W.w_out[l, 1, at : at + n]
            )
            up_s[l, :, at : at + n] = up
            act_s[:, at : at + n] = low(gelu_parts(gate)[0] * up)
            ship_b(4 + at // WIDE, l, [act_s[:, at : at + n]], again, 0)
        need(load.down, load.d_in)

        shrink_rank = dot(act_s[...], W.d_in[l])
        side_part[1, :, :rank] = shrink_rank
        shrink_parts = split3(shrink_rank)

        def fill_feed(at, n):
            value = dot(act_s[...], W.down[:, at : at + n])
            for piece in shrink_parts:
                value = value + dot(piece, W.d_out[l, :, at : at + n])
            part[:, at : at + n] = value

        def idle_feed():
            ship_x(0, l, fed, again, 0)
            ship_r(0, l, widen_rank[:, :rank], again, 0)
            ship_r(1, l, widen_rank[:, rank:], again, 0)

            @pl.when(again)
            def _():
                pass_rows(0, 0)

        def finish_before_feed():
            or_s[l] = finish_side(0, rank)

        sum_over_mp(fill_feed, 1, rank, finish_before_feed, idle_feed)
        h_s[l + 1] = mid_s[l] + total[...]
        return carry

    lax.fori_loop(0, loops, forward, 0)
    out_ref[...] = low(h_s[loops])

    g_s[...] = cot[...].astype(jnp.float32)
    gain_s[...] = jnp.zeros_like(gain_s)
    padded_quarter = select.shape[0] // blocks
    row = lax.broadcasted_iota(jnp.int32, (padded_quarter, width), 0)
    column = lax.broadcasted_iota(jnp.int32, (padded_quarter, width), 1)
    for b in range(blocks):
        hit = jnp.logical_and(column == row + (b * 4 + mp) * quarter, row < quarter)
        select[b * padded_quarter : (b + 1) * padded_quarter] = low(
            jnp.where(hit, 1.0, 0.0)
        )
    small_row = lax.broadcasted_iota(jnp.int32, (rank_quarter, rank), 0)
    small_column = lax.broadcasted_iota(jnp.int32, (rank_quarter, rank), 1)
    rank_select = low(
        jnp.concatenate(
            [
                jnp.where(small_column == small_row + (b * 4 + mp) * rank_quarter, 1.0, 0.0)
                for b in range(blocks)
            ],
            axis=0,
        )
    )
    raw_rows = raw_layout(quarter, rank_quarter, loops)

    tall = raw_rows.tall

    def put(start, size, stride, value, add=False):
        for b in range(blocks):
            piece = value[b * stride : b * stride + size]
            if add:
                raw_ref[b % 2, b // 2, start : start + size] += piece
            else:
                raw_ref[b % 2, b // 2, start : start + size] = piece

    def pair_ranks(l, grad_keys, grad_values):
        return low(
            jnp.concatenate(
                [product_t(grad_keys, W.kv_out[l, 0]), product_t(grad_values, W.kv_out[l, 1])], axis=1
            )
        )

    def raw_of(l):
        grad_rank = late_s[l, :, :rank]
        grad_pair = late_s[l, :, rank:]
        grad_pair_rank = pair_ranks(l, grad_pair[:, :head], grad_pair[:, head:])
        grad_widen = er_grad_s[l]
        normed_own = low(product_t(select[...], normed_s[l]))
        pair_weight = dot(normed_own, grad_pair)
        for j in range(2):
            value = pair_weight[:, j * head : (j + 1) * head]
            put(j * tall, tall, padded_quarter, value, l < loops - 1)
        base = 2 * tall + l * raw_rows.loop

        def put_loop(i, value):
            put(base + i * tall, tall, padded_quarter, value)

        put_loop(0, dot(normed_own, grad_rank))
        for j in range(2):
            put_loop(1 + j, dot(normed_own, grad_pair_rank[:, j * rank : (j + 1) * rank]))
        fed_own = low(product_t(select[...], fed_s[l]))
        for j in range(2):
            put_loop(3 + j, dot(fed_own, grad_widen[:, j * rank : (j + 1) * rank]))
        put_loop(5, sum(dot(chosen_s[l, 1], piece) for piece in split3(or_s[l])))
        put_loop(6, sum(dot(chosen_s[l, 0], piece) for piece in split3(sr_s[l])))
        for j in range(2):
            rank_own = low(product_t(rank_select, kvr_s[l, :, j * rank : (j + 1) * rank]))
            put(
                base + 7 * tall + j * rank_quarter, rank_quarter, rank_quarter,
                dot(rank_own, grad_pair[:, j * head : (j + 1) * head]),
            )

    raw_go = [
        pltpu.make_async_copy(raw_ref.at[:, :, rows], raw_out.at[:, :, rows], raw_sems.at[i])
        for i, rows in enumerate((pl.ds(0, raw_rows.gains), pl.ds(raw_rows.gains, 8)))
    ]

    def back(step, carry):
        l = loops - 1 - step
        again = step > 0
        before = loops - 1

        upstream = g_s[...]
        grad_feed = low(upstream)
        grad_shrink = low(product_t(grad_feed, W.d_out[l]))
        for i, (at, n) in enumerate(chunks):
            grad_act = product_t(grad_feed, W.down[at : at + n]) + product_t(
                grad_shrink, W.d_in[l, at : at + n]
            )
            gelu, slope = gelu_parts(gate_s[l, :, at : at + n])
            grad_gate = low(grad_act * up_s[l, :, at : at + n] * slope)
            grad_up = low(grad_act * gelu)
            gg_s[:, at : at + n] = grad_gate
            gu_s[:, at : at + n] = grad_up
            if i == 0:
                ship_b(0, l, [grad_gate], again, before)
                ship_b(2, l, [grad_up], again, before)
            else:
                ahead = WIDE - n
                grad_up = grad_up.astype(jnp.float32)
                ship_b(1, l, [grad_gate, grad_up[:, :ahead]], again, before)
                ship_b(3, l, [grad_up[:, ahead:]], again, before)

        for j, value in enumerate((gg_s, gu_s)):
            side_part[0, :, j * rank : (j + 1) * rank] = dot(value[...], W.w_out[l, j])
        grad_widen = low(side_part[0, :, : 2 * rank])

        def fill_fed(at, n):
            part[:, at : at + n] = (
                dot(gg_s[...], W.wide[0, :, at : at + n])
                + dot(gu_s[...], W.wide[1, :, at : at + n])
                + product_t(grad_widen, w_flat[l, at : at + n])
            )

        def finish_before_fed():
            @pl.when(step == 0)
            def _():
                sr_s[loops - 1] = finish_side(1, rank)

            @pl.when(again)
            def _():
                late_s[loops - 1] = low(finish_side(1, rank + 2 * head))

        def idle_fed():
            @pl.when(again)
            def _():
                ship_x(1, l, grad_feed, True, before)
                ship_r(2, l, grad_shrink, True, before)

            chosen_s[l, 0] = low(product_t(select[...], grad_feed))

            @pl.when(again)
            def _():
                raw_of(loops - 1)

        sum_over_mp(fill_fed, 0, 2 * rank, finish_before_fed, idle_fed)
        grad_fed = total[...]
        middle = mid_s[l]
        factor = factor_of(middle)
        unit = middle * factor
        scaled = grad_fed * feed
        grad_middle = upstream + factor * (
            scaled - unit * jnp.mean(scaled * unit, axis=-1, keepdims=True)
        )
        gain_s[1:2] += jnp.sum(grad_fed * unit, axis=0, keepdims=True)
        g_s[...] = grad_middle
        grad_attend = low(grad_middle)
        grad_output = low(product_t(grad_attend, W.o_out[l]))
        grad_mixed = low(
            product_t(grad_attend, W.output[...]) + product_t(grad_output, W.o_in[l])
        )
        probs = probs_s[l]
        grad_probs = product_t(grad_mixed, v_s[l])
        delta = jnp.sum(grad_probs * probs, axis=-1, keepdims=True)
        grad_scores = low(probs * (grad_probs - delta))
        grad_query = low(spin(dot(grad_scores, k_s[l]) * scale, -1.0))

        grad_rank = product_t(grad_query, W.q_out[l])
        grad_keys = spin(product_tn(grad_scores, q_s[l]) * scale, -1.0)
        grad_values = product_tn(low(probs), grad_mixed)
        side_part[1, :, :rank] = grad_rank
        side_part[1, :, rank : rank + head] = grad_keys
        side_part[1, :, rank + head :] = grad_values
        grad_rank, grad_keys, grad_values = low(grad_rank), low(grad_keys), low(grad_values)
        grad_pair = jnp.concatenate([grad_keys, grad_values], axis=1)
        grad_pair_rank = pair_ranks(l, grad_keys, grad_values)

        def fill_normed(at, n):
            part[:, at : at + n] = (
                product_t(grad_query, W.query[at : at + n])
                + product_t(grad_rank, W.q_in[l, at : at + n])
                + product_t(grad_pair, W.pair[at : at + n])
                + product_t(grad_pair_rank, kv_flat[l, at : at + n])
            )

        def finish_before_normed():
            er_grad_s[l] = low(finish_side(0, 2 * rank))

        def idle_normed():
            ship_q(0, l, grad_query, again, before)
            ship_x(3, l, grad_attend, again, before)
            ship_r(4, l, grad_output, again, before)
            chosen_s[l, 1] = low(product_t(select[...], grad_attend))

            @pl.when(step == 0)
            def _():
                pass_act(loops - 1)
                pass_rows(0, loops - 1)

            @pl.when(again)
            def _():
                pass_rows(1, 0)
                late_s[0] = low(finish_side(1, rank + 2 * head))
                raw_of(0)
                raw_go[0].start()

        sum_over_mp(fill_normed, 1, rank + 2 * head, finish_before_normed, idle_normed, again)
        grad_normed = total[...]
        h = h_s[l]
        factor = factor_of(h)
        unit = h * factor
        scaled = grad_normed * mixer
        g_s[...] += factor * (scaled - unit * jnp.mean(scaled * unit, axis=-1, keepdims=True))
        gain_s[0:1] += jnp.sum(grad_normed * unit, axis=0, keepdims=True)

        return carry

    lax.fori_loop(0, loops, back, 0)
    grad_ref[...] = g_s[...]
    for b in range(blocks):
        ends = jnp.zeros((8, head), jnp.float32)
        raw_ref[b % 2, b // 2, raw_rows.gains :] = ends
        raw_ref[b % 2, b // 2, raw_rows.gains : raw_rows.gains + 2, :block] = gain_s[
            :2, b * block : (b + 1) * block
        ]
    raw_go[1].start()
    for copy in raw_go:
        copy.wait()
    last = loops - 1
    for copies in (
        x_copies(0, last), x_copies(2, last), r_copies(0, last), r_copies(1, last), r_copies(3, last),
        q_copies(1, last), x_copies(1, 0), x_copies(3, 0), r_copies(2, 0), r_copies(4, 0),
        q_copies(0, 0),
    ):
        finish(copies, False)
    for copies in (
        b_copies(4, last), b_copies(5, last), b_copies(0, 0), b_copies(1, 0), b_copies(2, 0),
        b_copies(3, 0),
    ):
        finish(copies)

    def to_core(i, l, half):
        lanes = end_span(l, half)
        x_part, r_part = x_end.at[i, :, :, lanes], r_end.at[i, :, :, lanes]
        return [
            remote(x_part, x_part, xc_s.at[i, l], xc_r.at[i, l], core),
            remote(r_part, r_part, rc_s.at[i, l], rc_r.at[i, l], core),
        ]

    both = [(i, l) for l in range(loops) for i in range(2)]
    for l in range(loops):
        for copies in (r_copies(0, l), b_copies(0, l)):
            copies[1].wait_recv()

    @pl.when(is_end)
    def _():
        for l in range(loops):
            far_act(l).wait_send()

    @pl.when(jnp.logical_and(is_end, side == 1))
    def _():
        for i, l in both:
            for copy in far_rows(i, l):
                copy.wait_send()

    for half in range(2):

        @pl.when(jnp.logical_and(jnp.logical_not(is_end), side == half))
        def _():
            for i, l in both:
                came = far_rows(i, l) if half else [x_copies(i, l)[2], r_copies(i + 1, l)[2]]
                for copy, onward in zip(came, to_core(i, l, half)):
                    copy.wait_recv()
                    onward.start()

    @pl.when(jnp.logical_not(is_end))
    def _():
        for l in range(loops):
            for copy in [b_copies(i, l)[2] for i in (3, 4, 5)] + [far_act(l)]:
                copy.wait_recv()
        for i, l in both:
            for copy in to_core(i, l, 0):
                copy.wait_send()
                copy.wait_recv()


def raw_layout(quarter, rank_quarter, loops):
    tall = quarter
    loop = 7 * tall + 2 * rank_quarter
    gains = 2 * tall + loops * loop
    return SimpleNamespace(tall=tall, loop=loop, gains=gains, all=gains + 8)


def block_and_factors(block_input, cotangent, segments, shared, stacked, dp_size):
    (mixer_gain, feed_gain, query, pair, output, widen, down) = shared
    (q_in, q_out, kv_in, kv_out, o_in, o_out, w_in, w_out, d_in, d_out) = stacked
    tokens, width = block_input.shape
    head = query.shape[1]
    loops, _, rank = q_in.shape
    hidden = down.shape[0]
    weights = (
        q_in, query, q_out, kv_in, pair, kv_out, output, o_in, o_out,
        widen.transpose(1, 2, 0), w_out.swapaxes(2, 3), down, d_in, d_out, w_in,
    )
    layout = raw_layout(width // (4 * dp_size), rank // (4 * dp_size), loops)
    line = dp_size // 2
    f32, bf16 = jnp.float32, jnp.bfloat16
    shape = jax.ShapeDtypeStruct
    block, rank_block, both = width // dp_size, rank // dp_size, loops * tokens
    out_shape = (
        shape((tokens, width), bf16),
        shape((tokens, width), f32),
        shape((2, line, layout.all, head), f32),
        shape((4, 2, line, block, both), f32),
        shape((5, 2, line, rank_block, both), f32),
        shape((6, both, WIDE), f32),
        shape((2, both, head), f32),
        shape((2, line, block, both), f32),
        shape((3, line, rank_block, both), f32),
        shape((3, both, WIDE), f32),
        shape((2, line, block, 2 * both), f32),
        shape((2, line, rank_block, 2 * both), f32),
        shape((3, 2 * both, WIDE), f32),
    )
    vmem = pl.BlockSpec(memory_space=pltpu.VMEM)
    hbm = pl.BlockSpec(memory_space=pl.ANY)
    widest = rank + 2 * head
    pieces = -(-width // SUM_STEP)
    dma = pltpu.SemaphoreType.DMA

    def kept(columns, dtype, count=loops):
        return pltpu.VMEM((count, tokens, columns), dtype)

    scratch = [pltpu.VMEM(w.shape, bf16) for w in weights[:-1]] + [
        kept(width, f32, loops + 1), kept(width, f32), kept(width, bf16), kept(rank, bf16),
        kept(2 * rank, bf16), kept(head, bf16), kept(head, bf16), kept(head, bf16), kept(tokens, f32),
        kept(head, bf16), kept(rank, f32), kept(width, bf16), kept(2 * rank, bf16),
        kept(hidden, f32), kept(hidden, f32), pltpu.VMEM((tokens, hidden), bf16), kept(rank, f32),
        pltpu.VMEM((tokens, hidden), bf16), pltpu.VMEM((tokens, hidden), bf16),
        pltpu.VMEM((tokens, width), f32), pltpu.VMEM((8, width), f32),
        pltpu.VMEM((dp_size * 48, width), bf16),
        pltpu.VMEM((tokens, width), f32), pltpu.VMEM((tokens, width), f32),
        pltpu.VMEM((tokens // 2, width), f32), pltpu.VMEM((tokens // 2, width), f32),
        pltpu.VMEM((2, tokens // 2, width), f32),
        pltpu.VMEM((2, tokens, widest), f32), pltpu.VMEM((2, tokens // 2, widest), f32),
        pltpu.VMEM((2, tokens // 2, widest), f32), pltpu.VMEM((2, tokens // 2, widest), f32),
        pltpu.VMEM((2, tokens, widest), f32),
        kept(widest, bf16), kept(2 * rank, bf16), pltpu.VMEM((loops, 2, dp_size * 48, tokens), bf16),
        pltpu.VMEM((4, 2, line, block, tokens), f32), pltpu.VMEM((5, 2, line, rank_block, tokens), f32),
        pltpu.VMEM((6, tokens, WIDE), f32), pltpu.VMEM((2, tokens, head), f32),
        pltpu.VMEM((loops, width, 2 * rank), bf16), pltpu.VMEM((loops, width, 2 * rank), bf16),
        pltpu.VMEM((tokens, head // 2), f32), pltpu.VMEM((tokens, head // 2), f32),
        pltpu.VMEM((tokens, tokens), f32),
        dma((len(weights),)), dma((pieces,)), dma((pieces,)), dma((2, pieces)), dma((2, pieces)),
        dma((pieces,)), dma((pieces,)),
        dma((4, loops)), dma((5, loops)), dma((6, loops)), dma((2, loops)),
    ]
    scratch += [dma((2, loops))] * 2 + [dma((3, loops))] * 4
    scratch += [dma((2, 2, loops))] * 4 + [dma((3, loops))] * 2 + [dma((loops,))] * 2
    scratch += [dma((2,))] * 6 + [dma((2, loops))] * 4
    scratch += [pltpu.VMEM((2, line, layout.all, head), f32), dma((2,))]
    return pl.pallas_call(
        block_kernel,
        out_shape=out_shape,
        in_specs=[vmem] * 5 + [hbm] * len(weights),
        out_specs=(vmem,) * 2 + (hbm,) * 11,
        scratch_shapes=scratch,
        compiler_params=pltpu.CompilerParams(
            collective_id=21, has_side_effects=True, vmem_limit_bytes=63 << 20
        ),
    )(
        block_input, cotangent, segments, mixer_gain, feed_gain,
        *weights,
    )


def line_kernel(
    raw_all, x_all, r_all, b_all, q_all, x_got, r_got, b_got, x_end_all, r_end_all, b_end_all,
    mixer_out, feed_out, q_w, pair_w, o_w, e_w, s_w, q_i, q_o, p_i, p_o, o_i, o_o, e_i, e_o, s_i, s_o,
    main_out, side_out, raw_out, around,
    x_own, r_own, b_own, q_own, x_far, r_far, b_far, q_far, x_end, r_end, b_end, raw_own, raw_far, product_ref,
    main_right, main_left, side_right, side_left, raw_right, raw_left,
    x_s, x_r, r_s, r_r, b_s, b_r, q_s, q_r, w_s, w_r, local_sems, step_sems, around_s, around_r, ee_s, ee_r,
    mr_s, mr_r, ml_s, ml_r, sr_s, sr_r, sl_s, sl_r, rr_s, rr_r, rl_s, rl_r,
    credit_right, credit_left,
):
    dp, mp = lax.axis_index("dp"), lax.axis_index("mp")
    x = lax.rem(dp, 2)
    z = dp // 2
    last = 3
    pair = (dp + 1 - 2 * x, mp)
    up, down = (dp + 2, mp), (dp - 2, mp)

    core, other = (dp, mp + 1 - 2 * lax.rem(mp, 2)), (dp, lax.rem(mp + 2, 4))
    hidden = s_w.shape[1]
    block, rank_block, quarter = s_w.shape[0], s_i.shape[1], pair_w.shape[0]
    loops, head = s_i.shape[0], q_w.shape[1]
    layout = raw_layout(quarter, rank_block // 4, loops)
    tall = layout.tall
    tail = hidden - WIDE
    short = 2 * hidden - 3 * WIDE

    barrier = pltpu.get_barrier_semaphore()
    for device in (pair, core, other):
        pl.semaphore_signal(barrier, inc=1, device_id=device, device_id_type=MESH)

    @pl.when(z > 0)
    def _():
        pl.semaphore_signal(barrier, inc=1, device_id=down, device_id_type=MESH)

    @pl.when(z < last)
    def _():
        pl.semaphore_signal(barrier, inc=1, device_id=up, device_id_type=MESH)

    def across(source, target, send, recv):
        return pltpu.make_async_remote_copy(
            source, target, send, recv, device_id=pair, device_id_type=MESH
        )

    def x_copy(i):
        return across(x_all.at[i, 1 - x], x_far.at[i], x_s.at[i - 2], x_r.at[i - 2])

    def r_copy(i):
        return across(r_all.at[i, 1 - x], r_far.at[i], r_s.at[i - 3], r_r.at[i - 3])

    def b_copy(i):
        return across(b_all.at[i], b_far.at[i], b_s.at[i], b_r.at[i])

    q_copy = across(q_all, q_far, q_s, q_r)
    w_copy = across(raw_all.at[1 - x], raw_far, w_s, w_r)

    def here(source, target, i):
        return pltpu.make_async_copy(source, target, local_sems.at[i])

    at_start = [
        here(x_all.at[:, x], x_own, 0),
        here(r_all.at[:, x], r_own, 1),
        here(x_got, x_far.at[0:2], 2),
        here(r_got, r_far.at[0:3], 3),
        here(b_got.at[0], b_far.at[0], 4),
        here(b_got.at[1:3], b_far.at[4:6], 5),
        here(q_all, q_own, 6),
    ]
    tokens = b_end.shape[1] // 4

    def end_rows(at):
        return pl.ds(at * tokens, tokens)

    for_ends = [
        here(x_end_all, x_end, 7), here(r_end_all, r_end, 8), here(b_end_all.at[0], b_end.at[0], 9)
    ] + [
        here(b_end_all.at[k, end_rows(2 * l)], b_end.at[k, end_rows(2 * l)], 9 + 2 * k + l)
        for k in (1, 2) for l in range(loops)
    ]

    def end_copies(k):
        return [
            across(
                b_end_all.at[k, end_rows(2 * l)], b_end.at[k, end_rows(2 * l + 1)],
                ee_s.at[k - 1, l], ee_r.at[k - 1, l],
            )
            for l in range(loops)
        ]

    own_copy = here(raw_all.at[x], raw_own, 10)
    inner = jnp.logical_and(z > 0, z < last)

    def chunk_of(step):
        return jnp.where(lax.rem(step, 3) == 0, 4 + step // 3, step - 1 - step // 3)

    def begins_inside(step):
        return jnp.logical_or(lax.rem(step, 3) == 0, step == 5)

    def b_load(step):
        slot = lax.rem(step, 2)
        return pltpu.make_async_copy(b_all.at[chunk_of(step)], b_own.at[slot], step_sems.at[slot])

    b_load(0).start()
    for copy in at_start:
        copy.start()

    @pl.when(inner)
    def _():
        for copy in for_ends:
            copy.start()

    own_copy.start()
    pl.semaphore_wait(barrier, 3 + jnp.minimum(z, 1) + jnp.minimum(last - z, 1))
    b_copy(1).start()
    for copy in at_start[:-1]:
        copy.wait()

    @pl.when(inner)
    def _():
        for copy in for_ends:
            copy.wait()

    def chain(target, step, slot, steps, value, out, right, left, r_s, r_r, l_s, l_r, credits):
        def move(buffer, send, recv, i, s, device, size):
            piece = buffer.at[i, s, :, pl.ds(0, size)]
            return pltpu.make_async_remote_copy(
                piece, piece, send.at[i, s], recv.at[i, s], device_id=device, device_id_type=MESH
            )

        def at_size(act):
            full = right.shape[3]
            if credits:
                pl.when(step < steps - 1)(lambda: act(full))
                pl.when(step == steps - 1)(lambda: act(short))
            else:
                act(full)

        def inside(at):
            return begins_inside(at) if credits else at < 0

        def free(credit, i, source, at, from_end):
            @pl.when(
                jnp.logical_and(
                    at <= steps - 1,
                    jnp.logical_not(jnp.logical_and(from_end, inside(at))),
                )
            )
            def _():
                pl.semaphore_signal(credit.at[i], inc=1, device_id=source, device_id_type=MESH)

        def pass_on(i, place, buffer, send, recv, onward, source, at_end, next_to_end, credit):
            def here(i, s, size=right.shape[3]):
                return move(buffer, send, recv, i, s, onward, size)

            def begin():
                if credits:

                    @pl.when(step >= 3)
                    def _():
                        pl.semaphore_wait(credit.at[i], 1)

                at_size(lambda size: here(i, slot, size).start())

            @pl.when(jnp.logical_and(at_end, jnp.logical_not(inside(step))))
            def _():
                buffer[i, slot] = value()
                if credits:
                    before = lax.rem(step + 2 - inside(step - 1).astype(jnp.int32), 3)
                    after = jnp.where(onward[0] > dp, i - 1, i + 1)

                    @pl.when(jnp.logical_and(place < 2, step >= 2))
                    def _():
                        here(after, before).wait_send()

                    @pl.when(place == 2)
                    def _():
                        at_size(lambda size: here(2 - i, slot, size).wait_send())

                    begin()
                else:
                    begin()
                    here(i, slot).wait_send()

            @pl.when(jnp.logical_not(at_end))
            def _():
                if credits:

                    @pl.when(step >= 1)
                    def _():
                        here(i, lax.rem(step + 2, 3)).wait_send()
                        free(credit, i, source, step + 2, next_to_end)

                has_source = jnp.logical_not(jnp.logical_and(next_to_end, inside(step)))

                @pl.when(jnp.logical_not(has_source))
                def _():
                    buffer[i, slot] = value()

                @pl.when(has_source)
                def _():
                    product = value()
                    at_size(lambda size: here(i, slot, size).wait_recv())
                    buffer[i, slot] += product

                begin()

        @pl.when(target > z)
        def _():
            pass_on(target - 1, 3 - target, right, r_s, r_r, up, down, z == 0, z == 1, credit_right)

        @pl.when(target < z)
        def _():
            pass_on(target, target, left, l_s, l_r, down, up, z == last, z == last - 1, credit_left)

        @pl.when(target == z)
        def _():
            out[...] = value()

    def arrive(step, slot, steps, out, right, left, r_s, r_r, l_s, l_r, credits):
        def take(buffer, send, recv, i, size):
            piece = buffer.at[i, slot, :, pl.ds(0, size)]
            pltpu.make_async_remote_copy(
                piece, piece, send.at[i, slot], recv.at[i, slot], device_id=pair, device_id_type=MESH
            ).wait_recv()
            out[:, :size] += buffer[i, slot, :, :size]

        started_inside = begins_inside(step) if credits else step < 0

        def side_of(there, from_end, buffer, send, recv, i, credit, source):
            @pl.when(there)
            def _():
                quiet = jnp.logical_and(from_end, started_inside)

                @pl.when(jnp.logical_not(quiet))
                def _():
                    full = buffer.shape[3]
                    if credits:
                        pl.when(step < steps - 1)(lambda: take(buffer, send, recv, i, full))
                        pl.when(step == steps - 1)(lambda: take(buffer, send, recv, i, short))
                    else:
                        take(buffer, send, recv, i, full)

                if credits:
                    skip = jnp.logical_and(from_end, begins_inside(step + 3))

                    @pl.when(jnp.logical_and(step + 3 <= steps - 1, jnp.logical_not(skip)))
                    def _():
                        pl.semaphore_signal(
                            credit.at[i], inc=1, device_id=source, device_id_type=MESH
                        )

        side_of(z > 0, z == 1, right, r_s, r_r, jnp.maximum(z - 1, 0), credit_right, down)
        side_of(z < last, z == last - 1, left, l_s, l_r, jnp.minimum(z, last - 1), credit_left, up)

    def settle(right, left, r_s, l_s, main):
        def wait(buffer, send, i, slot, size, device):
            piece = buffer.at[i, slot, :, pl.ds(0, size)]
            pltpu.make_async_remote_copy(
                piece, piece, send.at[i, slot], send.at[i, slot], device_id=device, device_id_type=MESH
            ).wait_send()

        full = right.shape[3]
        slot, size = (2, short) if main else (0, full)
        for target in range(1, 4):

            @pl.when(jnp.logical_and(target > z, z > 0))
            def _():
                wait(right, r_s, target - 1, slot, size, up)

        for target in range(3):

            @pl.when(jnp.logical_and(target < z, z < last))
            def _():
                wait(left, l_s, target, slot, size, down)

        if main:

            @pl.when(z == 0)
            def _():
                for i in (0, 1):
                    wait(right, r_s, i, 1, full, up)

            @pl.when(z == last)
            def _():
                for i in (1, 2):
                    wait(left, l_s, i, 1, full, down)

    def order(turn):
        def near(end):
            return jnp.where(end == 0, 3 - turn, jnp.where(turn < 2, 3 - turn, turn - 2))

        return jnp.where(z < 2, near(z), 3 - near(3 - z))

    def dot(left, right):
        return jnp.dot(
            left.astype(jnp.bfloat16), right.astype(jnp.bfloat16), preferred_element_type=jnp.float32
        )

    steps = b_all.shape[0]

    def left_times(x_index, group, target, own, far):
        shared = dot(x_own[x_index, target], own) + dot(x_far[x_index, target], far)
        return [shared, *rank_times(group, target, own, far)]

    def rank_times(group, target, own, far):
        half = own.shape[0] // 2
        rank_own, rank_far = r_own[group, target], r_far[group, target]
        return [
            dot(rank_own[:, :half], own[:half]) + dot(rank_far[:, :half], far[:half]),
            dot(rank_own[:, half:], own[half:]) + dot(rank_far[:, half:], far[half:]),
        ]

    def main_arrive(step):
        slot = lax.rem(step, 3)
        chunk = chunk_of(step)
        arrive(
            step, slot, steps, main_out.at[slot], main_right, main_left, mr_s, mr_r, ml_s, ml_r, True,
        )
        parts = (
            (0, 0, 0, 0, WIDE), (1, 0, 0, WIDE, tail), (1, tail, 1, WIDE, WIDE - tail),
            (2, 0, 1, 0, WIDE), (3, 0, 1, 2 * WIDE - tail, short),
        )
        for which, start, j, at, n in parts:

            @pl.when(chunk == which)
            def _():
                e_w[:, j, at : at + n] = main_out[slot, :block, start : start + n]
                for l in range(loops):
                    first = block + l * rank_block
                    e_o[l, j, :, at : at + n] = main_out[
                        slot, first : first + rank_block, start : start + n
                    ]

        for part, (at, n) in enumerate(((0, WIDE), (WIDE, tail))):

            @pl.when(chunk == 4 + part)
            def _():
                s_w[:, at : at + n] = main_out[slot, :block, :n]
                for l in range(loops):
                    first = block + l * rank_block
                    s_i[l, :, at : at + n] = main_out[slot, first : first + rank_block, :n]

    def turn_body(at, carry):
        step, turn = at // 4, lax.rem(at, 4)
        slot = lax.rem(step, 3)
        chunk = chunk_of(step)
        group = chunk // 2
        target = order(turn)

        @pl.when(turn == 0)
        def _():
            b_load(step).wait()

            @pl.when(step < steps - 1)
            def _():
                b_load(step + 1).start()

            @pl.when(jnp.logical_and(chunk >= 1, chunk <= 3))
            def _():
                b_copy(chunk).wait_recv()

            @pl.when(step == 1)
            def _():
                @pl.when(inner)
                def _():
                    for copy in end_copies(1):
                        copy.start()

                b_copy(2).start()

            @pl.when(step == 2)
            def _():
                @pl.when(inner)
                def _():
                    for copy in end_copies(2):
                        copy.start()

                b_copy(3).start()

            @pl.when(step == 3)
            def _():
                w_copy.start()

                @pl.when(inner)
                def _():
                    for copy in end_copies(1):
                        copy.wait_recv()

            @pl.when(step == 4)
            def _():
                x_copy(2).start()
                x_copy(3).start()
                r_copy(3).start()
                r_copy(4).start()
                q_copy.start()

            @pl.when(jnp.logical_and(step == 5, inner))
            def _():
                for copy in end_copies(2):
                    copy.wait_recv()

        def value():
            parts = left_times(
                group // 2, group, target,
                b_own[lax.rem(step, 2)].astype(jnp.bfloat16), b_far[chunk].astype(jnp.bfloat16),
            )
            product_ref[...] = jnp.concatenate(parts, axis=0)

            @pl.when(chunk == 1)
            def _():
                other_rank = rank_times(
                    1, target, b_own[lax.rem(step, 2)].astype(jnp.bfloat16),
                    b_far[1].astype(jnp.bfloat16),
                )
                kept = product_ref[block:]
                column = lax.broadcasted_iota(jnp.int32, kept.shape, 1)
                product_ref[block:] = jnp.where(
                    column < tail, kept, jnp.concatenate(other_rank, axis=0)
                )

            beyond = jnp.logical_or(
                jnp.logical_and(z == 1, target >= 1),
                jnp.logical_and(z == last - 1, target <= last - 1),
            )

            @pl.when(jnp.logical_and(beyond, chunk >= 3))
            def _():
                end = b_end[jnp.where(chunk == 3, 2, jnp.maximum(chunk - 4, 0))].astype(jnp.bfloat16)
                shared = jnp.where(chunk == 3, 0, 1)
                middle = end.shape[0] // 2
                product_ref[...] += jnp.concatenate(
                    [
                        dot(x_end[shared, target], end),
                        dot(r_end[shared, target, :, :middle], end[:middle]),
                        dot(r_end[shared, target, :, middle:], end[middle:]),
                    ],
                    axis=0,
                )

            return product_ref[...]

        chain(
            target, step, slot, steps, value, main_out.at[slot], main_right, main_left,
            mr_s, mr_r, ml_s, ml_r, True,
        )

        @pl.when(jnp.logical_and(turn == 3, step >= 2))
        def _():
            main_arrive(step - 2)

        return carry

    lax.fori_loop(0, 4 * steps, turn_body, 0)

    w_copy.wait_recv()
    own_copy.wait()
    at_start[-1].wait()

    def raw_body(turn, carry):
        target = order(turn)
        chain(
            target, 0, 0, 1, lambda: raw_own[target] + raw_far[target], raw_out, raw_right, raw_left,
            rr_s, rr_r, rl_s, rl_r, False,
        )
        return carry

    lax.fori_loop(0, 4, raw_body, 0)
    main_arrive(jnp.int32(steps - 2))

    for i in (2, 3):
        x_copy(i).wait_recv()
    for i in (3, 4):
        r_copy(i).wait_recv()
    q_copy.wait_recv()

    def side_body(turn, carry):
        target = order(turn)

        def value():
            parts = [
                left_times(
                    2 + i, 3 + i, target, q_own[i].astype(jnp.bfloat16), q_far[i].astype(jnp.bfloat16)
                )
                for i in range(2)
            ]
            return jnp.concatenate([jnp.concatenate(p, axis=0) for p in parts], axis=1)

        chain(
            target, 0, 0, 1, value, side_out, side_right, side_left,
            sr_s, sr_r, sl_s, sl_r, False,
        )
        return carry

    lax.fori_loop(0, 4, side_body, 0)
    main_arrive(jnp.int32(steps - 1))
    arrive(0, 0, 1, raw_out, raw_right, raw_left, rr_s, rr_r, rl_s, rl_r, False)

    def share(device, owner, i):
        return pltpu.make_async_remote_copy(
            around.at[owner], around.at[owner], around_s.at[i], around_r.at[i],
            device_id=device, device_id_type=MESH,
        )

    far_owner = lax.rem(mp + 2, 4)
    for l in range(loops):
        start = 2 * tall + l * layout.loop + 5 * tall
        around[mp, l] = raw_out[start : start + 2 * tall]
    along, same, passed = share(other, mp, 0), share(core, mp, 1), share(core, far_owner, 2)
    along.start()
    same.start()
    arrive(0, 0, 1, side_out, side_right, side_left, sr_s, sr_r, sl_s, sl_r, False)
    along.wait_recv()
    passed.start()
    q_w[...] = side_out[:block, :head]
    o_w[...] = side_out[:block, head:]
    for l in range(loops):
        start = block + l * rank_block
        q_o[l] = side_out[start : start + rank_block, :head]
        o_i[l] = side_out[start : start + rank_block, head:]
    mixer_out[...] = raw_out[layout.gains, :block]
    feed_out[...] = raw_out[layout.gains + 1, :block]
    for j in range(2):
        pair_w[:, j * head : (j + 1) * head] = raw_out[j * tall : j * tall + quarter]
    for l in range(loops):
        base = 2 * tall + l * layout.loop
        q_i[:, l] = raw_out[base : base + quarter]
        for j in range(2):
            start = base + (1 + j) * tall
            p_i[l, :, j] = raw_out[start : start + quarter]
            e_i[l, :, j] = raw_out[start + 2 * tall : start + 2 * tall + quarter]
            start = base + 7 * tall + j * (rank_block // 4)
            p_o[l, j] = raw_out[start : start + rank_block // 4]
    same.wait_recv()
    passed.wait_recv()
    for l in range(loops):
        for m in range(4):
            o_o[l, m * quarter : (m + 1) * quarter] = around[m, l, :quarter]
            s_o[l, m * quarter : (m + 1) * quarter] = around[m, l, tall : tall + quarter]
    for copy in (along, same, passed):
        copy.wait_send()

    settle(main_right, main_left, mr_s, ml_s, True)
    settle(side_right, side_left, sr_s, sl_s, False)
    settle(raw_right, raw_left, rr_s, rl_s, False)
    @pl.when(inner)
    def _():
        for copy in end_copies(1) + end_copies(2):
            copy.wait_send()

    for copy in (x_copy(2), x_copy(3), r_copy(3), r_copy(4), b_copy(1), b_copy(2), b_copy(3)):
        copy.wait_send()
    q_copy.wait_send()
    w_copy.wait_send()


def line_gradients(factors, loops, dp_size, mp_size, hidden):
    raw, x_all, r_all, b_all, q_all, x_got, r_got, b_got, x_end, r_end, b_end = factors
    block, rank_block, head = x_all.shape[3], r_all.shape[3], q_all.shape[2]
    quarter, rank_quarter = block // mp_size, rank_block // mp_size
    layout = raw_layout(quarter, rank_quarter, loops)
    rows = block + loops * rank_block
    steps = b_all.shape[0]
    vmem = pl.BlockSpec(memory_space=pltpu.VMEM)
    hbm = pl.BlockSpec(memory_space=pl.ANY)
    dma = pltpu.SemaphoreType.DMA
    f32 = jnp.float32
    line = dp_size // 2 - 1
    half_x = pltpu.VMEM((x_all.shape[0], *x_all.shape[2:]), f32)
    half_r = pltpu.VMEM((r_all.shape[0], *r_all.shape[2:]), f32)
    whole_b, whole_q = pltpu.VMEM(b_all.shape, f32), pltpu.VMEM(q_all.shape, f32)
    shapes = (
        (block,), (block,), (block, head), (quarter, 2 * head), (block, head), (block, 2, hidden),
        (block, hidden), (quarter, loops, head), (loops, rank_block, head), (loops, quarter, 2, head),
        (loops, 2, rank_quarter, head), (loops, rank_block, head), (loops, block, head),
        (loops, quarter, 2, head), (loops, 2, rank_block, hidden), (loops, rank_block, hidden),
        (loops, block, head),
    )
    return pl.pallas_call(
        line_kernel,
        out_shape=tuple(jax.ShapeDtypeStruct(v, f32) for v in shapes),
        in_specs=[hbm] * 11,
        out_specs=(vmem,) * len(shapes),
        scratch_shapes=[
            pltpu.VMEM((3, rows, WIDE), f32), pltpu.VMEM((rows, 2 * head), f32),
            pltpu.VMEM((layout.all, head), f32), pltpu.VMEM((4, loops, 2 * layout.tall, head), f32),
        ]
        + [half_x, half_r, pltpu.VMEM((2, *b_all.shape[1:]), f32), whole_q]
        + [half_x, half_r, whole_b, whole_q]
        + [pltpu.VMEM(v.shape, f32) for v in (x_end, r_end, b_end)]
        + [pltpu.VMEM(raw.shape[1:], f32)] * 2
        + [pltpu.VMEM((rows, WIDE), f32)]
        + [pltpu.VMEM((line, 3, rows, WIDE), f32)] * 2
        + [pltpu.VMEM((line, 1, rows, 2 * head), f32)] * 2
        + [pltpu.VMEM((line, 1, layout.all, head), f32)] * 2
        + [dma((2,))] * 4 + [dma((steps,))] * 2 + [dma] * 4 + [dma((15,)), dma((2,)), dma((3,)), dma((3,))]
        + [dma((2, loops))] * 2
        + [dma((line, 3))] * 4 + [dma((line, 1))] * 8
        + [pltpu.SemaphoreType.REGULAR((line,))] * 2,
        compiler_params=pltpu.CompilerParams(
            collective_id=20, has_side_effects=True, vmem_limit_bytes=63 << 20
        ),
    )(*factors)


def in_place(results):
    mixer, feed, q_w, pair_w, o_w, e_w, s_w, q_i, q_o, p_i, p_o, o_i, o_o, e_i, e_o, s_i, s_o = results
    return (
        mixer, feed, q_w, pair_w, o_w.T, e_w, s_w.T, q_i.swapaxes(0, 1), q_o, p_i, p_o,
        o_i.swapaxes(1, 2), o_o.swapaxes(1, 2), e_i, e_o, s_i.swapaxes(1, 2), s_o.swapaxes(1, 2),
    )


def copy_kernel(*refs):
    count = (len(refs) - 2) // 3
    sources, targets, rooms = refs[:count], refs[count : 2 * count], refs[2 * count : 3 * count]
    come = [pltpu.make_async_copy(v, room, refs[-2].at[i]) for i, (v, room) in enumerate(zip(sources, rooms))]
    go = [pltpu.make_async_copy(room, v, refs[-1].at[i]) for i, (v, room) in enumerate(zip(targets, rooms))]
    for copy in come:
        copy.start()
    for first, second in zip(come, go):
        first.wait()
        second.start()
    for copy in go:
        copy.wait()


def placed(values):
    hbm = pl.BlockSpec(memory_space=pl.ANY)
    sems = pltpu.SemaphoreType.DMA((len(values),))
    return pl.pallas_call(
        copy_kernel,
        out_shape=tuple(jax.ShapeDtypeStruct(v.shape, v.dtype) for v in values),
        in_specs=[hbm] * len(values),
        out_specs=(hbm,) * len(values),
        scratch_shapes=[pltpu.VMEM(v.shape, v.dtype) for v in values] + [sems, sems],
        compiler_params=pltpu.CompilerParams(vmem_limit_bytes=60 << 20),
    )(*values)


def per_device(dp_size, mp_size, block_input, cotangent, segments, *parameters):
    shared, stacked = parameters[:7], parameters[7:]
    loops = stacked[0].shape[0]
    if dp_size == 8 and mp_size == 4 and loops == 2:
        output, input_grad, *factors = block_and_factors(
            block_input, cotangent, segments, shared, stacked, dp_size
        )
        gradients = line_gradients(factors, loops, dp_size, mp_size, shared[6].shape[0])
        output, input_grad, *gradients = placed((output, input_grad, *gradients))
        gradients = in_place(gradients)
        return (output, input_grad, *gradients)
    tables = rotary_tables(segments[0], shared[3].shape[1] // 2)
    total = mp_total(mp_size)
    state = block_input.astype(jnp.float32)
    kept_all = []
    for i in range(loops):
        state, kept = forward_loop(state, shared, [v[i] for v in stacked], tables, total, 1)
        kept_all.append(kept)
    upstream = cotangent.astype(jnp.float32)
    for i in reversed(range(loops)):
        upstream = reverse_loop(
            upstream, kept_all[i], shared, [v[i] for v in stacked], tables, total, 3
        )
    return (state.astype(jnp.bfloat16), upstream, *scattered_gradients(kept_all, dp_size, mp_size))


def solution(mesh):
    in_specs = (
        P("dp", None),
        P("dp", None),
        P("dp", None),
        P(),
        P(),
        P(None, "mp"),
        P(),
        P("mp", None),
        P(None, None, "mp"),
        P("mp", None),
        P(),
        P(None, None, "mp"),
        P(),
        P(),
        P(None, "mp", None),
        P(),
        P(),
        P(None, None, None, "mp"),
        P(None, "mp", None),
        P(),
    )
    out_specs = (
        P("dp", None),
        P("dp", None),
        P("dp"),
        P("dp"),
        P("dp", "mp"),
        P(("dp", "mp"), None),
        P("mp", "dp"),
        P("dp", None, "mp"),
        P("mp", "dp"),
        P(None, ("dp", "mp"), None),
        P(None, "dp", "mp"),
        P(None, ("dp", "mp"), None, None),
        P(None, None, ("dp", "mp"), None),
        P(None, "mp", "dp"),
        P(None, None, "dp"),
        P(None, ("dp", "mp"), None, None),
        P(None, None, "dp", "mp"),
        P(None, "mp", "dp"),
        P(None, None, "dp"),
    )
    return jax.shard_map(
        functools.partial(per_device, mesh.shape["dp"], mesh.shape["mp"]),
        mesh=mesh, in_specs=in_specs, out_specs=out_specs, check_vma=False
    )
```

```python
import functools
import math
from types import SimpleNamespace

import jax
import jax.numpy as jnp
from jax import lax
from jax.experimental import pallas as pl
from jax.experimental.pallas import tpu as pltpu
from jax.sharding import PartitionSpec as P

EPSILON = 1e-06
MASKED = -1e30
MESH = pl.DeviceIdType.MESH


def product(left, right):
    return jnp.dot(left, right, preferred_element_type=jnp.float32)


def product_t(left, right):
    return lax.dot_general(
        left, right, (((1,), (1,)), ((), ())), preferred_element_type=jnp.float32
    )


def product_tn(left, right):
    return lax.dot_general(
        left, right, (((0,), (0,)), ((), ())), preferred_element_type=jnp.float32
    )


def exact_product(left, right):
    return jnp.dot(left, right, precision=lax.Precision.HIGHEST, preferred_element_type=jnp.float32)


def exact_tn(left, right):
    return lax.dot_general(
        left,
        right,
        (((0,), (0,)), ((), ())),
        precision=lax.Precision.HIGHEST,
        preferred_element_type=jnp.float32,
    )


def normalize(hidden_state, gain):
    factor = lax.rsqrt(jnp.mean(hidden_state * hidden_state, axis=-1, keepdims=True) + EPSILON)
    return (hidden_state * factor * gain, factor)


def normalize_back(hidden_state, factor, gain, upstream_gradient):
    unit = hidden_state * factor
    scaled = upstream_gradient * gain
    downstream = factor * (scaled - unit * jnp.mean(scaled * unit, axis=-1, keepdims=True))
    return (downstream, jnp.sum(upstream_gradient * unit, axis=0))


def rotate(values, cosine_table, sine_table):
    half_width = values.shape[-1] // 2
    first = values[..., :half_width]
    second = values[..., half_width:]
    return jnp.concatenate(
        [first * cosine_table - second * sine_table, second * cosine_table + first * sine_table],
        axis=-1,
    )


def rotary_tables(segment_row, head_size):
    length_value = segment_row.shape[0]
    earlier = jnp.sum((segment_row[None, :] < segment_row[:, None]).astype(jnp.int32), axis=1)
    position = (jnp.arange(length_value, dtype=jnp.int32) - earlier).astype(jnp.float32)
    steps_half = jnp.arange(head_size // 2, dtype=jnp.float32)
    frequency = 10000.0 ** (-2.0 * steps_half / head_size)
    angles = position[:, None] * frequency[None, :]
    same_segment = segment_row[:, None] == segment_row[None, :]
    ordinal = jnp.arange(length_value, dtype=jnp.int32)
    allowed_mask = same_segment & (ordinal[:, None] >= ordinal[None, :])
    return (jnp.cos(angles), jnp.sin(angles), allowed_mask)


def gelu_tanh(values):
    return jax.nn.gelu(values, approximate=True)


def attention_probs(queries, keys, allowed_mask, score_scale):
    scores = (
        jnp.einsum("ihd,jd->hij", queries, keys, preferred_element_type=jnp.float32) * score_scale
    )
    return jnp.where(allowed_mask[None], scores, MASKED)


def mp_total(size):
    def kernel(part, out, near, mine, far, core_send, core_recv, y_send, y_recv, back_send, back_recv):
        dp, mp = lax.axis_index("dp"), lax.axis_index("mp")
        side = lax.rem(mp, 2)
        core = (dp, mp + 1 - 2 * side)
        other = (dp, lax.rem(mp + 2, 4))
        half = part.shape[0] // 2
        pieces = near.shape[0]
        width = part.shape[1] // pieces
        own = pl.ds(pl.multiple_of(side * half, half), half)
        theirs = pl.ds(pl.multiple_of((1 - side) * half, half), half)

        def columns(i):
            return pl.ds(i * width, width)

        barrier = pltpu.get_barrier_semaphore()
        for device in (core, other):
            pl.semaphore_signal(barrier, inc=1, device_id=device, device_id_type=MESH)
        pl.semaphore_wait(barrier, 2)
        first = [
            pltpu.make_async_remote_copy(
                part.at[theirs, columns(i)], near.at[i], core_send.at[i], core_recv.at[i],
                device_id=core, device_id_type=MESH,
            )
            for i in range(pieces)
        ]
        second = [
            pltpu.make_async_remote_copy(
                mine.at[i], far.at[i], y_send.at[i], y_recv.at[i],
                device_id=other, device_id_type=MESH,
            )
            for i in range(pieces)
        ]
        third = [
            pltpu.make_async_remote_copy(
                out.at[own, columns(i)], out.at[own, columns(i)], back_send.at[i], back_recv.at[i],
                device_id=core, device_id_type=MESH,
            )
            for i in range(pieces)
        ]
        for copy in first:
            copy.start()
        for i in range(pieces):
            first[i].wait_recv()
            mine[i] = part[own, columns(i)] + near[i]
            second[i].start()
        for i in range(pieces):
            second[i].wait_recv()
            out[own, columns(i)] = mine[i] + far[i]
            third[i].start()
        for copy in third:
            copy.wait_recv()
        for copy in first + second + third:
            copy.wait_send()

    def total(identity, *parts):
        if size != 4:
            return lax.psum(parts, "mp")
        joined = jnp.concatenate(parts, axis=1)
        tokens_here, columns_here = joined.shape
        pieces = 1
        for count in (5, 4, 3, 2):
            if columns_here % (128 * count) == 0:
                pieces = count
                break
        half = (pieces, tokens_here // 2, columns_here // pieces)
        summed = pl.pallas_call(
            kernel,
            out_shape=jax.ShapeDtypeStruct(joined.shape, jnp.float32),
            in_specs=[pl.BlockSpec(memory_space=pltpu.VMEM)],
            out_specs=pl.BlockSpec(memory_space=pltpu.VMEM),
            scratch_shapes=[pltpu.VMEM(half, jnp.float32)] * 3
            + [pltpu.SemaphoreType.DMA((pieces,))] * 6,
            compiler_params=pltpu.CompilerParams(
                collective_id=identity, has_side_effects=True, vmem_limit_bytes=16 << 20
            ),
        )(joined)
        edges, start = [], 0
        for part in parts:
            edges.append(summed[:, start : start + part.shape[1]])
            start += part.shape[1]
        return tuple(edges)

    return total


def forward_loop(hidden_state, shared, adapters, tables, total, identity):
    (mixer_gain, feed_gain, query_matrix, pair_matrix, output_matrix, widen_matrix, down_matrix) = shared
    (q_in, q_out, kv_in, kv_out, o_in, o_out, w_in, w_out, d_in, d_out) = adapters
    cosine, sine, allowed = tables
    tokens_here, width = hidden_state.shape
    head = pair_matrix.shape[1] // 2
    heads = query_matrix.shape[1] // head
    rank = q_in.shape[1]
    hidden = down_matrix.shape[0]
    kept = SimpleNamespace(h=hidden_state)
    normed, kept.mixer_factor = normalize(hidden_state, mixer_gain)
    normed = normed.astype(jnp.bfloat16)
    query_rank = product(normed, q_in).astype(jnp.bfloat16)
    query_linear = product(normed, query_matrix) + product(query_rank, q_out)
    pair_rank = product(normed, kv_in.reshape(width, 2 * rank)).astype(jnp.bfloat16)
    pair_linear = product(normed, pair_matrix) + jnp.concatenate(
        [product(pair_rank[:, :rank], kv_out[0]), product(pair_rank[:, rank:], kv_out[1])], axis=1
    )
    queries = rotate(
        query_linear.reshape(tokens_here, heads, head), cosine[:, None], sine[:, None]
    ).astype(jnp.bfloat16)
    keys = rotate(pair_linear[:, :head], cosine, sine).astype(jnp.bfloat16)
    values = pair_linear[:, head:].astype(jnp.bfloat16)
    masked = attention_probs(queries, keys, allowed, 1.0 / math.sqrt(head))
    expo = jnp.exp(masked - jnp.max(masked, axis=-1, keepdims=True))
    probs = expo / jnp.sum(expo, axis=-1, keepdims=True)
    mixed = jnp.einsum(
        "hij,jd->ihd", probs.astype(jnp.bfloat16), values, preferred_element_type=jnp.float32
    )
    mixed = mixed.reshape(tokens_here, heads * head).astype(jnp.bfloat16)
    summed, output_rank = total(identity, product(mixed, output_matrix), product(mixed, o_in))
    middle = hidden_state + summed + exact_product(output_rank, o_out.astype(jnp.float32))
    fed, kept.feed_factor = normalize(middle, feed_gain)
    fed = fed.astype(jnp.bfloat16)
    widen_rank = product(fed, w_in.reshape(width, 2 * rank)).astype(jnp.bfloat16)
    gate = product(fed, widen_matrix[:, 0]) + product(widen_rank[:, :rank], w_out[0])
    up = product(fed, widen_matrix[:, 1]) + product(widen_rank[:, rank:], w_out[1])
    activated = (gelu_tanh(gate) * up).astype(jnp.bfloat16)
    shrunk, shrink_rank = total(identity + 1, product(activated, down_matrix), product(activated, d_in))
    result = middle + shrunk + exact_product(shrink_rank, d_out.astype(jnp.float32))
    vars(kept).update(
        normed=normed, query_rank=query_rank, pair_rank=pair_rank, queries=queries, keys=keys,
        values=values, probs=probs, mixed=mixed, output_rank=output_rank, middle=middle, fed=fed,
        widen_rank=widen_rank, gate=gate, up=up, activated=activated, shrink_rank=shrink_rank,
    )
    return result, kept


def reverse_loop(upstream, kept, shared, adapters, tables, total, identity):
    (mixer_gain, feed_gain, query_matrix, pair_matrix, output_matrix, widen_matrix, down_matrix) = shared
    (q_in, q_out, kv_in, kv_out, o_in, o_out, w_in, w_out, d_in, d_out) = adapters
    cosine, sine, allowed = tables
    tokens_here, width = upstream.shape
    head = pair_matrix.shape[1] // 2
    heads = query_matrix.shape[1] // head
    rank = q_in.shape[1]
    scale = 1.0 / math.sqrt(head)
    grad_feed = upstream.astype(jnp.bfloat16)
    grad_shrink_rank = product_t(grad_feed, d_out).astype(jnp.bfloat16)
    grad_activated = product_t(grad_feed, down_matrix) + product_t(grad_shrink_rank, d_in)
    gelu_value, gelu_pullback = jax.vjp(gelu_tanh, kept.gate)
    grad_gate = gelu_pullback(grad_activated * kept.up)[0].astype(jnp.bfloat16)
    grad_up = (grad_activated * gelu_value).astype(jnp.bfloat16)
    grad_fed, grad_widen_rank = total(
        identity,
        product_t(grad_gate, widen_matrix[:, 0]) + product_t(grad_up, widen_matrix[:, 1]),
        jnp.concatenate([product_t(grad_gate, w_out[0]), product_t(grad_up, w_out[1])], axis=1),
    )
    grad_widen_rank = grad_widen_rank.astype(jnp.bfloat16)
    grad_fed = grad_fed + product_t(grad_widen_rank, w_in.reshape(width, 2 * rank))
    grad_norm, feed_gain_grad = normalize_back(kept.middle, kept.feed_factor, feed_gain, grad_fed)
    grad_middle = upstream + grad_norm
    grad_attend = grad_middle.astype(jnp.bfloat16)
    grad_output_rank = product_t(grad_attend, o_out).astype(jnp.bfloat16)
    grad_mixed = product_t(grad_attend, output_matrix) + product_t(grad_output_rank, o_in)
    grad_mixed = grad_mixed.astype(jnp.bfloat16).reshape(tokens_here, heads, head)
    queries, keys, values, probs = kept.queries, kept.keys, kept.values, kept.probs
    grad_probs = jnp.einsum("ihd,jd->hij", grad_mixed, values, preferred_element_type=jnp.float32)
    delta = jnp.sum(grad_probs * probs, axis=-1, keepdims=True)
    grad_scores = (probs * (grad_probs - delta)).astype(jnp.bfloat16)
    grad_queries = scale * jnp.einsum(
        "hij,jd->ihd", grad_scores, keys, preferred_element_type=jnp.float32
    )
    grad_keys = scale * jnp.einsum(
        "hij,ihd->jd", grad_scores, queries, preferred_element_type=jnp.float32
    )
    grad_values = jnp.einsum(
        "hij,ihd->jd", probs.astype(jnp.bfloat16), grad_mixed, preferred_element_type=jnp.float32
    )
    grad_query = rotate(grad_queries, cosine[:, None], -sine[:, None])
    grad_query = grad_query.reshape(tokens_here, heads * head).astype(jnp.bfloat16)
    grad_normed, grad_query_rank, grad_pair = total(
        identity + 1,
        product_t(grad_query, query_matrix),
        product_t(grad_query, q_out),
        jnp.concatenate([rotate(grad_keys, cosine, -sine), grad_values], axis=1),
    )
    grad_query_rank = grad_query_rank.astype(jnp.bfloat16)
    grad_pair = grad_pair.astype(jnp.bfloat16)
    grad_pair_rank = jnp.concatenate(
        [product_t(grad_pair[:, :head], kv_out[0]), product_t(grad_pair[:, head:], kv_out[1])], axis=1
    ).astype(jnp.bfloat16)
    grad_normed = (
        grad_normed
        + product_t(grad_query_rank, q_in)
        + product_t(grad_pair, pair_matrix)
        + product_t(grad_pair_rank, kv_in.reshape(width, 2 * rank))
    )
    grad_norm, mixer_gain_grad = normalize_back(
        kept.h, kept.mixer_factor, mixer_gain, grad_normed
    )
    vars(kept).update(
        grad_feed=grad_feed, grad_shrink_rank=grad_shrink_rank, grad_gate=grad_gate, grad_up=grad_up,
        grad_widen_rank=grad_widen_rank, grad_attend=grad_attend, grad_output_rank=grad_output_rank,
        grad_query=grad_query, grad_query_rank=grad_query_rank, grad_pair=grad_pair,
        grad_pair_rank=grad_pair_rank, feed_gain_grad=feed_gain_grad, mixer_gain_grad=mixer_gain_grad,
    )
    return grad_middle + grad_norm


def scattered_gradients(kept, dp_size, mp_size):
    def scatter(value, axis):
        return lax.psum_scatter(value, "dp", scatter_dimension=axis, tiled=True)

    def shared_of(factors):
        return sum(product_tn(*factors(k)) for k in kept)

    def each(function):
        return jnp.stack([function(k) for k in kept], axis=0)

    def quarter(value, axis):
        block = scatter(value, axis)
        size = block.shape[axis] // mp_size
        return lax.dynamic_slice_in_dim(block, lax.axis_index("mp") * size, size, axis)

    width = kept[0].normed.shape[1]
    rank = kept[0].query_rank.shape[1]
    head = kept[0].grad_pair.shape[1] // 2

    def pair_outer(k):
        left, right = k.pair_rank, k.grad_pair
        return jnp.stack(
            [product_tn(left[:, :rank], right[:, :head]), product_tn(left[:, rank:], right[:, head:])]
        )

    def expand_outer(k):
        left = k.widen_rank
        return jnp.stack(
            [product_tn(left[:, :rank], k.grad_gate), product_tn(left[:, rank:], k.grad_up)]
        )

    return (
        scatter(sum(k.mixer_gain_grad for k in kept), 0),
        scatter(sum(k.feed_gain_grad for k in kept), 0),
        scatter(shared_of(lambda k: (k.normed, k.grad_query)), 0),
        quarter(shared_of(lambda k: (k.normed, k.grad_pair)), 0),
        scatter(shared_of(lambda k: (k.mixed, k.grad_attend)), 1),
        scatter(jnp.stack([shared_of(lambda k: (k.fed, k.grad_gate)), shared_of(lambda k: (k.fed, k.grad_up))], axis=1), 0),
        scatter(shared_of(lambda k: (k.activated, k.grad_feed)), 1),
        quarter(each(lambda k: product_tn(k.normed, k.grad_query_rank)), 1),
        scatter(each(lambda k: product_tn(k.query_rank, k.grad_query)), 1),
        quarter(
            each(lambda k: product_tn(k.normed, k.grad_pair_rank).reshape(width, 2, rank)), 1
        ),
        quarter(each(pair_outer), 2),
        scatter(each(lambda k: product_tn(k.mixed, k.grad_output_rank)), 2),
        scatter(
            each(lambda k: exact_tn(k.output_rank, k.grad_attend.astype(jnp.float32))), 2
        ),
        quarter(
            each(lambda k: product_tn(k.fed, k.grad_widen_rank).reshape(width, 2, rank)), 1
        ),
        scatter(each(expand_outer), 2),
        scatter(each(lambda k: product_tn(k.activated, k.grad_shrink_rank)), 2),
        scatter(each(lambda k: exact_tn(k.shrink_rank, k.grad_feed.astype(jnp.float32))), 2),
    )


WIDE = 896


def split3(value):
    high = value.astype(jnp.bfloat16)
    rest = value - high.astype(jnp.float32)
    middle = rest.astype(jnp.bfloat16)
    low = (rest - middle.astype(jnp.float32)).astype(jnp.bfloat16)
    return high, middle, low


WEIGHTS = (
    "q_in", "query", "q_out", "kv_in", "pair", "kv_out", "output", "o_in", "o_out",
    "wide", "w_out", "down", "d_in", "d_out", "w_in",
)
SUM_STEP = 384


def block_kernel(*refs):
    (h_in, cot, segments, mixer_gain, feed_gain), refs = refs[:5], refs[5:]
    count = len(WEIGHTS)
    sources, refs = refs[:count], refs[count:]
    (
        out_ref, grad_ref, raw_out, x_all, r_all, b_all, q_all, x_got, r_got, b_got, x_end, r_end, b_end,
    ), refs = refs[:13], refs[13:]
    weights, refs = (*refs[: count - 1], refs[WEIGHTS.index("kv_in")]), refs[count - 1 :]
    (
        h_s, mid_s, normed_s, qr_s, kvr_s, q_s, k_s, v_s, probs_s, mixed_s, or_s, fed_s, er_s,
        gate_s, up_s, act_s, sr_s, gg_s, gu_s, g_s, gain_s, select,
        part, total, near, mine, far, side_part, side_near, side_mine, side_far, side_total,
        late_s, er_grad_s, chosen_s, xs, rs, bs, qs, kv_flat, w_flat, cosine_ref, sine_ref, mask_ref,
        load_sems, c_s, c_r, y_s, y_r, e_s, e_r,
        xl, rl, bl, ql, x_s, x_r, r_s, r_r, b_s, b_r, xe_s, xe_r, re_s, re_r, be_s, be_r, bf_s, bf_r,
        sc_s, sc_r, sy_s, sy_r, se_s, se_r, xc_s, xc_r, rc_s, rc_r, raw_ref, raw_sems,
    ) = refs
    W = SimpleNamespace(**dict(zip(WEIGHTS, weights)))
    dp, mp = lax.axis_index("dp"), lax.axis_index("mp")
    side = lax.rem(mp, 2)
    core = (dp, mp + 1 - 2 * side)
    other = (dp, lax.rem(mp + 2, 4))
    loads = [
        pltpu.make_async_copy(source, target, load_sems.at[i])
        for i, (source, target) in enumerate(zip(sources, weights))
    ]
    load = SimpleNamespace(**dict(zip(WEIGHTS, loads)))
    for copy in loads[:-1]:
        copy.start()
    x = lax.rem(dp, 2)
    z = dp // 2
    pair = (dp + 1 - 2 * x, mp)
    near_end = (dp + 2 - 4 * lax.rem(z, 2), mp)
    is_end = jnp.logical_or(z == 0, z == 3)
    barrier = pltpu.get_barrier_semaphore()
    for device in (core, other, pair, near_end):
        pl.semaphore_signal(barrier, inc=1, device_id=device, device_id_type=MESH)
    pl.semaphore_wait(barrier, 4)

    tokens, width = h_in.shape
    half = tokens // 2
    head = W.query.shape[1]
    rank = W.q_in.shape[2]
    hidden = W.down.shape[0]
    loops = W.q_in.shape[0]
    scale = 1.0 / math.sqrt(head)
    own = pl.ds(pl.multiple_of(side * half, half), half)
    theirs = pl.ds(pl.multiple_of((1 - side) * half, half), half)
    blocks = x_all.shape[1] * x_all.shape[2]
    block = width // blocks
    quarter = block // 4
    rank_quarter = rank // (4 * blocks)
    chunks = [(0, WIDE), (WIDE, hidden - WIDE)]

    def remote(source, target, send, recv, device):
        return pltpu.make_async_remote_copy(
            source, target, send, recv, device_id=device, device_id_type=MESH
        )

    def span(l):
        return pl.ds(pl.multiple_of(l * tokens, tokens), tokens)

    def end_span(l, is_far):
        return pl.ds(pl.multiple_of((2 * l + is_far) * tokens, tokens), tokens)

    def x_copies(i, l):
        across = onward = None
        if i < 2:
            across = remote(
                xs.at[i, 1 - x], x_got.at[i, :, :, span(l)], x_s.at[i, l], x_r.at[i, l], pair
            )
            onward = remote(
                xs.at[i, x], x_end.at[i, :, :, end_span(l, 0)],
                xe_s.at[0, i, l], xe_r.at[0, i, l], near_end,
            )
        return pltpu.make_async_copy(xs.at[i], x_all.at[i, :, :, :, span(l)], xl.at[i, l]), across, onward

    def r_copies(i, l):
        across = onward = None
        if i < 3:
            across = remote(
                rs.at[i, 1 - x], r_got.at[i, :, :, span(l)], r_s.at[i, l], r_r.at[i, l], pair
            )
        if i in (1, 2):
            onward = remote(
                rs.at[i, x], r_end.at[i - 1, :, :, end_span(l, 0)],
                re_s.at[0, i - 1, l], re_r.at[0, i - 1, l], near_end,
            )
        return pltpu.make_async_copy(rs.at[i], r_all.at[i, :, :, :, span(l)], rl.at[i, l]), across, onward

    def b_copies(i, l):
        across = onward = None
        if i in (0, 4, 5):
            k = max(0, i - 3)
            across = remote(bs.at[i], b_got.at[k, span(l)], b_s.at[k, l], b_r.at[k, l], pair)
        if i >= 3:
            k = (i - 4) % 3
            onward = remote(
                bs.at[i], b_end.at[k, end_span(l, 0)], be_s.at[k, l], be_r.at[k, l], near_end
            )
        return pltpu.make_async_copy(bs.at[i], b_all.at[i, span(l)], bl.at[i, l]), across, onward

    def q_copies(i, l):
        return pltpu.make_async_copy(qs.at[i], q_all.at[i, span(l)], ql.at[i, l]), None, None

    def launch(copies, whole=True):
        local, across, onward = copies
        local.start()
        if across is not None:
            across.start()
        if onward is not None:

            @pl.when(is_end if whole else jnp.logical_and(is_end, side == 0))
            def _():
                onward.start()

    def finish(copies, whole=True):
        local, across, onward = copies
        local.wait()
        if across is not None:
            across.wait_send()
        if onward is not None:

            @pl.when(is_end if whole else jnp.logical_and(is_end, side == 0))
            def _():
                onward.wait_send()

    def far_rows(i, l):
        return [
            remote(
                x_got.at[i, :, :, span(l)], x_end.at[i, :, :, end_span(l, 1)],
                xe_s.at[1, i, l], xe_r.at[1, i, l], near_end,
            ),
            remote(
                r_got.at[i + 1, :, :, span(l)], r_end.at[i, :, :, end_span(l, 1)],
                re_s.at[1, i, l], re_r.at[1, i, l], near_end,
            ),
        ]

    def far_act(l):
        return remote(
            b_got.at[1, span(l)], b_end.at[0, end_span(l, 1)], bf_s.at[l], bf_r.at[l], near_end
        )

    def pass_act(l):
        for i in (4, 5):
            b_copies(i, l)[1].wait_recv()

        @pl.when(is_end)
        def _():
            far_act(l).start()

    def pass_rows(i, l):
        x_copies(i, l)[1].wait_recv()
        r_copies(i + 1, l)[1].wait_recv()

        @pl.when(jnp.logical_and(is_end, side == 1))
        def _():
            for copy in far_rows(i, l):
                copy.start()

    def ship_x(i, l, value, again, before):
        @pl.when(again)
        def _():
            finish(x_copies(i, before), False)

        turned = value.astype(jnp.float32).T
        for b in range(blocks):
            xs[i, b % 2, b // 2] = turned[b * block : (b + 1) * block]
        launch(x_copies(i, l), False)

    def ship_r(i, l, value, again, before):
        @pl.when(again)
        def _():
            finish(r_copies(i, before), False)

        turned = value.astype(jnp.float32).T
        size = rank // blocks
        for b in range(blocks):
            rs[i, b % 2, b // 2] = turned[b * size : (b + 1) * size]
        launch(r_copies(i, l), False)

    def ship_b(i, l, values, again, before):
        @pl.when(again)
        def _():
            finish(b_copies(i, before))

        filled = 0
        for value in values:
            n = value.shape[1]
            bs[i, :, filled : filled + n] = value.astype(jnp.float32)
            filled += n
        if filled < WIDE:
            bs[i, :, filled:] = jnp.zeros((tokens, WIDE - filled), jnp.float32)
        launch(b_copies(i, l))

    def ship_q(i, l, value, again, before):
        @pl.when(again)
        def _():
            finish(q_copies(i, before))

        qs[i] = value.astype(jnp.float32)
        launch(q_copies(i, l))

    def columns_of(size):
        return [(at, min(SUM_STEP, size - at)) for at in range(0, size, SUM_STEP)]

    def side_copies(turn, size):
        columns = pl.ds(0, size)
        return (
            remote(
                side_part.at[turn, theirs, columns], side_near.at[turn, :, columns],
                sc_s.at[turn], sc_r.at[turn], core,
            ),
            remote(
                side_mine.at[turn, :, columns], side_far.at[turn, :, columns],
                sy_s.at[turn], sy_r.at[turn], other,
            ),
            remote(
                side_total.at[turn, own, columns], side_total.at[turn, own, columns],
                se_s.at[turn], se_r.at[turn], core,
            ),
        )

    def finish_side(turn, size):
        first, second, third = side_copies(turn, size)
        second.wait_recv()
        side_total[turn, own, :size] = side_mine[turn, :, :size] + side_far[turn, :, :size]
        third.start()
        third.wait_recv()
        for copy in (first, second, third):
            copy.wait_send()
        return side_total[turn, :, :size]

    def sum_over_mp(fill, turn, side_size, finish_previous, idle, side_ahead=False):
        pieces = columns_of(width)

        def pieces_of(make):
            return [make(i, pl.ds(at, n)) for i, (at, n) in enumerate(pieces)]

        first = pieces_of(
            lambda i, c: remote(part.at[theirs, c], near.at[:, c], c_s.at[i], c_r.at[i], core)
        )
        second = pieces_of(
            lambda i, c: remote(
                mine.at[:, c], far.at[turn, :, c], y_s.at[turn, i], y_r.at[turn, i], other
            )
        )
        third = pieces_of(
            lambda i, c: remote(total.at[own, c], total.at[own, c], e_s.at[i], e_r.at[i], core)
        )
        side_first, side_second, _ = side_copies(turn, side_size)

        def middle(i):
            at, n = pieces[i]
            first[i].wait_recv()
            mine[:, at : at + n] = part[own, at : at + n] + near[:, at : at + n]
            second[i].start()

        def begin_side():
            side_first.wait_recv()
            side_mine[turn, :, :side_size] = (
                side_part[turn, own, :side_size] + side_near[turn, :, :side_size]
            )
            finish_previous()
            side_second.start()

        side_behind = jnp.logical_not(side_ahead)
        pl.when(side_ahead)(side_first.start)
        for i, (at, n) in enumerate(pieces):
            fill(at, n)
            first[i].start()
            if i:
                middle(i - 1)
            else:
                pl.when(side_ahead)(begin_side)
        pl.when(side_behind)(side_first.start)
        middle(len(first) - 1)
        pl.when(side_behind)(begin_side)
        idle()
        for i, (at, n) in enumerate(pieces):
            second[i].wait_recv()
            total[own, at : at + n] = mine[:, at : at + n] + far[turn, :, at : at + n]
            third[i].start()
        for copy in third:
            copy.wait_recv()
        for copy in first + second + third:
            copy.wait_send()

    def dot(left, right):
        return jnp.dot(left, right, preferred_element_type=jnp.float32)

    def low(value):
        return value.astype(jnp.bfloat16)

    def spin(value, sign):
        a, b = value[:, : head // 2], value[:, head // 2 :]
        cosine, sine = cosine_ref[...], sign * sine_ref[...]
        return jnp.concatenate([a * cosine - b * sine, b * cosine + a * sine], axis=1)

    def factor_of(value):
        return lax.rsqrt(jnp.mean(value * value, axis=-1, keepdims=True) + EPSILON)

    def gelu_parts(value):
        c = math.sqrt(2.0 / math.pi)
        square = value * value
        t = jnp.tanh(c * value * (1.0 + 0.044715 * square))
        gelu = 0.5 * value * (1.0 + t)
        slope = 0.5 * (1.0 + t) + 0.5 * value * (1.0 - t * t) * c * (1.0 + 3 * 0.044715 * square)
        return gelu, slope

    across_row = jnp.broadcast_to(segments[...].astype(jnp.float32), (tokens, tokens))
    down_row = across_row.T
    at_row = lax.broadcasted_iota(jnp.int32, (tokens, tokens), 0)
    at_column = lax.broadcasted_iota(jnp.int32, (tokens, tokens), 1)
    earlier = jnp.sum(jnp.where(across_row < down_row, 1.0, 0.0), axis=1, keepdims=True)
    position = at_row[:, : head // 2].astype(jnp.float32) - earlier
    exponent = at_column[:, : head // 2].astype(jnp.float32) * (-2.0 / head)
    angles = position * jnp.exp(exponent * math.log(10000.0))
    cosine_ref[...] = jnp.cos(angles)
    sine_ref[...] = jnp.sin(angles)
    mask_ref[...] = jnp.where(
        jnp.logical_and(across_row == down_row, at_row >= at_column), 1.0, 0.0
    )
    h_s[0] = h_in[...].astype(jnp.float32)
    mixer, feed = mixer_gain[...].reshape(1, width), feed_gain[...].reshape(1, width)

    def forward(l, carry):
        def need(*copies):
            @pl.when(l == 0)
            def _():
                for copy in copies:
                    copy.wait()

        h = h_s[l]
        normed = low(h * factor_of(h) * mixer)
        normed_s[l] = normed
        need(load.q_in, load.query, load.q_out, load.kv_in, load.pair, load.kv_out)

        @pl.when(l == 0)
        def _():
            kv_flat[0] = W.kv_in[0].reshape(width, 2 * rank)

        query_rank = low(dot(normed, W.q_in[l]))
        qr_s[l] = query_rank
        queries = dot(normed, W.query[...]) + dot(query_rank, W.q_out[l])
        q_s[l] = low(spin(queries, 1.0))
        pair_rank = low(dot(normed, kv_flat[l]))
        kvr_s[l] = pair_rank
        keys = dot(normed, W.pair[:, :head]) + dot(pair_rank[:, :rank], W.kv_out[l, 0])
        k_s[l] = low(spin(keys, 1.0))
        values = dot(normed, W.pair[:, head:]) + dot(pair_rank[:, rank:], W.kv_out[l, 1])
        v_s[l] = low(values)
        scores = product_t(q_s[l], k_s[l]) * scale
        scores = jnp.where(mask_ref[...] > 0, scores, MASKED)
        expo = jnp.exp(scores - jnp.max(scores, axis=-1, keepdims=True))
        probs = expo / jnp.sum(expo, axis=-1, keepdims=True)
        probs_s[l] = probs
        mixed = low(dot(low(probs), v_s[l]))
        mixed_s[l] = mixed
        need(load.output, load.o_in, load.o_out)

        output_rank = dot(mixed, W.o_in[l])
        side_part[0, :, :rank] = output_rank
        output_parts = split3(output_rank)

        def fill_attend(at, n):
            value = dot(mixed, W.output[:, at : at + n])
            for piece in output_parts:
                value = value + dot(piece, W.o_out[l, :, at : at + n])
            part[:, at : at + n] = value

        again = l > 0

        def idle_attend():
            @pl.when(l == 0)
            def _():
                for i in range(1, loops):
                    kv_flat[i] = W.kv_in[i].reshape(width, 2 * rank)
                load.w_in.start()

            ship_x(2, l, normed, again, 0)
            ship_r(3, l, query_rank, again, 0)
            ship_q(1, l, mixed, again, 0)

            @pl.when(again)
            def _():
                pass_act(0)
                pass_rows(1, loops - 1)

            @pl.when(l == 0)
            def _():
                load.d_out.wait()
                shrink = product_t(cot[...], W.d_out[loops - 1])
                ship_x(1, loops - 1, cot[...], False, 0)
                ship_r(2, loops - 1, low(shrink), False, 0)
                load.w_in.wait()
                w_flat[0] = W.w_in[0].reshape(width, 2 * rank)

        def finish_before_attend():
            @pl.when(again)
            def _():
                sr_s[jnp.maximum(l - 1, 0)] = finish_side(1, rank)

        sum_over_mp(fill_attend, 0, rank, finish_before_attend, idle_attend)
        middle = h_s[l] + total[...]
        mid_s[l] = middle
        fed = low(middle * factor_of(middle) * feed)
        fed_s[l] = fed
        need(load.wide, load.w_out)
        widen_rank = low(dot(fed, w_flat[l]))
        er_s[l] = widen_rank
        for at, n in chunks:
            gate = product_t(fed, W.wide[0, at : at + n]) + product_t(
                widen_rank[:, :rank], W.w_out[l, 0, at : at + n]
            )
            gate_s[l, :, at : at + n] = gate
            up = product_t(fed, W.wide[1, at : at + n]) + product_t(
                widen_rank[:, rank:], W.w_out[l, 1, at : at + n]
            )
            up_s[l, :, at : at + n] = up
            act_s[:, at : at + n] = low(gelu_parts(gate)[0] * up)
            ship_b(4 + at // WIDE, l, [act_s[:, at : at + n]], again, 0)
        need(load.down, load.d_in)

        shrink_rank = dot(act_s[...], W.d_in[l])
        side_part[1, :, :rank] = shrink_rank
        shrink_parts = split3(shrink_rank)

        def fill_feed(at, n):
            value = dot(act_s[...], W.down[:, at : at + n])
            for piece in shrink_parts:
                value = value + dot(piece, W.d_out[l, :, at : at + n])
            part[:, at : at + n] = value

        def idle_feed():
            ship_x(0, l, fed, again, 0)
            ship_r(0, l, widen_rank[:, :rank], again, 0)
            ship_r(1, l, widen_rank[:, rank:], again, 0)

            @pl.when(again)
            def _():
                pass_rows(0, 0)

            @pl.when(l == 0)
            def _():
                for i in range(1, loops):
                    w_flat[i] = W.w_in[i].reshape(width, 2 * rank)

        def finish_before_feed():
            or_s[l] = finish_side(0, rank)

        sum_over_mp(fill_feed, 1, rank, finish_before_feed, idle_feed)
        h_s[l + 1] = mid_s[l] + total[...]
        return carry

    lax.fori_loop(0, loops, forward, 0)
    out_ref[...] = low(h_s[loops])

    g_s[...] = cot[...].astype(jnp.float32)
    gain_s[...] = jnp.zeros_like(gain_s)
    padded_quarter = select.shape[0] // blocks
    row = lax.broadcasted_iota(jnp.int32, (padded_quarter, width), 0)
    column = lax.broadcasted_iota(jnp.int32, (padded_quarter, width), 1)
    for b in range(blocks):
        hit = jnp.logical_and(column == row + (b * 4 + mp) * quarter, row < quarter)
        select[b * padded_quarter : (b + 1) * padded_quarter] = low(
            jnp.where(hit, 1.0, 0.0)
        )
    small_row = lax.broadcasted_iota(jnp.int32, (rank_quarter, rank), 0)
    small_column = lax.broadcasted_iota(jnp.int32, (rank_quarter, rank), 1)
    rank_select = low(
        jnp.concatenate(
            [
                jnp.where(small_column == small_row + (b * 4 + mp) * rank_quarter, 1.0, 0.0)
                for b in range(blocks)
            ],
            axis=0,
        )
    )
    raw_rows = raw_layout(quarter, rank_quarter, loops)

    tall = raw_rows.tall

    def put(start, size, stride, value, add=False):
        for b in range(blocks):
            piece = value[b * stride : b * stride + size]
            if add:
                raw_ref[b % 2, b // 2, start : start + size] += piece
            else:
                raw_ref[b % 2, b // 2, start : start + size] = piece

    def pair_ranks(l, grad_keys, grad_values):
        return low(
            jnp.concatenate(
                [product_t(grad_keys, W.kv_out[l, 0]), product_t(grad_values, W.kv_out[l, 1])], axis=1
            )
        )

    def raw_of(l):
        grad_rank = late_s[l, :, :rank]
        grad_pair = late_s[l, :, rank:]
        grad_pair_rank = pair_ranks(l, grad_pair[:, :head], grad_pair[:, head:])
        grad_widen = er_grad_s[l]
        normed_own = low(product_t(select[...], normed_s[l]))
        pair_weight = dot(normed_own, grad_pair)
        for j in range(2):
            value = pair_weight[:, j * head : (j + 1) * head]
            put(j * tall, tall, padded_quarter, value, l < loops - 1)
        base = 2 * tall + l * raw_rows.loop

        def put_loop(i, value):
            put(base + i * tall, tall, padded_quarter, value)

        put_loop(0, dot(normed_own, grad_rank))
        for j in range(2):
            put_loop(1 + j, dot(normed_own, grad_pair_rank[:, j * rank : (j + 1) * rank]))
        fed_own = low(product_t(select[...], fed_s[l]))
        for j in range(2):
            put_loop(3 + j, dot(fed_own, grad_widen[:, j * rank : (j + 1) * rank]))
        put_loop(5, sum(dot(chosen_s[l, 1], piece) for piece in split3(or_s[l])))
        put_loop(6, sum(dot(chosen_s[l, 0], piece) for piece in split3(sr_s[l])))
        for j in range(2):
            rank_own = low(product_t(rank_select, kvr_s[l, :, j * rank : (j + 1) * rank]))
            put(
                base + 7 * tall + j * rank_quarter, rank_quarter, rank_quarter,
                dot(rank_own, grad_pair[:, j * head : (j + 1) * head]),
            )

    raw_go = [
        pltpu.make_async_copy(raw_ref.at[:, :, rows], raw_out.at[:, :, rows], raw_sems.at[i])
        for i, rows in enumerate((pl.ds(0, raw_rows.gains), pl.ds(raw_rows.gains, 8)))
    ]

    def back(step, carry):
        l = loops - 1 - step
        again = step > 0
        before = loops - 1

        upstream = g_s[...]
        grad_feed = low(upstream)
        grad_shrink = low(product_t(grad_feed, W.d_out[l]))
        for i, (at, n) in enumerate(chunks):
            grad_act = product_t(grad_feed, W.down[at : at + n]) + product_t(
                grad_shrink, W.d_in[l, at : at + n]
            )
            gelu, slope = gelu_parts(gate_s[l, :, at : at + n])
            grad_gate = low(grad_act * up_s[l, :, at : at + n] * slope)
            grad_up = low(grad_act * gelu)
            gg_s[:, at : at + n] = grad_gate
            gu_s[:, at : at + n] = grad_up
            if i == 0:
                ship_b(0, l, [grad_gate], again, before)
                ship_b(2, l, [grad_up], again, before)
            else:
                ahead = WIDE - n
                grad_up = grad_up.astype(jnp.float32)
                ship_b(1, l, [grad_gate, grad_up[:, :ahead]], again, before)
                ship_b(3, l, [grad_up[:, ahead:]], again, before)

        for j, value in enumerate((gg_s, gu_s)):
            side_part[0, :, j * rank : (j + 1) * rank] = dot(value[...], W.w_out[l, j])
        grad_widen = low(side_part[0, :, : 2 * rank])

        def fill_fed(at, n):
            part[:, at : at + n] = (
                dot(gg_s[...], W.wide[0, :, at : at + n])
                + dot(gu_s[...], W.wide[1, :, at : at + n])
                + product_t(grad_widen, w_flat[l, at : at + n])
            )

        def finish_before_fed():
            @pl.when(step == 0)
            def _():
                sr_s[loops - 1] = finish_side(1, rank)

            @pl.when(again)
            def _():
                late_s[loops - 1] = low(finish_side(1, rank + 2 * head))

        def idle_fed():
            @pl.when(again)
            def _():
                ship_x(1, l, grad_feed, True, before)
                ship_r(2, l, grad_shrink, True, before)

            chosen_s[l, 0] = low(product_t(select[...], grad_feed))

            @pl.when(again)
            def _():
                raw_of(loops - 1)

        sum_over_mp(fill_fed, 0, 2 * rank, finish_before_fed, idle_fed)
        grad_fed = total[...]
        middle = mid_s[l]
        factor = factor_of(middle)
        unit = middle * factor
        scaled = grad_fed * feed
        grad_middle = upstream + factor * (
            scaled - unit * jnp.mean(scaled * unit, axis=-1, keepdims=True)
        )
        gain_s[1:2] += jnp.sum(grad_fed * unit, axis=0, keepdims=True)
        g_s[...] = grad_middle
        grad_attend = low(grad_middle)
        grad_output = low(product_t(grad_attend, W.o_out[l]))
        grad_mixed = low(
            product_t(grad_attend, W.output[...]) + product_t(grad_output, W.o_in[l])
        )
        probs = probs_s[l]
        grad_probs = product_t(grad_mixed, v_s[l])
        delta = jnp.sum(grad_probs * probs, axis=-1, keepdims=True)
        grad_scores = low(probs * (grad_probs - delta))
        grad_query = low(spin(dot(grad_scores, k_s[l]) * scale, -1.0))

        grad_rank = product_t(grad_query, W.q_out[l])
        grad_keys = spin(product_tn(grad_scores, q_s[l]) * scale, -1.0)
        grad_values = product_tn(low(probs), grad_mixed)
        side_part[1, :, :rank] = grad_rank
        side_part[1, :, rank : rank + head] = grad_keys
        side_part[1, :, rank + head :] = grad_values
        grad_rank, grad_keys, grad_values = low(grad_rank), low(grad_keys), low(grad_values)
        grad_pair = jnp.concatenate([grad_keys, grad_values], axis=1)
        grad_pair_rank = pair_ranks(l, grad_keys, grad_values)

        def fill_normed(at, n):
            part[:, at : at + n] = (
                product_t(grad_query, W.query[at : at + n])
                + product_t(grad_rank, W.q_in[l, at : at + n])
                + product_t(grad_pair, W.pair[at : at + n])
                + product_t(grad_pair_rank, kv_flat[l, at : at + n])
            )

        def finish_before_normed():
            er_grad_s[l] = low(finish_side(0, 2 * rank))

        def idle_normed():
            ship_q(0, l, grad_query, again, before)
            ship_x(3, l, grad_attend, again, before)
            ship_r(4, l, grad_output, again, before)
            chosen_s[l, 1] = low(product_t(select[...], grad_attend))

            @pl.when(step == 0)
            def _():
                pass_act(loops - 1)
                pass_rows(0, loops - 1)

            @pl.when(again)
            def _():
                pass_rows(1, 0)
                late_s[0] = low(finish_side(1, rank + 2 * head))
                raw_of(0)
                raw_go[0].start()

        sum_over_mp(fill_normed, 1, rank + 2 * head, finish_before_normed, idle_normed, again)
        grad_normed = total[...]
        h = h_s[l]
        factor = factor_of(h)
        unit = h * factor
        scaled = grad_normed * mixer
        g_s[...] += factor * (scaled - unit * jnp.mean(scaled * unit, axis=-1, keepdims=True))
        gain_s[0:1] += jnp.sum(grad_normed * unit, axis=0, keepdims=True)

        return carry

    lax.fori_loop(0, loops, back, 0)
    grad_ref[...] = g_s[...]
    for b in range(blocks):
        ends = jnp.zeros((8, head), jnp.float32)
        raw_ref[b % 2, b // 2, raw_rows.gains :] = ends
        raw_ref[b % 2, b // 2, raw_rows.gains : raw_rows.gains + 2, :block] = gain_s[
            :2, b * block : (b + 1) * block
        ]
    raw_go[1].start()
    for copy in raw_go:
        copy.wait()
    last = loops - 1
    for copies in (
        x_copies(0, last), x_copies(2, last), r_copies(0, last), r_copies(1, last), r_copies(3, last),
        q_copies(1, last), x_copies(1, 0), x_copies(3, 0), r_copies(2, 0), r_copies(4, 0),
        q_copies(0, 0),
    ):
        finish(copies, False)
    for copies in (
        b_copies(4, last), b_copies(5, last), b_copies(0, 0), b_copies(1, 0), b_copies(2, 0),
        b_copies(3, 0),
    ):
        finish(copies)

    def to_core(i, l, half):
        lanes = end_span(l, half)
        x_part, r_part = x_end.at[i, :, :, lanes], r_end.at[i, :, :, lanes]
        return [
            remote(x_part, x_part, xc_s.at[i, l], xc_r.at[i, l], core),
            remote(r_part, r_part, rc_s.at[i, l], rc_r.at[i, l], core),
        ]

    both = [(i, l) for l in range(loops) for i in range(2)]
    for l in range(loops):
        for copies in (r_copies(0, l), b_copies(0, l)):
            copies[1].wait_recv()

    @pl.when(is_end)
    def _():
        for l in range(loops):
            far_act(l).wait_send()

    @pl.when(jnp.logical_and(is_end, side == 1))
    def _():
        for i, l in both:
            for copy in far_rows(i, l):
                copy.wait_send()

    for half in range(2):

        @pl.when(jnp.logical_and(jnp.logical_not(is_end), side == half))
        def _():
            for i, l in both:
                came = far_rows(i, l) if half else [x_copies(i, l)[2], r_copies(i + 1, l)[2]]
                for copy, onward in zip(came, to_core(i, l, half)):
                    copy.wait_recv()
                    onward.start()

    @pl.when(jnp.logical_not(is_end))
    def _():
        for l in range(loops):
            for copy in [b_copies(i, l)[2] for i in (3, 4, 5)] + [far_act(l)]:
                copy.wait_recv()
        for i, l in both:
            for copy in to_core(i, l, 0):
                copy.wait_send()
                copy.wait_recv()


def raw_layout(quarter, rank_quarter, loops):
    tall = quarter
    loop = 7 * tall + 2 * rank_quarter
    gains = 2 * tall + loops * loop
    return SimpleNamespace(tall=tall, loop=loop, gains=gains, all=gains + 8)


def block_and_factors(block_input, cotangent, segments, shared, stacked, dp_size):
    (mixer_gain, feed_gain, query, pair, output, widen, down) = shared
    (q_in, q_out, kv_in, kv_out, o_in, o_out, w_in, w_out, d_in, d_out) = stacked
    tokens, width = block_input.shape
    head = query.shape[1]
    loops, _, rank = q_in.shape
    hidden = down.shape[0]
    weights = (
        q_in, query, q_out, kv_in, pair, kv_out, output, o_in, o_out,
        widen.transpose(1, 2, 0), w_out.swapaxes(2, 3), down, d_in, d_out, w_in,
    )
    layout = raw_layout(width // (4 * dp_size), rank // (4 * dp_size), loops)
    line = dp_size // 2
    f32, bf16 = jnp.float32, jnp.bfloat16
    shape = jax.ShapeDtypeStruct
    block, rank_block, both = width // dp_size, rank // dp_size, loops * tokens
    out_shape = (
        shape((tokens, width), bf16),
        shape((tokens, width), f32),
        shape((2, line, layout.all, head), f32),
        shape((4, 2, line, block, both), f32),
        shape((5, 2, line, rank_block, both), f32),
        shape((6, both, WIDE), f32),
        shape((2, both, head), f32),
        shape((2, line, block, both), f32),
        shape((3, line, rank_block, both), f32),
        shape((3, both, WIDE), f32),
        shape((2, line, block, 2 * both), f32),
        shape((2, line, rank_block, 2 * both), f32),
        shape((3, 2 * both, WIDE), f32),
    )
    vmem = pl.BlockSpec(memory_space=pltpu.VMEM)
    hbm = pl.BlockSpec(memory_space=pl.ANY)
    widest = rank + 2 * head
    pieces = -(-width // SUM_STEP)
    dma = pltpu.SemaphoreType.DMA

    def kept(columns, dtype, count=loops):
        return pltpu.VMEM((count, tokens, columns), dtype)

    scratch = [pltpu.VMEM(w.shape, bf16) for w in weights[:-1]] + [
        kept(width, f32, loops + 1), kept(width, f32), kept(width, bf16), kept(rank, bf16),
        kept(2 * rank, bf16), kept(head, bf16), kept(head, bf16), kept(head, bf16), kept(tokens, f32),
        kept(head, bf16), kept(rank, f32), kept(width, bf16), kept(2 * rank, bf16),
        kept(hidden, f32), kept(hidden, f32), pltpu.VMEM((tokens, hidden), bf16), kept(rank, f32),
        pltpu.VMEM((tokens, hidden), bf16), pltpu.VMEM((tokens, hidden), bf16),
        pltpu.VMEM((tokens, width), f32), pltpu.VMEM((8, width), f32),
        pltpu.VMEM((dp_size * 48, width), bf16),
        pltpu.VMEM((tokens, width), f32), pltpu.VMEM((tokens, width), f32),
        pltpu.VMEM((tokens // 2, width), f32), pltpu.VMEM((tokens // 2, width), f32),
        pltpu.VMEM((2, tokens // 2, width), f32),
        pltpu.VMEM((2, tokens, widest), f32), pltpu.VMEM((2, tokens // 2, widest), f32),
        pltpu.VMEM((2, tokens // 2, widest), f32), pltpu.VMEM((2, tokens // 2, widest), f32),
        pltpu.VMEM((2, tokens, widest), f32),
        kept(widest, bf16), kept(2 * rank, bf16), pltpu.VMEM((loops, 2, dp_size * 48, tokens), bf16),
        pltpu.VMEM((4, 2, line, block, tokens), f32), pltpu.VMEM((5, 2, line, rank_block, tokens), f32),
        pltpu.VMEM((6, tokens, WIDE), f32), pltpu.VMEM((2, tokens, head), f32),
        pltpu.VMEM((loops, width, 2 * rank), bf16), pltpu.VMEM((loops, width, 2 * rank), bf16),
        pltpu.VMEM((tokens, head // 2), f32), pltpu.VMEM((tokens, head // 2), f32),
        pltpu.VMEM((tokens, tokens), f32),
        dma((len(weights),)), dma((pieces,)), dma((pieces,)), dma((2, pieces)), dma((2, pieces)),
        dma((pieces,)), dma((pieces,)),
        dma((4, loops)), dma((5, loops)), dma((6, loops)), dma((2, loops)),
    ]
    scratch += [dma((2, loops))] * 2 + [dma((3, loops))] * 4
    scratch += [dma((2, 2, loops))] * 4 + [dma((3, loops))] * 2 + [dma((loops,))] * 2
    scratch += [dma((2,))] * 6 + [dma((2, loops))] * 4
    scratch += [pltpu.VMEM((2, line, layout.all, head), f32), dma((2,))]
    return pl.pallas_call(
        block_kernel,
        out_shape=out_shape,
        in_specs=[vmem] * 5 + [hbm] * len(weights),
        out_specs=(vmem,) * 2 + (hbm,) * 11,
        scratch_shapes=scratch,
        compiler_params=pltpu.CompilerParams(
            collective_id=21, has_side_effects=True, vmem_limit_bytes=63 << 20
        ),
    )(
        block_input, cotangent, segments, mixer_gain, feed_gain,
        *weights,
    )


def line_kernel(
    raw_all, x_all, r_all, b_all, q_all, x_got, r_got, b_got, x_end_all, r_end_all, b_end_all,
    mixer_out, feed_out, q_w, pair_w, o_w, e_w, s_w, q_i, q_o, p_i, p_o, o_i, o_o, e_i, e_o, s_i, s_o,
    main_out, side_out, raw_out, around,
    x_own, r_own, b_own, q_own, x_far, r_far, b_far, q_far, x_end, r_end, b_end, raw_own, raw_far, product_ref,
    main_right, main_left, side_right, side_left, raw_right, raw_left,
    x_s, x_r, r_s, r_r, b_s, b_r, q_s, q_r, w_s, w_r, local_sems, step_sems, around_s, around_r, ee_s, ee_r,
    mr_s, mr_r, ml_s, ml_r, sr_s, sr_r, sl_s, sl_r, rr_s, rr_r, rl_s, rl_r,
    credit_right, credit_left,
):
    dp, mp = lax.axis_index("dp"), lax.axis_index("mp")
    x = lax.rem(dp, 2)
    z = dp // 2
    last = 3
    pair = (dp + 1 - 2 * x, mp)
    up, down = (dp + 2, mp), (dp - 2, mp)

    core, other = (dp, mp + 1 - 2 * lax.rem(mp, 2)), (dp, lax.rem(mp + 2, 4))
    hidden = s_w.shape[1]
    block, rank_block, quarter = s_w.shape[0], s_i.shape[1], pair_w.shape[0]
    loops, head = s_i.shape[0], q_w.shape[1]
    layout = raw_layout(quarter, rank_block // 4, loops)
    tall = layout.tall
    tail = hidden - WIDE
    short = 2 * hidden - 3 * WIDE

    barrier = pltpu.get_barrier_semaphore()
    for device in (pair, core, other):
        pl.semaphore_signal(barrier, inc=1, device_id=device, device_id_type=MESH)

    @pl.when(z > 0)
    def _():
        pl.semaphore_signal(barrier, inc=1, device_id=down, device_id_type=MESH)

    @pl.when(z < last)
    def _():
        pl.semaphore_signal(barrier, inc=1, device_id=up, device_id_type=MESH)

    def across(source, target, send, recv):
        return pltpu.make_async_remote_copy(
            source, target, send, recv, device_id=pair, device_id_type=MESH
        )

    def x_copy(i):
        return across(x_all.at[i, 1 - x], x_far.at[i], x_s.at[i - 2], x_r.at[i - 2])

    def r_copy(i):
        return across(r_all.at[i, 1 - x], r_far.at[i], r_s.at[i - 3], r_r.at[i - 3])

    def b_copy(i):
        return across(b_all.at[i], b_far.at[i], b_s.at[i], b_r.at[i])

    q_copy = across(q_all, q_far, q_s, q_r)
    w_copy = across(raw_all.at[1 - x], raw_far, w_s, w_r)

    def here(source, target, i):
        return pltpu.make_async_copy(source, target, local_sems.at[i])

    at_start = [
        here(x_all.at[:, x], x_own, 0),
        here(r_all.at[:, x], r_own, 1),
        here(x_got, x_far.at[0:2], 2),
        here(r_got, r_far.at[0:3], 3),
        here(b_got.at[0], b_far.at[0], 4),
        here(b_got.at[1:3], b_far.at[4:6], 5),
        here(q_all, q_own, 6),
    ]
    tokens = b_end.shape[1] // 4

    def end_rows(at):
        return pl.ds(at * tokens, tokens)

    for_ends = [
        here(x_end_all, x_end, 7), here(r_end_all, r_end, 8), here(b_end_all.at[0], b_end.at[0], 9)
    ] + [
        here(b_end_all.at[k, end_rows(2 * l)], b_end.at[k, end_rows(2 * l)], 9 + 2 * k + l)
        for k in (1, 2) for l in range(loops)
    ]

    def end_copies(k):
        return [
            across(
                b_end_all.at[k, end_rows(2 * l)], b_end.at[k, end_rows(2 * l + 1)],
                ee_s.at[k - 1, l], ee_r.at[k - 1, l],
            )
            for l in range(loops)
        ]

    own_copy = here(raw_all.at[x], raw_own, 10)
    inner = jnp.logical_and(z > 0, z < last)

    def chunk_of(step):
        return jnp.where(lax.rem(step, 3) == 0, 4 + step // 3, step - 1 - step // 3)

    def begins_inside(step):
        return jnp.logical_or(lax.rem(step, 3) == 0, step == 5)

    def b_load(step):
        slot = lax.rem(step, 2)
        return pltpu.make_async_copy(b_all.at[chunk_of(step)], b_own.at[slot], step_sems.at[slot])

    b_load(0).start()
    for copy in at_start:
        copy.start()

    @pl.when(inner)
    def _():
        for copy in for_ends:
            copy.start()

    own_copy.start()
    pl.semaphore_wait(barrier, 3 + jnp.minimum(z, 1) + jnp.minimum(last - z, 1))
    b_copy(1).start()
    for copy in at_start[:-1]:
        copy.wait()

    @pl.when(inner)
    def _():
        for copy in for_ends:
            copy.wait()

    def chain(target, step, slot, steps, value, out, right, left, r_s, r_r, l_s, l_r, credits):
        def move(buffer, send, recv, i, s, device, size):
            piece = buffer.at[i, s, :, pl.ds(0, size)]
            return pltpu.make_async_remote_copy(
                piece, piece, send.at[i, s], recv.at[i, s], device_id=device, device_id_type=MESH
            )

        def at_size(act):
            full = right.shape[3]
            if credits:
                pl.when(step < steps - 1)(lambda: act(full))
                pl.when(step == steps - 1)(lambda: act(short))
            else:
                act(full)

        def inside(at):
            return begins_inside(at) if credits else at < 0

        def free(credit, i, source, at, from_end):
            @pl.when(
                jnp.logical_and(
                    at <= steps - 1,
                    jnp.logical_not(jnp.logical_and(from_end, inside(at))),
                )
            )
            def _():
                pl.semaphore_signal(credit.at[i], inc=1, device_id=source, device_id_type=MESH)

        def pass_on(i, place, buffer, send, recv, onward, source, at_end, next_to_end, credit):
            def here(i, s, size=right.shape[3]):
                return move(buffer, send, recv, i, s, onward, size)

            def begin():
                if credits:

                    @pl.when(step >= 3)
                    def _():
                        pl.semaphore_wait(credit.at[i], 1)

                at_size(lambda size: here(i, slot, size).start())

            @pl.when(jnp.logical_and(at_end, jnp.logical_not(inside(step))))
            def _():
                buffer[i, slot] = value()
                if credits:
                    before = lax.rem(step + 2 - inside(step - 1).astype(jnp.int32), 3)
                    after = jnp.where(onward[0] > dp, i - 1, i + 1)

                    @pl.when(jnp.logical_and(place < 2, step >= 2))
                    def _():
                        here(after, before).wait_send()

                    @pl.when(place == 2)
                    def _():
                        at_size(lambda size: here(2 - i, slot, size).wait_send())

                    begin()
                else:
                    begin()
                    here(i, slot).wait_send()

            @pl.when(jnp.logical_not(at_end))
            def _():
                if credits:

                    @pl.when(step >= 1)
                    def _():
                        here(i, lax.rem(step + 2, 3)).wait_send()
                        free(credit, i, source, step + 2, next_to_end)

                has_source = jnp.logical_not(jnp.logical_and(next_to_end, inside(step)))

                @pl.when(jnp.logical_not(has_source))
                def _():
                    buffer[i, slot] = value()

                @pl.when(has_source)
                def _():
                    product = value()
                    at_size(lambda size: here(i, slot, size).wait_recv())
                    buffer[i, slot] += product

                begin()

        @pl.when(target > z)
        def _():
            pass_on(target - 1, 3 - target, right, r_s, r_r, up, down, z == 0, z == 1, credit_right)

        @pl.when(target < z)
        def _():
            pass_on(target, target, left, l_s, l_r, down, up, z == last, z == last - 1, credit_left)

        @pl.when(target == z)
        def _():
            out[...] = value()

    def arrive(step, slot, steps, out, right, left, r_s, r_r, l_s, l_r, credits):
        def take(buffer, send, recv, i, size):
            piece = buffer.at[i, slot, :, pl.ds(0, size)]
            pltpu.make_async_remote_copy(
                piece, piece, send.at[i, slot], recv.at[i, slot], device_id=pair, device_id_type=MESH
            ).wait_recv()
            out[:, :size] += buffer[i, slot, :, :size]

        started_inside = begins_inside(step) if credits else step < 0

        def side_of(there, from_end, buffer, send, recv, i, credit, source):
            @pl.when(there)
            def _():
                quiet = jnp.logical_and(from_end, started_inside)

                @pl.when(jnp.logical_not(quiet))
                def _():
                    full = buffer.shape[3]
                    if credits:
                        pl.when(step < steps - 1)(lambda: take(buffer, send, recv, i, full))
                        pl.when(step == steps - 1)(lambda: take(buffer, send, recv, i, short))
                    else:
                        take(buffer, send, recv, i, full)

                if credits:
                    skip = jnp.logical_and(from_end, begins_inside(step + 3))

                    @pl.when(jnp.logical_and(step + 3 <= steps - 1, jnp.logical_not(skip)))
                    def _():
                        pl.semaphore_signal(
                            credit.at[i], inc=1, device_id=source, device_id_type=MESH
                        )

        side_of(z > 0, z == 1, right, r_s, r_r, jnp.maximum(z - 1, 0), credit_right, down)
        side_of(z < last, z == last - 1, left, l_s, l_r, jnp.minimum(z, last - 1), credit_left, up)

    def settle(right, left, r_s, l_s, main):
        def wait(buffer, send, i, slot, size, device):
            piece = buffer.at[i, slot, :, pl.ds(0, size)]
            pltpu.make_async_remote_copy(
                piece, piece, send.at[i, slot], send.at[i, slot], device_id=device, device_id_type=MESH
            ).wait_send()

        full = right.shape[3]
        slot, size = (2, short) if main else (0, full)
        for target in range(1, 4):

            @pl.when(jnp.logical_and(target > z, z > 0))
            def _():
                wait(right, r_s, target - 1, slot, size, up)

        for target in range(3):

            @pl.when(jnp.logical_and(target < z, z < last))
            def _():
                wait(left, l_s, target, slot, size, down)

        if main:

            @pl.when(z == 0)
            def _():
                for i in (0, 1):
                    wait(right, r_s, i, 1, full, up)

            @pl.when(z == last)
            def _():
                for i in (1, 2):
                    wait(left, l_s, i, 1, full, down)

    def order(turn):
        def near(end):
            return jnp.where(end == 0, 3 - turn, jnp.where(turn < 2, 3 - turn, turn - 2))

        return jnp.where(z < 2, near(z), 3 - near(3 - z))

    def dot(left, right):
        return jnp.dot(
            left.astype(jnp.bfloat16), right.astype(jnp.bfloat16), preferred_element_type=jnp.float32
        )

    steps = b_all.shape[0]

    def left_times(x_index, group, target, own, far):
        shared = dot(x_own[x_index, target], own) + dot(x_far[x_index, target], far)
        return [shared, *rank_times(group, target, own, far)]

    def rank_times(group, target, own, far):
        half = own.shape[0] // 2
        rank_own, rank_far = r_own[group, target], r_far[group, target]
        return [
            dot(rank_own[:, :half], own[:half]) + dot(rank_far[:, :half], far[:half]),
            dot(rank_own[:, half:], own[half:]) + dot(rank_far[:, half:], far[half:]),
        ]

    def main_arrive(step):
        slot = lax.rem(step, 3)
        chunk = chunk_of(step)
        arrive(
            step, slot, steps, main_out.at[slot], main_right, main_left, mr_s, mr_r, ml_s, ml_r, True,
        )
        parts = (
            (0, 0, 0, 0, WIDE), (1, 0, 0, WIDE, tail), (1, tail, 1, WIDE, WIDE - tail),
            (2, 0, 1, 0, WIDE), (3, 0, 1, 2 * WIDE - tail, short),
        )
        for which, start, j, at, n in parts:

            @pl.when(chunk == which)
            def _():
                e_w[:, j, at : at + n] = main_out[slot, :block, start : start + n]
                for l in range(loops):
                    first = block + l * rank_block
                    e_o[l, j, :, at : at + n] = main_out[
                        slot, first : first + rank_block, start : start + n
                    ]

        for part, (at, n) in enumerate(((0, WIDE), (WIDE, tail))):

            @pl.when(chunk == 4 + part)
            def _():
                s_w[:, at : at + n] = main_out[slot, :block, :n]
                for l in range(loops):
                    first = block + l * rank_block
                    s_i[l, :, at : at + n] = main_out[slot, first : first + rank_block, :n]

    def turn_body(at, carry):
        step, turn = at // 4, lax.rem(at, 4)
        slot = lax.rem(step, 3)
        chunk = chunk_of(step)
        group = chunk // 2
        target = order(turn)

        @pl.when(turn == 0)
        def _():
            b_load(step).wait()

            @pl.when(step < steps - 1)
            def _():
                b_load(step + 1).start()

            @pl.when(jnp.logical_and(chunk >= 1, chunk <= 3))
            def _():
                b_copy(chunk).wait_recv()

            @pl.when(step == 1)
            def _():
                @pl.when(inner)
                def _():
                    for copy in end_copies(1):
                        copy.start()

                b_copy(2).start()

            @pl.when(step == 2)
            def _():
                @pl.when(inner)
                def _():
                    for copy in end_copies(2):
                        copy.start()

                b_copy(3).start()

            @pl.when(step == 3)
            def _():
                w_copy.start()

                @pl.when(inner)
                def _():
                    for copy in end_copies(1):
                        copy.wait_recv()

            @pl.when(step == 4)
            def _():
                x_copy(2).start()
                x_copy(3).start()
                r_copy(3).start()
                r_copy(4).start()
                q_copy.start()

            @pl.when(jnp.logical_and(step == 5, inner))
            def _():
                for copy in end_copies(2):
                    copy.wait_recv()

        def value():
            parts = left_times(
                group // 2, group, target,
                b_own[lax.rem(step, 2)].astype(jnp.bfloat16), b_far[chunk].astype(jnp.bfloat16),
            )
            product_ref[...] = jnp.concatenate(parts, axis=0)

            @pl.when(chunk == 1)
            def _():
                other_rank = rank_times(
                    1, target, b_own[lax.rem(step, 2)].astype(jnp.bfloat16),
                    b_far[1].astype(jnp.bfloat16),
                )
                kept = product_ref[block:]
                column = lax.broadcasted_iota(jnp.int32, kept.shape, 1)
                product_ref[block:] = jnp.where(
                    column < tail, kept, jnp.concatenate(other_rank, axis=0)
                )

            beyond = jnp.logical_or(
                jnp.logical_and(z == 1, target >= 1),
                jnp.logical_and(z == last - 1, target <= last - 1),
            )

            @pl.when(jnp.logical_and(beyond, chunk >= 3))
            def _():
                end = b_end[jnp.where(chunk == 3, 2, jnp.maximum(chunk - 4, 0))].astype(jnp.bfloat16)
                shared = jnp.where(chunk == 3, 0, 1)
                middle = end.shape[0] // 2
                product_ref[...] += jnp.concatenate(
                    [
                        dot(x_end[shared, target], end),
                        dot(r_end[shared, target, :, :middle], end[:middle]),
                        dot(r_end[shared, target, :, middle:], end[middle:]),
                    ],
                    axis=0,
                )

            return product_ref[...]

        chain(
            target, step, slot, steps, value, main_out.at[slot], main_right, main_left,
            mr_s, mr_r, ml_s, ml_r, True,
        )

        @pl.when(jnp.logical_and(turn == 3, step >= 2))
        def _():
            main_arrive(step - 2)

        return carry

    lax.fori_loop(0, 4 * steps, turn_body, 0)

    w_copy.wait_recv()
    own_copy.wait()
    at_start[-1].wait()

    def raw_body(turn, carry):
        target = order(turn)
        chain(
            target, 0, 0, 1, lambda: raw_own[target] + raw_far[target], raw_out, raw_right, raw_left,
            rr_s, rr_r, rl_s, rl_r, False,
        )
        return carry

    lax.fori_loop(0, 4, raw_body, 0)
    main_arrive(jnp.int32(steps - 2))

    for i in (2, 3):
        x_copy(i).wait_recv()
    for i in (3, 4):
        r_copy(i).wait_recv()
    q_copy.wait_recv()

    def side_body(turn, carry):
        target = order(turn)

        def value():
            parts = [
                left_times(
                    2 + i, 3 + i, target, q_own[i].astype(jnp.bfloat16), q_far[i].astype(jnp.bfloat16)
                )
                for i in range(2)
            ]
            return jnp.concatenate([jnp.concatenate(p, axis=0) for p in parts], axis=1)

        chain(
            target, 0, 0, 1, value, side_out, side_right, side_left,
            sr_s, sr_r, sl_s, sl_r, False,
        )
        return carry

    lax.fori_loop(0, 4, side_body, 0)
    main_arrive(jnp.int32(steps - 1))
    arrive(0, 0, 1, raw_out, raw_right, raw_left, rr_s, rr_r, rl_s, rl_r, False)

    def share(device, owner, i):
        return pltpu.make_async_remote_copy(
            around.at[owner], around.at[owner], around_s.at[i], around_r.at[i],
            device_id=device, device_id_type=MESH,
        )

    far_owner = lax.rem(mp + 2, 4)
    for l in range(loops):
        start = 2 * tall + l * layout.loop + 5 * tall
        around[mp, l] = raw_out[start : start + 2 * tall]
    along, same, passed = share(other, mp, 0), share(core, mp, 1), share(core, far_owner, 2)
    along.start()
    same.start()
    arrive(0, 0, 1, side_out, side_right, side_left, sr_s, sr_r, sl_s, sl_r, False)
    along.wait_recv()
    passed.start()
    q_w[...] = side_out[:block, :head]
    o_w[...] = side_out[:block, head:]
    for l in range(loops):
        start = block + l * rank_block
        q_o[l] = side_out[start : start + rank_block, :head]
        o_i[l] = side_out[start : start + rank_block, head:]
    mixer_out[...] = raw_out[layout.gains, :block]
    feed_out[...] = raw_out[layout.gains + 1, :block]
    for j in range(2):
        pair_w[:, j * head : (j + 1) * head] = raw_out[j * tall : j * tall + quarter]
    for l in range(loops):
        base = 2 * tall + l * layout.loop
        q_i[:, l] = raw_out[base : base + quarter]
        for j in range(2):
            start = base + (1 + j) * tall
            p_i[l, :, j] = raw_out[start : start + quarter]
            e_i[l, :, j] = raw_out[start + 2 * tall : start + 2 * tall + quarter]
            start = base + 7 * tall + j * (rank_block // 4)
            p_o[l, j] = raw_out[start : start + rank_block // 4]
    same.wait_recv()
    passed.wait_recv()
    for l in range(loops):
        for m in range(4):
            o_o[l, m * quarter : (m + 1) * quarter] = around[m, l, :quarter]
            s_o[l, m * quarter : (m + 1) * quarter] = around[m, l, tall : tall + quarter]
    for copy in (along, same, passed):
        copy.wait_send()

    settle(main_right, main_left, mr_s, ml_s, True)
    settle(side_right, side_left, sr_s, sl_s, False)
    settle(raw_right, raw_left, rr_s, rl_s, False)
    @pl.when(inner)
    def _():
        for copy in end_copies(1) + end_copies(2):
            copy.wait_send()

    for copy in (x_copy(2), x_copy(3), r_copy(3), r_copy(4), b_copy(1), b_copy(2), b_copy(3)):
        copy.wait_send()
    q_copy.wait_send()
    w_copy.wait_send()


def line_gradients(factors, loops, dp_size, mp_size, hidden):
    raw, x_all, r_all, b_all, q_all, x_got, r_got, b_got, x_end, r_end, b_end = factors
    block, rank_block, head = x_all.shape[3], r_all.shape[3], q_all.shape[2]
    quarter, rank_quarter = block // mp_size, rank_block // mp_size
    layout = raw_layout(quarter, rank_quarter, loops)
    rows = block + loops * rank_block
    steps = b_all.shape[0]
    vmem = pl.BlockSpec(memory_space=pltpu.VMEM)
    hbm = pl.BlockSpec(memory_space=pl.ANY)
    dma = pltpu.SemaphoreType.DMA
    f32 = jnp.float32
    line = dp_size // 2 - 1
    half_x = pltpu.VMEM((x_all.shape[0], *x_all.shape[2:]), f32)
    half_r = pltpu.VMEM((r_all.shape[0], *r_all.shape[2:]), f32)
    whole_b, whole_q = pltpu.VMEM(b_all.shape, f32), pltpu.VMEM(q_all.shape, f32)
    shapes = (
        (block,), (block,), (block, head), (quarter, 2 * head), (block, head), (block, 2, hidden),
        (block, hidden), (quarter, loops, head), (loops, rank_block, head), (loops, quarter, 2, head),
        (loops, 2, rank_quarter, head), (loops, rank_block, head), (loops, block, head),
        (loops, quarter, 2, head), (loops, 2, rank_block, hidden), (loops, rank_block, hidden),
        (loops, block, head),
    )
    return pl.pallas_call(
        line_kernel,
        out_shape=tuple(jax.ShapeDtypeStruct(v, f32) for v in shapes),
        in_specs=[hbm] * 11,
        out_specs=(vmem,) * len(shapes),
        scratch_shapes=[
            pltpu.VMEM((3, rows, WIDE), f32), pltpu.VMEM((rows, 2 * head), f32),
            pltpu.VMEM((layout.all, head), f32), pltpu.VMEM((4, loops, 2 * layout.tall, head), f32),
        ]
        + [half_x, half_r, pltpu.VMEM((2, *b_all.shape[1:]), f32), whole_q]
        + [half_x, half_r, whole_b, whole_q]
        + [pltpu.VMEM(v.shape, f32) for v in (x_end, r_end, b_end)]
        + [pltpu.VMEM(raw.shape[1:], f32)] * 2
        + [pltpu.VMEM((rows, WIDE), f32)]
        + [pltpu.VMEM((line, 3, rows, WIDE), f32)] * 2
        + [pltpu.VMEM((line, 1, rows, 2 * head), f32)] * 2
        + [pltpu.VMEM((line, 1, layout.all, head), f32)] * 2
        + [dma((2,))] * 4 + [dma((steps,))] * 2 + [dma] * 4 + [dma((15,)), dma((2,)), dma((3,)), dma((3,))]
        + [dma((2, loops))] * 2
        + [dma((line, 3))] * 4 + [dma((line, 1))] * 8
        + [pltpu.SemaphoreType.REGULAR((line,))] * 2,
        compiler_params=pltpu.CompilerParams(
            collective_id=20, has_side_effects=True, vmem_limit_bytes=63 << 20
        ),
    )(*factors)


def in_place(results):
    mixer, feed, q_w, pair_w, o_w, e_w, s_w, q_i, q_o, p_i, p_o, o_i, o_o, e_i, e_o, s_i, s_o = results
    return (
        mixer, feed, q_w, pair_w, o_w.T, e_w, s_w.T, q_i.swapaxes(0, 1), q_o, p_i, p_o,
        o_i.swapaxes(1, 2), o_o.swapaxes(1, 2), e_i, e_o, s_i.swapaxes(1, 2), s_o.swapaxes(1, 2),
    )


def copy_kernel(*refs):
    count = (len(refs) - 2) // 3
    sources, targets, rooms = refs[:count], refs[count : 2 * count], refs[2 * count : 3 * count]
    come = [pltpu.make_async_copy(v, room, refs[-2].at[i]) for i, (v, room) in enumerate(zip(sources, rooms))]
    go = [pltpu.make_async_copy(room, v, refs[-1].at[i]) for i, (v, room) in enumerate(zip(targets, rooms))]
    by_size = sorted(range(count), key=lambda i: -math.prod(sources[i].shape))
    for i in by_size:
        come[i].start()
    for i in by_size:
        come[i].wait()
        go[i].start()
    for copy in go:
        copy.wait()


def placed(values):
    hbm = pl.BlockSpec(memory_space=pl.ANY)
    sems = pltpu.SemaphoreType.DMA((len(values),))
    return pl.pallas_call(
        copy_kernel,
        out_shape=tuple(jax.ShapeDtypeStruct(v.shape, v.dtype) for v in values),
        in_specs=[hbm] * len(values),
        out_specs=(hbm,) * len(values),
        scratch_shapes=[pltpu.VMEM(v.shape, v.dtype) for v in values] + [sems, sems],
        compiler_params=pltpu.CompilerParams(vmem_limit_bytes=60 << 20),
    )(*values)


def per_device(dp_size, mp_size, block_input, cotangent, segments, *parameters):
    shared, stacked = parameters[:7], parameters[7:]
    loops = stacked[0].shape[0]
    if dp_size == 8 and mp_size == 4 and loops == 2:
        output, input_grad, *factors = block_and_factors(
            block_input, cotangent, segments, shared, stacked, dp_size
        )
        gradients = line_gradients(factors, loops, dp_size, mp_size, shared[6].shape[0])
        output, input_grad, *gradients = placed((output, input_grad, *gradients))
        gradients = in_place(gradients)
        return (output, input_grad, *gradients)
    tables = rotary_tables(segments[0], shared[3].shape[1] // 2)
    total = mp_total(mp_size)
    state = block_input.astype(jnp.float32)
    kept_all = []
    for i in range(loops):
        state, kept = forward_loop(state, shared, [v[i] for v in stacked], tables, total, 1)
        kept_all.append(kept)
    upstream = cotangent.astype(jnp.float32)
    for i in reversed(range(loops)):
        upstream = reverse_loop(
            upstream, kept_all[i], shared, [v[i] for v in stacked], tables, total, 3
        )
    return (state.astype(jnp.bfloat16), upstream, *scattered_gradients(kept_all, dp_size, mp_size))


def solution(mesh):
    in_specs = (
        P("dp", None),
        P("dp", None),
        P("dp", None),
        P(),
        P(),
        P(None, "mp"),
        P(),
        P("mp", None),
        P(None, None, "mp"),
        P("mp", None),
        P(),
        P(None, None, "mp"),
        P(),
        P(),
        P(None, "mp", None),
        P(),
        P(),
        P(None, None, None, "mp"),
        P(None, "mp", None),
        P(),
    )
    out_specs = (
        P("dp", None),
        P("dp", None),
        P("dp"),
        P("dp"),
        P("dp", "mp"),
        P(("dp", "mp"), None),
        P("mp", "dp"),
        P("dp", None, "mp"),
        P("mp", "dp"),
        P(None, ("dp", "mp"), None),
        P(None, "dp", "mp"),
        P(None, ("dp", "mp"), None, None),
        P(None, None, ("dp", "mp"), None),
        P(None, "mp", "dp"),
        P(None, None, "dp"),
        P(None, ("dp", "mp"), None, None),
        P(None, None, "dp", "mp"),
        P(None, "mp", "dp"),
        P(None, None, "dp"),
    )
    return jax.shard_map(
        functools.partial(per_device, mesh.shape["dp"], mesh.shape["mp"]),
        mesh=mesh, in_specs=in_specs, out_specs=out_specs, check_vma=False
    )
```
